256 devices in a mesh: rep: 32 (over z_hi, y, core), fsdp: 8 (over z_lo, x).
Axes of the slice: x: 4, y: 4, z: 8 (z_hi: 4, z_lo: 2; z = z_hi * 2 + z_lo), core: 2. Of those that a mesh axis runs over, the one named last changes fastest.
Arguments:
- gradients: bfloat16 [32, 8, 4, 64, 5120], P('rep', 'fsdp'), may hold values from -6 to 6
- momentum: float32 [32, 4, 64, 5120], P('rep', None, 'fsdp'), may hold values from -45 to 45
Outputs:
- new_momentum: float32 [32, 4, 64, 5120], P('rep', None, 'fsdp')
- update: float32 [4, 64, 5120], P(None, 'fsdp')
The draws below stay inside these ranges and needn't reach their ends.
All inputs are finite; a program needn't handle non-finite values.
Results may differ from the reference program's by a relative error of at most 0.0003.
Values sent between devices are 32-bit elements; how exact they have to be, the bound alone decides.
A program may use at most 64 MiB of HBM per device.

```python
import math
import jax
import jax.numpy as jnp
from jax import lax

D = 5120
MATS = 4
GROUP = 64
KEEP = 8
ROWS = 64
N_REP = 32
N_FSDP = 8


def draw_momentum(key, part):
    key = jax.random.fold_in(key, 11)
    base_key, row_key, col_key = jax.random.split(key, 3)
    full_shape = (N_REP, MATS, ROWS, D)
    row_scale = jnp.exp(jax.random.uniform(row_key, (N_REP, MATS, ROWS, 1), jnp.float32, 0.0, math.log(3.2)))
    col_scale = jnp.exp(jax.random.uniform(col_key, (1, 1, 1, D), jnp.float32, 0.0, math.log(3.2)))
    entries = jnp.clip(jax.random.normal(base_key, full_shape, jnp.float32), -4.0, 4.0)
    return (entries * row_scale * col_scale).astype(jnp.float32)


def strengthened(array, rng, source, target, blocks, factor):
    def block_of(position):
        return (jnp.arange(array.shape[position]) // (array.shape[position] // blocks)).reshape((-1,) + (1,) * (array.ndim - 1 - position))

    first = jax.random.permutation(rng, blocks)[block_of(target)]
    second = (block_of(target) + blocks // 2) % blocks
    return jnp.where((block_of(source) == first) | (block_of(source) == second), factor * array, array)


def levels(stream_key, shape, pieces, least, top_value):
    loudness = 1.0
    for position, shards_of in pieces:
        draws = jax.random.uniform(jax.random.fold_in(jax.random.fold_in(stream_key, 6), position), (shards_of,), jnp.float32, least / len(pieces), top_value / len(pieces))
        loudness = loudness * jnp.repeat(jnp.exp(draws), shape[position] // shards_of).reshape((-1,) + (1,) * (len(shape) - 1 - position))
    return loudness


def heavy_noise(stream_key, dims, deviation, limit, pieces, heavy, held_as=jnp.bfloat16):
    values = deviation * jax.random.normal(stream_key, dims, jnp.float32)
    if pieces:
        values = values * levels(stream_key, dims, pieces, -0.22, 0.18)
    return jnp.clip(strengthened(values, jax.random.fold_in(stream_key, 3), *heavy), -limit, limit).astype(held_as)


def setup_inputs(seed: int = 0) -> dict:
    key_list = jax.random.split(jax.random.key(seed), 3)
    return {
        "gradients": heavy_noise(key_list[0], (N_REP, N_FSDP, MATS, ROWS, D), 0.35, 6.0, ((0, 32), (1, 8)), (1, 3, 8, 2.0)),
        "momentum": draw_momentum(jax.random.fold_in(key_list[2], 71), 0),
    }


BETA = 0.999
EPS = 1e-06

def dct_table():
    freq_index = jnp.arange(KEEP, dtype=jnp.float32)[:, None]
    cell_index = jnp.arange(GROUP, dtype=jnp.float32)[None, :]
    cosines = jnp.sqrt(2.0 / GROUP) * jnp.cos(jnp.pi * (cell_index + 0.5) * freq_index / GROUP)
    first_row = jnp.where(jnp.arange(KEEP)[:, None] == 0, jnp.sqrt(0.5), 1.0)
    return cosines * first_row

def forward(field, cosines):
    blocks = field.reshape(field.shape[:-1] + (D // GROUP, GROUP))
    coeffs = jnp.einsum('...cn,kn->...ck', blocks, cosines, precision=lax.Precision.HIGHEST)
    return coeffs.reshape(field.shape[:-1] + (D // GROUP * KEEP,))

def inverse(coeffs, cosines):
    blocks = coeffs.reshape(coeffs.shape[:-1] + (D // GROUP, KEEP))
    field = jnp.einsum('...ck,kn->...cn', blocks, cosines, precision=lax.Precision.HIGHEST)
    return field.reshape(coeffs.shape[:-1] + (D,))

def soft_sign(low_field):
    blocks = low_field.reshape(low_field.shape[:-1] + (D // GROUP, GROUP))
    mean_square = lax.optimization_barrier(jnp.mean(blocks * blocks, axis=-1, keepdims=True))
    result = blocks / jnp.sqrt(blocks * blocks + mean_square + EPS)
    return result.reshape(low_field.shape)

def reference(gradients, momentum):
    cosines = dct_table()

    def per_replica(pair):
        grad_block, moment_block = pair
        summed = lax.optimization_barrier(jnp.sum(grad_block.astype(jnp.float32), axis=0))
        accumulated = BETA * moment_block + summed
        coeffs = forward(accumulated, cosines)
        return (accumulated - inverse(coeffs, cosines), coeffs)
    new_momentum, coeffs = lax.map(per_replica, (gradients, momentum))
    mean_coeffs = lax.optimization_barrier(jnp.sum(coeffs, axis=0)) / N_REP
    update = soft_sign(inverse(mean_coeffs, cosines))
    return (new_momentum, update)
```

```python
import jax
import jax.numpy as jnp
import ml_dtypes
import numpy as np
from jax import lax
from jax.experimental import pallas as pl
from jax.experimental.pallas import tpu as pltpu
from jax.sharding import PartitionSpec as P

D, MATS, GROUP, KEEP, ROWS = 5120, 4, 64, 8, 64
BETA, EPS = 0.999, 1e-06
NX, NY, NZL, NZH, NC, N_REP = 4, 4, 2, 4, 2, 32
OWN = 8
LANES = 128
TILES = 8
SPAN = LANES * TILES
GROUPS = D // SPAN
HIGH = 7 * LANES
LOW = GROUPS * LANES
GRAD = MATS * ROWS
MINE = MATS * OWN
NM = 2

Z_GROUPS = (0, 1)
X_GROUPS = (2, 3, 4)
F32, BF16 = jnp.float32, jnp.bfloat16
MESH = pl.DeviceIdType.MESH


def split(table):
    high = table.astype(ml_dtypes.bfloat16)
    low = (table - high.astype(np.float64)).astype(ml_dtypes.bfloat16)
    return high, low


def tables():
    n, k = np.arange(GROUP), np.arange(GROUP)[:, None]
    basis = np.sqrt(2.0 / GROUP) * np.cos(np.pi * (n + 0.5) * k / GROUP)
    basis[0] *= np.sqrt(0.5)
    rest = GROUP - KEEP
    high = np.zeros((LANES, 2 * rest))
    for b in range(2):
        high[b * GROUP : (b + 1) * GROUP, b * rest : (b + 1) * rest] = basis[KEEP:].T
    forward = np.zeros((7, 2 * LANES, LANES))
    for t in range(7):
        forward[t, :LANES, : 2 * rest] = high
        forward[t, LANES:, 2 * rest :] = high[:, 16 * t : 16 * t + 16]
    inverse = np.zeros((7, LANES, 2 * LANES))
    for t in range(7):
        inverse[t] = forward[t].T
    blocks = SPAN // GROUP
    keep = np.zeros((SPAN, LANES))
    mean = np.zeros((LANES, SPAN))
    for c in range(blocks):
        keep[c * GROUP : (c + 1) * GROUP, c * KEEP : (c + 1) * KEEP] = basis[:KEEP].T
        mean[c * KEEP : (c + 1) * KEEP, c * GROUP : (c + 1) * GROUP] = 1.0 / GROUP
    both = lambda table: np.concatenate(split(table), axis=-1)
    back = np.concatenate([both(keep.T), mean.astype(ml_dtypes.bfloat16)], axis=-1)
    return both(forward), both(keep), both(inverse), back


def halves(value):
    top = value.astype(BF16)
    return top, (value - top.astype(F32)).astype(BF16)


def dot(a, b):
    return jnp.dot(a, b, preferred_element_type=F32)


X_UNITS = [(g, h * NM) for g in X_GROUPS for h in range(MATS // NM)]
Z_UNITS = [(g, h * NM) for g in Z_GROUPS for h in range(MATS // NM)]
N_SEMS = 4 * len(X_UNITS) + 4 * len(Z_UNITS) + 1 + 3 + 3 + 1 + 3 + 7
N_RECV = N_SEMS


def kernel(
    grads, momentum, fw_hbm, fl_hbm, iv_hbm, lv_hbm, new_out, upd_out,
    xin, mom, fw, fl, iv, lv, s, lw,
    xr2, xra, xrb, xrz, zr4, zr2, zra, zrb,
    la, lb, lc, ld, le, total, nm, up,
    load_sem, store_sem, send_sem, recv_sem,
):
    rep, fsdp = lax.axis_index("rep"), lax.axis_index("fsdp")
    core, y, zh = lax.rem(rep, 2), lax.rem(lax.div(rep, 2), 4), lax.div(rep, 8)
    x, z = lax.rem(fsdp, 4), lax.div(fsdp, 4)

    def ring(v, d):
        return lax.rem(v + (d + 4), 4)

    def device(dzh=0, dy=0, dcore=0, dz=0, dx=0):
        c2 = 1 - core if dcore else core
        z2 = 1 - z if dz else z
        return ((ring(zh, dzh) * 4 + ring(y, dy)) * 2 + c2, z2 * 4 + ring(x, dx))

    partners = [device(dy=dy, dcore=dc) for dy in range(4) for dc in range(2) if dy or dc]
    partners += [device(dx=1), device(dx=2), device(dx=3), device(dz=1)]
    partners += [device(dzh=d) for d in (1, 2, 3)]
    barrier = pltpu.get_barrier_semaphore()
    for p in partners:
        pl.semaphore_signal(barrier, inc=1, device_id=p, device_id_type=MESH)

    used = [0]
    pending = []

    def remote(src, dst, to, sem=None):
        i = used[0]
        used[0] += 1
        return pltpu.make_async_remote_copy(
            src_ref=src, dst_ref=dst, send_sem=send_sem.at[i], recv_sem=recv_sem.at[i],
            device_id=to, device_id_type=MESH,
        )

    def send(src, dst, to):
        copy = remote(src, dst, to)
        copy.start()
        pending.append(copy)
        return copy

    loads = []

    def load(src, dst):
        copy = pltpu.make_async_copy(src, dst, load_sem.at[len(loads)])
        copy.start()
        loads.append(copy)
        return copy

    def load_group(g):
        cols = pl.ds(g * SPAN, SPAN)
        return load(grads.at[:, cols], xin.at[pl.ds(0, GRAD), cols])

    order = (X_GROUPS[0], Z_GROUPS[0], X_GROUPS[1], Z_GROUPS[1], X_GROUPS[2])
    load_mom = load(momentum, mom)
    load_fw = load(fw_hbm, fw)
    group_loads = {order[0]: load_group(order[0])}
    load_fl = load(fl_hbm, fl)
    for g in order[1:]:
        group_loads[g] = load_group(g)
    load_iv = load(iv_hbm, iv)
    load_lv = load(lv_hbm, lv)

    load_mom.wait()
    for g in range(GROUPS):
        cols = slice(g * SPAN, (g + 1) * SPAN)
        top, rest = halves(BETA * mom[:, cols])
        xin[GRAD : GRAD + MINE, cols] = top
        xin[GRAD + MINE :, cols] = rest
    load_fw.wait()

    def fold(v):
        v = v[:, :LANES] + v[:, LANES:]
        own = v[GRAD : GRAD + MINE] + v[GRAD + MINE :]
        return v[:GRAD].reshape(MATS, NZL, NX, OWN, LANES), own.reshape(MATS, OWN, LANES)

    def forward(g):
        group_loads[g].wait()
        base = g * SPAN
        last = xin[:, base + HIGH : base + SPAN]
        for t in range(7):
            both = jnp.concatenate([xin[:, base + t * LANES : base + (t + 1) * LANES], last], axis=1)
            value, own = fold(dot(both, fw[t]))
            lanes = slice(t * LANES, (t + 1) * LANES)
            s[g, :, :, :, :, lanes] = value
            s[g, :, z, x, :, lanes] += own

    def forward_low(g):
        value, own = fold(dot(xin[:, g * SPAN : (g + 1) * SPAN], fl[...]))
        lanes = slice(g * LANES, (g + 1) * LANES)
        lw[:, :, :, :, lanes] = value
        lw[:, z, x, :, lanes] += own

    xd, zd = {}, {}
    way = lambda u: 1 if u % 2 == 0 else -1

    def x_start(u):
        g, m = X_UNITS[u]
        d, part = way(u), s.at[g, pl.ds(m, NM)]
        two = send(part.at[:, :, ring(x, 2)], xr2.at[u], device(dx=d))
        one = send(part.at[:, :, ring(x, -d)], xra.at[u], device(dx=-d))
        xd[u] = [two, one]

    def x_pass(u):
        g, m = X_UNITS[u]
        d = way(u)
        xd[u][0].wait_recv()
        to = ring(x, d)
        s[g, m : m + NM, :, to] += xr2[u]
        xd[u].append(send(s.at[g, pl.ds(m, NM), :, to], xrb.at[u], device(dx=d)))

    def x_cross(u):
        g, m = X_UNITS[u]
        xd[u][1].wait_recv()
        xd[u][2].wait_recv()
        s[g, m : m + NM, :, x] += xra[u] + xrb[u]
        xd[u].append(send(s.at[g, pl.ds(m, NM), 1 - z, x], xrz.at[u], device(dz=1)))

    def x_end(u):
        g, m = X_UNITS[u]
        xd[u][3].wait_recv()
        return s[g, m : m + NM, z, x] + xrz[u]

    def z_start(u):
        g, m = Z_UNITS[u]
        zd[u] = [send(s.at[g, pl.ds(m, NM), 1 - z], zr4.at[u], device(dz=1))]

    def z_cross(u):
        g, m = Z_UNITS[u]
        d, part = way(u), s.at[g, pl.ds(m, NM), z]
        zd[u][0].wait_recv()
        s[g, m : m + NM, z] += zr4[u]
        zd[u].append(send(part.at[:, ring(x, 2)], zr2.at[u], device(dx=d)))
        zd[u].append(send(part.at[:, ring(x, -d)], zra.at[u], device(dx=-d)))

    def z_pass(u):
        g, m = Z_UNITS[u]
        d = way(u)
        zd[u][1].wait_recv()
        to = ring(x, d)
        s[g, m : m + NM, z, to] += zr2[u]
        zd[u].append(send(s.at[g, pl.ds(m, NM), z, to], zrb.at[u], device(dx=d)))

    def z_end(u):
        g, m = Z_UNITS[u]
        zd[u][2].wait_recv()
        zd[u][3].wait_recv()
        return s[g, m : m + NM, z, x] + (zra[u] + zrb[u])

    stores = []

    def store(src, dst):
        copy = pltpu.make_async_copy(src, dst, store_sem.at[len(stores)])
        copy.start()
        stores.append(copy)

    def backward(g, parts):
        field = jnp.concatenate(parts, axis=0).reshape(MINE, HIGH)
        last = jnp.zeros((MINE, LANES), F32)
        for t in range(7):
            top, rest = halves(field[:, t * LANES : (t + 1) * LANES])
            v = dot(jnp.concatenate([top, rest], axis=0), iv[t])
            v = v[:MINE, : 2 * LANES] + (v[MINE:, : 2 * LANES] + v[:MINE, 2 * LANES :])
            base = g * SPAN + t * LANES
            nm[:, base : base + LANES] = v[:, :LANES]
            last += v[:, LANES:]
        nm[:, g * SPAN + HIGH : (g + 1) * SPAN] = last
        cols = pl.ds(g * SPAN, SPAN)
        store(nm.at[:, cols], new_out.at[:, cols])

    def units(all_units, g):
        return [u for u, (h, _) in enumerate(all_units) if h == g]

    def each(step, all_units, g):
        return [step(u) for u in units(all_units, g)]

    def normalise():
        for g in range(GROUPS):
            lanes = slice(g * LANES, (g + 1) * LANES)
            mean = total[:, :, lanes].reshape(MINE, LANES) * (1.0 / N_REP)
            v = dot(jnp.concatenate(halves(mean), axis=0), lv[:, : 2 * SPAN])
            low = v[:MINE, :SPAN] + (v[MINE:, :SPAN] + v[:MINE, SPAN:])
            v = dot(jnp.concatenate(halves(mean * mean), axis=0), lv[:, 2 * SPAN :])
            square = v[:MINE] + v[MINE:]
            up[:, g * SPAN : (g + 1) * SPAN] = low * lax.rsqrt(low * low + square + EPS)
        store(up, upd_out)

    inside = core == z

    forward(order[0])
    pl.semaphore_wait(barrier, len(partners))
    each(x_start, X_UNITS, order[0])
    forward(order[1])
    each(z_start, Z_UNITS, order[1])
    load_fl.wait()
    for g in order[2:]:
        forward(g)
        if g in X_GROUPS:
            each(x_start, X_UNITS, g)
        else:
            each(z_start, Z_UNITS, g)
    for g in range(GROUPS):
        forward_low(g)

    low_a = send(lw.at[:, 1 - core], la, device(dcore=1))
    each(x_pass, X_UNITS, X_GROUPS[0])
    low_a.wait_recv()
    lw[:, core] += la[...]
    low_b = [send(lw.at[ring(y, d), core], lb.at[d - 1], device(dy=d)) for d in (1, 2, 3)]
    each(x_pass, X_UNITS, X_GROUPS[1])
    for copy in low_b:
        copy.wait_recv()
    lw[y, core] += lb[0] + lb[1] + lb[2]
    low_c = [send(lw.at[y, core, ring(x, d)], lc.at[d - 1], device(dx=d)) for d in (1, 2, 3)]
    each(x_pass, X_UNITS, X_GROUPS[2])
    each(x_cross, X_UNITS, X_GROUPS[0])
    for copy in low_c:
        copy.wait_recv()
    lw[y, core, x] += lc[0] + lc[1] + lc[2]
    low_d = remote(lw.at[y, core, x], ld, device(dz=1))

    @pl.when(core != z)
    def _():
        low_d.start()

    each(z_cross, Z_UNITS, Z_GROUPS[0])
    each(x_cross, X_UNITS, X_GROUPS[1])
    low_e = [remote(lw.at[y, core, x], le.at[d - 1], device(dzh=d)) for d in (1, 2, 3)]

    @pl.when(core == z)
    def _():
        low_d.wait_recv()
        lw[y, core, x] += ld[...]
        for copy in low_e:
            copy.start()

    each(z_cross, Z_UNITS, Z_GROUPS[1])
    each(x_cross, X_UNITS, X_GROUPS[2])
    low_f = [
        remote(total.at[y], total.at[y], device(dy=dy, dcore=dc))
        for dy in range(4) for dc in range(2) if dy or dc
    ]

    @pl.when(core == z)
    def _():
        for copy in low_e:
            copy.wait_recv()
        total[y] = lw[y, core, x] + (le[0] + le[1] + le[2])
        for copy in low_f:
            copy.start()

    each(z_pass, Z_UNITS, Z_GROUPS[0])
    each(z_pass, Z_UNITS, Z_GROUPS[1])
    load_iv.wait()
    load_lv.wait()
    for g in X_GROUPS[:2]:
        backward(g, each(x_end, X_UNITS, g))

    same = [copy for copy, (dy, dc) in zip(low_f, [(a, b) for a in range(4) for b in range(2) if a or b]) if dc == 0]
    across = [copy for copy, (dy, dc) in zip(low_f, [(a, b) for a in range(4) for b in range(2) if a or b]) if dc == 1]

    @pl.when(core == z)
    def _():
        for copy in same:
            copy.wait_recv()

    @pl.when(core != z)
    def _():
        for copy in across:
            copy.wait_recv()

    normalise()
    backward(X_GROUPS[2], each(x_end, X_UNITS, X_GROUPS[2]))
    for g in Z_GROUPS:
        backward(g, each(z_end, Z_UNITS, g))

    for copy in pending:
        copy.wait_send()

    @pl.when(core != z)
    def _():
        low_d.wait_send()

    @pl.when(core == z)
    def _():
        for copy in low_e + low_f:
            copy.wait_send()

    for copy in stores:
        copy.wait()


def per_device(gradients, momentum):
    fw, fl, iv, lv = tables()
    any_space = pl.BlockSpec(memory_space=pl.ANY)
    nx, nz = len(X_UNITS), len(Z_UNITS)
    new_momentum, update = pl.pallas_call(
        kernel,
        out_shape=[jax.ShapeDtypeStruct((MINE, D), F32)] * 2,
        in_specs=[any_space] * 6,
        out_specs=[any_space] * 2,
        scratch_shapes=[
            pltpu.VMEM((GRAD + 2 * MINE, D), BF16),
            pltpu.VMEM((MINE, D), F32),
            pltpu.VMEM(fw.shape, BF16),
            pltpu.VMEM(fl.shape, BF16),
            pltpu.VMEM(iv.shape, BF16),
            pltpu.VMEM(lv.shape, BF16),
            pltpu.VMEM((GROUPS, MATS, NZL, NX, OWN, HIGH), F32),
            pltpu.VMEM((MATS, NZL, NX, OWN, LOW), F32),
            pltpu.VMEM((nx, NM, NZL, OWN, HIGH), F32),
            pltpu.VMEM((nx, NM, NZL, OWN, HIGH), F32),
            pltpu.VMEM((nx, NM, NZL, OWN, HIGH), F32),
            pltpu.VMEM((nx, NM, OWN, HIGH), F32),
            pltpu.VMEM((nz, NM, NX, OWN, HIGH), F32),
            pltpu.VMEM((nz, NM, OWN, HIGH), F32),
            pltpu.VMEM((nz, NM, OWN, HIGH), F32),
            pltpu.VMEM((nz, NM, OWN, HIGH), F32),
            pltpu.VMEM((MATS, NX, OWN, LOW), F32),
            pltpu.VMEM((3, NX, OWN, LOW), F32),
            pltpu.VMEM((3, OWN, LOW), F32),
            pltpu.VMEM((OWN, LOW), F32),
            pltpu.VMEM((3, OWN, LOW), F32),
            pltpu.VMEM((MATS, OWN, LOW), F32),
            pltpu.VMEM((MINE, D), F32),
            pltpu.VMEM((MINE, D), F32),
            pltpu.SemaphoreType.DMA((GROUPS + 5,)),
            pltpu.SemaphoreType.DMA((GROUPS + 1,)),
            pltpu.SemaphoreType.DMA((N_SEMS,)),
            pltpu.SemaphoreType.DMA((N_SEMS,)),
        ],
        compiler_params=pltpu.CompilerParams(
            collective_id=0, has_side_effects=True, vmem_limit_bytes=48 * 1024 * 1024
        ),
        cost_estimate=pl.CostEstimate(flops=2_000_000_000, bytes_accessed=8_000_000, transcendentals=200_000),
    )(gradients.reshape(GRAD, D), momentum.reshape(MINE, D), fw, fl, iv, lv)
    return new_momentum.reshape(1, MATS, OWN, D), update.reshape(MATS, OWN, D)


def solution(mesh):
    return jax.shard_map(
        per_device,
        mesh=mesh,
        in_specs=(P("rep", "fsdp", None, None, None), P("rep", None, "fsdp", None)),
        out_specs=(P("rep", None, "fsdp", None), P(None, "fsdp", None)),
        check_vma=False,
    )
```

```python
import jax
import jax.numpy as jnp
import ml_dtypes
import numpy as np
from jax import lax
from jax.experimental import pallas as pl
from jax.experimental.pallas import tpu as pltpu
from jax.sharding import PartitionSpec as P

D, MATS, GROUP, KEEP, ROWS = 5120, 4, 64, 8, 64
BETA, EPS = 0.999, 1e-06
NX, NY, NZL, NZH, NC, N_REP = 4, 4, 2, 4, 2, 32
OWN = 8
LANES = 128
TILES = 8
SPAN = LANES * TILES
GROUPS = D // SPAN
HIGH = 7 * LANES
LOW = GROUPS * LANES
GRAD = MATS * ROWS
MINE = MATS * OWN
NM = 2

Z_GROUPS = (0, 1)
X_GROUPS = (2, 3, 4)
F32, BF16 = jnp.float32, jnp.bfloat16
MESH = pl.DeviceIdType.MESH


def split(table):
    high = table.astype(ml_dtypes.bfloat16)
    low = (table - high.astype(np.float64)).astype(ml_dtypes.bfloat16)
    return high, low


def tables():
    n, k = np.arange(GROUP), np.arange(GROUP)[:, None]
    basis = np.sqrt(2.0 / GROUP) * np.cos(np.pi * (n + 0.5) * k / GROUP)
    basis[0] *= np.sqrt(0.5)
    rest = GROUP - KEEP
    high = np.zeros((LANES, 2 * rest))
    for b in range(2):
        high[b * GROUP : (b + 1) * GROUP, b * rest : (b + 1) * rest] = basis[KEEP:].T
    forward = np.zeros((7, 2 * LANES, LANES))
    for t in range(7):
        forward[t, :LANES, : 2 * rest] = high
        forward[t, LANES:, 2 * rest :] = high[:, 16 * t : 16 * t + 16]
    inverse = np.zeros((7, LANES, 2 * LANES))
    for t in range(7):
        inverse[t] = forward[t].T
    blocks = SPAN // GROUP
    keep = np.zeros((SPAN, LANES))
    mean = np.zeros((LANES, SPAN))
    for c in range(blocks):
        keep[c * GROUP : (c + 1) * GROUP, c * KEEP : (c + 1) * KEEP] = basis[:KEEP].T
        mean[c * KEEP : (c + 1) * KEEP, c * GROUP : (c + 1) * GROUP] = 1.0 / GROUP
    both = lambda table: np.concatenate(split(table), axis=-1)
    back = np.concatenate([both(keep.T), mean.astype(ml_dtypes.bfloat16)], axis=-1)
    return both(forward), both(keep), both(inverse), back


def halves(value):
    top = value.astype(BF16)
    return top, (value - top.astype(F32)).astype(BF16)


def dot(a, b):
    return jnp.dot(a, b, preferred_element_type=F32)


X_UNITS = [(g, h * NM) for g in X_GROUPS for h in range(MATS // NM)]
Z_UNITS = [(g, h * NM) for g in Z_GROUPS for h in range(MATS // NM)]
N_SEMS = 4 * len(X_UNITS) + 4 * len(Z_UNITS) + 1 + 3 + 3 + 1 + 3 + 7
N_RECV = N_SEMS


def kernel(
    grads, momentum, fw_hbm, fl_hbm, iv_hbm, lv_hbm, new_out, upd_out,
    xin, mom, fw, fl, iv, lv, s, lw,
    xr2, xra, xrb, xrz, zr4, zr2, zra, zrb,
    la, lb, lc, ld, le, total, nm, up,
    load_sem, store_sem, send_sem, recv_sem,
):
    rep, fsdp = lax.axis_index("rep"), lax.axis_index("fsdp")
    core, y, zh = lax.rem(rep, 2), lax.rem(lax.div(rep, 2), 4), lax.div(rep, 8)
    x, z = lax.rem(fsdp, 4), lax.div(fsdp, 4)

    def ring(v, d):
        return lax.rem(v + (d + 4), 4)

    def device(dzh=0, dy=0, dcore=0, dz=0, dx=0):
        c2 = 1 - core if dcore else core
        z2 = 1 - z if dz else z
        return ((ring(zh, dzh) * 4 + ring(y, dy)) * 2 + c2, z2 * 4 + ring(x, dx))

    partners = [device(dy=dy, dcore=dc) for dy in range(4) for dc in range(2) if dy or dc]
    partners += [device(dx=1), device(dx=2), device(dx=3), device(dz=1)]
    partners += [device(dzh=d) for d in (1, 2, 3)]
    barrier = pltpu.get_barrier_semaphore()
    for p in partners:
        pl.semaphore_signal(barrier, inc=1, device_id=p, device_id_type=MESH)

    used = [0]
    pending = []

    def remote(src, dst, to, sem=None):
        i = used[0]
        used[0] += 1
        return pltpu.make_async_remote_copy(
            src_ref=src, dst_ref=dst, send_sem=send_sem.at[i], recv_sem=recv_sem.at[i],
            device_id=to, device_id_type=MESH,
        )

    def send(src, dst, to):
        copy = remote(src, dst, to)
        copy.start()
        pending.append(copy)
        return copy

    loads = []

    def load(src, dst):
        copy = pltpu.make_async_copy(src, dst, load_sem.at[len(loads)])
        copy.start()
        loads.append(copy)
        return copy

    def load_group(g):
        cols = pl.ds(g * SPAN, SPAN)
        return load(grads.at[:, cols], xin.at[pl.ds(0, GRAD), cols])

    order = (X_GROUPS[0], Z_GROUPS[0], X_GROUPS[1], Z_GROUPS[1], X_GROUPS[2])
    load_mom = load(momentum, mom)
    load_fw = load(fw_hbm, fw)
    group_loads = {order[0]: load_group(order[0])}
    load_fl = load(fl_hbm, fl)
    for g in order[1:]:
        group_loads[g] = load_group(g)
    load_iv = load(iv_hbm, iv)
    load_lv = load(lv_hbm, lv)

    load_mom.wait()
    for g in range(GROUPS):
        cols = slice(g * SPAN, (g + 1) * SPAN)
        top, rest = halves(BETA * mom[:, cols])
        xin[GRAD : GRAD + MINE, cols] = top
        xin[GRAD + MINE :, cols] = rest
    load_fw.wait()

    def fold(v):
        v = v[:, :LANES] + v[:, LANES:]
        own = v[GRAD : GRAD + MINE] + v[GRAD + MINE :]
        return v[:GRAD].reshape(MATS, NZL, NX, OWN, LANES), own.reshape(MATS, OWN, LANES)

    def forward(g):
        group_loads[g].wait()
        base = g * SPAN
        last = xin[:, base + HIGH : base + SPAN]
        for t in range(7):
            both = jnp.concatenate([xin[:, base + t * LANES : base + (t + 1) * LANES], last], axis=1)
            value, own = fold(dot(both, fw[t]))
            lanes = slice(t * LANES, (t + 1) * LANES)
            s[g, :, :, :, :, lanes] = value
            s[g, :, z, x, :, lanes] += own

    def forward_low(g):
        value, own = fold(dot(xin[:, g * SPAN : (g + 1) * SPAN], fl[...]))
        lanes = slice(g * LANES, (g + 1) * LANES)
        lw[:, :, :, :, lanes] = value
        lw[:, z, x, :, lanes] += own

    xd, zd = {}, {}
    way = lambda u: 1 if u % 2 == 0 else -1

    def x_start(u):
        g, m = X_UNITS[u]
        d, part = way(u), s.at[g, pl.ds(m, NM)]
        two = send(part.at[:, :, ring(x, 2)], xr2.at[u], device(dx=d))
        one = send(part.at[:, :, ring(x, -d)], xra.at[u], device(dx=-d))
        xd[u] = [two, one]

    def x_pass(u):
        g, m = X_UNITS[u]
        d = way(u)
        xd[u][0].wait_recv()
        to = ring(x, d)
        s[g, m : m + NM, :, to] += xr2[u]
        xd[u].append(send(s.at[g, pl.ds(m, NM), :, to], xrb.at[u], device(dx=d)))

    def x_cross(u):
        g, m = X_UNITS[u]
        xd[u][1].wait_recv()
        xd[u][2].wait_recv()
        s[g, m : m + NM, :, x] += xra[u] + xrb[u]
        xd[u].append(send(s.at[g, pl.ds(m, NM), 1 - z, x], xrz.at[u], device(dz=1)))

    def x_end(u):
        g, m = X_UNITS[u]
        xd[u][3].wait_recv()
        return s[g, m : m + NM, z, x] + xrz[u]

    def z_start(u):
        g, m = Z_UNITS[u]
        zd[u] = [send(s.at[g, pl.ds(m, NM), 1 - z], zr4.at[u], device(dz=1))]

    def z_cross(u):
        g, m = Z_UNITS[u]
        d, part = way(u), s.at[g, pl.ds(m, NM), z]
        zd[u][0].wait_recv()
        s[g, m : m + NM, z] += zr4[u]
        zd[u].append(send(part.at[:, ring(x, 2)], zr2.at[u], device(dx=d)))
        zd[u].append(send(part.at[:, ring(x, -d)], zra.at[u], device(dx=-d)))

    def z_pass(u):
        g, m = Z_UNITS[u]
        d = way(u)
        zd[u][1].wait_recv()
        to = ring(x, d)
        s[g, m : m + NM, z, to] += zr2[u]
        zd[u].append(send(s.at[g, pl.ds(m, NM), z, to], zrb.at[u], device(dx=d)))

    def z_end(u):
        g, m = Z_UNITS[u]
        zd[u][2].wait_recv()
        zd[u][3].wait_recv()
        return s[g, m : m + NM, z, x] + (zra[u] + zrb[u])

    stores = []

    def store(src, dst):
        copy = pltpu.make_async_copy(src, dst, store_sem.at[len(stores)])
        copy.start()
        stores.append(copy)

    def backward(g, parts):
        field = jnp.concatenate(parts, axis=0).reshape(MINE, HIGH)
        last = jnp.zeros((MINE, LANES), F32)
        for t in range(7):
            top, rest = halves(field[:, t * LANES : (t + 1) * LANES])
            v = dot(jnp.concatenate([top, rest], axis=0), iv[t])
            v = v[:MINE, : 2 * LANES] + (v[MINE:, : 2 * LANES] + v[:MINE, 2 * LANES :])
            base = g * SPAN + t * LANES
            nm[:, base : base + LANES] = v[:, :LANES]
            last += v[:, LANES:]
        nm[:, g * SPAN + HIGH : (g + 1) * SPAN] = last
        cols = pl.ds(g * SPAN, SPAN)
        store(nm.at[:, cols], new_out.at[:, cols])

    def units(all_units, g):
        return [u for u, (h, _) in enumerate(all_units) if h == g]

    def each(step, all_units, g):
        return [step(u) for u in units(all_units, g)]

    def normalise():
        for g in range(GROUPS):
            lanes = slice(g * LANES, (g + 1) * LANES)
            mean = total[:, :, lanes].reshape(MINE, LANES) * (1.0 / N_REP)
            v = dot(jnp.concatenate(halves(mean), axis=0), lv[:, : 2 * SPAN])
            low = v[:MINE, :SPAN] + (v[MINE:, :SPAN] + v[:MINE, SPAN:])
            v = dot(jnp.concatenate(halves(mean * mean), axis=0), lv[:, 2 * SPAN :])
            square = v[:MINE] + v[MINE:]
            up[:, g * SPAN : (g + 1) * SPAN] = low * lax.rsqrt(low * low + square + EPS)
        store(up, upd_out)

    inside = core == z

    forward(order[0])
    pl.semaphore_wait(barrier, len(partners))
    each(x_start, X_UNITS, order[0])
    forward(order[1])
    each(z_start, Z_UNITS, order[1])
    load_fl.wait()
    for g in order[2:]:
        forward(g)
        if g in X_GROUPS:
            each(x_start, X_UNITS, g)
        else:
            each(z_start, Z_UNITS, g)
    for g in range(GROUPS):
        forward_low(g)

    low_a = send(lw.at[:, 1 - core], la, device(dcore=1))
    each(x_pass, X_UNITS, X_GROUPS[0])
    low_a.wait_recv()
    lw[:, core] += la[...]
    low_b = [send(lw.at[ring(y, d), core], lb.at[d - 1], device(dy=d)) for d in (1, 2, 3)]
    each(x_pass, X_UNITS, X_GROUPS[1])
    for copy in low_b:
        copy.wait_recv()
    lw[y, core] += lb[0] + lb[1] + lb[2]
    low_c = [send(lw.at[y, core, ring(x, d)], lc.at[d - 1], device(dx=d)) for d in (1, 2, 3)]
    each(x_pass, X_UNITS, X_GROUPS[2])
    each(x_cross, X_UNITS, X_GROUPS[0])
    for copy in low_c:
        copy.wait_recv()
    lw[y, core, x] += lc[0] + lc[1] + lc[2]
    low_d = remote(lw.at[y, core, x], ld, device(dz=1))

    @pl.when(core != z)
    def _():
        low_d.start()

    each(z_cross, Z_UNITS, Z_GROUPS[0])
    each(x_cross, X_UNITS, X_GROUPS[1])
    low_e = [remote(lw.at[y, core, x], le.at[d - 1], device(dzh=d)) for d in (1, 2, 3)]

    @pl.when(core == z)
    def _():
        low_d.wait_recv()
        lw[y, core, x] += ld[...]
        for copy in low_e:
            copy.start()

    each(z_cross, Z_UNITS, Z_GROUPS[1])
    each(x_cross, X_UNITS, X_GROUPS[2])
    low_f = [
        remote(total.at[y], total.at[y], device(dy=dy, dcore=dc))
        for dy in range(4) for dc in range(2) if dy or dc
    ]

    @pl.when(core == z)
    def _():
        for copy in low_e:
            copy.wait_recv()
        total[y] = lw[y, core, x] + (le[0] + le[1] + le[2])
        for copy in low_f:
            copy.start()

    each(z_pass, Z_UNITS, Z_GROUPS[0])
    each(z_pass, Z_UNITS, Z_GROUPS[1])
    load_iv.wait()
    load_lv.wait()
    for g in X_GROUPS[:2]:
        backward(g, each(x_end, X_UNITS, g))

    same = [copy for copy, (dy, dc) in zip(low_f, [(a, b) for a in range(4) for b in range(2) if a or b]) if dc == 0]
    across = [copy for copy, (dy, dc) in zip(low_f, [(a, b) for a in range(4) for b in range(2) if a or b]) if dc == 1]

    @pl.when(core == z)
    def _():
        for copy in same:
            copy.wait_recv()

    @pl.when(core != z)
    def _():
        for copy in across:
            copy.wait_recv()

    normalise()
    backward(X_GROUPS[2], each(x_end, X_UNITS, X_GROUPS[2]))
    for g in Z_GROUPS:
        backward(g, each(z_end, Z_UNITS, g))

    for copy in pending:
        copy.wait_send()

    @pl.when(core != z)
    def _():
        low_d.wait_send()

    @pl.when(core == z)
    def _():
        for copy in low_e + low_f:
            copy.wait_send()

    for copy in stores:
        copy.wait()


def per_device(gradients, momentum):
    fw, fl, iv, lv = tables()
    hbm = pl.BlockSpec(memory_space=pltpu.HBM)
    nx, nz = len(X_UNITS), len(Z_UNITS)
    new_momentum, update = pl.pallas_call(
        kernel,
        out_shape=[jax.ShapeDtypeStruct((MINE, D), F32)] * 2,
        in_specs=[hbm] * 6,
        out_specs=[hbm] * 2,
        scratch_shapes=[
            pltpu.VMEM((GRAD + 2 * MINE, D), BF16),
            pltpu.VMEM((MINE, D), F32),
            pltpu.VMEM(fw.shape, BF16),
            pltpu.VMEM(fl.shape, BF16),
            pltpu.VMEM(iv.shape, BF16),
            pltpu.VMEM(lv.shape, BF16),
            pltpu.VMEM((GROUPS, MATS, NZL, NX, OWN, HIGH), F32),
            pltpu.VMEM((MATS, NZL, NX, OWN, LOW), F32),
            pltpu.VMEM((nx, NM, NZL, OWN, HIGH), F32),
            pltpu.VMEM((nx, NM, NZL, OWN, HIGH), F32),
            pltpu.VMEM((nx, NM, NZL, OWN, HIGH), F32),
            pltpu.VMEM((nx, NM, OWN, HIGH), F32),
            pltpu.VMEM((nz, NM, NX, OWN, HIGH), F32),
            pltpu.VMEM((nz, NM, OWN, HIGH), F32),
            pltpu.VMEM((nz, NM, OWN, HIGH), F32),
            pltpu.VMEM((nz, NM, OWN, HIGH), F32),
            pltpu.VMEM((MATS, NX, OWN, LOW), F32),
            pltpu.VMEM((3, NX, OWN, LOW), F32),
            pltpu.VMEM((3, OWN, LOW), F32),
            pltpu.VMEM((OWN, LOW), F32),
            pltpu.VMEM((3, OWN, LOW), F32),
            pltpu.VMEM((MATS, OWN, LOW), F32),
            pltpu.VMEM((MINE, D), F32),
            pltpu.VMEM((MINE, D), F32),
            pltpu.SemaphoreType.DMA((GROUPS + 5,)),
            pltpu.SemaphoreType.DMA((GROUPS + 1,)),
            pltpu.SemaphoreType.DMA((N_SEMS,)),
            pltpu.SemaphoreType.DMA((N_SEMS,)),
        ],
        compiler_params=pltpu.CompilerParams(
            collective_id=0, has_side_effects=True, vmem_limit_bytes=60 * 1024 * 1024
        ),
        cost_estimate=pl.CostEstimate(flops=2_000_000_000, bytes_accessed=8_000_000, transcendentals=200_000),
    )(gradients.reshape(GRAD, D), momentum.reshape(MINE, D), fw, fl, iv, lv)
    return new_momentum.reshape(1, MATS, OWN, D), update.reshape(MATS, OWN, D)


def solution(mesh):
    return jax.shard_map(
        per_device,
        mesh=mesh,
        in_specs=(P("rep", "fsdp", None, None, None), P("rep", None, "fsdp", None)),
        out_specs=(P("rep", None, "fsdp", None), P(None, "fsdp", None)),
        check_vma=False,
    )
```

```python
import jax
import jax.numpy as jnp
import ml_dtypes
import numpy as np
from jax import lax
from jax.experimental import pallas as pl
from jax.experimental.pallas import tpu as pltpu
from jax.sharding import PartitionSpec as P

D, MATS, GROUP, KEEP, ROWS = 5120, 4, 64, 8, 64
BETA, EPS = 0.999, 1e-06
NX, NY, NZL, NZH, NC, N_REP = 4, 4, 2, 4, 2, 32
OWN = 8
LANES = 128
TILES = 8
SPAN = LANES * TILES
GROUPS = D // SPAN
HIGH = 7 * LANES
LOW = GROUPS * LANES
GRAD = MATS * ROWS
MINE = MATS * OWN
NM = 2
WIDE = 4 * LANES

Z_GROUPS = (0, 1)
X_GROUPS = (2, 3, 4)
F32, BF16 = jnp.float32, jnp.bfloat16
MESH = pl.DeviceIdType.MESH


def split(table):
    high = table.astype(ml_dtypes.bfloat16)
    low = (table - high.astype(np.float64)).astype(ml_dtypes.bfloat16)
    return high, low


def tables():
    n, k = np.arange(GROUP), np.arange(GROUP)[:, None]
    basis = np.sqrt(2.0 / GROUP) * np.cos(np.pi * (n + 0.5) * k / GROUP)
    basis[0] *= np.sqrt(0.5)
    rest = GROUP - KEEP
    high = np.zeros((LANES, 2 * rest))
    for b in range(2):
        high[b * GROUP : (b + 1) * GROUP, b * rest : (b + 1) * rest] = basis[KEEP:].T
    forward = np.zeros((7, 2 * LANES, LANES))
    for t in range(7):
        forward[t, :LANES, : 2 * rest] = high
        forward[t, LANES:, 2 * rest :] = high[:, 16 * t : 16 * t + 16]
    inverse = np.zeros((7, LANES, 2 * LANES))
    for t in range(7):
        inverse[t] = forward[t].T
    blocks = SPAN // GROUP
    keep = np.zeros((SPAN, LANES))
    mean = np.zeros((LANES, SPAN))
    for c in range(blocks):
        keep[c * GROUP : (c + 1) * GROUP, c * KEEP : (c + 1) * KEEP] = basis[:KEEP].T
        mean[c * KEEP : (c + 1) * KEEP, c * GROUP : (c + 1) * GROUP] = 1.0 / GROUP
    both = lambda table: np.concatenate(split(table), axis=-1)
    wide = np.concatenate([both(forward).reshape(-1, 2 * LANES), both(keep)], axis=0)
    back = np.concatenate([both(keep.T), mean.astype(ml_dtypes.bfloat16)], axis=-1)
    back = back.reshape(LANES, 6, WIDE).transpose(1, 0, 2).reshape(-1, WIDE)
    return wide, np.concatenate([both(inverse).reshape(-1, WIDE), back], axis=0)


def halves(value):
    top = value.astype(BF16)
    return top, (value - top.astype(F32)).astype(BF16)


def dot(a, b):
    return jnp.dot(a, b, preferred_element_type=F32)


X_UNITS = [(g, h * NM) for g in X_GROUPS for h in range(MATS // NM)]
Z_UNITS = [(g, h * NM) for g in Z_GROUPS for h in range(MATS // NM)]
N_SEMS = 4 * len(X_UNITS) + 4 * len(Z_UNITS) + 1 + 6 + 3 + 1 + 2 + 7
PLAN = [
    ("F", 2), ("XS", 1), ("XS", 0), ("F", 0), ("ZS", 0), ("F", 1),
    ("F", 3), ("FL", 3), ("XS", 3), ("ZS", 3), ("FL", 4), ("XS", 2),
    ("FL", 2), ("FL", 0), ("FL", 1), ("LA", 0), ("F", 4), ("XS", 4),
    ("ZC", 0), ("ZS", 1), ("LB1", 0), ("XP", 3), ("XP", 0), ("LB2", 0),
    ("LC1", 0), ("ZS", 2), ("XP", 1), ("ZP", 0), ("LC2", 0), ("XP", 2),
    ("ZC", 1), ("XS", 5), ("LD", 0), ("XP", 4), ("XC", 3), ("ZP", 1),
    ("ZE", 0), ("LE1", 0), ("XC", 2), ("XP", 5), ("XC", 1), ("ZC", 2),
    ("LE2", 0), ("XC", 0), ("XE", 3), ("XE", 2), ("ZC", 3), ("BK", 3),
    ("ZE", 1), ("BK", 0), ("XC", 5), ("LF", 0), ("XC", 4), ("XE", 1),
    ("XE", 0), ("BK", 2), ("ZP", 2), ("ZP", 3), ("NORM", 0), ("XE", 4),
    ("XE", 5), ("BK", 4), ("ZE", 2), ("ZE", 3), ("BK", 1),
]


def kernel(
    grads, momentum, wide_hbm, back_hbm, new_out, upd_out,
    xin, mom, wide, back, s, lw,
    xr2, xra, xrb, xrz, zr4, zr2, zra, zrb,
    la, lb, lc, le, es, total, nm, up,
    load_sem, store_sem, send_sem, recv_sem,
):
    rep, fsdp = lax.axis_index("rep"), lax.axis_index("fsdp")
    core, y, zh = lax.rem(rep, 2), lax.rem(lax.div(rep, 2), 4), lax.div(rep, 8)
    x, z = lax.rem(fsdp, 4), lax.div(fsdp, 4)

    def ring(v, d):
        return lax.rem(v + (d + 4), 4)

    def device(z_high=None, dy=0, dcore=0, dz=0, dx=0):
        c2 = 1 - core if dcore else core
        z2 = 1 - z if dz else z
        z3 = zh if z_high is None else z_high
        return ((z3 * 4 + ring(y, dy)) * 2 + c2, z2 * 4 + ring(x, dx))

    near, far = zh + 1 - 2 * lax.rem(zh, 2), 3 - zh
    column = [(dy, dc) for dy in range(4) for dc in range(2) if dy or dc]
    partners = [device(dy=dy, dcore=dc) for dy, dc in column]
    partners += [device(dx=1), device(dx=-1), device(dz=1), device(z_high=near), device(z_high=far)]
    barrier = pltpu.get_barrier_semaphore()
    for p in partners:
        pl.semaphore_signal(barrier, inc=1, device_id=p, device_id_type=MESH)

    used = [0]
    pending = []

    def remote(src, dst, to):
        i = used[0]
        used[0] += 1
        return pltpu.make_async_remote_copy(
            src_ref=src, dst_ref=dst, send_sem=send_sem.at[i], recv_sem=recv_sem.at[i],
            device_id=to, device_id_type=MESH,
        )

    def send(src, dst, to):
        copy = remote(src, dst, to)
        copy.start()
        pending.append(copy)
        return copy

    loads = []

    def load(src, dst):
        copy = pltpu.make_async_copy(src, dst, load_sem.at[len(loads)])
        copy.start()
        loads.append(copy)
        return copy

    waited = set()

    def arrived(copy):
        if id(copy) not in waited:
            waited.add(id(copy))
            copy.wait()

    def load_group(g):
        cols = pl.ds(g * SPAN, SPAN)
        return load(grads.at[:, cols], xin.at[pl.ds(0, GRAD), cols])

    order = [g for name, g in PLAN if name == "F"]
    load_mom = load(momentum, mom)
    load_wide = load(wide_hbm, wide)
    group_loads = {g: load_group(g) for g in order}
    load_back = load(back_hbm, back)

    split_done = set()

    def prepare(g):
        arrived(load_mom)
        arrived(load_wide)
        arrived(group_loads[g])
        if g not in split_done:
            split_done.add(g)
            cols = slice(g * SPAN, (g + 1) * SPAN)
            top, rest = halves(BETA * mom[:, cols])
            xin[GRAD : GRAD + MINE, cols] = top
            xin[GRAD + MINE :, cols] = rest

    def fold(v):
        v = v[:, :LANES] + v[:, LANES:]
        own = v[GRAD : GRAD + MINE] + v[GRAD + MINE :]
        return v[:GRAD].reshape(MATS, NZL, NX, OWN, LANES), own.reshape(MATS, OWN, LANES)

    def forward(g):
        prepare(g)
        base = g * SPAN
        last = xin[:, base + HIGH : base + SPAN]
        for t in range(7):
            both = jnp.concatenate([xin[:, base + t * LANES : base + (t + 1) * LANES], last], axis=1)
            value, own = fold(dot(both, wide[t * 2 * LANES : (t + 1) * 2 * LANES]))
            lanes = slice(t * LANES, (t + 1) * LANES)
            s[g, :, :, :, :, lanes] = value
            s[g, :, z, x, :, lanes] += own

    def forward_low(g):
        prepare(g)
        value, own = fold(dot(xin[:, g * SPAN : (g + 1) * SPAN], wide[7 * 2 * LANES :]))
        lanes = slice(g * LANES, (g + 1) * LANES)
        lw[:, :, :, :, lanes] = value
        lw[:, z, x, :, lanes] += own

    xd, zd, low = {}, {}, {}
    way = lambda u: 1 if u % 2 == 0 else -1

    def x_start(u):
        g, m = X_UNITS[u]
        d, part = way(u), s.at[g, pl.ds(m, NM)]
        two = send(part.at[:, :, ring(x, 2)], xr2.at[u], device(dx=d))
        one = send(part.at[:, :, ring(x, -d)], xra.at[u], device(dx=-d))
        xd[u] = [two, one]

    def x_pass(u):
        g, m = X_UNITS[u]
        d = way(u)
        xd[u][0].wait_recv()
        to = ring(x, d)
        s[g, m : m + NM, :, to] += xr2[u]
        xd[u].append(send(s.at[g, pl.ds(m, NM), :, to], xrb.at[u], device(dx=d)))

    def x_cross(u):
        g, m = X_UNITS[u]
        xd[u][1].wait_recv()
        xd[u][2].wait_recv()
        s[g, m : m + NM, :, x] += xra[u] + xrb[u]
        xd[u].append(send(s.at[g, pl.ds(m, NM), 1 - z, x], xrz.at[u], device(dz=1)))

    def z_start(u):
        g, m = Z_UNITS[u]
        zd[u] = [send(s.at[g, pl.ds(m, NM), 1 - z], zr4.at[u], device(dz=1))]

    def z_cross(u):
        g, m = Z_UNITS[u]
        d, part = way(u), s.at[g, pl.ds(m, NM), z]
        zd[u][0].wait_recv()
        s[g, m : m + NM, z] += zr4[u]
        zd[u].append(send(part.at[:, ring(x, 2)], zr2.at[u], device(dx=d)))
        zd[u].append(send(part.at[:, ring(x, -d)], zra.at[u], device(dx=-d)))

    def z_pass(u):
        g, m = Z_UNITS[u]
        d = way(u)
        zd[u][1].wait_recv()
        to = ring(x, d)
        s[g, m : m + NM, z, to] += zr2[u]
        zd[u].append(send(s.at[g, pl.ds(m, NM), z, to], zrb.at[u], device(dx=d)))

    parts = {}

    def x_end(u):
        g, m = X_UNITS[u]
        xd[u][3].wait_recv()
        parts[g, m] = s[g, m : m + NM, z, x] + xrz[u]

    def z_end(u):
        g, m = Z_UNITS[u]
        zd[u][2].wait_recv()
        zd[u][3].wait_recv()
        parts[g, m] = s[g, m : m + NM, z, x] + (zra[u] + zrb[u])

    stores = []

    def store(src, dst):
        copy = pltpu.make_async_copy(src, dst, store_sem.at[len(stores)])
        copy.start()
        stores.append(copy)

    def backward(g):
        arrived(load_back)
        field = jnp.concatenate([parts[g, m] for m in range(0, MATS, NM)], axis=0).reshape(MINE, HIGH)
        last = jnp.zeros((MINE, LANES), F32)
        for t in range(7):
            top, rest = halves(field[:, t * LANES : (t + 1) * LANES])
            v = dot(jnp.concatenate([top, rest], axis=0), back[t * LANES : (t + 1) * LANES])
            v = v[:MINE, : 2 * LANES] + (v[MINE:, : 2 * LANES] + v[:MINE, 2 * LANES :])
            base = g * SPAN + t * LANES
            nm[:, base : base + LANES] = v[:, :LANES]
            last += v[:, LANES:]
        nm[:, g * SPAN + HIGH : (g + 1) * SPAN] = last
        cols = pl.ds(g * SPAN, SPAN)
        store(nm.at[:, cols], new_out.at[:, cols])

    def low_a(_):
        low["a"] = send(lw.at[:, 1 - core], la, device(dcore=1))

    def low_b(_):
        low["a"].wait_recv()
        lw[:, core] += la[...]
        half = lambda dy, k: lw.at[ring(y, dy), core, pl.ds(2 * k, 2)]
        low["b"] = [
            send(half(2, 0), lb.at[0], device(dy=1)),
            send(half(2, 1), lb.at[1], device(dy=-1)),
            send(half(1, 1), lb.at[2], device(dy=1)),
            send(half(-1, 0), lb.at[3], device(dy=-1)),
        ]

    def low_c(_):
        for k, d in ((0, 1), (1, -1)):
            low["b"][k].wait_recv()
            lw[ring(y, d), core, 2 * k : 2 * k + 2] += lb[k]
            half = lw.at[ring(y, d), core, pl.ds(2 * k, 2)]
            low["b"].append(send(half, lb.at[4 + k], device(dy=d)))

    side = 1 - 2 * core

    def low_d(_):
        for copy in low["b"][2:]:
            copy.wait_recv()
        lw[y, core, 0:2] += lb[4] + lb[3]
        lw[y, core, 2:4] += lb[2] + lb[5]
        low["d"] = [
            send(lw.at[y, core, ring(x, 2)], lc.at[0], device(dx=side)),
            send(lw.at[y, core, ring(x, -side)], lc.at[1], device(dx=-side)),
        ]

    def low_e(_):
        low["d"][0].wait_recv()
        to = ring(x, side)
        lw[y, core, to] += lc[0]
        low["d"].append(send(lw.at[y, core, to], lc.at[2], device(dx=side)))

    def low_f(_):
        low["d"][1].wait_recv()
        low["d"][2].wait_recv()
        es[0] = lw[y, core, x] + lc[1] + lc[2]
        low["f"] = remote(es.at[0], le.at[0], device(dz=1))

        @pl.when(core != z)
        def _():
            low["f"].start()

    def low_g(_):
        low["g"] = remote(es.at[1], le.at[1], device(z_high=near))

        @pl.when(core == z)
        def _():
            low["f"].wait_recv()
            es[1] = es[0] + le[0]
            low["g"].start()

    def low_h(_):
        low["h"] = remote(es.at[2], le.at[2], device(z_high=far))

        @pl.when(core == z)
        def _():
            low["g"].wait_recv()
            es[2] = es[1] + le[1]
            low["h"].start()

    def low_i(_):
        low["i"] = [remote(total.at[y], total.at[y], device(dy=dy, dcore=dc)) for dy, dc in column]

        @pl.when(core == z)
        def _():
            low["h"].wait_recv()
            total[y] = es[2] + le[2]
            for copy in low["i"]:
                copy.start()

    def normalise(_):
        arrived(load_back)

        @pl.when(core == z)
        def _():
            for copy, (dy, dc) in zip(low["i"], column):
                if dc == 0:
                    copy.wait_recv()

        @pl.when(core != z)
        def _():
            for copy, (dy, dc) in zip(low["i"], column):
                if dc == 1:
                    copy.wait_recv()

        table = lambda i: back[(7 + i) * LANES : (8 + i) * LANES]
        for g in range(GROUPS):
            lanes = slice(g * LANES, (g + 1) * LANES)
            mean = total[:, :, lanes].reshape(MINE, LANES) * (1.0 / N_REP)
            top, rest = halves(mean)
            pair = jnp.concatenate([top, rest], axis=0)
            squares = jnp.concatenate(halves(mean * mean), axis=0)
            for h in range(2):
                v, w = dot(pair, table(h)), dot(squares, table(4 + h))
                field = v[:MINE] + (v[MINE:] + dot(top, table(2 + h)))
                square = w[:MINE] + w[MINE:]
                base = g * SPAN + h * WIDE
                up[:, base : base + WIDE] = field * lax.rsqrt(field * field + square + EPS)
        store(up, upd_out)

    steps = {
        "F": forward, "FL": forward_low,
        "XS": x_start, "XP": x_pass, "XC": x_cross, "XE": x_end,
        "ZS": z_start, "ZC": z_cross, "ZP": z_pass, "ZE": z_end,
        "LA": low_a, "LB1": low_b, "LB2": low_c, "LC1": low_d, "LC2": low_e,
        "LD": low_f, "LE1": low_g, "LE2": low_h, "LF": low_i,
        "NORM": normalise, "BK": backward,
    }
    entered = False
    for name, u in PLAN:
        if not entered and name not in ("F", "FL"):
            pl.semaphore_wait(barrier, len(partners))
            entered = True
        steps[name](u)

    for copy in pending:
        copy.wait_send()

    @pl.when(core != z)
    def _():
        low["f"].wait_send()

    @pl.when(core == z)
    def _():
        for copy in [low["g"], low["h"]] + low["i"]:
            copy.wait_send()

    for copy in stores:
        copy.wait()


def per_device(gradients, momentum):
    wide, back = tables()
    hbm = pl.BlockSpec(memory_space=pl.ANY)
    nx, nz = len(X_UNITS), len(Z_UNITS)
    new_momentum, update = pl.pallas_call(
        kernel,
        out_shape=[jax.ShapeDtypeStruct((MINE, D), F32)] * 2,
        in_specs=[hbm] * 4,
        out_specs=[hbm] * 2,
        scratch_shapes=[
            pltpu.VMEM((GRAD + 2 * MINE, D), BF16),
            pltpu.VMEM((MINE, D), F32),
            pltpu.VMEM(wide.shape, BF16),
            pltpu.VMEM(back.shape, BF16),
            pltpu.VMEM((GROUPS, MATS, NZL, NX, OWN, HIGH), F32),
            pltpu.VMEM((MATS, NZL, NX, OWN, LOW), F32),
            pltpu.VMEM((nx, NM, NZL, OWN, HIGH), F32),
            pltpu.VMEM((nx, NM, NZL, OWN, HIGH), F32),
            pltpu.VMEM((nx, NM, NZL, OWN, HIGH), F32),
            pltpu.VMEM((nx, NM, OWN, HIGH), F32),
            pltpu.VMEM((nz, NM, NX, OWN, HIGH), F32),
            pltpu.VMEM((nz, NM, OWN, HIGH), F32),
            pltpu.VMEM((nz, NM, OWN, HIGH), F32),
            pltpu.VMEM((nz, NM, OWN, HIGH), F32),
            pltpu.VMEM((MATS, NX, OWN, LOW), F32),
            pltpu.VMEM((6, 2, OWN, LOW), F32),
            pltpu.VMEM((3, OWN, LOW), F32),
            pltpu.VMEM((3, OWN, LOW), F32),
            pltpu.VMEM((3, OWN, LOW), F32),
            pltpu.VMEM((MATS, OWN, LOW), F32),
            pltpu.VMEM((MINE, D), F32),
            pltpu.VMEM((MINE, D), F32),
            pltpu.SemaphoreType.DMA((GROUPS + 3,)),
            pltpu.SemaphoreType.DMA((GROUPS + 1,)),
            pltpu.SemaphoreType.DMA((N_SEMS,)),
            pltpu.SemaphoreType.DMA((N_SEMS,)),
        ],
        compiler_params=pltpu.CompilerParams(
            collective_id=0, has_side_effects=True, vmem_limit_bytes=(52 * 1024 + 384) * 1024
        ),
        cost_estimate=pl.CostEstimate(flops=2_000_000_000, bytes_accessed=8_000_000, transcendentals=200_000),
    )(gradients.reshape(GRAD, D), momentum.reshape(MINE, D), wide, back)
    return new_momentum.reshape(1, MATS, OWN, D), update.reshape(MATS, OWN, D)


def solution(mesh):
    return jax.shard_map(
        per_device,
        mesh=mesh,
        in_specs=(P("rep", "fsdp", None, None, None), P("rep", None, "fsdp", None)),
        out_specs=(P("rep", None, "fsdp", None), P(None, "fsdp", None)),
        check_vma=False,
    )
```

```python
import jax
import jax.numpy as jnp
import ml_dtypes
import numpy as np
from jax import lax
from jax.experimental import pallas as pl
from jax.experimental.pallas import tpu as pltpu
from jax.sharding import PartitionSpec as P

D, MATS, GROUP, KEEP, ROWS = 5120, 4, 64, 8, 64
BETA, EPS = 0.999, 1e-06
NX, NY, NZL, NZH, NC, N_REP = 4, 4, 2, 4, 2, 32
OWN = 8
LANES = 128
TILES = 8
SPAN = LANES * TILES
GROUPS = D // SPAN
HIGH = 7 * LANES
LOW = GROUPS * LANES
GRAD = MATS * ROWS
MINE = MATS * OWN
NM = 2
WIDE = 4 * LANES

F32, BF16 = jnp.float32, jnp.bfloat16
MESH = pl.DeviceIdType.MESH


def split(table):
    high = table.astype(ml_dtypes.bfloat16)
    low = (table - high.astype(np.float64)).astype(ml_dtypes.bfloat16)
    return high, low


def tables():
    n, k = np.arange(GROUP), np.arange(GROUP)[:, None]
    basis = np.sqrt(2.0 / GROUP) * np.cos(np.pi * (n + 0.5) * k / GROUP)
    basis[0] *= np.sqrt(0.5)
    rest = GROUP - KEEP
    high = np.zeros((LANES, 2 * rest))
    for b in range(2):
        high[b * GROUP : (b + 1) * GROUP, b * rest : (b + 1) * rest] = basis[KEEP:].T
    forward = np.zeros((7, 2 * LANES, LANES))
    for t in range(7):
        forward[t, :LANES, : 2 * rest] = high
        forward[t, LANES:, 2 * rest :] = high[:, 16 * t : 16 * t + 16]
    inverse = np.zeros((7, LANES, 2 * LANES))
    for t in range(7):
        inverse[t] = forward[t].T
    blocks = SPAN // GROUP
    keep = np.zeros((SPAN, LANES))
    mean = np.zeros((LANES, SPAN))
    for c in range(blocks):
        keep[c * GROUP : (c + 1) * GROUP, c * KEEP : (c + 1) * KEEP] = basis[:KEEP].T
        mean[c * KEEP : (c + 1) * KEEP, c * GROUP : (c + 1) * GROUP] = 1.0 / GROUP
    both = lambda table: np.concatenate(split(table), axis=-1)
    wide = np.concatenate([both(forward).reshape(-1, 2 * LANES), both(keep)], axis=0)
    back = np.concatenate([both(keep.T), mean.astype(ml_dtypes.bfloat16)], axis=-1)
    back = back.reshape(LANES, 6, WIDE).transpose(1, 0, 2).reshape(-1, WIDE)
    return wide, np.concatenate([both(inverse).reshape(-1, WIDE), back], axis=0)


def halves(value):
    top = value.astype(BF16)
    return top, (value - top.astype(F32)).astype(BF16)


def dot(a, b):
    return jnp.dot(a, b, preferred_element_type=F32)


X_UNITS = [(2, 0), (2, 2), (3, 0), (3, 2), (4, 0), (4, 2), (1, 2)]
Z_UNITS = [(0, 0), (0, 2), (1, 0)]
N_SEMS = 4 * len(X_UNITS) + 4 * len(Z_UNITS) + 1 + 6 + 3 + 1 + 2 + 7
PLAN = [
    ("F", 2), ("XS", 0), ("F", 0), ("ZS", 1), ("ZS", 0), ("XS", 1),
    ("FL", 2), ("F", 3), ("XS", 2), ("FL", 4), ("FL", 1), ("F", 4),
    ("FL", 3), ("FL", 0), ("LA", 0), ("XS", 4), ("F", 1), ("ZS", 2),
    ("XS", 6), ("LB1", 0), ("XP", 2), ("XP", 1), ("LB2", 0), ("LC1", 0),
    ("XS", 5), ("XC", 1), ("LC2", 0), ("XP", 4), ("XS", 3), ("XP", 0),
    ("XP", 5), ("XP", 6), ("LD", 0), ("XC", 2), ("LE1", 0), ("ZC", 1),
    ("XC", 4), ("ZC", 0), ("XP", 3), ("XC", 5), ("LE2", 0), ("XE", 4),
    ("XE", 2), ("ZC", 2), ("XC", 0), ("ZP", 0), ("XE", 5), ("BK", 4),
    ("LF", 0), ("XC", 3), ("XC", 6), ("XE", 1), ("XE", 0), ("ZP", 2),
    ("BK", 2), ("ZP", 1), ("NORM", 0), ("XE", 3), ("ZE", 0), ("BK", 3),
    ("ZE", 2), ("XE", 6), ("BK", 1), ("ZE", 1), ("BK", 0),
]


def kernel(
    grads, momentum, wide_hbm, back_hbm, new_out, upd_out,
    xin, mom, wide, back, s, lw,
    xr2, xra, xrb, xrz, zr4, zr2, zra, zrb,
    la, lb, lc, le, es, total, nm, up,
    load_sem, store_sem, send_sem, recv_sem,
):
    rep, fsdp = lax.axis_index("rep"), lax.axis_index("fsdp")
    core, y, zh = lax.rem(rep, 2), lax.rem(lax.div(rep, 2), 4), lax.div(rep, 8)
    x, z = lax.rem(fsdp, 4), lax.div(fsdp, 4)

    def ring(v, d):
        return lax.rem(v + (d + 4), 4)

    def device(z_high=None, dy=0, dcore=0, dz=0, dx=0):
        c2 = 1 - core if dcore else core
        z2 = 1 - z if dz else z
        z3 = zh if z_high is None else z_high
        return ((z3 * 4 + ring(y, dy)) * 2 + c2, z2 * 4 + ring(x, dx))

    near, far = zh + 1 - 2 * lax.rem(zh, 2), 3 - zh
    column = [(dy, dc) for dy in range(4) for dc in range(2) if dy or dc]
    partners = [device(dy=dy, dcore=dc) for dy, dc in column]
    partners += [device(dx=1), device(dx=-1), device(dz=1), device(z_high=near), device(z_high=far)]
    barrier = pltpu.get_barrier_semaphore()
    for p in partners:
        pl.semaphore_signal(barrier, inc=1, device_id=p, device_id_type=MESH)

    used = [0]
    pending = []

    def remote(src, dst, to):
        i = used[0]
        used[0] += 1
        return pltpu.make_async_remote_copy(
            src_ref=src, dst_ref=dst, send_sem=send_sem.at[i], recv_sem=recv_sem.at[i],
            device_id=to, device_id_type=MESH,
        )

    def send(src, dst, to):
        copy = remote(src, dst, to)
        copy.start()
        pending.append(copy)
        return copy

    loads = []

    def load(src, dst):
        copy = pltpu.make_async_copy(src, dst, load_sem.at[len(loads)])
        copy.start()
        loads.append(copy)
        return copy

    waited = set()

    def arrived(copy):
        if id(copy) not in waited:
            waited.add(id(copy))
            copy.wait()

    def load_group(g):
        cols = pl.ds(g * SPAN, SPAN)
        return load(grads.at[:, cols], xin.at[pl.ds(0, GRAD), cols])

    order = [g for name, g in PLAN if name == "F"]
    load_mom = load(momentum, mom)
    load_wide = load(wide_hbm, wide)
    group_loads = {g: load_group(g) for g in order}
    load_back = load(back_hbm, back)

    split_done = set()

    def prepare(g):
        arrived(load_mom)
        arrived(load_wide)
        arrived(group_loads[g])
        if g not in split_done:
            split_done.add(g)
            cols = slice(g * SPAN, (g + 1) * SPAN)
            top, rest = halves(BETA * mom[:, cols])
            xin[GRAD : GRAD + MINE, cols] = top
            xin[GRAD + MINE :, cols] = rest

    def fold(v):
        v = v[:, :LANES] + v[:, LANES:]
        own = v[GRAD : GRAD + MINE] + v[GRAD + MINE :]
        return v[:GRAD].reshape(MATS, NZL, NX, OWN, LANES), own.reshape(MATS, OWN, LANES)

    def forward(g):
        prepare(g)
        base = g * SPAN
        last = xin[:, base + HIGH : base + SPAN]
        for t in range(7):
            both = jnp.concatenate([xin[:, base + t * LANES : base + (t + 1) * LANES], last], axis=1)
            value, own = fold(dot(both, wide[t * 2 * LANES : (t + 1) * 2 * LANES]))
            lanes = slice(t * LANES, (t + 1) * LANES)
            s[g, :, :, :, :, lanes] = value
            s[g, :, z, x, :, lanes] += own

    def forward_low(g):
        prepare(g)
        value, own = fold(dot(xin[:, g * SPAN : (g + 1) * SPAN], wide[7 * 2 * LANES :]))
        lanes = slice(g * LANES, (g + 1) * LANES)
        lw[:, :, :, :, lanes] = value
        lw[:, z, x, :, lanes] += own

    xd, zd, low = {}, {}, {}
    way = lambda u: 1 if u % 2 == 0 else -1
    z_way = lambda u: -way(u)

    def x_start(u):
        g, m = X_UNITS[u]
        d, part = way(u), s.at[g, pl.ds(m, NM)]
        two = send(part.at[:, :, ring(x, 2)], xr2.at[u], device(dx=d))
        one = send(part.at[:, :, ring(x, -d)], xra.at[u], device(dx=-d))
        xd[u] = [two, one]

    def x_pass(u):
        g, m = X_UNITS[u]
        d = way(u)
        xd[u][0].wait_recv()
        to = ring(x, d)
        s[g, m : m + NM, :, to] += xr2[u]
        xd[u].append(send(s.at[g, pl.ds(m, NM), :, to], xrb.at[u], device(dx=d)))

    def x_cross(u):
        g, m = X_UNITS[u]
        xd[u][1].wait_recv()
        xd[u][2].wait_recv()
        s[g, m : m + NM, :, x] += xra[u] + xrb[u]
        xd[u].append(send(s.at[g, pl.ds(m, NM), 1 - z, x], xrz.at[u], device(dz=1)))

    def z_start(u):
        g, m = Z_UNITS[u]
        zd[u] = [send(s.at[g, pl.ds(m, NM), 1 - z], zr4.at[u], device(dz=1))]

    def z_cross(u):
        g, m = Z_UNITS[u]
        d, part = z_way(u), s.at[g, pl.ds(m, NM), z]
        zd[u][0].wait_recv()
        s[g, m : m + NM, z] += zr4[u]
        zd[u].append(send(part.at[:, ring(x, 2)], zr2.at[u], device(dx=d)))
        zd[u].append(send(part.at[:, ring(x, -d)], zra.at[u], device(dx=-d)))

    def z_pass(u):
        g, m = Z_UNITS[u]
        d = z_way(u)
        zd[u][1].wait_recv()
        to = ring(x, d)
        s[g, m : m + NM, z, to] += zr2[u]
        zd[u].append(send(s.at[g, pl.ds(m, NM), z, to], zrb.at[u], device(dx=d)))

    parts = {}

    def x_end(u):
        g, m = X_UNITS[u]
        xd[u][3].wait_recv()
        parts[g, m] = s[g, m : m + NM, z, x] + xrz[u]

    def z_end(u):
        g, m = Z_UNITS[u]
        zd[u][2].wait_recv()
        zd[u][3].wait_recv()
        parts[g, m] = s[g, m : m + NM, z, x] + (zra[u] + zrb[u])

    stores = []

    def store(src, dst):
        copy = pltpu.make_async_copy(src, dst, store_sem.at[len(stores)])
        copy.start()
        stores.append(copy)

    def backward(g):
        arrived(load_back)
        field = jnp.concatenate([parts[g, m] for m in range(0, MATS, NM)], axis=0).reshape(MINE, HIGH)
        last = jnp.zeros((MINE, LANES), F32)
        for t in range(7):
            top, rest = halves(field[:, t * LANES : (t + 1) * LANES])
            v = dot(jnp.concatenate([top, rest], axis=0), back[t * LANES : (t + 1) * LANES])
            v = v[:MINE, : 2 * LANES] + (v[MINE:, : 2 * LANES] + v[:MINE, 2 * LANES :])
            base = g * SPAN + t * LANES
            nm[:, base : base + LANES] = v[:, :LANES]
            last += v[:, LANES:]
        nm[:, g * SPAN + HIGH : (g + 1) * SPAN] = last
        cols = pl.ds(g * SPAN, SPAN)
        store(nm.at[:, cols], new_out.at[:, cols])

    def low_a(_):
        low["a"] = send(lw.at[:, 1 - core], la, device(dcore=1))

    def low_b(_):
        low["a"].wait_recv()
        lw[:, core] += la[...]
        half = lambda dy, k: lw.at[ring(y, dy), core, pl.ds(2 * k, 2)]
        low["b"] = [
            send(half(2, 0), lb.at[0], device(dy=1)),
            send(half(2, 1), lb.at[1], device(dy=-1)),
            send(half(1, 1), lb.at[2], device(dy=1)),
            send(half(-1, 0), lb.at[3], device(dy=-1)),
        ]

    def low_c(_):
        for k, d in ((0, 1), (1, -1)):
            low["b"][k].wait_recv()
            lw[ring(y, d), core, 2 * k : 2 * k + 2] += lb[k]
            half = lw.at[ring(y, d), core, pl.ds(2 * k, 2)]
            low["b"].append(send(half, lb.at[4 + k], device(dy=d)))

    side = 1 - 2 * core

    def low_d(_):
        for copy in low["b"][2:]:
            copy.wait_recv()
        lw[y, core, 0:2] += lb[4] + lb[3]
        lw[y, core, 2:4] += lb[2] + lb[5]
        low["d"] = [
            send(lw.at[y, core, ring(x, 2)], lc.at[0], device(dx=side)),
            send(lw.at[y, core, ring(x, -side)], lc.at[1], device(dx=-side)),
        ]

    def low_e(_):
        low["d"][0].wait_recv()
        to = ring(x, side)
        lw[y, core, to] += lc[0]
        low["d"].append(send(lw.at[y, core, to], lc.at[2], device(dx=side)))

    def low_f(_):
        low["d"][1].wait_recv()
        low["d"][2].wait_recv()
        es[0] = lw[y, core, x] + lc[1] + lc[2]
        low["f"] = remote(es.at[0], le.at[0], device(dz=1))

        @pl.when(core != z)
        def _():
            low["f"].start()

    def low_g(_):
        low["g"] = remote(es.at[1], le.at[1], device(z_high=near))

        @pl.when(core == z)
        def _():
            low["f"].wait_recv()
            es[1] = es[0] + le[0]
            low["g"].start()

    def low_h(_):
        low["h"] = remote(es.at[2], le.at[2], device(z_high=far))

        @pl.when(core == z)
        def _():
            low["g"].wait_recv()
            es[2] = es[1] + le[1]
            low["h"].start()

    def low_i(_):
        low["i"] = [remote(total.at[y], total.at[y], device(dy=dy, dcore=dc)) for dy, dc in column]

        @pl.when(core == z)
        def _():
            low["h"].wait_recv()
            total[y] = es[2] + le[2]
            for copy in low["i"]:
                copy.start()

    def normalise(_):
        arrived(load_back)

        @pl.when(core == z)
        def _():
            for copy, (dy, dc) in zip(low["i"], column):
                if dc == 0:
                    copy.wait_recv()

        @pl.when(core != z)
        def _():
            for copy, (dy, dc) in zip(low["i"], column):
                if dc == 1:
                    copy.wait_recv()

        table = lambda i: back[(7 + i) * LANES : (8 + i) * LANES]
        for g in range(GROUPS):
            lanes = slice(g * LANES, (g + 1) * LANES)
            mean = total[:, :, lanes].reshape(MINE, LANES) * (1.0 / N_REP)
            top, rest = halves(mean)
            pair = jnp.concatenate([top, rest], axis=0)
            squares = jnp.concatenate(halves(mean * mean), axis=0)
            for h in range(2):
                v, w = dot(pair, table(h)), dot(squares, table(4 + h))
                field = v[:MINE] + (v[MINE:] + dot(top, table(2 + h)))
                square = w[:MINE] + w[MINE:]
                base = g * SPAN + h * WIDE
                up[:, base : base + WIDE] = field * lax.rsqrt(field * field + square + EPS)
        store(up, upd_out)

    steps = {
        "F": forward, "FL": forward_low,
        "XS": x_start, "XP": x_pass, "XC": x_cross, "XE": x_end,
        "ZS": z_start, "ZC": z_cross, "ZP": z_pass, "ZE": z_end,
        "LA": low_a, "LB1": low_b, "LB2": low_c, "LC1": low_d, "LC2": low_e,
        "LD": low_f, "LE1": low_g, "LE2": low_h, "LF": low_i,
        "NORM": normalise, "BK": backward,
    }
    entered = False
    for name, u in PLAN:
        if not entered and name not in ("F", "FL"):
            pl.semaphore_wait(barrier, len(partners))
            entered = True
        steps[name](u)

    for copy in pending:
        copy.wait_send()

    @pl.when(core != z)
    def _():
        low["f"].wait_send()

    @pl.when(core == z)
    def _():
        for copy in [low["g"], low["h"]] + low["i"]:
            copy.wait_send()

    for copy in stores:
        copy.wait()


def per_device(gradients, momentum):
    wide, back = tables()
    hbm = pl.BlockSpec(memory_space=pl.ANY)
    nx, nz = len(X_UNITS), len(Z_UNITS)
    new_momentum, update = pl.pallas_call(
        kernel,
        out_shape=[jax.ShapeDtypeStruct((MINE, D), F32)] * 2,
        in_specs=[hbm] * 4,
        out_specs=[hbm] * 2,
        scratch_shapes=[
            pltpu.VMEM((GRAD + 2 * MINE, D), BF16),
            pltpu.VMEM((MINE, D), F32),
            pltpu.VMEM(wide.shape, BF16),
            pltpu.VMEM(back.shape, BF16),
            pltpu.VMEM((GROUPS, MATS, NZL, NX, OWN, HIGH), F32),
            pltpu.VMEM((MATS, NZL, NX, OWN, LOW), F32),
            pltpu.VMEM((nx, NM, NZL, OWN, HIGH), F32),
            pltpu.VMEM((nx, NM, NZL, OWN, HIGH), F32),
            pltpu.VMEM((nx, NM, NZL, OWN, HIGH), F32),
            pltpu.VMEM((nx, NM, OWN, HIGH), F32),
            pltpu.VMEM((nz, NM, NX, OWN, HIGH), F32),
            pltpu.VMEM((nz, NM, OWN, HIGH), F32),
            pltpu.VMEM((nz, NM, OWN, HIGH), F32),
            pltpu.VMEM((nz, NM, OWN, HIGH), F32),
            pltpu.VMEM((MATS, NX, OWN, LOW), F32),
            pltpu.VMEM((6, 2, OWN, LOW), F32),
            pltpu.VMEM((3, OWN, LOW), F32),
            pltpu.VMEM((3, OWN, LOW), F32),
            pltpu.VMEM((3, OWN, LOW), F32),
            pltpu.VMEM((MATS, OWN, LOW), F32),
            pltpu.VMEM((MINE, D), F32),
            pltpu.VMEM((MINE, D), F32),
            pltpu.SemaphoreType.DMA((GROUPS + 3,)),
            pltpu.SemaphoreType.DMA((GROUPS + 1,)),
            pltpu.SemaphoreType.DMA((N_SEMS,)),
            pltpu.SemaphoreType.DMA((N_SEMS,)),
        ],
        compiler_params=pltpu.CompilerParams(
            collective_id=0, has_side_effects=True, vmem_limit_bytes=(52 * 1024 + 384) * 1024
        ),
        cost_estimate=pl.CostEstimate(flops=2_000_000_000, bytes_accessed=8_000_000, transcendentals=200_000),
    )(gradients.reshape(GRAD, D), momentum.reshape(MINE, D), wide, back)
    return new_momentum.reshape(1, MATS, OWN, D), update.reshape(MATS, OWN, D)


def solution(mesh):
    return jax.shard_map(
        per_device,
        mesh=mesh,
        in_specs=(P("rep", "fsdp", None, None, None), P("rep", None, "fsdp", None)),
        out_specs=(P("rep", None, "fsdp", None), P(None, "fsdp", None)),
        check_vma=False,
    )
```

```python
import jax
import jax.numpy as jnp
import ml_dtypes
import numpy as np
from jax import lax
from jax.experimental import pallas as pl
from jax.experimental.pallas import tpu as pltpu
from jax.sharding import PartitionSpec as P

D, MATS, GROUP, KEEP, ROWS = 5120, 4, 64, 8, 64
BETA, EPS = 0.999, 1e-06
NX, NY, NZL, NZH, NC, N_REP = 4, 4, 2, 4, 2, 32
OWN = 8
LANES = 128
TILES = 8
SPAN = LANES * TILES
GROUPS = D // SPAN
HIGH = 7 * LANES
LOW = GROUPS * LANES
GRAD = MATS * ROWS
MINE = MATS * OWN
NM = 2
WIDE = 4 * LANES

F32, BF16 = jnp.float32, jnp.bfloat16
MESH = pl.DeviceIdType.MESH


def split(table):
    high = table.astype(ml_dtypes.bfloat16)
    low = (table - high.astype(np.float64)).astype(ml_dtypes.bfloat16)
    return high, low


def tables():
    n, k = np.arange(GROUP), np.arange(GROUP)[:, None]
    basis = np.sqrt(2.0 / GROUP) * np.cos(np.pi * (n + 0.5) * k / GROUP)
    basis[0] *= np.sqrt(0.5)
    rest = GROUP - KEEP
    high = np.zeros((LANES, 2 * rest))
    for b in range(2):
        high[b * GROUP : (b + 1) * GROUP, b * rest : (b + 1) * rest] = basis[KEEP:].T
    forward = np.zeros((7, 2 * LANES, LANES))
    for t in range(7):
        forward[t, :LANES, : 2 * rest] = high
        forward[t, LANES:, 2 * rest :] = high[:, 16 * t : 16 * t + 16]
    inverse = np.zeros((7, LANES, 2 * LANES))
    for t in range(7):
        inverse[t] = forward[t].T
    blocks = SPAN // GROUP
    keep = np.zeros((SPAN, LANES))
    mean = np.zeros((LANES, SPAN))
    for c in range(blocks):
        keep[c * GROUP : (c + 1) * GROUP, c * KEEP : (c + 1) * KEEP] = basis[:KEEP].T
        mean[c * KEEP : (c + 1) * KEEP, c * GROUP : (c + 1) * GROUP] = 1.0 / GROUP
    both = lambda table: np.concatenate(split(table), axis=-1)
    wide = np.concatenate([both(forward).reshape(-1, 2 * LANES), both(keep)], axis=0)
    back = np.concatenate([both(keep.T), mean.astype(ml_dtypes.bfloat16)], axis=-1)
    back = back.reshape(LANES, 6, WIDE).transpose(1, 0, 2).reshape(-1, WIDE)
    return wide, np.concatenate([both(inverse).reshape(-1, WIDE), back], axis=0)


def halves(value):
    top = value.astype(BF16)
    return top, (value - top.astype(F32)).astype(BF16)


def dot(a, b):
    return jnp.dot(a, b, preferred_element_type=F32)


X_UNITS = [(2, 0), (2, 2), (3, 0), (3, 2), (4, 0), (4, 2)]
Z_UNITS = [(0, 0), (0, 2), (1, 0), (1, 2)]
N_SEMS = 4 * len(X_UNITS) + 4 * len(Z_UNITS) + 1 + 6 + 3 + 7 + 7
PLAN = [
    ("F", 2), ("XS", 1), ("F", 0), ("ZS", 0), ("XS", 0), ("F", 3),
    ("FL", 3), ("FL", 4), ("XS", 2), ("ZS", 1), ("FL", 0), ("XS", 3),
    ("FL", 2), ("FL", 1), ("LA", 0), ("F", 1), ("ZC", 0), ("ZS", 2),
    ("XP", 1), ("XP", 2), ("LB1", 0), ("ZS", 3), ("F", 4), ("XS", 4),
    ("LB2", 0), ("ZC", 1), ("XC", 2), ("LC", 0), ("XP", 3), ("XP", 0),
    ("XP", 4), ("XS", 5), ("ZP", 0), ("ZP", 1), ("LD", 0), ("ZC", 3),
    ("XC", 3), ("ZC", 2), ("XC", 1), ("XC", 0), ("XC", 4), ("XP", 5),
    ("XE", 2), ("LF", 0), ("XE", 3), ("ZE", 0), ("BK", 3), ("ZP", 2),
    ("ZE", 1), ("BK", 0), ("ZP", 3), ("XC", 5), ("NORM", 0), ("XE", 0),
    ("XE", 1), ("ZE", 2), ("BK", 2), ("XE", 4), ("ZE", 3), ("BK", 1),
    ("XE", 5), ("BK", 4),
]


def kernel(
    grads, momentum, wide_hbm, back_hbm, new_out, upd_out,
    xin, mom, wide, back, s, lw,
    xr2, xra, xrb, xrz, zr4, zr2, zra, zrb,
    la, lb, lc, le, es, total, nm, up,
    load_sem, store_sem, send_sem, recv_sem,
):
    rep, fsdp = lax.axis_index("rep"), lax.axis_index("fsdp")
    core, y, zh = lax.rem(rep, 2), lax.rem(lax.div(rep, 2), 4), lax.div(rep, 8)
    x, z = lax.rem(fsdp, 4), lax.div(fsdp, 4)

    def ring(v, d):
        return lax.rem(v + (d + 4), 4)

    def device(z_high=None, dy=0, dcore=0, dz=0, dx=0):
        c2 = 1 - core if dcore else core
        z2 = 1 - z if dz else z
        z3 = zh if z_high is None else z_high
        return ((z3 * 4 + ring(y, dy)) * 2 + c2, z2 * 4 + ring(x, dx))

    column = [(dy, dc) for dy in range(4) for dc in range(2) if dy or dc]
    partners = [device(dy=dy, dcore=dc) for dy, dc in column]
    partners += [device(dx=d) for d in (1, 2, 3)]
    partners += [device(z_high=ring(zh, d), dz=dz) for d in range(4) for dz in range(2) if d or dz]
    barrier = pltpu.get_barrier_semaphore()
    for p in partners:
        pl.semaphore_signal(barrier, inc=1, device_id=p, device_id_type=MESH)

    used = [0]
    pending = []

    def remote(src, dst, to):
        i = used[0]
        used[0] += 1
        return pltpu.make_async_remote_copy(
            src_ref=src, dst_ref=dst, send_sem=send_sem.at[i], recv_sem=recv_sem.at[i],
            device_id=to, device_id_type=MESH,
        )

    def send(src, dst, to):
        copy = remote(src, dst, to)
        copy.start()
        pending.append(copy)
        return copy

    loads = []

    def load(src, dst):
        copy = pltpu.make_async_copy(src, dst, load_sem.at[len(loads)])
        copy.start()
        loads.append(copy)
        return copy

    waited = set()

    def arrived(copy):
        if id(copy) not in waited:
            waited.add(id(copy))
            copy.wait()

    def load_group(g):
        cols = pl.ds(g * SPAN, SPAN)
        return load(grads.at[:, cols], xin.at[pl.ds(0, GRAD), cols])

    order = [g for name, g in PLAN if name == "F"]
    load_mom = load(momentum, mom)
    load_wide = load(wide_hbm, wide)
    group_loads = {g: load_group(g) for g in order}
    load_back = load(back_hbm, back)

    split_done = set()

    def prepare(g):
        arrived(load_mom)
        arrived(load_wide)
        arrived(group_loads[g])
        if g not in split_done:
            split_done.add(g)
            cols = slice(g * SPAN, (g + 1) * SPAN)
            top, rest = halves(BETA * mom[:, cols])
            xin[GRAD : GRAD + MINE, cols] = top
            xin[GRAD + MINE :, cols] = rest

    def fold(v):
        v = v[:, :LANES] + v[:, LANES:]
        own = v[GRAD : GRAD + MINE] + v[GRAD + MINE :]
        return v[:GRAD].reshape(MATS, NZL, NX, OWN, LANES), own.reshape(MATS, OWN, LANES)

    def forward(g):
        prepare(g)
        base = g * SPAN
        last = xin[:, base + HIGH : base + SPAN]
        for t in range(7):
            both = jnp.concatenate([xin[:, base + t * LANES : base + (t + 1) * LANES], last], axis=1)
            value, own = fold(dot(both, wide[t * 2 * LANES : (t + 1) * 2 * LANES]))
            lanes = slice(t * LANES, (t + 1) * LANES)
            s[g, :, :, :, :, lanes] = value
            s[g, :, z, x, :, lanes] += own

    def forward_low(g):
        prepare(g)
        value, own = fold(dot(xin[:, g * SPAN : (g + 1) * SPAN], wide[7 * 2 * LANES :]))
        lanes = slice(g * LANES, (g + 1) * LANES)
        lw[:, :, :, :, lanes] = value
        lw[:, z, x, :, lanes] += own

    xd, zd, low = {}, {}, {}
    way = lambda u: 1 if u % 2 == 0 else -1
    z_way = lambda u: -way(u)

    def x_start(u):
        g, m = X_UNITS[u]
        d, part = way(u), s.at[g, pl.ds(m, NM)]
        two = send(part.at[:, :, ring(x, 2)], xr2.at[u], device(dx=d))
        one = send(part.at[:, :, ring(x, -d)], xra.at[u], device(dx=-d))
        xd[u] = [two, one]

    def x_pass(u):
        g, m = X_UNITS[u]
        d = way(u)
        xd[u][0].wait_recv()
        to = ring(x, d)
        s[g, m : m + NM, :, to] += xr2[u]
        xd[u].append(send(s.at[g, pl.ds(m, NM), :, to], xrb.at[u], device(dx=d)))

    def x_cross(u):
        g, m = X_UNITS[u]
        xd[u][1].wait_recv()
        xd[u][2].wait_recv()
        s[g, m : m + NM, :, x] += xra[u] + xrb[u]
        xd[u].append(send(s.at[g, pl.ds(m, NM), 1 - z, x], xrz.at[u], device(dz=1)))

    def z_start(u):
        g, m = Z_UNITS[u]
        zd[u] = [send(s.at[g, pl.ds(m, NM), 1 - z], zr4.at[u], device(dz=1))]

    def z_cross(u):
        g, m = Z_UNITS[u]
        d, part = z_way(u), s.at[g, pl.ds(m, NM), z]
        zd[u][0].wait_recv()
        s[g, m : m + NM, z] += zr4[u]
        zd[u].append(send(part.at[:, ring(x, 2)], zr2.at[u], device(dx=d)))
        zd[u].append(send(part.at[:, ring(x, -d)], zra.at[u], device(dx=-d)))

    def z_pass(u):
        g, m = Z_UNITS[u]
        d = z_way(u)
        zd[u][1].wait_recv()
        to = ring(x, d)
        s[g, m : m + NM, z, to] += zr2[u]
        zd[u].append(send(s.at[g, pl.ds(m, NM), z, to], zrb.at[u], device(dx=d)))

    parts = {}

    def x_end(u):
        g, m = X_UNITS[u]
        xd[u][3].wait_recv()
        parts[g, m] = s[g, m : m + NM, z, x] + xrz[u]

    def z_end(u):
        g, m = Z_UNITS[u]
        zd[u][2].wait_recv()
        zd[u][3].wait_recv()
        parts[g, m] = s[g, m : m + NM, z, x] + (zra[u] + zrb[u])

    stores = []

    def store(src, dst):
        copy = pltpu.make_async_copy(src, dst, store_sem.at[len(stores)])
        copy.start()
        stores.append(copy)

    def backward(g):
        arrived(load_back)
        field = jnp.concatenate([parts[g, m] for m in range(0, MATS, NM)], axis=0).reshape(MINE, HIGH)
        last = jnp.zeros((MINE, LANES), F32)
        for t in range(7):
            top, rest = halves(field[:, t * LANES : (t + 1) * LANES])
            v = dot(jnp.concatenate([top, rest], axis=0), back[t * LANES : (t + 1) * LANES])
            v = v[:MINE, : 2 * LANES] + (v[MINE:, : 2 * LANES] + v[:MINE, 2 * LANES :])
            base = g * SPAN + t * LANES
            nm[:, base : base + LANES] = v[:, :LANES]
            last += v[:, LANES:]
        nm[:, g * SPAN + HIGH : (g + 1) * SPAN] = last
        cols = pl.ds(g * SPAN, SPAN)
        store(nm.at[:, cols], new_out.at[:, cols])

    def low_a(_):
        low["a"] = send(lw.at[:, 1 - core], la, device(dcore=1))

    def low_b(_):
        low["a"].wait_recv()
        lw[:, core] += la[...]
        half = lambda dy, k: lw.at[ring(y, dy), core, pl.ds(2 * k, 2)]
        low["b"] = [
            send(half(2, 0), lb.at[0], device(dy=1)),
            send(half(2, 1), lb.at[1], device(dy=-1)),
            send(half(1, 1), lb.at[2], device(dy=1)),
            send(half(-1, 0), lb.at[3], device(dy=-1)),
        ]

    def low_c(_):
        for k, d in ((0, 1), (1, -1)):
            low["b"][k].wait_recv()
            lw[ring(y, d), core, 2 * k : 2 * k + 2] += lb[k]
            half = lw.at[ring(y, d), core, pl.ds(2 * k, 2)]
            low["b"].append(send(half, lb.at[4 + k], device(dy=d)))

    def low_d(_):
        for copy in low["b"][2:]:
            copy.wait_recv()
        lw[y, core, 0:2] += lb[4] + lb[3]
        lw[y, core, 2:4] += lb[2] + lb[5]
        low["d"] = [send(lw.at[y, core, ring(x, d)], lc.at[d - 1], device(dx=d)) for d in (1, 2, 3)]

    def low_e(_):
        for copy in low["d"]:
            copy.wait_recv()
        es[...] = lw[y, core, x] + (lc[0] + lc[1] + lc[2])
        low["in"] = [remote(es, le.at[d - 1], device(z_high=ring(zh, d))) for d in (1, 2, 3)]
        low["out"] = [remote(es, le.at[3 + d], device(z_high=ring(zh, d), dz=1)) for d in range(4)]

        @pl.when(core == z)
        def _():
            for copy in low["in"]:
                copy.start()

        @pl.when(core != z)
        def _():
            for copy in low["out"]:
                copy.start()

    def low_i(_):
        low["i"] = [remote(total.at[y], total.at[y], device(dy=dy, dcore=dc)) for dy, dc in column]

        @pl.when(core == z)
        def _():
            for copy in low["in"] + low["out"]:
                copy.wait_recv()
            total[y] = es[...] + ((le[0] + le[1] + le[2]) + (le[3] + le[4] + le[5] + le[6]))
            for copy in low["i"]:
                copy.start()

    def normalise(_):
        arrived(load_back)

        @pl.when(core == z)
        def _():
            for copy, (dy, dc) in zip(low["i"], column):
                if dc == 0:
                    copy.wait_recv()

        @pl.when(core != z)
        def _():
            for copy, (dy, dc) in zip(low["i"], column):
                if dc == 1:
                    copy.wait_recv()

        table = lambda i: back[(7 + i) * LANES : (8 + i) * LANES]
        for g in range(GROUPS):
            lanes = slice(g * LANES, (g + 1) * LANES)
            mean = total[:, :, lanes].reshape(MINE, LANES) * (1.0 / N_REP)
            top, rest = halves(mean)
            pair = jnp.concatenate([top, rest], axis=0)
            squares = jnp.concatenate(halves(mean * mean), axis=0)
            for h in range(2):
                v, w = dot(pair, table(h)), dot(squares, table(4 + h))
                field = v[:MINE] + (v[MINE:] + dot(top, table(2 + h)))
                square = w[:MINE] + w[MINE:]
                base = g * SPAN + h * WIDE
                up[:, base : base + WIDE] = field * lax.rsqrt(field * field + square + EPS)
        store(up, upd_out)

    steps = {
        "F": forward, "FL": forward_low,
        "XS": x_start, "XP": x_pass, "XC": x_cross, "XE": x_end,
        "ZS": z_start, "ZC": z_cross, "ZP": z_pass, "ZE": z_end,
        "LA": low_a, "LB1": low_b, "LB2": low_c, "LC": low_d, "LD": low_e, "LF": low_i,
        "NORM": normalise, "BK": backward,
    }
    entered = False
    for name, u in PLAN:
        if not entered and name not in ("F", "FL"):
            pl.semaphore_wait(barrier, len(partners))
            entered = True
        steps[name](u)

    for copy in pending:
        copy.wait_send()

    @pl.when(core != z)
    def _():
        for copy in low["out"]:
            copy.wait_send()

    @pl.when(core == z)
    def _():
        for copy in low["in"] + low["i"]:
            copy.wait_send()

    for copy in stores:
        copy.wait()


def per_device(gradients, momentum):
    wide, back = tables()
    hbm = pl.BlockSpec(memory_space=pl.ANY)
    nx, nz = len(X_UNITS), len(Z_UNITS)
    new_momentum, update = pl.pallas_call(
        kernel,
        out_shape=[jax.ShapeDtypeStruct((MINE, D), F32)] * 2,
        in_specs=[hbm] * 4,
        out_specs=[hbm] * 2,
        scratch_shapes=[
            pltpu.VMEM((GRAD + 2 * MINE, D), BF16),
            pltpu.VMEM((MINE, D), F32),
            pltpu.VMEM(wide.shape, BF16),
            pltpu.VMEM(back.shape, BF16),
            pltpu.VMEM((GROUPS, MATS, NZL, NX, OWN, HIGH), F32),
            pltpu.VMEM((MATS, NZL, NX, OWN, LOW), F32),
            pltpu.VMEM((nx, NM, NZL, OWN, HIGH), F32),
            pltpu.VMEM((nx, NM, NZL, OWN, HIGH), F32),
            pltpu.VMEM((nx, NM, NZL, OWN, HIGH), F32),
            pltpu.VMEM((nx, NM, OWN, HIGH), F32),
            pltpu.VMEM((nz, NM, NX, OWN, HIGH), F32),
            pltpu.VMEM((nz, NM, OWN, HIGH), F32),
            pltpu.VMEM((nz, NM, OWN, HIGH), F32),
            pltpu.VMEM((nz, NM, OWN, HIGH), F32),
            pltpu.VMEM((MATS, NX, OWN, LOW), F32),
            pltpu.VMEM((6, 2, OWN, LOW), F32),
            pltpu.VMEM((3, OWN, LOW), F32),
            pltpu.VMEM((7, OWN, LOW), F32),
            pltpu.VMEM((OWN, LOW), F32),
            pltpu.VMEM((MATS, OWN, LOW), F32),
            pltpu.VMEM((MINE, D), F32),
            pltpu.VMEM((MINE, D), F32),
            pltpu.SemaphoreType.DMA((GROUPS + 3,)),
            pltpu.SemaphoreType.DMA((GROUPS + 1,)),
            pltpu.SemaphoreType.DMA((N_SEMS,)),
            pltpu.SemaphoreType.DMA((N_SEMS,)),
        ],
        compiler_params=pltpu.CompilerParams(
            collective_id=0, has_side_effects=True, vmem_limit_bytes=(52 * 1024 + 384) * 1024
        ),
        cost_estimate=pl.CostEstimate(flops=2_000_000_000, bytes_accessed=8_000_000, transcendentals=200_000),
    )(gradients.reshape(GRAD, D), momentum.reshape(MINE, D), wide, back)
    return new_momentum.reshape(1, MATS, OWN, D), update.reshape(MATS, OWN, D)


def solution(mesh):
    return jax.shard_map(
        per_device,
        mesh=mesh,
        in_specs=(P("rep", "fsdp", None, None, None), P("rep", None, "fsdp", None)),
        out_specs=(P("rep", None, "fsdp", None), P(None, "fsdp", None)),
        check_vma=False,
    )
```

```python
import jax
import jax.numpy as jnp
import ml_dtypes
import numpy as np
from jax import lax
from jax.experimental import pallas as pl
from jax.experimental.pallas import tpu as pltpu
from jax.sharding import PartitionSpec as P

D, MATS, GROUP, KEEP, ROWS = 5120, 4, 64, 8, 64
BETA, EPS = 0.999, 1e-06
NX, NY, NZL, NZH, NC, N_REP = 4, 4, 2, 4, 2, 32
OWN = 8
LANES = 128
TILES = 8
SPAN = LANES * TILES
GROUPS = D // SPAN
HIGH = 7 * LANES
LOW = GROUPS * LANES
GRAD = MATS * ROWS
MINE = MATS * OWN
WIDE = 4 * LANES

F32, BF16 = jnp.float32, jnp.bfloat16
MESH = pl.DeviceIdType.MESH


def split(table):
    high = table.astype(ml_dtypes.bfloat16)
    low = (table - high.astype(np.float64)).astype(ml_dtypes.bfloat16)
    return high, low


def tables():
    n, k = np.arange(GROUP), np.arange(GROUP)[:, None]
    basis = np.sqrt(2.0 / GROUP) * np.cos(np.pi * (n + 0.5) * k / GROUP)
    basis[0] *= np.sqrt(0.5)
    rest = GROUP - KEEP
    high = np.zeros((LANES, 2 * rest))
    for b in range(2):
        high[b * GROUP : (b + 1) * GROUP, b * rest : (b + 1) * rest] = basis[KEEP:].T
    forward = np.zeros((7, 2 * LANES, LANES))
    for t in range(7):
        forward[t, :LANES, : 2 * rest] = high
        forward[t, LANES:, 2 * rest :] = high[:, 16 * t : 16 * t + 16]
    inverse = np.zeros((7, LANES, 2 * LANES))
    for t in range(7):
        inverse[t] = forward[t].T
    blocks = SPAN // GROUP
    keep = np.zeros((SPAN, LANES))
    mean = np.zeros((LANES, SPAN))
    for c in range(blocks):
        keep[c * GROUP : (c + 1) * GROUP, c * KEEP : (c + 1) * KEEP] = basis[:KEEP].T
        mean[c * KEEP : (c + 1) * KEEP, c * GROUP : (c + 1) * GROUP] = 1.0 / GROUP
    both = lambda table: np.concatenate(split(table), axis=-1)
    wide = np.concatenate([both(forward).reshape(-1, 2 * LANES), both(keep)], axis=0)
    back = np.concatenate([both(keep.T), mean.astype(ml_dtypes.bfloat16)], axis=-1)
    back = back.reshape(LANES, 6, WIDE).transpose(1, 0, 2).reshape(-1, WIDE)
    return wide, np.concatenate([both(inverse).reshape(-1, WIDE), back], axis=0)


def halves(value):
    top = value.astype(BF16)
    return top, (value - top.astype(F32)).astype(BF16)


def dot(a, b):
    return jnp.dot(a, b, preferred_element_type=F32)


X_UNITS = [(2, 0, 2), (2, 2, 2), (3, 0, 2), (3, 2, 2), (4, 0, 2), (4, 2, 2)]
Z_UNITS = [(0, 0, 2), (0, 2, 2), (1, 0, 2), (1, 2, 2)]
N_SEMS = 4 * len(X_UNITS) + 4 * len(Z_UNITS) + 1 + 6 + 3 + 7 + 7
PLAN = [
    ("F", 2), ("XS", 1), ("F", 0), ("ZS", 0), ("XS", 0), ("F", 3),
    ("FL", 3), ("FL", 4), ("XS", 2), ("ZS", 1), ("FL", 0), ("XS", 3),
    ("FL", 2), ("FL", 1), ("LA", 0), ("F", 1), ("ZC", 0), ("ZS", 2),
    ("XP", 1), ("XP", 2), ("LB1", 0), ("ZS", 3), ("F", 4), ("XS", 4),
    ("LB2", 0), ("ZC", 1), ("XC", 2), ("LC", 0), ("XP", 3), ("XP", 0),
    ("XP", 4), ("XS", 5), ("ZP", 0), ("ZP", 1), ("LD", 0), ("ZC", 3),
    ("XC", 3), ("ZC", 2), ("XC", 1), ("XC", 0), ("XC", 4), ("XP", 5),
    ("XE", 2), ("LF", 0), ("XE", 3), ("ZE", 0), ("BK", 3), ("ZP", 2),
    ("ZE", 1), ("BK", 0), ("ZP", 3), ("XC", 5), ("NORM", 0), ("XE", 0),
    ("XE", 1), ("ZE", 2), ("BK", 2), ("XE", 4), ("ZE", 3), ("BK", 1),
    ("XE", 5), ("BK", 4),
]


def kernel(
    grads, momentum, wide_hbm, back_hbm, new_out, upd_out,
    xin, mom, wide, back, s, lw,
    xr2, xra, xrb, xrz, zr4, zr2, zra, zrb,
    la, lb, lc, le, es, total, nm, up,
    load_sem, store_sem, send_sem, recv_sem,
):
    rep, fsdp = lax.axis_index("rep"), lax.axis_index("fsdp")
    core, y, zh = lax.rem(rep, 2), lax.rem(lax.div(rep, 2), 4), lax.div(rep, 8)
    x, z = lax.rem(fsdp, 4), lax.div(fsdp, 4)

    def ring(v, d):
        return lax.rem(v + (d + 4), 4)

    def device(z_high=None, dy=0, dcore=0, dz=0, dx=0):
        c2 = 1 - core if dcore else core
        z2 = 1 - z if dz else z
        z3 = zh if z_high is None else z_high
        return ((z3 * 4 + ring(y, dy)) * 2 + c2, z2 * 4 + ring(x, dx))

    column = [(dy, dc) for dy in range(4) for dc in range(2) if dy or dc]
    partners = [device(dy=dy, dcore=dc) for dy, dc in column]
    partners += [device(dx=d) for d in (1, 2, 3)]
    partners += [device(z_high=ring(zh, d), dz=dz) for d in range(4) for dz in range(2) if d or dz]
    barrier = pltpu.get_barrier_semaphore()
    for p in partners:
        pl.semaphore_signal(barrier, inc=1, device_id=p, device_id_type=MESH)

    used = [0]
    pending = []

    def remote(src, dst, to):
        i = used[0]
        used[0] += 1
        return pltpu.make_async_remote_copy(
            src_ref=src, dst_ref=dst, send_sem=send_sem.at[i], recv_sem=recv_sem.at[i],
            device_id=to, device_id_type=MESH,
        )

    def send(src, dst, to):
        copy = remote(src, dst, to)
        copy.start()
        pending.append(copy)
        return copy

    loads = []

    def load(src, dst):
        copy = pltpu.make_async_copy(src, dst, load_sem.at[len(loads)])
        copy.start()
        loads.append(copy)
        return copy

    waited = set()

    def arrived(copy):
        if id(copy) not in waited:
            waited.add(id(copy))
            copy.wait()

    def load_group(g):
        cols = pl.ds(g * SPAN, SPAN)
        return load(momentum.at[:, cols], mom.at[:, cols]), load(grads.at[:, cols], xin.at[pl.ds(0, GRAD), cols])

    order = [g for name, g in PLAN if name == "F"]
    front = pl.ds(0, 7 * 2 * LANES)
    rest = pl.ds(7 * 2 * LANES, SPAN)
    group_loads = {order[0]: load_group(order[0])}
    load_wide = load(wide_hbm.at[front], wide.at[front])
    load_rest = []

    def load_others():
        for g in order[1:]:
            group_loads[g] = load_group(g)
        load_rest.append(load(wide_hbm.at[rest], wide.at[rest]))
        load_rest.append(load(back_hbm, back))

    ready = set()

    def prepare(g):
        if g not in ready:
            ready.add(g)
            for copy in group_loads[g]:
                copy.wait()
            cols = slice(g * SPAN, (g + 1) * SPAN)
            top, low_part = halves(BETA * mom[:, cols])
            xin[GRAD : GRAD + MINE, cols] = top
            xin[GRAD + MINE :, cols] = low_part

    def fold(v):
        v = v[:, :LANES] + v[:, LANES:]
        own = v[GRAD : GRAD + MINE] + v[GRAD + MINE :]
        return v[:GRAD].reshape(MATS, NZL, NX, OWN, LANES), own.reshape(MATS, OWN, LANES)

    def forward(g):
        prepare(g)
        arrived(load_wide)
        if not load_rest:
            load_others()
        base = g * SPAN
        last = xin[:, base + HIGH : base + SPAN]
        for t in range(7):
            both = jnp.concatenate([xin[:, base + t * LANES : base + (t + 1) * LANES], last], axis=1)
            value, own = fold(dot(both, wide[t * 2 * LANES : (t + 1) * 2 * LANES]))
            lanes = slice(t * LANES, (t + 1) * LANES)
            s[g, :, :, :, :, lanes] = value
            s[g, :, z, x, :, lanes] += own

    def forward_low(g):
        prepare(g)
        arrived(load_rest[0])
        value, own = fold(dot(xin[:, g * SPAN : (g + 1) * SPAN], wide[7 * 2 * LANES :]))
        lanes = slice(g * LANES, (g + 1) * LANES)
        lw[:, :, :, :, lanes] = value
        lw[:, z, x, :, lanes] += own

    xd, zd, low = {}, {}, {}
    way = lambda u: 1 if u % 2 == 0 else -1
    z_way = lambda u: -way(u)

    def x_start(u):
        g, m, n = X_UNITS[u]
        d, part, rows = way(u), s.at[g, pl.ds(m, n)], (g, pl.ds(m, n))
        two = send(part.at[:, :, ring(x, 2)], xr2.at[rows], device(dx=d))
        one = send(part.at[:, :, ring(x, -d)], xra.at[rows], device(dx=-d))
        xd[u] = [two, one]

    def x_pass(u):
        g, m, n = X_UNITS[u]
        d, rows = way(u), (g, pl.ds(m, n))
        xd[u][0].wait_recv()
        to = ring(x, d)
        s[g, m : m + n, :, to] += xr2[g, m : m + n]
        xd[u].append(send(s.at[g, pl.ds(m, n), :, to], xrb.at[rows], device(dx=d)))

    def x_cross(u):
        g, m, n = X_UNITS[u]
        xd[u][1].wait_recv()
        xd[u][2].wait_recv()
        s[g, m : m + n, :, x] += xra[g, m : m + n] + xrb[g, m : m + n]
        rows = (g, pl.ds(m, n))
        xd[u].append(send(s.at[g, pl.ds(m, n), 1 - z, x], xrz.at[rows], device(dz=1)))

    def z_start(u):
        g, m, n = Z_UNITS[u]
        zd[u] = [send(s.at[g, pl.ds(m, n), 1 - z], zr4.at[g, pl.ds(m, n)], device(dz=1))]

    def z_cross(u):
        g, m, n = Z_UNITS[u]
        d, part, rows = z_way(u), s.at[g, pl.ds(m, n), z], (g, pl.ds(m, n))
        zd[u][0].wait_recv()
        s[g, m : m + n, z] += zr4[g, m : m + n]
        zd[u].append(send(part.at[:, ring(x, 2)], zr2.at[rows], device(dx=d)))
        zd[u].append(send(part.at[:, ring(x, -d)], zra.at[rows], device(dx=-d)))

    def z_pass(u):
        g, m, n = Z_UNITS[u]
        d, rows = z_way(u), (g, pl.ds(m, n))
        zd[u][1].wait_recv()
        to = ring(x, d)
        s[g, m : m + n, z, to] += zr2[g, m : m + n]
        zd[u].append(send(s.at[g, pl.ds(m, n), z, to], zrb.at[rows], device(dx=d)))

    parts = {}

    def x_end(u):
        g, m, n = X_UNITS[u]
        xd[u][3].wait_recv()
        parts[g, m] = s[g, m : m + n, z, x] + xrz[g, m : m + n]

    def z_end(u):
        g, m, n = Z_UNITS[u]
        zd[u][2].wait_recv()
        zd[u][3].wait_recv()
        parts[g, m] = s[g, m : m + n, z, x] + (zra[g, m : m + n] + zrb[g, m : m + n])

    stores = []

    def store(src, dst):
        copy = pltpu.make_async_copy(src, dst, store_sem.at[len(stores)])
        copy.start()
        stores.append(copy)

    def backward(g):
        arrived(load_rest[1])
        field = jnp.concatenate([parts[k] for k in sorted(parts) if k[0] == g], axis=0).reshape(MINE, HIGH)
        last = jnp.zeros((MINE, LANES), F32)
        for t in range(7):
            top, rest = halves(field[:, t * LANES : (t + 1) * LANES])
            v = dot(jnp.concatenate([top, rest], axis=0), back[t * LANES : (t + 1) * LANES])
            v = v[:MINE, : 2 * LANES] + (v[MINE:, : 2 * LANES] + v[:MINE, 2 * LANES :])
            base = g * SPAN + t * LANES
            nm[:, base : base + LANES] = v[:, :LANES]
            last += v[:, LANES:]
        nm[:, g * SPAN + HIGH : (g + 1) * SPAN] = last
        cols = pl.ds(g * SPAN, SPAN)
        store(nm.at[:, cols], new_out.at[:, cols])

    def low_a(_):
        low["a"] = send(lw.at[:, 1 - core], la, device(dcore=1))

    def low_b(_):
        low["a"].wait_recv()
        lw[:, core] += la[...]
        half = lambda dy, k: lw.at[ring(y, dy), core, pl.ds(2 * k, 2)]
        low["b"] = [
            send(half(2, 0), lb.at[0], device(dy=1)),
            send(half(2, 1), lb.at[1], device(dy=-1)),
            send(half(1, 1), lb.at[2], device(dy=1)),
            send(half(-1, 0), lb.at[3], device(dy=-1)),
        ]

    def low_c(_):
        for k, d in ((0, 1), (1, -1)):
            low["b"][k].wait_recv()
            lw[ring(y, d), core, 2 * k : 2 * k + 2] += lb[k]
            half = lw.at[ring(y, d), core, pl.ds(2 * k, 2)]
            low["b"].append(send(half, lb.at[4 + k], device(dy=d)))

    def low_d(_):
        for copy in low["b"][2:]:
            copy.wait_recv()
        lw[y, core, 0:2] += lb[4] + lb[3]
        lw[y, core, 2:4] += lb[2] + lb[5]
        low["d"] = [send(lw.at[y, core, ring(x, d)], lc.at[d - 1], device(dx=d)) for d in (1, 2, 3)]

    def low_e(_):
        for copy in low["d"]:
            copy.wait_recv()
        es[...] = lw[y, core, x] + (lc[0] + lc[1] + lc[2])
        low["in"] = [remote(es, le.at[d - 1], device(z_high=ring(zh, d))) for d in (1, 2, 3)]
        low["out"] = [remote(es, le.at[3 + d], device(z_high=ring(zh, d), dz=1)) for d in range(4)]

        @pl.when(core == z)
        def _():
            for copy in low["in"]:
                copy.start()

        @pl.when(core != z)
        def _():
            for copy in low["out"]:
                copy.start()

    def low_i(_):
        low["i"] = [remote(total.at[y], total.at[y], device(dy=dy, dcore=dc)) for dy, dc in column]

        @pl.when(core == z)
        def _():
            for copy in low["in"] + low["out"]:
                copy.wait_recv()
            total[y] = es[...] + ((le[0] + le[1] + le[2]) + (le[3] + le[4] + le[5] + le[6]))
            for copy in low["i"]:
                copy.start()

    def normalise(_):
        arrived(load_rest[1])

        @pl.when(core == z)
        def _():
            for copy, (dy, dc) in zip(low["i"], column):
                if dc == 0:
                    copy.wait_recv()

        @pl.when(core != z)
        def _():
            for copy, (dy, dc) in zip(low["i"], column):
                if dc == 1:
                    copy.wait_recv()

        table = lambda i: back[(7 + i) * LANES : (8 + i) * LANES]
        for g in range(GROUPS):
            lanes = slice(g * LANES, (g + 1) * LANES)
            mean = total[:, :, lanes].reshape(MINE, LANES) * (1.0 / N_REP)
            top, rest = halves(mean)
            pair = jnp.concatenate([top, rest], axis=0)
            squares = jnp.concatenate(halves(mean * mean), axis=0)
            for h in range(2):
                v, w = dot(pair, table(h)), dot(squares, table(4 + h))
                field = v[:MINE] + (v[MINE:] + dot(top, table(2 + h)))
                square = w[:MINE] + w[MINE:]
                base = g * SPAN + h * WIDE
                up[:, base : base + WIDE] = field * lax.rsqrt(field * field + square + EPS)
        store(up, upd_out)

    steps = {
        "F": forward, "FL": forward_low,
        "XS": x_start, "XP": x_pass, "XC": x_cross, "XE": x_end,
        "ZS": z_start, "ZC": z_cross, "ZP": z_pass, "ZE": z_end,
        "LA": low_a, "LB1": low_b, "LB2": low_c, "LC": low_d, "LD": low_e, "LF": low_i,
        "NORM": normalise, "BK": backward,
    }
    entered = False
    for name, u in PLAN:
        if not entered and name not in ("F", "FL"):
            pl.semaphore_wait(barrier, len(partners))
            entered = True
        steps[name](u)

    for copy in pending:
        copy.wait_send()

    @pl.when(core != z)
    def _():
        for copy in low["out"]:
            copy.wait_send()

    @pl.when(core == z)
    def _():
        for copy in low["in"] + low["i"]:
            copy.wait_send()

    for copy in stores:
        copy.wait()


def write_out(new_in, upd_in, new_out, upd_out, sems):
    copies = []
    for k, (src, dst) in enumerate([(new_in, new_out), (upd_in, upd_out)]):
        for m in range(MATS):
            rows = pl.ds(m * OWN, OWN)
            copies.append(pltpu.make_async_copy(src.at[rows], dst.at[rows], sems.at[k, m]))
    for copy in copies:
        copy.start()
    for copy in copies:
        copy.wait()


def per_device(gradients, momentum):
    wide, back = tables()
    anywhere = pl.BlockSpec(memory_space=pl.ANY)
    new_momentum, update = pl.pallas_call(
        kernel,
        out_shape=[jax.ShapeDtypeStruct((MINE, D), F32)] * 2,
        in_specs=[anywhere] * 4,
        out_specs=[anywhere] * 2,
        scratch_shapes=[
            pltpu.VMEM((GRAD + 2 * MINE, D), BF16),
            pltpu.VMEM((MINE, D), F32),
            pltpu.VMEM(wide.shape, BF16),
            pltpu.VMEM(back.shape, BF16),
            pltpu.VMEM((GROUPS, MATS, NZL, NX, OWN, HIGH), F32),
            pltpu.VMEM((MATS, NZL, NX, OWN, LOW), F32),
            *[pltpu.VMEM((GROUPS, MATS, NZL, OWN, HIGH), F32)] * 3,
            pltpu.VMEM((GROUPS, MATS, OWN, HIGH), F32),
            pltpu.VMEM((GROUPS, MATS, NX, OWN, HIGH), F32),
            *[pltpu.VMEM((GROUPS, MATS, OWN, HIGH), F32)] * 3,
            pltpu.VMEM((MATS, NX, OWN, LOW), F32),
            pltpu.VMEM((6, 2, OWN, LOW), F32),
            pltpu.VMEM((3, OWN, LOW), F32),
            pltpu.VMEM((7, OWN, LOW), F32),
            pltpu.VMEM((OWN, LOW), F32),
            pltpu.VMEM((MATS, OWN, LOW), F32),
            pltpu.VMEM((MINE, D), F32),
            pltpu.VMEM((MINE, D), F32),
            pltpu.SemaphoreType.DMA((2 * GROUPS + 3,)),
            pltpu.SemaphoreType.DMA((GROUPS + 1,)),
            pltpu.SemaphoreType.DMA((N_SEMS,)),
            pltpu.SemaphoreType.DMA((N_SEMS,)),
        ],
        compiler_params=pltpu.CompilerParams(
            collective_id=0, has_side_effects=True, vmem_limit_bytes=(52 * 1024 + 384) * 1024
        ),
        cost_estimate=pl.CostEstimate(flops=2_000_000_000, bytes_accessed=8_000_000, transcendentals=200_000),
    )(gradients.reshape(GRAD, D), momentum.reshape(MINE, D), wide, back)
    new_momentum, update = pl.pallas_call(
        write_out,
        out_shape=[jax.ShapeDtypeStruct((MINE, D), F32)] * 2,
        in_specs=[anywhere] * 2,
        out_specs=[anywhere] * 2,
        scratch_shapes=[pltpu.SemaphoreType.DMA((2, 4))],
        cost_estimate=pl.CostEstimate(flops=0, bytes_accessed=2_600_000, transcendentals=0),
    )(new_momentum, update)
    return new_momentum.reshape(1, MATS, OWN, D), update.reshape(MATS, OWN, D)


def solution(mesh):
    return jax.shard_map(
        per_device,
        mesh=mesh,
        in_specs=(P("rep", "fsdp", None, None, None), P("rep", None, "fsdp", None)),
        out_specs=(P("rep", None, "fsdp", None), P(None, "fsdp", None)),
        check_vma=False,
    )
```

```python
import jax
import jax.numpy as jnp
import ml_dtypes
import numpy as np
from jax import lax
from jax.experimental import pallas as pl
from jax.experimental.pallas import tpu as pltpu
from jax.sharding import PartitionSpec as P

D, MATS, GROUP, KEEP, ROWS = 5120, 4, 64, 8, 64
BETA, EPS = 0.999, 1e-06
NX, NY, NZL, NZH, NC, N_REP = 4, 4, 2, 4, 2, 32
OWN = 8
LANES = 128
TILES = 8
SPAN = LANES * TILES
GROUPS = D // SPAN
HIGH = 7 * LANES
LOW = GROUPS * LANES
GRAD = MATS * ROWS
MINE = MATS * OWN
WIDE = 4 * LANES

F32, BF16 = jnp.float32, jnp.bfloat16
MESH = pl.DeviceIdType.MESH


def split(table):
    high = table.astype(ml_dtypes.bfloat16)
    low = (table - high.astype(np.float64)).astype(ml_dtypes.bfloat16)
    return high, low


def tables():
    n, k = np.arange(GROUP), np.arange(GROUP)[:, None]
    basis = np.sqrt(2.0 / GROUP) * np.cos(np.pi * (n + 0.5) * k / GROUP)
    basis[0] *= np.sqrt(0.5)
    rest = GROUP - KEEP
    high = np.zeros((LANES, 2 * rest))
    for b in range(2):
        high[b * GROUP : (b + 1) * GROUP, b * rest : (b + 1) * rest] = basis[KEEP:].T
    forward = np.zeros((7, 2 * LANES, LANES))
    for t in range(7):
        forward[t, :LANES, : 2 * rest] = high
        forward[t, LANES:, 2 * rest :] = high[:, 16 * t : 16 * t + 16]
    inverse = np.zeros((7, LANES, 2 * LANES))
    for t in range(7):
        inverse[t] = forward[t].T
    blocks = SPAN // GROUP
    keep = np.zeros((SPAN, LANES))
    mean = np.zeros((LANES, SPAN))
    for c in range(blocks):
        keep[c * GROUP : (c + 1) * GROUP, c * KEEP : (c + 1) * KEEP] = basis[:KEEP].T
        mean[c * KEEP : (c + 1) * KEEP, c * GROUP : (c + 1) * GROUP] = 1.0 / GROUP
    both = lambda table: np.concatenate(split(table), axis=-1)
    wide = np.concatenate([both(forward).reshape(-1, 2 * LANES), both(keep)], axis=0)
    back = np.concatenate([both(keep.T), mean.astype(ml_dtypes.bfloat16)], axis=-1)
    back = back.reshape(LANES, 6, WIDE).transpose(1, 0, 2).reshape(-1, WIDE)
    return wide, np.concatenate([both(inverse).reshape(-1, WIDE), back], axis=0)


def halves(value):
    top = value.astype(BF16)
    return top, (value - top.astype(F32)).astype(BF16)


def dot(a, b):
    return jnp.dot(a, b, preferred_element_type=F32)


X_UNITS = [(2, 0, 2), (2, 2, 2), (3, 0, 2), (3, 2, 2), (4, 0, 2), (4, 2, 2)]
Z_UNITS = [(0, 0, 2), (0, 2, 2), (1, 0, 2), (1, 2, 2)]
N_SEMS = 4 * len(X_UNITS) + 4 * len(Z_UNITS) + 1 + 6 + 3 + 7 + 7
PLAN = [
    ("F", 2), ("XS", 1), ("F", 0), ("ZS", 0), ("XS", 0), ("F", 3),
    ("FL", 3), ("FL", 4), ("XS", 2), ("ZS", 1), ("FL", 0), ("XS", 3),
    ("FL", 2), ("FL", 1), ("LA", 0), ("F", 1), ("ZC", 0), ("ZS", 2),
    ("XP", 1), ("XP", 2), ("LB1", 0), ("ZS", 3), ("F", 4), ("XS", 4),
    ("LB2", 0), ("ZC", 1), ("XC", 2), ("LC", 0), ("XP", 3), ("XP", 0),
    ("XP", 4), ("XS", 5), ("ZP", 0), ("ZP", 1), ("LD", 0), ("ZC", 3),
    ("XC", 3), ("ZC", 2), ("XC", 1), ("XC", 0), ("XC", 4), ("XP", 5),
    ("XE", 2), ("LF", 0), ("XE", 3), ("ZE", 0), ("BK", 3), ("ZP", 2),
    ("ZE", 1), ("BK", 0), ("ZP", 3), ("XC", 5), ("NORM", 0), ("XE", 0),
    ("XE", 1), ("ZE", 2), ("BK", 2), ("XE", 4), ("ZE", 3), ("BK", 1),
    ("XE", 5), ("BK", 4),
]


def kernel(
    grads, momentum, wide_hbm, back_hbm, new_out, upd_out,
    xin, mom, wide, back, s, lw,
    xr2, xra, xrb, xrz, zr4, zr2, zra, zrb,
    la, lb, lc, le, es, total, nm, up,
    load_sem, store_sem, send_sem, recv_sem,
):
    rep, fsdp = lax.axis_index("rep"), lax.axis_index("fsdp")
    core, y, zh = lax.rem(rep, 2), lax.rem(lax.div(rep, 2), 4), lax.div(rep, 8)
    x, z = lax.rem(fsdp, 4), lax.div(fsdp, 4)

    def ring(v, d):
        return lax.rem(v + (d + 4), 4)

    def device(z_high=None, dy=0, dcore=0, dz=0, dx=0):
        c2 = 1 - core if dcore else core
        z2 = 1 - z if dz else z
        z3 = zh if z_high is None else z_high
        return ((z3 * 4 + ring(y, dy)) * 2 + c2, z2 * 4 + ring(x, dx))

    column = [(dy, dc) for dy in range(4) for dc in range(2) if dy or dc]
    partners = [device(dy=dy, dcore=dc) for dy, dc in column]
    partners += [device(dx=d) for d in (1, 2, 3)]
    partners += [device(z_high=ring(zh, d), dz=dz) for d in range(4) for dz in range(2) if d or dz]
    barrier = pltpu.get_barrier_semaphore()
    for p in partners:
        pl.semaphore_signal(barrier, inc=1, device_id=p, device_id_type=MESH)

    used = [0]
    pending = []

    def remote(src, dst, to):
        i = used[0]
        used[0] += 1
        return pltpu.make_async_remote_copy(
            src_ref=src, dst_ref=dst, send_sem=send_sem.at[i], recv_sem=recv_sem.at[i],
            device_id=to, device_id_type=MESH,
        )

    def send(src, dst, to):
        copy = remote(src, dst, to)
        copy.start()
        pending.append(copy)
        return copy

    loads = []

    def load(src, dst):
        copy = pltpu.make_async_copy(src, dst, load_sem.at[len(loads)])
        copy.start()
        loads.append(copy)
        return copy

    waited = set()

    def arrived(copy):
        if id(copy) not in waited:
            waited.add(id(copy))
            copy.wait()

    def load_group(g):
        cols = pl.ds(g * SPAN, SPAN)
        return load(momentum.at[:, cols], mom.at[:, cols]), load(grads.at[:, cols], xin.at[pl.ds(0, GRAD), cols])

    order = [g for name, g in PLAN if name == "F"]
    front = pl.ds(0, 7 * 2 * LANES)
    rest = pl.ds(7 * 2 * LANES, SPAN)
    group_loads = {order[0]: load_group(order[0])}
    load_wide = load(wide_hbm.at[front], wide.at[front])
    load_rest = []

    def load_others():
        for g in order[1:]:
            group_loads[g] = load_group(g)
        load_rest.append(load(wide_hbm.at[rest], wide.at[rest]))
        load_rest.append(load(back_hbm, back))

    ready = set()

    def prepare(g):
        if g not in ready:
            ready.add(g)
            for copy in group_loads[g]:
                copy.wait()
            cols = slice(g * SPAN, (g + 1) * SPAN)
            top, low_part = halves(BETA * mom[:, cols])
            xin[GRAD : GRAD + MINE, cols] = top
            xin[GRAD + MINE :, cols] = low_part

    def fold(v):
        v = v[:, :LANES] + v[:, LANES:]
        own = v[GRAD : GRAD + MINE] + v[GRAD + MINE :]
        return v[:GRAD].reshape(MATS, NZL, NX, OWN, LANES), own.reshape(MATS, OWN, LANES)

    def forward(g):
        prepare(g)
        arrived(load_wide)
        if not load_rest:
            load_others()
        base = g * SPAN
        last = xin[:, base + HIGH : base + SPAN]
        for t in range(7):
            both = jnp.concatenate([xin[:, base + t * LANES : base + (t + 1) * LANES], last], axis=1)
            value, own = fold(dot(both, wide[t * 2 * LANES : (t + 1) * 2 * LANES]))
            lanes = slice(t * LANES, (t + 1) * LANES)
            s[g, :, :, :, :, lanes] = value
            s[g, :, z, x, :, lanes] += own

    def forward_low(g):
        prepare(g)
        arrived(load_rest[0])
        value, own = fold(dot(xin[:, g * SPAN : (g + 1) * SPAN], wide[7 * 2 * LANES :]))
        lanes = slice(g * LANES, (g + 1) * LANES)
        lw[:, :, :, :, lanes] = value
        lw[:, z, x, :, lanes] += own

    xd, zd, low = {}, {}, {}
    way = lambda u: 1 if u % 2 == 0 else -1
    z_way = lambda u: -way(u)

    def x_start(u):
        g, m, n = X_UNITS[u]
        d, part, rows = way(u), s.at[g, pl.ds(m, n)], (g, pl.ds(m, n))
        two = send(part.at[:, :, ring(x, 2)], xr2.at[rows], device(dx=d))
        one = send(part.at[:, :, ring(x, -d)], xra.at[rows], device(dx=-d))
        xd[u] = [two, one]

    def x_pass(u):
        g, m, n = X_UNITS[u]
        d, rows = way(u), (g, pl.ds(m, n))
        xd[u][0].wait_recv()
        to = ring(x, d)
        s[g, m : m + n, :, to] += xr2[g, m : m + n]
        xd[u].append(send(s.at[g, pl.ds(m, n), :, to], xrb.at[rows], device(dx=d)))

    def x_cross(u):
        g, m, n = X_UNITS[u]
        xd[u][1].wait_recv()
        xd[u][2].wait_recv()
        s[g, m : m + n, :, x] += xra[g, m : m + n] + xrb[g, m : m + n]
        rows = (g, pl.ds(m, n))
        xd[u].append(send(s.at[g, pl.ds(m, n), 1 - z, x], xrz.at[rows], device(dz=1)))

    def z_start(u):
        g, m, n = Z_UNITS[u]
        zd[u] = [send(s.at[g, pl.ds(m, n), 1 - z], zr4.at[g, pl.ds(m, n)], device(dz=1))]

    def z_cross(u):
        g, m, n = Z_UNITS[u]
        d, part, rows = z_way(u), s.at[g, pl.ds(m, n), z], (g, pl.ds(m, n))
        zd[u][0].wait_recv()
        s[g, m : m + n, z] += zr4[g, m : m + n]
        zd[u].append(send(part.at[:, ring(x, 2)], zr2.at[rows], device(dx=d)))
        zd[u].append(send(part.at[:, ring(x, -d)], zra.at[rows], device(dx=-d)))

    def z_pass(u):
        g, m, n = Z_UNITS[u]
        d, rows = z_way(u), (g, pl.ds(m, n))
        zd[u][1].wait_recv()
        to = ring(x, d)
        s[g, m : m + n, z, to] += zr2[g, m : m + n]
        zd[u].append(send(s.at[g, pl.ds(m, n), z, to], zrb.at[rows], device(dx=d)))

    parts = {}

    def x_end(u):
        g, m, n = X_UNITS[u]
        xd[u][3].wait_recv()
        parts[g, m] = s[g, m : m + n, z, x] + xrz[g, m : m + n]

    def z_end(u):
        g, m, n = Z_UNITS[u]
        zd[u][2].wait_recv()
        zd[u][3].wait_recv()
        parts[g, m] = s[g, m : m + n, z, x] + (zra[g, m : m + n] + zrb[g, m : m + n])

    stores = []

    def store(src, dst):
        copy = pltpu.make_async_copy(src, dst, store_sem.at[len(stores)])
        copy.start()
        stores.append(copy)

    def backward(g):
        arrived(load_rest[1])
        field = jnp.concatenate([parts[k] for k in sorted(parts) if k[0] == g], axis=0).reshape(MINE, HIGH)
        last = jnp.zeros((MINE, LANES), F32)
        for t in range(7):
            top, rest = halves(field[:, t * LANES : (t + 1) * LANES])
            v = dot(jnp.concatenate([top, rest], axis=0), back[t * LANES : (t + 1) * LANES])
            v = v[:MINE, : 2 * LANES] + (v[MINE:, : 2 * LANES] + v[:MINE, 2 * LANES :])
            base = g * SPAN + t * LANES
            nm[:, base : base + LANES] = v[:, :LANES]
            last += v[:, LANES:]
        nm[:, g * SPAN + HIGH : (g + 1) * SPAN] = last
        cols = pl.ds(g * SPAN, SPAN)
        store(nm.at[:, cols], new_out.at[:, cols])

    def low_a(_):
        low["a"] = send(lw.at[:, 1 - core], la, device(dcore=1))

    def low_b(_):
        low["a"].wait_recv()
        lw[:, core] += la[...]
        half = lambda dy, k: lw.at[ring(y, dy), core, pl.ds(2 * k, 2)]
        low["b"] = [
            send(half(2, 0), lb.at[0], device(dy=1)),
            send(half(2, 1), lb.at[1], device(dy=-1)),
            send(half(1, 1), lb.at[2], device(dy=1)),
            send(half(-1, 0), lb.at[3], device(dy=-1)),
        ]

    def low_c(_):
        for k, d in ((0, 1), (1, -1)):
            low["b"][k].wait_recv()
            lw[ring(y, d), core, 2 * k : 2 * k + 2] += lb[k]
            half = lw.at[ring(y, d), core, pl.ds(2 * k, 2)]
            low["b"].append(send(half, lb.at[4 + k], device(dy=d)))

    def low_d(_):
        for copy in low["b"][2:]:
            copy.wait_recv()
        lw[y, core, 0:2] += lb[4] + lb[3]
        lw[y, core, 2:4] += lb[2] + lb[5]
        low["d"] = [send(lw.at[y, core, ring(x, d)], lc.at[d - 1], device(dx=d)) for d in (1, 2, 3)]

    def low_e(_):
        for copy in low["d"]:
            copy.wait_recv()
        es[...] = lw[y, core, x] + (lc[0] + lc[1] + lc[2])
        low["in"] = [remote(es, le.at[d - 1], device(z_high=ring(zh, d))) for d in (1, 2, 3)]
        low["out"] = [remote(es, le.at[3 + d], device(z_high=ring(zh, d), dz=1)) for d in range(4)]

        @pl.when(core == z)
        def _():
            for copy in low["in"]:
                copy.start()

        @pl.when(core != z)
        def _():
            for copy in low["out"]:
                copy.start()

    def low_i(_):
        low["i"] = [remote(total.at[y], total.at[y], device(dy=dy, dcore=dc)) for dy, dc in column]

        @pl.when(core == z)
        def _():
            for copy in low["in"] + low["out"]:
                copy.wait_recv()
            total[y] = es[...] + ((le[0] + le[1] + le[2]) + (le[3] + le[4] + le[5] + le[6]))
            for copy in low["i"]:
                copy.start()

    def normalise(_):
        arrived(load_rest[1])

        @pl.when(core == z)
        def _():
            for copy, (dy, dc) in zip(low["i"], column):
                if dc == 0:
                    copy.wait_recv()

        @pl.when(core != z)
        def _():
            for copy, (dy, dc) in zip(low["i"], column):
                if dc == 1:
                    copy.wait_recv()

        table = lambda i: back[(7 + i) * LANES : (8 + i) * LANES]
        for g in range(GROUPS):
            lanes = slice(g * LANES, (g + 1) * LANES)
            mean = total[:, :, lanes].reshape(MINE, LANES) * (1.0 / N_REP)
            top, rest = halves(mean)
            pair = jnp.concatenate([top, rest], axis=0)
            squares = jnp.concatenate(halves(mean * mean), axis=0)
            for h in range(2):
                v, w = dot(pair, table(h)), dot(squares, table(4 + h))
                field = v[:MINE] + (v[MINE:] + dot(top, table(2 + h)))
                square = w[:MINE] + w[MINE:]
                base = g * SPAN + h * WIDE
                up[:, base : base + WIDE] = field * lax.rsqrt(field * field + square + EPS)
        store(up, upd_out)

    steps = {
        "F": forward, "FL": forward_low,
        "XS": x_start, "XP": x_pass, "XC": x_cross, "XE": x_end,
        "ZS": z_start, "ZC": z_cross, "ZP": z_pass, "ZE": z_end,
        "LA": low_a, "LB1": low_b, "LB2": low_c, "LC": low_d, "LD": low_e, "LF": low_i,
        "NORM": normalise, "BK": backward,
    }
    entered = False
    for name, u in PLAN:
        if not entered and name not in ("F", "FL"):
            pl.semaphore_wait(barrier, len(partners))
            entered = True
        steps[name](u)

    for copy in pending:
        copy.wait_send()

    @pl.when(core != z)
    def _():
        for copy in low["out"]:
            copy.wait_send()

    @pl.when(core == z)
    def _():
        for copy in low["in"] + low["i"]:
            copy.wait_send()

    for copy in stores:
        copy.wait()


def write_out(new_in, upd_in, new_out, upd_out, sems):
    copies = []
    for k, (src, dst) in enumerate([(new_in, new_out), (upd_in, upd_out)]):
        for m in range(MATS):
            rows = pl.ds(m * OWN, OWN)
            copies.append(pltpu.make_async_copy(src.at[rows], dst.at[rows], sems.at[k, m]))
    for copy in copies:
        copy.start()
    for copy in copies:
        copy.wait()


def per_device(gradients, momentum):
    wide, back = tables()
    anywhere = pl.BlockSpec(memory_space=pl.ANY)
    new_momentum, update = pl.pallas_call(
        kernel,
        out_shape=[jax.ShapeDtypeStruct((MINE, D), F32)] * 2,
        in_specs=[anywhere] * 4,
        out_specs=[anywhere] * 2,
        scratch_shapes=[
            pltpu.VMEM((GRAD + 2 * MINE, D), BF16),
            pltpu.VMEM((MINE, D), F32),
            pltpu.VMEM(wide.shape, BF16),
            pltpu.VMEM(back.shape, BF16),
            pltpu.VMEM((GROUPS, MATS, NZL, NX, OWN, HIGH), F32),
            pltpu.VMEM((MATS, NZL, NX, OWN, LOW), F32),
            *[pltpu.VMEM((GROUPS, MATS, NZL, OWN, HIGH), F32)] * 3,
            pltpu.VMEM((GROUPS, MATS, OWN, HIGH), F32),
            pltpu.VMEM((GROUPS, MATS, NX, OWN, HIGH), F32),
            *[pltpu.VMEM((GROUPS, MATS, OWN, HIGH), F32)] * 3,
            pltpu.VMEM((MATS, NX, OWN, LOW), F32),
            pltpu.VMEM((6, 2, OWN, LOW), F32),
            pltpu.VMEM((3, OWN, LOW), F32),
            pltpu.VMEM((7, OWN, LOW), F32),
            pltpu.VMEM((OWN, LOW), F32),
            pltpu.VMEM((MATS, OWN, LOW), F32),
            pltpu.VMEM((MINE, D), F32),
            pltpu.VMEM((MINE, D), F32),
            pltpu.SemaphoreType.DMA((2 * GROUPS + 3,)),
            pltpu.SemaphoreType.DMA((GROUPS + 1,)),
            pltpu.SemaphoreType.DMA((N_SEMS,)),
            pltpu.SemaphoreType.DMA((N_SEMS,)),
        ],
        compiler_params=pltpu.CompilerParams(
            collective_id=0, has_side_effects=True, vmem_limit_bytes=(52 * 1024 + 384) * 1024
        ),
        cost_estimate=pl.CostEstimate(flops=2_000_000_000, bytes_accessed=8_000_000, transcendentals=200_000),
    )(gradients.reshape(GRAD, D), momentum.reshape(MINE, D), wide, back)
    new_momentum, update = pl.pallas_call(
        write_out,
        out_shape=[jax.ShapeDtypeStruct((MINE, D), F32)] * 2,
        in_specs=[anywhere] * 2,
        out_specs=[anywhere] * 2,
        scratch_shapes=[pltpu.SemaphoreType.DMA((2, 4))],
        compiler_params=pltpu.CompilerParams(vmem_limit_bytes=4 * 1024 * 1024),
        cost_estimate=pl.CostEstimate(flops=0, bytes_accessed=2_600_000, transcendentals=0),
    )(new_momentum, update)
    return new_momentum.reshape(1, MATS, OWN, D), update.reshape(MATS, OWN, D)


def solution(mesh):
    return jax.shard_map(
        per_device,
        mesh=mesh,
        in_specs=(P("rep", "fsdp", None, None, None), P("rep", None, "fsdp", None)),
        out_specs=(P("rep", None, "fsdp", None), P(None, "fsdp", None)),
        check_vma=False,
    )
```

```python
import jax
import jax.numpy as jnp
import ml_dtypes
import numpy as np
from jax import lax
from jax.experimental import pallas as pl
from jax.experimental.pallas import tpu as pltpu
from jax.sharding import PartitionSpec as P

D, MATS, GROUP, KEEP, ROWS = 5120, 4, 64, 8, 64
BETA, EPS = 0.999, 1e-06
NX, NY, NZL, NZH, NC, N_REP = 4, 4, 2, 4, 2, 32
OWN = 8
LANES = 128
TILES = 8
SPAN = LANES * TILES
GROUPS = D // SPAN
HIGH = 7 * LANES
LOW = GROUPS * LANES
GRAD = MATS * ROWS
MINE = MATS * OWN
WIDE = 4 * LANES

F32, BF16 = jnp.float32, jnp.bfloat16
MESH = pl.DeviceIdType.MESH


def split(table):
    high = table.astype(ml_dtypes.bfloat16)
    low = (table - high.astype(np.float64)).astype(ml_dtypes.bfloat16)
    return high, low


def tables():
    n, k = np.arange(GROUP), np.arange(GROUP)[:, None]
    basis = np.sqrt(2.0 / GROUP) * np.cos(np.pi * (n + 0.5) * k / GROUP)
    basis[0] *= np.sqrt(0.5)
    rest = GROUP - KEEP
    high = np.zeros((LANES, 2 * rest))
    for b in range(2):
        high[b * GROUP : (b + 1) * GROUP, b * rest : (b + 1) * rest] = basis[KEEP:].T
    forward = np.zeros((7, 2 * LANES, LANES))
    for t in range(7):
        forward[t, :LANES, : 2 * rest] = high
        forward[t, LANES:, 2 * rest :] = high[:, 16 * t : 16 * t + 16]
    inverse = np.zeros((7, LANES, 2 * LANES))
    for t in range(7):
        inverse[t] = forward[t].T
    blocks = SPAN // GROUP
    keep = np.zeros((SPAN, LANES))
    mean = np.zeros((LANES, SPAN))
    for c in range(blocks):
        keep[c * GROUP : (c + 1) * GROUP, c * KEEP : (c + 1) * KEEP] = basis[:KEEP].T
        mean[c * KEEP : (c + 1) * KEEP, c * GROUP : (c + 1) * GROUP] = 1.0 / GROUP
    both = lambda table: np.concatenate(split(table), axis=-1)
    wide = np.concatenate([both(forward).reshape(-1, 2 * LANES), both(keep)], axis=0)
    back = np.concatenate([both(keep.T), mean.astype(ml_dtypes.bfloat16)], axis=-1)
    back = back.reshape(LANES, 6, WIDE).transpose(1, 0, 2).reshape(-1, WIDE)
    return wide, np.concatenate([both(inverse).reshape(-1, WIDE), back], axis=0)


def halves(value):
    top = value.astype(BF16)
    return top, (value - top.astype(F32)).astype(BF16)


def dot(a, b):
    return jnp.dot(a, b, preferred_element_type=F32)


X_UNITS = [(2, 0, 2), (2, 2, 2), (3, 0, 2), (3, 2, 2), (4, 0, 2), (4, 2, 2)]
Z_UNITS = [(0, 0, 2), (0, 2, 2), (1, 0, 2), (1, 2, 2)]
N_SEMS = 4 * len(X_UNITS) + 4 * len(Z_UNITS) + 1 + 6 + 3 + 7 + 7
PLAN = [
    ("F", 2), ("XS", 1), ("F", 1), ("ZS", 2), ("XS", 0), ("FL", 0),
    ("FL", 4), ("FL", 3), ("FL", 2), ("FL", 1), ("LA", 0), ("F", 3),
    ("XS", 2), ("ZS", 3), ("F", 4), ("XP", 0), ("XS", 4), ("LB1", 0),
    ("XS", 3), ("XS", 5), ("XP", 1), ("F", 0), ("ZS", 0), ("LB2", 0),
    ("ZS", 1), ("LC", 0), ("XP", 4), ("ZC", 2), ("ZC", 3), ("ZC", 0),
    ("XP", 3), ("LD", 0), ("XP", 5), ("XC", 1), ("ZP", 0), ("XP", 2),
    ("XC", 0), ("XC", 3), ("ZP", 2), ("ZC", 1), ("ZP", 3), ("XC", 4),
    ("XC", 5), ("XE", 1), ("XE", 3), ("XC", 2), ("XE", 0), ("ZE", 0),
    ("BK", 2), ("XE", 4), ("ZP", 1), ("LF", 0), ("XE", 5), ("BK", 4),
    ("ZE", 3), ("ZE", 2), ("BK", 1), ("XE", 2), ("BK", 3), ("ZE", 1),
    ("BK", 0), ("NORM", 0),
]


def kernel(
    grads, momentum, wide_hbm, back_hbm, new_out, upd_out,
    xin, mom, wide, back, s, lw,
    xr2, xra, xrb, xrz, zr4, zr2, zra, zrb,
    la, lb, lc, le, es, total, nm, up,
    load_sem, store_sem, send_sem, recv_sem, column_sem, stack_sem,
):
    rep, fsdp = lax.axis_index("rep"), lax.axis_index("fsdp")
    core, y, zh = lax.rem(rep, 2), lax.rem(lax.div(rep, 2), 4), lax.div(rep, 8)
    x, z = lax.rem(fsdp, 4), lax.div(fsdp, 4)

    def ring(v, d):
        return lax.rem(v + (d + 4), 4)

    def device(z_high=None, dy=0, dcore=0, dz=0, dx=0):
        c2 = 1 - core if dcore else core
        z2 = 1 - z if dz else z
        z3 = zh if z_high is None else z_high
        return ((z3 * 4 + ring(y, dy)) * 2 + c2, z2 * 4 + ring(x, dx))

    column = [(dy, dc) for dy in range(4) for dc in range(2) if dy or dc]
    stack = [(d, dz) for d in (1, 2, 3) for dz in range(2)]
    barrier = pltpu.get_barrier_semaphore()

    def greet(sem, p):
        pl.semaphore_signal(sem, inc=1, device_id=p, device_id_type=MESH)

    def later_in_column(dy, dc):
        if dy:
            return ring(y, dy) > y
        return core == 1

    def later_in_stack(d):
        return ring(zh, d) > zh

    def greet_others(sem_of, later):
        for dy, dc in column:
            test = later_in_column(dy, dc)

            @pl.when(test if later else jnp.logical_not(test))
            def _():
                greet(sem_of[0], device(dy=dy, dcore=dc))

        for d, dz in stack:
            test = later_in_stack(d)

            @pl.when(test if later else jnp.logical_not(test))
            def _():
                greet(sem_of[1], device(z_high=ring(zh, d), dz=dz))

    for d in (1, 2, 3):
        greet(barrier, device(dx=d))
    greet(barrier, device(dz=1))
    greet_others((barrier, barrier), True)
    column_later = 2 * (3 - y) + core
    stack_later = 2 * (3 - zh)

    def enter():
        pl.semaphore_wait(barrier, 4 + (7 - column_later) + (6 - stack_later))
        greet_others((column_sem, stack_sem), False)

    used = [0]
    pending = []

    def remote(src, dst, to):
        i = used[0]
        used[0] += 1
        return pltpu.make_async_remote_copy(
            src_ref=src, dst_ref=dst, send_sem=send_sem.at[i], recv_sem=recv_sem.at[i],
            device_id=to, device_id_type=MESH,
        )

    def send(src, dst, to):
        copy = remote(src, dst, to)
        copy.start()
        pending.append(copy)
        return copy

    loads = []

    def load(src, dst):
        copy = pltpu.make_async_copy(src, dst, load_sem.at[len(loads)])
        copy.start()
        loads.append(copy)
        return copy

    waited = set()

    def arrived(copy):
        if id(copy) not in waited:
            waited.add(id(copy))
            copy.wait()

    def load_group(g):
        cols = pl.ds(g * SPAN, SPAN)
        return load(momentum.at[:, cols], mom.at[:, cols]), load(grads.at[:, cols], xin.at[pl.ds(0, GRAD), cols])

    order = [g for name, g in PLAN if name == "F"]
    front = pl.ds(0, 7 * 2 * LANES)
    rest = pl.ds(7 * 2 * LANES, SPAN)
    group_loads = {order[0]: load_group(order[0])}
    load_wide = load(wide_hbm.at[front], wide.at[front])
    load_rest = []

    def load_others():
        for g in order[1:]:
            group_loads[g] = load_group(g)
        load_rest.append(load(wide_hbm.at[rest], wide.at[rest]))
        load_rest.append(load(back_hbm, back))

    ready = set()

    def prepare(g):
        if g not in ready:
            ready.add(g)
            for copy in group_loads[g]:
                copy.wait()
            cols = slice(g * SPAN, (g + 1) * SPAN)
            top, low_part = halves(BETA * mom[:, cols])
            xin[GRAD : GRAD + MINE, cols] = top
            xin[GRAD + MINE :, cols] = low_part

    def fold(v):
        v = v[:, :LANES] + v[:, LANES:]
        own = v[GRAD : GRAD + MINE] + v[GRAD + MINE :]
        return v[:GRAD].reshape(MATS, NZL, NX, OWN, LANES), own.reshape(MATS, OWN, LANES)

    def forward(g):
        prepare(g)
        arrived(load_wide)
        if not load_rest:
            load_others()
        base = g * SPAN
        last = xin[:, base + HIGH : base + SPAN]
        for t in range(7):
            both = jnp.concatenate([xin[:, base + t * LANES : base + (t + 1) * LANES], last], axis=1)
            value, own = fold(dot(both, wide[t * 2 * LANES : (t + 1) * 2 * LANES]))
            lanes = slice(t * LANES, (t + 1) * LANES)
            s[g, :, :, :, :, lanes] = value
            s[g, :, z, x, :, lanes] += own

    def forward_low(g):
        prepare(g)
        arrived(load_rest[0])
        value, own = fold(dot(xin[:, g * SPAN : (g + 1) * SPAN], wide[7 * 2 * LANES :]))
        lanes = slice(g * LANES, (g + 1) * LANES)
        lw[:, :, :, :, lanes] = value
        lw[:, z, x, :, lanes] += own

    xd, zd, low = {}, {}, {}
    way = lambda u: 1 if u % 2 == 0 else -1
    z_way = lambda u: -way(u)

    def x_start(u):
        g, m, n = X_UNITS[u]
        d, part, rows = way(u), s.at[g, pl.ds(m, n)], (g, pl.ds(m, n))
        two = send(part.at[:, :, ring(x, 2)], xr2.at[rows], device(dx=d))
        one = send(part.at[:, :, ring(x, -d)], xra.at[rows], device(dx=-d))
        xd[u] = [two, one]

    def x_pass(u):
        g, m, n = X_UNITS[u]
        d, rows = way(u), (g, pl.ds(m, n))
        xd[u][0].wait_recv()
        to = ring(x, d)
        s[g, m : m + n, :, to] += xr2[g, m : m + n]
        xd[u].append(send(s.at[g, pl.ds(m, n), :, to], xrb.at[rows], device(dx=d)))

    def x_cross(u):
        g, m, n = X_UNITS[u]
        xd[u][1].wait_recv()
        xd[u][2].wait_recv()
        s[g, m : m + n, :, x] += xra[g, m : m + n] + xrb[g, m : m + n]
        rows = (g, pl.ds(m, n))
        xd[u].append(send(s.at[g, pl.ds(m, n), 1 - z, x], xrz.at[rows], device(dz=1)))

    def z_start(u):
        g, m, n = Z_UNITS[u]
        zd[u] = [send(s.at[g, pl.ds(m, n), 1 - z], zr4.at[g, pl.ds(m, n)], device(dz=1))]

    def z_cross(u):
        g, m, n = Z_UNITS[u]
        d, part, rows = z_way(u), s.at[g, pl.ds(m, n), z], (g, pl.ds(m, n))
        zd[u][0].wait_recv()
        s[g, m : m + n, z] += zr4[g, m : m + n]
        zd[u].append(send(part.at[:, ring(x, 2)], zr2.at[rows], device(dx=d)))
        zd[u].append(send(part.at[:, ring(x, -d)], zra.at[rows], device(dx=-d)))

    def z_pass(u):
        g, m, n = Z_UNITS[u]
        d, rows = z_way(u), (g, pl.ds(m, n))
        zd[u][1].wait_recv()
        to = ring(x, d)
        s[g, m : m + n, z, to] += zr2[g, m : m + n]
        zd[u].append(send(s.at[g, pl.ds(m, n), z, to], zrb.at[rows], device(dx=d)))

    parts = {}

    def x_end(u):
        g, m, n = X_UNITS[u]
        xd[u][3].wait_recv()
        parts[g, m] = s[g, m : m + n, z, x] + xrz[g, m : m + n]

    def z_end(u):
        g, m, n = Z_UNITS[u]
        zd[u][2].wait_recv()
        zd[u][3].wait_recv()
        parts[g, m] = s[g, m : m + n, z, x] + (zra[g, m : m + n] + zrb[g, m : m + n])

    stores = []

    def store(src, dst):
        copy = pltpu.make_async_copy(src, dst, store_sem.at[len(stores)])
        copy.start()
        stores.append(copy)

    def backward(g):
        arrived(load_rest[1])
        field = jnp.concatenate([parts[k] for k in sorted(parts) if k[0] == g], axis=0).reshape(MINE, HIGH)
        last = jnp.zeros((MINE, LANES), F32)
        for t in range(7):
            top, rest = halves(field[:, t * LANES : (t + 1) * LANES])
            v = dot(jnp.concatenate([top, rest], axis=0), back[t * LANES : (t + 1) * LANES])
            v = v[:MINE, : 2 * LANES] + (v[MINE:, : 2 * LANES] + v[:MINE, 2 * LANES :])
            base = g * SPAN + t * LANES
            nm[:, base : base + LANES] = v[:, :LANES]
            last += v[:, LANES:]
        nm[:, g * SPAN + HIGH : (g + 1) * SPAN] = last
        cols = pl.ds(g * SPAN, SPAN)
        store(nm.at[:, cols], new_out.at[:, cols])

    def low_a(_):
        @pl.when(column_later > 0)
        def _():
            pl.semaphore_wait(column_sem, column_later)

        low["a"] = send(lw.at[:, 1 - core], la, device(dcore=1))

    def low_b(_):
        low["a"].wait_recv()
        lw[:, core] += la[...]
        half = lambda dy, k: lw.at[ring(y, dy), core, pl.ds(2 * k, 2)]
        low["b"] = [
            send(half(2, 0), lb.at[0], device(dy=1)),
            send(half(2, 1), lb.at[1], device(dy=-1)),
            send(half(1, 1), lb.at[2], device(dy=1)),
            send(half(-1, 0), lb.at[3], device(dy=-1)),
        ]

    def low_c(_):
        for k, d in ((0, 1), (1, -1)):
            low["b"][k].wait_recv()
            lw[ring(y, d), core, 2 * k : 2 * k + 2] += lb[k]
            half = lw.at[ring(y, d), core, pl.ds(2 * k, 2)]
            low["b"].append(send(half, lb.at[4 + k], device(dy=d)))

    def low_d(_):
        for copy in low["b"][2:]:
            copy.wait_recv()
        lw[y, core, 0:2] += lb[4] + lb[3]
        lw[y, core, 2:4] += lb[2] + lb[5]
        low["d"] = [send(lw.at[y, core, ring(x, d)], lc.at[d - 1], device(dx=d)) for d in (1, 2, 3)]

    def low_e(_):
        for copy in low["d"]:
            copy.wait_recv()
        es[...] = lw[y, core, x] + (lc[0] + lc[1] + lc[2])
        low["in"] = [remote(es, le.at[d - 1], device(z_high=ring(zh, d))) for d in (1, 2, 3)]
        @pl.when(stack_later > 0)
        def _():
            pl.semaphore_wait(stack_sem, stack_later)

        low["out"] = [remote(es, le.at[3 + d], device(z_high=ring(zh, d), dz=1)) for d in range(4)]

        @pl.when(core == z)
        def _():
            for copy in low["in"]:
                copy.start()

        @pl.when(core != z)
        def _():
            for copy in low["out"]:
                copy.start()

    def low_i(_):
        low["i"] = [remote(total.at[y], total.at[y], device(dy=dy, dcore=dc)) for dy, dc in column]

        @pl.when(core == z)
        def _():
            for copy in low["in"] + low["out"]:
                copy.wait_recv()
            total[y] = es[...] + ((le[0] + le[1] + le[2]) + (le[3] + le[4] + le[5] + le[6]))
            for copy in low["i"]:
                copy.start()

    def normalise(_):
        arrived(load_rest[1])

        @pl.when(core == z)
        def _():
            for copy, (dy, dc) in zip(low["i"], column):
                if dc == 0:
                    copy.wait_recv()

        @pl.when(core != z)
        def _():
            for copy, (dy, dc) in zip(low["i"], column):
                if dc == 1:
                    copy.wait_recv()

        table = lambda i: back[(7 + i) * LANES : (8 + i) * LANES]
        for g in range(GROUPS):
            lanes = slice(g * LANES, (g + 1) * LANES)
            mean = total[:, :, lanes].reshape(MINE, LANES) * (1.0 / N_REP)
            top, rest = halves(mean)
            pair = jnp.concatenate([top, rest], axis=0)
            squares = jnp.concatenate(halves(mean * mean), axis=0)
            for h in range(2):
                v, w = dot(pair, table(h)), dot(squares, table(4 + h))
                field = v[:MINE] + (v[MINE:] + dot(top, table(2 + h)))
                square = w[:MINE] + w[MINE:]
                base = g * SPAN + h * WIDE
                up[:, base : base + WIDE] = field * lax.rsqrt(field * field + square + EPS)
        store(up, upd_out)

    steps = {
        "F": forward, "FL": forward_low,
        "XS": x_start, "XP": x_pass, "XC": x_cross, "XE": x_end,
        "ZS": z_start, "ZC": z_cross, "ZP": z_pass, "ZE": z_end,
        "LA": low_a, "LB1": low_b, "LB2": low_c, "LC": low_d, "LD": low_e, "LF": low_i,
        "NORM": normalise, "BK": backward,
    }
    entered = False
    for name, u in PLAN:
        if not entered and name not in ("F", "FL"):
            enter()
            entered = True
        steps[name](u)

    for copy in pending:
        copy.wait_send()

    @pl.when(core != z)
    def _():
        for copy in low["out"]:
            copy.wait_send()

    @pl.when(core == z)
    def _():
        for copy in low["in"] + low["i"]:
            copy.wait_send()

    for copy in stores:
        copy.wait()


def write_out(new_in, upd_in, new_out, upd_out, sems):
    copies = []
    for k, (src, dst) in enumerate([(new_in, new_out), (upd_in, upd_out)]):
        for m in range(MATS):
            rows = pl.ds(m * OWN, OWN)
            copies.append(pltpu.make_async_copy(src.at[rows], dst.at[rows], sems.at[k, m]))
    for copy in copies:
        copy.start()
    for copy in copies:
        copy.wait()


def per_device(gradients, momentum):
    wide, back = tables()
    anywhere = pl.BlockSpec(memory_space=pl.ANY)
    new_momentum, update = pl.pallas_call(
        kernel,
        out_shape=[jax.ShapeDtypeStruct((MINE, D), F32)] * 2,
        in_specs=[anywhere] * 4,
        out_specs=[anywhere] * 2,
        scratch_shapes=[
            pltpu.VMEM((GRAD + 2 * MINE, D), BF16),
            pltpu.VMEM((MINE, D), F32),
            pltpu.VMEM(wide.shape, BF16),
            pltpu.VMEM(back.shape, BF16),
            pltpu.VMEM((GROUPS, MATS, NZL, NX, OWN, HIGH), F32),
            pltpu.VMEM((MATS, NZL, NX, OWN, LOW), F32),
            *[pltpu.VMEM((GROUPS, MATS, NZL, OWN, HIGH), F32)] * 3,
            pltpu.VMEM((GROUPS, MATS, OWN, HIGH), F32),
            pltpu.VMEM((GROUPS, MATS, NX, OWN, HIGH), F32),
            *[pltpu.VMEM((GROUPS, MATS, OWN, HIGH), F32)] * 3,
            pltpu.VMEM((MATS, NX, OWN, LOW), F32),
            pltpu.VMEM((6, 2, OWN, LOW), F32),
            pltpu.VMEM((3, OWN, LOW), F32),
            pltpu.VMEM((7, OWN, LOW), F32),
            pltpu.VMEM((OWN, LOW), F32),
            pltpu.VMEM((MATS, OWN, LOW), F32),
            pltpu.VMEM((MINE, D), F32),
            pltpu.VMEM((MINE, D), F32),
            pltpu.SemaphoreType.DMA((2 * GROUPS + 3,)),
            pltpu.SemaphoreType.DMA((GROUPS + 1,)),
            pltpu.SemaphoreType.DMA((N_SEMS,)),
            pltpu.SemaphoreType.DMA((N_SEMS,)),
            pltpu.SemaphoreType.REGULAR,
            pltpu.SemaphoreType.REGULAR,
        ],
        compiler_params=pltpu.CompilerParams(
            collective_id=0, has_side_effects=True, vmem_limit_bytes=(52 * 1024 + 384) * 1024
        ),
        cost_estimate=pl.CostEstimate(flops=2_000_000_000, bytes_accessed=8_000_000, transcendentals=200_000),
    )(gradients.reshape(GRAD, D), momentum.reshape(MINE, D), wide, back)
    new_momentum, update = pl.pallas_call(
        write_out,
        out_shape=[jax.ShapeDtypeStruct((MINE, D), F32)] * 2,
        in_specs=[anywhere] * 2,
        out_specs=[anywhere] * 2,
        scratch_shapes=[pltpu.SemaphoreType.DMA((2, 4))],
        compiler_params=pltpu.CompilerParams(vmem_limit_bytes=4 * 1024 * 1024),
        cost_estimate=pl.CostEstimate(flops=0, bytes_accessed=2_600_000, transcendentals=0),
    )(new_momentum, update)
    return new_momentum.reshape(1, MATS, OWN, D), update.reshape(MATS, OWN, D)


def solution(mesh):
    return jax.shard_map(
        per_device,
        mesh=mesh,
        in_specs=(P("rep", "fsdp", None, None, None), P("rep", None, "fsdp", None)),
        out_specs=(P("rep", None, "fsdp", None), P(None, "fsdp", None)),
        check_vma=False,
    )
```

```python
import jax
import jax.numpy as jnp
import ml_dtypes
import numpy as np
from jax import lax
from jax.experimental import pallas as pl
from jax.experimental.pallas import tpu as pltpu
from jax.sharding import PartitionSpec as P

D, MATS, GROUP, KEEP, ROWS = 5120, 4, 64, 8, 64
BETA, EPS = 0.999, 1e-06
NX, NY, NZL, NZH, NC, N_REP = 4, 4, 2, 4, 2, 32
OWN = 8
LANES = 128
TILES = 8
SPAN = LANES * TILES
GROUPS = D // SPAN
HIGH = 7 * LANES
LOW = GROUPS * LANES
GRAD = MATS * ROWS
MINE = MATS * OWN
WIDE = 4 * LANES

F32, BF16 = jnp.float32, jnp.bfloat16
MESH = pl.DeviceIdType.MESH


def split(table):
    high = table.astype(ml_dtypes.bfloat16)
    low = (table - high.astype(np.float64)).astype(ml_dtypes.bfloat16)
    return high, low


def tables():
    n, k = np.arange(GROUP), np.arange(GROUP)[:, None]
    basis = np.sqrt(2.0 / GROUP) * np.cos(np.pi * (n + 0.5) * k / GROUP)
    basis[0] *= np.sqrt(0.5)
    rest = GROUP - KEEP
    high = np.zeros((LANES, 2 * rest))
    for b in range(2):
        high[b * GROUP : (b + 1) * GROUP, b * rest : (b + 1) * rest] = basis[KEEP:].T
    forward = np.zeros((7, 2 * LANES, LANES))
    for t in range(7):
        forward[t, :LANES, : 2 * rest] = high
        forward[t, LANES:, 2 * rest :] = high[:, 16 * t : 16 * t + 16]
    inverse = np.zeros((7, LANES, 2 * LANES))
    for t in range(7):
        inverse[t] = forward[t].T
    blocks = SPAN // GROUP
    keep = np.zeros((SPAN, LANES))
    mean = np.zeros((LANES, SPAN))
    for c in range(blocks):
        keep[c * GROUP : (c + 1) * GROUP, c * KEEP : (c + 1) * KEEP] = basis[:KEEP].T
        mean[c * KEEP : (c + 1) * KEEP, c * GROUP : (c + 1) * GROUP] = 1.0 / GROUP
    both = lambda table: np.concatenate(split(table), axis=-1)
    wide = np.concatenate([both(forward).reshape(-1, 2 * LANES), both(keep)], axis=0)
    back = np.concatenate([both(keep.T), mean.astype(ml_dtypes.bfloat16)], axis=-1)
    back = back.reshape(LANES, 6, WIDE).transpose(1, 0, 2).reshape(-1, WIDE)
    return wide, np.concatenate([both(inverse).reshape(-1, WIDE), back], axis=0)


def halves(value):
    top = value.astype(BF16)
    return top, (value - top.astype(F32)).astype(BF16)


def dot(a, b):
    return jnp.dot(a, b, preferred_element_type=F32)


X_UNITS = [(2, 0, 2), (2, 2, 2), (3, 0, 2), (3, 2, 2), (4, 0, 2), (4, 2, 2)]
Z_UNITS = [(0, 0, 2), (0, 2, 2), (1, 0, 2), (1, 2, 2)]
N_SEMS = 4 * len(X_UNITS) + 4 * len(Z_UNITS) + 1 + 6 + 3 + 7 + 7
PLAN = [
    ("F", 0), ("ZS", 1), ("F", 2), ("XS", 1), ("FL", 2), ("FL", 3),
    ("FL", 1), ("XS", 0), ("FL", 4), ("FL", 0), ("LA", 0), ("ZS", 0),
    ("F", 4), ("XS", 5), ("ZC", 1), ("LB1", 0), ("F", 1), ("ZS", 3),
    ("XS", 4), ("F", 3), ("LB2", 0), ("ZP", 1), ("XP", 1), ("ZS", 2),
    ("XS", 2), ("LC", 0), ("XP", 4), ("ZE", 1), ("XP", 0), ("ZC", 0),
    ("XP", 2), ("XS", 3), ("LD", 0), ("XC", 1), ("XP", 5), ("XC", 4),
    ("ZP", 0), ("XP", 3), ("ZC", 3), ("ZC", 2), ("XC", 0), ("ZE", 0),
    ("XC", 5), ("BK", 0), ("XE", 4), ("XC", 2), ("XE", 1), ("LF", 0),
    ("XE", 0), ("BK", 2), ("XC", 3), ("XE", 5), ("BK", 4), ("ZP", 3),
    ("ZP", 2), ("XE", 2), ("N", 3), ("N", 0), ("N", 1), ("N", 2),
    ("N", 4), ("XE", 3), ("BK", 3), ("ZE", 3), ("ZE", 2), ("BK", 1),
]


def kernel(
    grads, momentum, wide_hbm, back_hbm, new_out, upd_out,
    xin, mom, wide, back, s, lw,
    xr2, xra, xrb, xrz, zr4, zr2, zra, zrb,
    la, lb, lc, le, es, total, nm, up,
    load_sem, store_sem, send_sem, recv_sem, column_sem, stack_sem,
):
    rep, fsdp = lax.axis_index("rep"), lax.axis_index("fsdp")
    core, y, zh = lax.rem(rep, 2), lax.rem(lax.div(rep, 2), 4), lax.div(rep, 8)
    x, z = lax.rem(fsdp, 4), lax.div(fsdp, 4)

    def ring(v, d):
        return lax.rem(v + (d + 4), 4)

    def device(z_high=None, dy=0, dcore=0, dz=0, dx=0):
        c2 = 1 - core if dcore else core
        z2 = 1 - z if dz else z
        z3 = zh if z_high is None else z_high
        return ((z3 * 4 + ring(y, dy)) * 2 + c2, z2 * 4 + ring(x, dx))

    column = [(dy, dc) for dy in range(4) for dc in range(2) if dy or dc]
    barrier = pltpu.get_barrier_semaphore()

    def greet(sem, p):
        pl.semaphore_signal(sem, inc=1, device_id=p, device_id_type=MESH)

    def later_in_column(dy, dc):
        if dy:
            return ring(y, dy) > y
        return core == 1

    def later_in_stack(d):
        return ring(zh, d) > zh

    def greet_others(sem_of, later):
        def where(test, sem, places):
            @pl.when(test if later else jnp.logical_not(test))
            def _():
                for place in places:
                    greet(sem, place)

        for d in range(4):
            cores = range(2) if d else (1,)
            where(later_in_column(d, 1), sem_of[0], [device(dy=d, dcore=dc) for dc in cores])
        for d in (1, 2, 3):
            where(later_in_stack(d), sem_of[1], [device(z_high=ring(zh, d), dz=dz) for dz in range(2)])

    for d in (1, 2, 3):
        greet(barrier, device(dx=d))
    greet(barrier, device(dz=1))
    column_later = 2 * (3 - y) + core
    stack_later = 2 * (3 - zh)

    def enter():
        pl.semaphore_wait(barrier, 4 + (7 - column_later) + (6 - stack_later))
    used = [0]
    pending = []

    def remote(src, dst, to):
        i = used[0]
        used[0] += 1
        return pltpu.make_async_remote_copy(
            src_ref=src, dst_ref=dst, send_sem=send_sem.at[i], recv_sem=recv_sem.at[i],
            device_id=to, device_id_type=MESH,
        )

    def send(src, dst, to):
        copy = remote(src, dst, to)
        copy.start()
        pending.append(copy)
        return copy

    loads = []

    def load(src, dst):
        copy = pltpu.make_async_copy(src, dst, load_sem.at[len(loads)])
        copy.start()
        loads.append(copy)
        return copy

    waited = set()

    def arrived(copy):
        if id(copy) not in waited:
            waited.add(id(copy))
            copy.wait()

    def load_group(g):
        cols = pl.ds(g * SPAN, SPAN)
        return load(momentum.at[:, cols], mom.at[:, cols]), load(grads.at[:, cols], xin.at[pl.ds(0, GRAD), cols])

    order = [g for name, g in PLAN if name == "F"]
    front = pl.ds(0, 7 * 2 * LANES)
    rest = pl.ds(7 * 2 * LANES, SPAN)
    group_loads = {order[0]: load_group(order[0])}
    load_wide = load(wide_hbm.at[front], wide.at[front])
    load_rest = []
    greet_others((barrier, barrier), True)

    def load_others():
        for g in order[1:]:
            group_loads[g] = load_group(g)
        load_rest.append(load(wide_hbm.at[rest], wide.at[rest]))
        load_rest.append(load(back_hbm, back))

    ready = set()

    def prepare(g):
        if g not in ready:
            ready.add(g)
            for copy in group_loads[g]:
                copy.wait()
            cols = slice(g * SPAN, (g + 1) * SPAN)
            top, low_part = halves(BETA * mom[:, cols])
            xin[GRAD : GRAD + MINE, cols] = top
            xin[GRAD + MINE :, cols] = low_part

    def fold(v):
        v = v[:, :LANES] + v[:, LANES:]
        own = v[GRAD : GRAD + MINE] + v[GRAD + MINE :]
        return v[:GRAD].reshape(MATS, NZL, NX, OWN, LANES), own.reshape(MATS, OWN, LANES)

    def forward(g):
        prepare(g)
        arrived(load_wide)
        if not load_rest:
            load_others()
        base = g * SPAN
        last = xin[:, base + HIGH : base + SPAN]
        for t in range(7):
            both = jnp.concatenate([xin[:, base + t * LANES : base + (t + 1) * LANES], last], axis=1)
            value, own = fold(dot(both, wide[t * 2 * LANES : (t + 1) * 2 * LANES]))
            lanes = slice(t * LANES, (t + 1) * LANES)
            s[g, :, :, :, :, lanes] = value
            s[g, :, z, x, :, lanes] += own

    def forward_low(g):
        prepare(g)
        arrived(load_rest[0])
        value, own = fold(dot(xin[:, g * SPAN : (g + 1) * SPAN], wide[7 * 2 * LANES :]))
        lanes = slice(g * LANES, (g + 1) * LANES)
        lw[:, :, :, :, lanes] = value
        lw[:, z, x, :, lanes] += own

    xd, zd, low = {}, {}, {}
    way = lambda u: 1 if u % 2 == 0 else -1
    z_way = lambda u: -way(u)

    def x_start(u):
        g, m, n = X_UNITS[u]
        d, part, rows = way(u), s.at[g, pl.ds(m, n)], (g, pl.ds(m, n))
        two = send(part.at[:, :, ring(x, 2)], xr2.at[rows], device(dx=d))
        one = send(part.at[:, :, ring(x, -d)], xra.at[rows], device(dx=-d))
        xd[u] = [two, one]

    def x_pass(u):
        g, m, n = X_UNITS[u]
        d, rows = way(u), (g, pl.ds(m, n))
        xd[u][0].wait_recv()
        to = ring(x, d)
        s[g, m : m + n, :, to] += xr2[g, m : m + n]
        xd[u].append(send(s.at[g, pl.ds(m, n), :, to], xrb.at[rows], device(dx=d)))

    def x_cross(u):
        g, m, n = X_UNITS[u]
        xd[u][1].wait_recv()
        xd[u][2].wait_recv()
        s[g, m : m + n, :, x] += xra[g, m : m + n] + xrb[g, m : m + n]
        rows = (g, pl.ds(m, n))
        xd[u].append(send(s.at[g, pl.ds(m, n), 1 - z, x], xrz.at[rows], device(dz=1)))

    def z_start(u):
        g, m, n = Z_UNITS[u]
        zd[u] = [send(s.at[g, pl.ds(m, n), 1 - z], zr4.at[g, pl.ds(m, n)], device(dz=1))]

    def z_cross(u):
        g, m, n = Z_UNITS[u]
        d, part, rows = z_way(u), s.at[g, pl.ds(m, n), z], (g, pl.ds(m, n))
        zd[u][0].wait_recv()
        s[g, m : m + n, z] += zr4[g, m : m + n]
        zd[u].append(send(part.at[:, ring(x, 2)], zr2.at[rows], device(dx=d)))
        zd[u].append(send(part.at[:, ring(x, -d)], zra.at[rows], device(dx=-d)))

    def z_pass(u):
        g, m, n = Z_UNITS[u]
        d, rows = z_way(u), (g, pl.ds(m, n))
        zd[u][1].wait_recv()
        to = ring(x, d)
        s[g, m : m + n, z, to] += zr2[g, m : m + n]
        zd[u].append(send(s.at[g, pl.ds(m, n), z, to], zrb.at[rows], device(dx=d)))

    parts = {}

    def x_end(u):
        g, m, n = X_UNITS[u]
        xd[u][3].wait_recv()
        parts[g, m] = s[g, m : m + n, z, x] + xrz[g, m : m + n]

    def z_end(u):
        g, m, n = Z_UNITS[u]
        zd[u][2].wait_recv()
        zd[u][3].wait_recv()
        parts[g, m] = s[g, m : m + n, z, x] + (zra[g, m : m + n] + zrb[g, m : m + n])

    stores = []

    def store(src, dst):
        copy = pltpu.make_async_copy(src, dst, store_sem.at[len(stores)])
        copy.start()
        stores.append(copy)

    def backward(g):
        arrived(load_rest[1])
        field = jnp.concatenate([parts[k] for k in sorted(parts) if k[0] == g], axis=0).reshape(MINE, HIGH)
        last = jnp.zeros((MINE, LANES), F32)
        for t in range(7):
            top, rest = halves(field[:, t * LANES : (t + 1) * LANES])
            v = dot(jnp.concatenate([top, rest], axis=0), back[t * LANES : (t + 1) * LANES])
            v = v[:MINE, : 2 * LANES] + (v[MINE:, : 2 * LANES] + v[:MINE, 2 * LANES :])
            base = g * SPAN + t * LANES
            nm[:, base : base + LANES] = v[:, :LANES]
            last += v[:, LANES:]
        nm[:, g * SPAN + HIGH : (g + 1) * SPAN] = last
        cols = pl.ds(g * SPAN, SPAN)
        store(nm.at[:, cols], new_out.at[:, cols])

    def low_a(_):
        @pl.when(column_later > 0)
        def _():
            pl.semaphore_wait(column_sem, column_later)

        low["a"] = send(lw.at[:, 1 - core], la, device(dcore=1))

    def low_b(_):
        low["a"].wait_recv()
        lw[:, core] += la[...]
        half = lambda dy, k: lw.at[ring(y, dy), core, pl.ds(2 * k, 2)]
        low["b"] = [
            send(half(2, 0), lb.at[0], device(dy=1)),
            send(half(2, 1), lb.at[1], device(dy=-1)),
            send(half(1, 1), lb.at[2], device(dy=1)),
            send(half(-1, 0), lb.at[3], device(dy=-1)),
        ]

    def low_c(_):
        for k, d in ((0, 1), (1, -1)):
            low["b"][k].wait_recv()
            lw[ring(y, d), core, 2 * k : 2 * k + 2] += lb[k]
            half = lw.at[ring(y, d), core, pl.ds(2 * k, 2)]
            low["b"].append(send(half, lb.at[4 + k], device(dy=d)))

    def low_d(_):
        for copy in low["b"][2:]:
            copy.wait_recv()
        lw[y, core, 0:2] += lb[4] + lb[3]
        lw[y, core, 2:4] += lb[2] + lb[5]
        low["d"] = [send(lw.at[y, core, ring(x, d)], lc.at[d - 1], device(dx=d)) for d in (1, 2, 3)]

    def low_e(_):
        for copy in low["d"]:
            copy.wait_recv()
        es[...] = lw[y, core, x] + (lc[0] + lc[1] + lc[2])
        low["in"] = [remote(es, le.at[d - 1], device(z_high=ring(zh, d))) for d in (1, 2, 3)]
        @pl.when(stack_later > 0)
        def _():
            pl.semaphore_wait(stack_sem, stack_later)

        low["out"] = [remote(es, le.at[3 + d], device(z_high=ring(zh, d), dz=1)) for d in range(4)]

        @pl.when(core == z)
        def _():
            for copy in low["in"]:
                copy.start()

        @pl.when(core != z)
        def _():
            for copy in low["out"]:
                copy.start()

    def low_i(_):
        low["i"] = [remote(total.at[y], total.at[y], device(dy=dy, dcore=dc)) for dy, dc in column]

        @pl.when(core == z)
        def _():
            for copy in low["in"] + low["out"]:
                copy.wait_recv()
            total[y] = es[...] + ((le[0] + le[1] + le[2]) + (le[3] + le[4] + le[5] + le[6]))
            for copy in low["i"]:
                copy.start()

    def low_end():
        arrived(load_rest[1])

        @pl.when(core == z)
        def _():
            for copy, (dy, dc) in zip(low["i"], column):
                if dc == 0:
                    copy.wait_recv()

        @pl.when(core != z)
        def _():
            for copy, (dy, dc) in zip(low["i"], column):
                if dc == 1:
                    copy.wait_recv()

    normalised = set()

    def normalise(g):
        if not normalised:
            low_end()
        normalised.add(g)
        table = lambda i: back[(7 + i) * LANES : (8 + i) * LANES]
        lanes = slice(g * LANES, (g + 1) * LANES)
        mean = total[:, :, lanes].reshape(MINE, LANES) * (1.0 / N_REP)
        top, rest = halves(mean)
        pair = jnp.concatenate([top, rest], axis=0)
        squares = jnp.concatenate(halves(mean * mean), axis=0)
        for h in range(2):
            v, w = dot(pair, table(h)), dot(squares, table(4 + h))
            field = v[:MINE] + (v[MINE:] + dot(top, table(2 + h)))
            square = w[:MINE] + w[MINE:]
            base = g * SPAN + h * WIDE
            up[:, base : base + WIDE] = field * lax.rsqrt(field * field + square + EPS)
        cols = pl.ds(g * SPAN, SPAN)
        store(up.at[:, cols], upd_out.at[:, cols])

    steps = {
        "F": forward, "FL": forward_low,
        "XS": x_start, "XP": x_pass, "XC": x_cross, "XE": x_end,
        "ZS": z_start, "ZC": z_cross, "ZP": z_pass, "ZE": z_end,
        "LA": low_a, "LB1": low_b, "LB2": low_c, "LC": low_d, "LD": low_e, "LF": low_i,
        "N": normalise, "BK": backward,
    }
    entered = answered = False
    for name, u in PLAN:
        if not entered and name not in ("F", "FL"):
            enter()
            entered = True
        if entered and not answered and name not in ("XS", "ZS"):
            greet_others((column_sem, stack_sem), False)
            answered = True
        steps[name](u)

    for copy in pending:
        copy.wait_send()

    @pl.when(core != z)
    def _():
        for copy in low["out"]:
            copy.wait_send()

    @pl.when(core == z)
    def _():
        for copy in low["in"] + low["i"]:
            copy.wait_send()

    for copy in stores:
        copy.wait()


def write_out(new_in, upd_in, new_out, upd_out, sems):
    copies = []
    for k, (src, dst) in enumerate([(new_in, new_out), (upd_in, upd_out)]):
        for m in range(MATS):
            rows = pl.ds(m * OWN, OWN)
            copies.append(pltpu.make_async_copy(src.at[rows], dst.at[rows], sems.at[k, m]))
    for copy in copies:
        copy.start()
    for copy in copies:
        copy.wait()


def per_device(gradients, momentum):
    wide, back = tables()
    anywhere = pl.BlockSpec(memory_space=pl.ANY)
    new_momentum, update = pl.pallas_call(
        kernel,
        out_shape=[jax.ShapeDtypeStruct((MINE, D), F32)] * 2,
        in_specs=[anywhere] * 4,
        out_specs=[anywhere] * 2,
        scratch_shapes=[
            pltpu.VMEM((GRAD + 2 * MINE, D), BF16),
            pltpu.VMEM((MINE, D), F32),
            pltpu.VMEM(wide.shape, BF16),
            pltpu.VMEM(back.shape, BF16),
            pltpu.VMEM((GROUPS, MATS, NZL, NX, OWN, HIGH), F32),
            pltpu.VMEM((MATS, NZL, NX, OWN, LOW), F32),
            *[pltpu.VMEM((GROUPS, MATS, NZL, OWN, HIGH), F32)] * 3,
            pltpu.VMEM((GROUPS, MATS, OWN, HIGH), F32),
            pltpu.VMEM((GROUPS, MATS, NX, OWN, HIGH), F32),
            *[pltpu.VMEM((GROUPS, MATS, OWN, HIGH), F32)] * 3,
            pltpu.VMEM((MATS, NX, OWN, LOW), F32),
            pltpu.VMEM((6, 2, OWN, LOW), F32),
            pltpu.VMEM((3, OWN, LOW), F32),
            pltpu.VMEM((7, OWN, LOW), F32),
            pltpu.VMEM((OWN, LOW), F32),
            pltpu.VMEM((MATS, OWN, LOW), F32),
            pltpu.VMEM((MINE, D), F32),
            pltpu.VMEM((MINE, D), F32),
            pltpu.SemaphoreType.DMA((2 * GROUPS + 3,)),
            pltpu.SemaphoreType.DMA((2 * GROUPS,)),
            pltpu.SemaphoreType.DMA((N_SEMS,)),
            pltpu.SemaphoreType.DMA((N_SEMS,)),
            pltpu.SemaphoreType.REGULAR,
            pltpu.SemaphoreType.REGULAR,
        ],
        compiler_params=pltpu.CompilerParams(
            collective_id=0, has_side_effects=True, vmem_limit_bytes=(52 * 1024 + 384) * 1024
        ),
        cost_estimate=pl.CostEstimate(flops=2_000_000_000, bytes_accessed=8_000_000, transcendentals=200_000),
    )(gradients.reshape(GRAD, D), momentum.reshape(MINE, D), wide, back)
    new_momentum, update = pl.pallas_call(
        write_out,
        out_shape=[jax.ShapeDtypeStruct((MINE, D), F32)] * 2,
        in_specs=[anywhere] * 2,
        out_specs=[anywhere] * 2,
        scratch_shapes=[pltpu.SemaphoreType.DMA((2, 4))],
        compiler_params=pltpu.CompilerParams(vmem_limit_bytes=4 * 1024 * 1024),
        cost_estimate=pl.CostEstimate(flops=0, bytes_accessed=2_600_000, transcendentals=0),
    )(new_momentum, update)
    return new_momentum.reshape(1, MATS, OWN, D), update.reshape(MATS, OWN, D)


def solution(mesh):
    return jax.shard_map(
        per_device,
        mesh=mesh,
        in_specs=(P("rep", "fsdp", None, None, None), P("rep", None, "fsdp", None)),
        out_specs=(P("rep", None, "fsdp", None), P(None, "fsdp", None)),
        check_vma=False,
    )
```

```python
import jax
import jax.numpy as jnp
import ml_dtypes
import numpy as np
from jax import lax
from jax.experimental import pallas as pl
from jax.experimental.pallas import tpu as pltpu
from jax.sharding import PartitionSpec as P

D, MATS, GROUP, KEEP, ROWS = 5120, 4, 64, 8, 64
BETA, EPS = 0.999, 1e-06
NX, NY, NZL, NZH, NC, N_REP = 4, 4, 2, 4, 2, 32
OWN = 8
LANES = 128
TILES = 8
SPAN = LANES * TILES
GROUPS = D // SPAN
HIGH = 7 * LANES
LOW = GROUPS * LANES
GRAD = MATS * ROWS
MINE = MATS * OWN
WIDE = 4 * LANES

F32, BF16 = jnp.float32, jnp.bfloat16
MESH = pl.DeviceIdType.MESH


def split(table):
    high = table.astype(ml_dtypes.bfloat16)
    low = (table - high.astype(np.float64)).astype(ml_dtypes.bfloat16)
    return high, low


def tables():
    n, k = np.arange(GROUP), np.arange(GROUP)[:, None]
    basis = np.sqrt(2.0 / GROUP) * np.cos(np.pi * (n + 0.5) * k / GROUP)
    basis[0] *= np.sqrt(0.5)
    rest = GROUP - KEEP
    high = np.zeros((LANES, 2 * rest))
    for b in range(2):
        high[b * GROUP : (b + 1) * GROUP, b * rest : (b + 1) * rest] = basis[KEEP:].T
    forward = np.zeros((7, 2 * LANES, LANES))
    for t in range(7):
        forward[t, :LANES, : 2 * rest] = high
        forward[t, LANES:, 2 * rest :] = high[:, 16 * t : 16 * t + 16]
    inverse = np.zeros((7, LANES, 2 * LANES))
    for t in range(7):
        inverse[t] = forward[t].T
    blocks = SPAN // GROUP
    keep = np.zeros((SPAN, LANES))
    mean = np.zeros((LANES, SPAN))
    for c in range(blocks):
        keep[c * GROUP : (c + 1) * GROUP, c * KEEP : (c + 1) * KEEP] = basis[:KEEP].T
        mean[c * KEEP : (c + 1) * KEEP, c * GROUP : (c + 1) * GROUP] = 1.0 / GROUP
    both = lambda table: np.concatenate(split(table), axis=-1)
    wide = np.concatenate([both(forward).reshape(-1, 2 * LANES), both(keep)], axis=0)
    back = np.concatenate([both(keep.T), mean.astype(ml_dtypes.bfloat16)], axis=-1)
    back = back.reshape(LANES, 6, WIDE).transpose(1, 0, 2).reshape(-1, WIDE)
    return wide, np.concatenate([both(inverse).reshape(-1, WIDE), back], axis=0)


def halves(value):
    top = value.astype(BF16)
    return top, (value - top.astype(F32)).astype(BF16)


def dot(a, b):
    return jnp.dot(a, b, preferred_element_type=F32)


X_UNITS = [(2, 0), (2, 2), (3, 0), (3, 2), (4, 0), (4, 2)]
Z_UNITS = [(0, 0), (0, 2), (1, 0), (1, 2)]
N_SEMS = 4 * len(X_UNITS) + 4 * len(Z_UNITS) + 1 + 6 + 3 + 7 + 7
PLAN = [
    ("F", 4), ("XS", 4), ("F", 0), ("ZS", 0), ("FL", 2), ("XS", 5),
    ("FL", 0), ("FL", 1), ("FL", 3), ("FL", 4), ("LA", 0), ("F", 2),
    ("XS", 0), ("ZS", 1), ("F", 3), ("XS", 2), ("XS", 1), ("LB1", 0),
    ("F", 1), ("ZS", 3), ("XP", 0), ("LB2", 0), ("XP", 5), ("ZS", 2),
    ("ZC", 1), ("LC", 0), ("XP", 4), ("XS", 3), ("XP", 1), ("XP", 2),
    ("ZP", 1), ("ZC", 3), ("LD", 0), ("ZC", 0), ("XC", 4), ("XC", 5),
    ("XC", 0), ("XP", 3), ("XC", 1), ("ZC", 2), ("XE", 4), ("ZP", 0),
    ("XC", 2), ("XE", 5), ("BK", 4), ("XE", 0), ("ZE", 1), ("XC", 3),
    ("ZP", 3), ("XE", 1), ("ZP", 2), ("LF", 0), ("BK", 2), ("XE", 2),
    ("ZE", 0), ("BK", 0), ("XE", 3), ("BK", 3), ("ZE", 3), ("ZE", 2),
    ("BK", 1), ("N", 1), ("N", 0), ("N", 3), ("N", 2), ("N", 4),
]


def kernel(
    grads, momentum, wide_hbm, back_hbm, new_out, upd_out,
    xin, mom, wide, back, sx, sz, lw,
    xr2, xra, xrb, xrz, zr4, zr2, zra, zrb,
    la, lb, lc, le, es, total, nm, up,
    load_sem, store_sem, send_sem, recv_sem, column_sem, stack_sem,
):
    rep, fsdp = lax.axis_index("rep"), lax.axis_index("fsdp")
    core, y, zh = lax.rem(rep, 2), lax.rem(lax.div(rep, 2), 4), lax.div(rep, 8)
    x, z = lax.rem(fsdp, 4), lax.div(fsdp, 4)

    def ring(v, d):
        return lax.rem(v + (d + 4), 4)

    def device(z_high=None, dy=0, dcore=0, dz=0, dx=0):
        c2 = 1 - core if dcore else core
        z2 = 1 - z if dz else z
        z3 = zh if z_high is None else z_high
        return ((z3 * 4 + ring(y, dy)) * 2 + c2, z2 * 4 + ring(x, dx))

    column = [(dy, dc) for dy in range(4) for dc in range(2) if dy or dc]
    barrier = pltpu.get_barrier_semaphore()

    def greet(sem, p):
        pl.semaphore_signal(sem, inc=1, device_id=p, device_id_type=MESH)

    def later_in_column(dy, dc):
        if dy:
            return ring(y, dy) > y
        return core == 1

    def later_in_stack(d):
        return ring(zh, d) > zh

    def greet_others(sem_of, later):
        def where(test, sem, places):
            @pl.when(test if later else jnp.logical_not(test))
            def _():
                for place in places:
                    greet(sem, place)

        for d in range(4):
            cores = range(2) if d else (1,)
            where(later_in_column(d, 1), sem_of[0], [device(dy=d, dcore=dc) for dc in cores])
        for d in (1, 2, 3):
            where(later_in_stack(d), sem_of[1], [device(z_high=ring(zh, d), dz=dz) for dz in range(2)])

    for d in (1, 2, 3):
        greet(barrier, device(dx=d))
    greet(barrier, device(dz=1))
    column_later = 2 * (3 - y) + core
    stack_later = 2 * (3 - zh)

    def enter():
        pl.semaphore_wait(barrier, 4 + (7 - column_later) + (6 - stack_later))
    used = [0]
    pending = []

    def remote(src, dst, to):
        i = used[0]
        used[0] += 1
        return pltpu.make_async_remote_copy(
            src_ref=src, dst_ref=dst, send_sem=send_sem.at[i], recv_sem=recv_sem.at[i],
            device_id=to, device_id_type=MESH,
        )

    def send(src, dst, to):
        copy = remote(src, dst, to)
        copy.start()
        pending.append(copy)
        return copy

    loads = []

    def load(src, dst):
        copy = pltpu.make_async_copy(src, dst, load_sem.at[len(loads)])
        copy.start()
        loads.append(copy)
        return copy

    waited = set()

    def arrived(copy):
        if id(copy) not in waited:
            waited.add(id(copy))
            copy.wait()

    def load_group(g):
        cols = pl.ds(g * SPAN, SPAN)
        return load(momentum.at[:, cols], mom.at[:, cols]), load(grads.at[:, cols], xin.at[pl.ds(0, GRAD), cols])

    order = [g for name, g in PLAN if name == "F"]
    front = pl.ds(0, 7 * 2 * LANES)
    rest = pl.ds(7 * 2 * LANES, SPAN)
    group_loads = {order[0]: load_group(order[0])}
    load_wide = load(wide_hbm.at[front], wide.at[front])
    load_rest = []
    greet_others((barrier, barrier), True)

    def load_others():
        for g in order[1:]:
            group_loads[g] = load_group(g)
        load_rest.append(load(wide_hbm.at[rest], wide.at[rest]))
        load_rest.append(load(back_hbm, back))

    ready = set()

    def prepare(g):
        if g not in ready:
            ready.add(g)
            for copy in group_loads[g]:
                copy.wait()
            cols = slice(g * SPAN, (g + 1) * SPAN)
            top, low_part = halves(BETA * mom[:, cols])
            xin[GRAD : GRAD + MINE, cols] = top
            xin[GRAD + MINE :, cols] = low_part

    def fold(v):
        v = v[:, :LANES] + v[:, LANES:]
        own = v[GRAD : GRAD + MINE] + v[GRAD + MINE :]
        return v[:GRAD].reshape(MATS, NZL, NX, OWN, LANES), own.reshape(MATS, OWN, LANES)

    def forward(g):
        prepare(g)
        arrived(load_wide)
        if not load_rest:
            load_others()
        base = g * SPAN
        last = xin[:, base + HIGH : base + SPAN]
        for t in range(7):
            both = jnp.concatenate([xin[:, base + t * LANES : base + (t + 1) * LANES], last], axis=1)
            value, own = fold(dot(both, wide[t * 2 * LANES : (t + 1) * 2 * LANES]))
            lanes = slice(t * LANES, (t + 1) * LANES)
            for h in range(2):
                mats = slice(2 * h, 2 * h + 2)
                if (g, 2 * h) in X_UNITS:
                    u = X_UNITS.index((g, 2 * h))
                    for m in range(2):
                        for k in range(NZL):
                            sx[u, :, k, m, :, lanes] = value[2 * h + m, k]
                    sx[u, x, z, :, :, lanes] += own[mats]
                else:
                    u = Z_UNITS.index((g, 2 * h))
                    for m in range(2):
                        for k in range(NZL):
                            sz[u, k, :, m, :, lanes] = value[2 * h + m, k]
                    sz[u, z, x, :, :, lanes] += own[mats]

    def forward_low(g):
        prepare(g)
        arrived(load_rest[0])
        value, own = fold(dot(xin[:, g * SPAN : (g + 1) * SPAN], wide[7 * 2 * LANES :]))
        lanes = slice(g * LANES, (g + 1) * LANES)
        lw[:, :, :, :, lanes] = value
        lw[:, z, x, :, lanes] += own

    xd, zd, low = {}, {}, {}
    way = lambda u: 1 if u % 2 == 0 else -1
    z_way = lambda u: -way(u)

    def x_start(u):
        d = way(u)
        two = send(sx.at[u, ring(x, 2)], xr2.at[u], device(dx=d))
        one = send(sx.at[u, ring(x, -d)], xra.at[u], device(dx=-d))
        xd[u] = [two, one]

    def x_pass(u):
        d = way(u)
        to = ring(x, d)
        xd[u][0].wait_recv()
        sx[u, to] += xr2[u]
        xd[u].append(send(sx.at[u, to], xrb.at[u], device(dx=d)))

    def x_cross(u):
        xd[u][1].wait_recv()
        xd[u][2].wait_recv()
        sx[u, x] += xra[u] + xrb[u]
        xd[u].append(send(sx.at[u, x, 1 - z], xrz.at[u], device(dz=1)))

    def z_start(u):
        zd[u] = [send(sz.at[u, 1 - z], zr4.at[u], device(dz=1))]

    def z_cross(u):
        d = z_way(u)
        zd[u][0].wait_recv()
        sz[u, z] += zr4[u]
        zd[u].append(send(sz.at[u, z, ring(x, 2)], zr2.at[u], device(dx=d)))
        zd[u].append(send(sz.at[u, z, ring(x, -d)], zra.at[u], device(dx=-d)))

    def z_pass(u):
        d = z_way(u)
        to = ring(x, d)
        zd[u][1].wait_recv()
        sz[u, z, to] += zr2[u]
        zd[u].append(send(sz.at[u, z, to], zrb.at[u], device(dx=d)))

    parts = {}

    def x_end(u):
        xd[u][3].wait_recv()
        parts[X_UNITS[u]] = sx[u, x, z] + xrz[u]

    def z_end(u):
        zd[u][2].wait_recv()
        zd[u][3].wait_recv()
        parts[Z_UNITS[u]] = sz[u, z, x] + (zra[u] + zrb[u])

    stores = []

    def store(src, dst):
        copy = pltpu.make_async_copy(src, dst, store_sem.at[len(stores)])
        copy.start()
        stores.append(copy)

    def backward(g):
        arrived(load_rest[1])
        field = jnp.concatenate([parts[k] for k in sorted(parts) if k[0] == g], axis=0).reshape(MINE, HIGH)
        last = jnp.zeros((MINE, LANES), F32)
        for t in range(7):
            top, rest = halves(field[:, t * LANES : (t + 1) * LANES])
            v = dot(jnp.concatenate([top, rest], axis=0), back[t * LANES : (t + 1) * LANES])
            v = v[:MINE, : 2 * LANES] + (v[MINE:, : 2 * LANES] + v[:MINE, 2 * LANES :])
            base = g * SPAN + t * LANES
            nm[:, base : base + LANES] = v[:, :LANES]
            last += v[:, LANES:]
        nm[:, g * SPAN + HIGH : (g + 1) * SPAN] = last
        cols = pl.ds(g * SPAN, SPAN)
        store(nm.at[:, cols], new_out.at[:, cols])

    def low_a(_):
        @pl.when(column_later > 0)
        def _():
            pl.semaphore_wait(column_sem, column_later)

        low["a"] = send(lw.at[:, 1 - core], la, device(dcore=1))

    def low_b(_):
        low["a"].wait_recv()
        lw[:, core] += la[...]
        half = lambda dy, k: lw.at[ring(y, dy), core, pl.ds(2 * k, 2)]
        low["b"] = [
            send(half(2, 0), lb.at[0], device(dy=1)),
            send(half(2, 1), lb.at[1], device(dy=-1)),
            send(half(1, 1), lb.at[2], device(dy=1)),
            send(half(-1, 0), lb.at[3], device(dy=-1)),
        ]

    def low_c(_):
        for k, d in ((0, 1), (1, -1)):
            low["b"][k].wait_recv()
            lw[ring(y, d), core, 2 * k : 2 * k + 2] += lb[k]
            half = lw.at[ring(y, d), core, pl.ds(2 * k, 2)]
            low["b"].append(send(half, lb.at[4 + k], device(dy=d)))

    def low_d(_):
        for copy in low["b"][2:]:
            copy.wait_recv()
        lw[y, core, 0:2] += lb[4] + lb[3]
        lw[y, core, 2:4] += lb[2] + lb[5]
        low["d"] = [send(lw.at[y, core, ring(x, d)], lc.at[d - 1], device(dx=d)) for d in (1, 2, 3)]

    def low_e(_):
        for copy in low["d"]:
            copy.wait_recv()
        es[...] = lw[y, core, x] + (lc[0] + lc[1] + lc[2])
        low["in"] = [remote(es, le.at[d - 1], device(z_high=ring(zh, d))) for d in (1, 2, 3)]
        @pl.when(stack_later > 0)
        def _():
            pl.semaphore_wait(stack_sem, stack_later)

        low["out"] = [remote(es, le.at[3 + d], device(z_high=ring(zh, d), dz=1)) for d in range(4)]

        @pl.when(core == z)
        def _():
            for copy in low["in"]:
                copy.start()

        @pl.when(core != z)
        def _():
            for copy in low["out"]:
                copy.start()

    def low_i(_):
        low["i"] = [remote(total.at[y], total.at[y], device(dy=dy, dcore=dc)) for dy, dc in column]

        @pl.when(core == z)
        def _():
            for copy in low["in"] + low["out"]:
                copy.wait_recv()
            total[y] = es[...] + ((le[0] + le[1] + le[2]) + (le[3] + le[4] + le[5] + le[6]))
            for copy in low["i"]:
                copy.start()

    def low_end():
        arrived(load_rest[1])

        @pl.when(core == z)
        def _():
            for copy, (dy, dc) in zip(low["i"], column):
                if dc == 0:
                    copy.wait_recv()

        @pl.when(core != z)
        def _():
            for copy, (dy, dc) in zip(low["i"], column):
                if dc == 1:
                    copy.wait_recv()

    normalised = set()

    def normalise(g):
        if not normalised:
            low_end()
        normalised.add(g)
        table = lambda i: back[(7 + i) * LANES : (8 + i) * LANES]
        lanes = slice(g * LANES, (g + 1) * LANES)
        mean = total[:, :, lanes].reshape(MINE, LANES) * (1.0 / N_REP)
        top, rest = halves(mean)
        pair = jnp.concatenate([top, rest], axis=0)
        squares = jnp.concatenate(halves(mean * mean), axis=0)
        for h in range(2):
            v, w = dot(pair, table(h)), dot(squares, table(4 + h))
            field = v[:MINE] + (v[MINE:] + dot(top, table(2 + h)))
            square = w[:MINE] + w[MINE:]
            base = g * SPAN + h * WIDE
            up[:, base : base + WIDE] = field * lax.rsqrt(field * field + square + EPS)
        cols = pl.ds(g * SPAN, SPAN)
        store(up.at[:, cols], upd_out.at[:, cols])

    steps = {
        "F": forward, "FL": forward_low,
        "XS": x_start, "XP": x_pass, "XC": x_cross, "XE": x_end,
        "ZS": z_start, "ZC": z_cross, "ZP": z_pass, "ZE": z_end,
        "LA": low_a, "LB1": low_b, "LB2": low_c, "LC": low_d, "LD": low_e, "LF": low_i,
        "N": normalise, "BK": backward,
    }
    entered = answered = False
    for name, u in PLAN:
        if not entered and name not in ("F", "FL"):
            enter()
            entered = True
        if entered and not answered and name not in ("XS", "ZS"):
            greet_others((column_sem, stack_sem), False)
            answered = True
        steps[name](u)

    for copy in pending:
        copy.wait_send()

    @pl.when(core != z)
    def _():
        for copy in low["out"]:
            copy.wait_send()

    @pl.when(core == z)
    def _():
        for copy in low["in"] + low["i"]:
            copy.wait_send()

    for copy in stores:
        copy.wait()


def write_out(new_in, upd_in, new_out, upd_out, sems):
    copies = []
    for k, (src, dst) in enumerate([(new_in, new_out), (upd_in, upd_out)]):
        for m in range(MATS):
            rows = pl.ds(m * OWN, OWN)
            copies.append(pltpu.make_async_copy(src.at[rows], dst.at[rows], sems.at[k, m]))
    for copy in copies:
        copy.start()
    for copy in copies:
        copy.wait()


def per_device(gradients, momentum):
    wide, back = tables()
    anywhere = pl.BlockSpec(memory_space=pl.ANY)
    new_momentum, update = pl.pallas_call(
        kernel,
        out_shape=[jax.ShapeDtypeStruct((MINE, D), F32)] * 2,
        in_specs=[anywhere] * 4,
        out_specs=[anywhere] * 2,
        scratch_shapes=[
            pltpu.VMEM((GRAD + 2 * MINE, D), BF16),
            pltpu.VMEM((MINE, D), F32),
            pltpu.VMEM(wide.shape, BF16),
            pltpu.VMEM(back.shape, BF16),
            pltpu.VMEM((len(X_UNITS), NX, NZL, 2, OWN, HIGH), F32),
            pltpu.VMEM((len(Z_UNITS), NZL, NX, 2, OWN, HIGH), F32),
            pltpu.VMEM((MATS, NZL, NX, OWN, LOW), F32),
            *[pltpu.VMEM((len(X_UNITS), NZL, 2, OWN, HIGH), F32)] * 3,
            pltpu.VMEM((len(X_UNITS), 2, OWN, HIGH), F32),
            pltpu.VMEM((len(Z_UNITS), NX, 2, OWN, HIGH), F32),
            *[pltpu.VMEM((len(Z_UNITS), 2, OWN, HIGH), F32)] * 3,
            pltpu.VMEM((MATS, NX, OWN, LOW), F32),
            pltpu.VMEM((6, 2, OWN, LOW), F32),
            pltpu.VMEM((3, OWN, LOW), F32),
            pltpu.VMEM((7, OWN, LOW), F32),
            pltpu.VMEM((OWN, LOW), F32),
            pltpu.VMEM((MATS, OWN, LOW), F32),
            pltpu.VMEM((MINE, D), F32),
            pltpu.VMEM((MINE, D), F32),
            pltpu.SemaphoreType.DMA((2 * GROUPS + 3,)),
            pltpu.SemaphoreType.DMA((2 * GROUPS,)),
            pltpu.SemaphoreType.DMA((N_SEMS,)),
            pltpu.SemaphoreType.DMA((N_SEMS,)),
            pltpu.SemaphoreType.REGULAR,
            pltpu.SemaphoreType.REGULAR,
        ],
        compiler_params=pltpu.CompilerParams(
            collective_id=0, has_side_effects=True, vmem_limit_bytes=(52 * 1024 + 384) * 1024
        ),
        cost_estimate=pl.CostEstimate(flops=2_000_000_000, bytes_accessed=8_000_000, transcendentals=200_000),
    )(gradients.reshape(GRAD, D), momentum.reshape(MINE, D), wide, back)
    new_momentum, update = pl.pallas_call(
        write_out,
        out_shape=[jax.ShapeDtypeStruct((MINE, D), F32)] * 2,
        in_specs=[anywhere] * 2,
        out_specs=[anywhere] * 2,
        scratch_shapes=[pltpu.SemaphoreType.DMA((2, 4))],
        compiler_params=pltpu.CompilerParams(vmem_limit_bytes=4 * 1024 * 1024),
        cost_estimate=pl.CostEstimate(flops=0, bytes_accessed=2_600_000, transcendentals=0),
    )(new_momentum, update)
    return new_momentum.reshape(1, MATS, OWN, D), update.reshape(MATS, OWN, D)


def solution(mesh):
    return jax.shard_map(
        per_device,
        mesh=mesh,
        in_specs=(P("rep", "fsdp", None, None, None), P("rep", None, "fsdp", None)),
        out_specs=(P("rep", None, "fsdp", None), P(None, "fsdp", None)),
        check_vma=False,
    )
```

```python
import jax
import jax.numpy as jnp
import ml_dtypes
import numpy as np
from jax import lax
from jax.experimental import pallas as pl
from jax.experimental.pallas import tpu as pltpu
from jax.sharding import PartitionSpec as P

D, MATS, GROUP, KEEP, ROWS = 5120, 4, 64, 8, 64
BETA, EPS = 0.999, 1e-06
NX, NY, NZL, NZH, NC, N_REP = 4, 4, 2, 4, 2, 32
OWN = 8
LANES = 128
TILES = 8
SPAN = LANES * TILES
GROUPS = D // SPAN
HIGH = 7 * LANES
LOW = GROUPS * LANES
GRAD = MATS * ROWS
MINE = MATS * OWN
WIDE = 4 * LANES

F32, BF16 = jnp.float32, jnp.bfloat16
MESH = pl.DeviceIdType.MESH


def split(table):
    high = table.astype(ml_dtypes.bfloat16)
    low = (table - high.astype(np.float64)).astype(ml_dtypes.bfloat16)
    return high, low


def tables():
    n, k = np.arange(GROUP), np.arange(GROUP)[:, None]
    basis = np.sqrt(2.0 / GROUP) * np.cos(np.pi * (n + 0.5) * k / GROUP)
    basis[0] *= np.sqrt(0.5)
    rest = GROUP - KEEP
    high = np.zeros((LANES, 2 * rest))
    for b in range(2):
        high[b * GROUP : (b + 1) * GROUP, b * rest : (b + 1) * rest] = basis[KEEP:].T
    forward = np.zeros((7, 2 * LANES, LANES))
    for t in range(7):
        forward[t, :LANES, : 2 * rest] = high
        forward[t, LANES:, 2 * rest :] = high[:, 16 * t : 16 * t + 16]
    inverse = np.zeros((7, LANES, 2 * LANES))
    for t in range(7):
        inverse[t] = forward[t].T
    blocks = SPAN // GROUP
    keep = np.zeros((SPAN, LANES))
    mean = np.zeros((LANES, SPAN))
    for c in range(blocks):
        keep[c * GROUP : (c + 1) * GROUP, c * KEEP : (c + 1) * KEEP] = basis[:KEEP].T
        mean[c * KEEP : (c + 1) * KEEP, c * GROUP : (c + 1) * GROUP] = 1.0 / GROUP
    both = lambda table: np.concatenate(split(table), axis=-1)
    wide = np.concatenate([both(forward).reshape(-1, 2 * LANES), both(keep)], axis=0)
    back = np.concatenate([both(keep.T), mean.astype(ml_dtypes.bfloat16)], axis=-1)
    back = back.reshape(LANES, 6, WIDE).transpose(1, 0, 2).reshape(-1, WIDE)
    return wide, np.concatenate([both(inverse).reshape(-1, WIDE), back], axis=0)


def halves(value):
    top = value.astype(BF16)
    return top, (value - top.astype(F32)).astype(BF16)


def dot(a, b):
    return jnp.dot(a, b, preferred_element_type=F32)


X_UNITS = [(2, 0), (2, 2), (3, 0), (3, 2), (4, 0), (4, 2)]
Z_UNITS = [(0, 0), (0, 2), (1, 0), (1, 2)]
N_SEMS = 4 * len(X_UNITS) + 4 * len(Z_UNITS) + 7 + 3 + 7 + 7
PLAN = [
    ("F", 4), ("XS", 4), ("F", 1), ("ZS", 3), ("FL", 4), ("FL", 3),
    ("XS", 5), ("FL", 2), ("FL", 1), ("FL", 0), ("LA", 0), ("F", 3),
    ("XS", 2), ("ZS", 2), ("F", 2), ("XS", 0), ("F", 0), ("XS", 3),
    ("XP", 5), ("ZS", 1), ("ZS", 0), ("XP", 2), ("LC", 0), ("XS", 1),
    ("XP", 3), ("XP", 4), ("ZC", 3), ("XP", 0), ("ZC", 1), ("LD", 0),
    ("ZC", 2), ("XP", 1), ("XC", 2), ("XC", 3), ("XC", 5), ("XC", 4),
    ("ZP", 3), ("ZC", 0), ("XE", 2), ("ZP", 2), ("XE", 3), ("BK", 3),
    ("XC", 0), ("XE", 5), ("ZP", 1), ("XC", 1), ("XE", 4), ("BK", 4),
    ("ZP", 0), ("LF", 0), ("ZE", 3), ("ZE", 2), ("BK", 1), ("XE", 1),
    ("XE", 0), ("BK", 2), ("ZE", 1), ("ZE", 0), ("BK", 0), ("N", 3),
    ("N", 1), ("N", 2), ("N", 0), ("N", 4),
]


def kernel(
    grads, momentum, wide_hbm, back_hbm, new_out, upd_out,
    xin, mom, wide, back, sx, sz, lw,
    xr2, xra, xrb, xrz, zr4, zr2, zra, zrb,
    la, lc, le, es, total, nm, up,
    load_sem, store_sem, send_sem, recv_sem, column_sem, stack_sem,
):
    rep, fsdp = lax.axis_index("rep"), lax.axis_index("fsdp")
    core, y, zh = lax.rem(rep, 2), lax.rem(lax.div(rep, 2), 4), lax.div(rep, 8)
    x, z = lax.rem(fsdp, 4), lax.div(fsdp, 4)

    def ring(v, d):
        return lax.rem(v + (d + 4), 4)

    def device(z_high=None, dy=0, dcore=0, dz=0, dx=0):
        c2 = 1 - core if dcore else core
        z2 = 1 - z if dz else z
        z3 = zh if z_high is None else z_high
        return ((z3 * 4 + ring(y, dy)) * 2 + c2, z2 * 4 + ring(x, dx))

    column = [(dy, dc) for dy in range(4) for dc in range(2) if dy or dc]
    barrier = pltpu.get_barrier_semaphore()

    def greet(sem, p):
        pl.semaphore_signal(sem, inc=1, device_id=p, device_id_type=MESH)

    def later_in_column(dy, dc):
        if dy:
            return ring(y, dy) > y
        return core == 1

    def later_in_stack(d):
        return ring(zh, d) > zh

    def greet_others(sem_of, later):
        def where(test, sem, places):
            @pl.when(test if later else jnp.logical_not(test))
            def _():
                for place in places:
                    greet(sem, place)

        for d in range(4):
            cores = range(2) if d else (1,)
            where(later_in_column(d, 1), sem_of[0], [device(dy=d, dcore=dc) for dc in cores])
        for d in (1, 2, 3):
            where(later_in_stack(d), sem_of[1], [device(z_high=ring(zh, d), dz=dz) for dz in range(2)])

    for d in (1, 2, 3):
        greet(barrier, device(dx=d))
    greet(barrier, device(dz=1))
    column_later = 2 * (3 - y) + core
    stack_later = 2 * (3 - zh)

    def enter():
        pl.semaphore_wait(barrier, 4 + (7 - column_later) + (6 - stack_later))
    used = [0]
    pending = []

    def remote(src, dst, to):
        i = used[0]
        used[0] += 1
        return pltpu.make_async_remote_copy(
            src_ref=src, dst_ref=dst, send_sem=send_sem.at[i], recv_sem=recv_sem.at[i],
            device_id=to, device_id_type=MESH,
        )

    def send(src, dst, to):
        copy = remote(src, dst, to)
        copy.start()
        pending.append(copy)
        return copy

    loads = []

    def load(src, dst):
        copy = pltpu.make_async_copy(src, dst, load_sem.at[len(loads)])
        copy.start()
        loads.append(copy)
        return copy

    waited = set()

    def arrived(copy):
        if id(copy) not in waited:
            waited.add(id(copy))
            copy.wait()

    def load_group(g):
        cols = pl.ds(g * SPAN, SPAN)
        return load(momentum.at[:, cols], mom.at[:, cols]), load(grads.at[:, cols], xin.at[pl.ds(0, GRAD), cols])

    order = [g for name, g in PLAN if name == "F"]
    front = pl.ds(0, 7 * 2 * LANES)
    rest = pl.ds(7 * 2 * LANES, SPAN)
    group_loads = {order[0]: load_group(order[0])}
    load_wide = load(wide_hbm.at[front], wide.at[front])
    load_rest = []
    greet_others((barrier, barrier), True)

    def load_others():
        for g in order[1:]:
            group_loads[g] = load_group(g)
        load_rest.append(load(wide_hbm.at[rest], wide.at[rest]))
        load_rest.append(load(back_hbm, back))

    ready = set()

    def prepare(g):
        if g not in ready:
            ready.add(g)
            for copy in group_loads[g]:
                copy.wait()
            cols = slice(g * SPAN, (g + 1) * SPAN)
            top, low_part = halves(BETA * mom[:, cols])
            xin[GRAD : GRAD + MINE, cols] = top
            xin[GRAD + MINE :, cols] = low_part

    def fold(v):
        v = v[:, :LANES] + v[:, LANES:]
        own = v[GRAD : GRAD + MINE] + v[GRAD + MINE :]
        return v[:GRAD].reshape(MATS, NZL, NX, OWN, LANES), own.reshape(MATS, OWN, LANES)

    def forward(g):
        prepare(g)
        arrived(load_wide)
        if not load_rest:
            load_others()
        base = g * SPAN
        last = xin[:, base + HIGH : base + SPAN]
        for t in range(7):
            both = jnp.concatenate([xin[:, base + t * LANES : base + (t + 1) * LANES], last], axis=1)
            value, own = fold(dot(both, wide[t * 2 * LANES : (t + 1) * 2 * LANES]))
            lanes = slice(t * LANES, (t + 1) * LANES)
            for h in range(2):
                mats = slice(2 * h, 2 * h + 2)
                if (g, 2 * h) in X_UNITS:
                    u = X_UNITS.index((g, 2 * h))
                    for m in range(2):
                        for k in range(NZL):
                            sx[u, :, k, m, :, lanes] = value[2 * h + m, k]
                    sx[u, x, z, :, :, lanes] += own[mats]
                else:
                    u = Z_UNITS.index((g, 2 * h))
                    for m in range(2):
                        for k in range(NZL):
                            sz[u, k, :, m, :, lanes] = value[2 * h + m, k]
                    sz[u, z, x, :, :, lanes] += own[mats]

    def forward_low(g):
        prepare(g)
        arrived(load_rest[0])
        value, own = fold(dot(xin[:, g * SPAN : (g + 1) * SPAN], wide[7 * 2 * LANES :]))
        lanes = slice(g * LANES, (g + 1) * LANES)
        lw[:, :, :, :, lanes] = value
        lw[:, z, x, :, lanes] += own

    xd, zd, low = {}, {}, {}
    way = lambda u: 1 if u % 2 == 0 else -1
    z_way = lambda u: -way(u)

    def x_start(u):
        d = way(u)
        two = send(sx.at[u, ring(x, 2)], xr2.at[u], device(dx=d))
        one = send(sx.at[u, ring(x, -d)], xra.at[u], device(dx=-d))
        xd[u] = [two, one]

    def x_pass(u):
        d = way(u)
        to = ring(x, d)
        xd[u][0].wait_recv()
        sx[u, to] += xr2[u]
        xd[u].append(send(sx.at[u, to], xrb.at[u], device(dx=d)))

    def x_cross(u):
        xd[u][1].wait_recv()
        xd[u][2].wait_recv()
        sx[u, x] += xra[u] + xrb[u]
        xd[u].append(send(sx.at[u, x, 1 - z], xrz.at[u], device(dz=1)))

    def z_start(u):
        zd[u] = [send(sz.at[u, 1 - z], zr4.at[u], device(dz=1))]

    def z_cross(u):
        d = z_way(u)
        zd[u][0].wait_recv()
        sz[u, z] += zr4[u]
        zd[u].append(send(sz.at[u, z, ring(x, 2)], zr2.at[u], device(dx=d)))
        zd[u].append(send(sz.at[u, z, ring(x, -d)], zra.at[u], device(dx=-d)))

    def z_pass(u):
        d = z_way(u)
        to = ring(x, d)
        zd[u][1].wait_recv()
        sz[u, z, to] += zr2[u]
        zd[u].append(send(sz.at[u, z, to], zrb.at[u], device(dx=d)))

    parts = {}

    def x_end(u):
        xd[u][3].wait_recv()
        parts[X_UNITS[u]] = sx[u, x, z] + xrz[u]

    def z_end(u):
        zd[u][2].wait_recv()
        zd[u][3].wait_recv()
        parts[Z_UNITS[u]] = sz[u, z, x] + (zra[u] + zrb[u])

    stores = []

    def store(src, dst):
        copy = pltpu.make_async_copy(src, dst, store_sem.at[len(stores)])
        copy.start()
        stores.append(copy)

    def backward(g):
        arrived(load_rest[1])
        field = jnp.concatenate([parts[k] for k in sorted(parts) if k[0] == g], axis=0).reshape(MINE, HIGH)
        last = jnp.zeros((MINE, LANES), F32)
        for t in range(7):
            top, rest = halves(field[:, t * LANES : (t + 1) * LANES])
            v = dot(jnp.concatenate([top, rest], axis=0), back[t * LANES : (t + 1) * LANES])
            v = v[:MINE, : 2 * LANES] + (v[MINE:, : 2 * LANES] + v[:MINE, 2 * LANES :])
            base = g * SPAN + t * LANES
            nm[:, base : base + LANES] = v[:, :LANES]
            last += v[:, LANES:]
        nm[:, g * SPAN + HIGH : (g + 1) * SPAN] = last
        cols = pl.ds(g * SPAN, SPAN)
        store(nm.at[:, cols], new_out.at[:, cols])

    def low_a(_):
        @pl.when(column_later > 0)
        def _():
            pl.semaphore_wait(column_sem, column_later)

        low["a"] = [
            send(lw.at[ring(y, dy), 1 - core if dc else core], la.at[k], device(dy=dy, dcore=dc))
            for k, (dy, dc) in enumerate(column)
        ]

    def low_d(_):
        for copy in low["a"]:
            copy.wait_recv()
        lw[y, core] += ((la[0] + la[1]) + (la[2] + la[3])) + ((la[4] + la[5]) + la[6])
        low["d"] = [send(lw.at[y, core, ring(x, d)], lc.at[d - 1], device(dx=d)) for d in (1, 2, 3)]

    def low_e(_):
        for copy in low["d"]:
            copy.wait_recv()
        es[...] = lw[y, core, x] + (lc[0] + lc[1] + lc[2])
        low["in"] = [remote(es, le.at[d - 1], device(z_high=ring(zh, d))) for d in (1, 2, 3)]
        @pl.when(stack_later > 0)
        def _():
            pl.semaphore_wait(stack_sem, stack_later)

        low["out"] = [remote(es, le.at[3 + d], device(z_high=ring(zh, d), dz=1)) for d in range(4)]

        @pl.when(core == z)
        def _():
            for copy in low["in"]:
                copy.start()

        @pl.when(core != z)
        def _():
            for copy in low["out"]:
                copy.start()

    def low_i(_):
        low["i"] = [remote(total.at[y], total.at[y], device(dy=dy, dcore=dc)) for dy, dc in column]

        @pl.when(core == z)
        def _():
            for copy in low["in"] + low["out"]:
                copy.wait_recv()
            total[y] = es[...] + ((le[0] + le[1] + le[2]) + (le[3] + le[4] + le[5] + le[6]))
            for copy in low["i"]:
                copy.start()

    def low_end():
        arrived(load_rest[1])

        @pl.when(core == z)
        def _():
            for copy, (dy, dc) in zip(low["i"], column):
                if dc == 0:
                    copy.wait_recv()

        @pl.when(core != z)
        def _():
            for copy, (dy, dc) in zip(low["i"], column):
                if dc == 1:
                    copy.wait_recv()

    normalised = set()

    def normalise(g):
        if not normalised:
            low_end()
        normalised.add(g)
        table = lambda i: back[(7 + i) * LANES : (8 + i) * LANES]
        lanes = slice(g * LANES, (g + 1) * LANES)
        mean = total[:, :, lanes].reshape(MINE, LANES) * (1.0 / N_REP)
        top, rest = halves(mean)
        pair = jnp.concatenate([top, rest], axis=0)
        squares = jnp.concatenate(halves(mean * mean), axis=0)
        for h in range(2):
            v, w = dot(pair, table(h)), dot(squares, table(4 + h))
            field = v[:MINE] + (v[MINE:] + dot(top, table(2 + h)))
            square = w[:MINE] + w[MINE:]
            base = g * SPAN + h * WIDE
            up[:, base : base + WIDE] = field * lax.rsqrt(field * field + square + EPS)
        cols = pl.ds(g * SPAN, SPAN)
        store(up.at[:, cols], upd_out.at[:, cols])

    steps = {
        "F": forward, "FL": forward_low,
        "XS": x_start, "XP": x_pass, "XC": x_cross, "XE": x_end,
        "ZS": z_start, "ZC": z_cross, "ZP": z_pass, "ZE": z_end,
        "LA": low_a, "LC": low_d, "LD": low_e, "LF": low_i,
        "N": normalise, "BK": backward,
    }
    entered = answered = False
    for name, u in PLAN:
        if not entered and name not in ("F", "FL"):
            enter()
            entered = True
        if entered and not answered and name not in ("XS", "ZS"):
            greet_others((column_sem, stack_sem), False)
            answered = True
        steps[name](u)

    for copy in pending:
        copy.wait_send()

    @pl.when(core != z)
    def _():
        for copy in low["out"]:
            copy.wait_send()

    @pl.when(core == z)
    def _():
        for copy in low["in"] + low["i"]:
            copy.wait_send()

    for copy in stores:
        copy.wait()


def write_out(new_in, upd_in, new_out, upd_out, sems):
    copies = []
    for k, (src, dst) in enumerate([(new_in, new_out), (upd_in, upd_out)]):
        for m in range(MATS):
            rows = pl.ds(m * OWN, OWN)
            copies.append(pltpu.make_async_copy(src.at[rows], dst.at[rows], sems.at[k, m]))
    for copy in copies:
        copy.start()
    for copy in copies:
        copy.wait()


def per_device(gradients, momentum):
    wide, back = tables()
    anywhere = pl.BlockSpec(memory_space=pl.ANY)
    new_momentum, update = pl.pallas_call(
        kernel,
        out_shape=[jax.ShapeDtypeStruct((MINE, D), F32)] * 2,
        in_specs=[anywhere] * 4,
        out_specs=[anywhere] * 2,
        scratch_shapes=[
            pltpu.VMEM((GRAD + 2 * MINE, D), BF16),
            pltpu.VMEM((MINE, D), F32),
            pltpu.VMEM(wide.shape, BF16),
            pltpu.VMEM(back.shape, BF16),
            pltpu.VMEM((len(X_UNITS), NX, NZL, 2, OWN, HIGH), F32),
            pltpu.VMEM((len(Z_UNITS), NZL, NX, 2, OWN, HIGH), F32),
            pltpu.VMEM((MATS, NZL, NX, OWN, LOW), F32),
            *[pltpu.VMEM((len(X_UNITS), NZL, 2, OWN, HIGH), F32)] * 3,
            pltpu.VMEM((len(X_UNITS), 2, OWN, HIGH), F32),
            pltpu.VMEM((len(Z_UNITS), NX, 2, OWN, HIGH), F32),
            *[pltpu.VMEM((len(Z_UNITS), 2, OWN, HIGH), F32)] * 3,
            pltpu.VMEM((7, NX, OWN, LOW), F32),
            pltpu.VMEM((3, OWN, LOW), F32),
            pltpu.VMEM((7, OWN, LOW), F32),
            pltpu.VMEM((OWN, LOW), F32),
            pltpu.VMEM((MATS, OWN, LOW), F32),
            pltpu.VMEM((MINE, D), F32),
            pltpu.VMEM((MINE, D), F32),
            pltpu.SemaphoreType.DMA((2 * GROUPS + 3,)),
            pltpu.SemaphoreType.DMA((2 * GROUPS,)),
            pltpu.SemaphoreType.DMA((N_SEMS,)),
            pltpu.SemaphoreType.DMA((N_SEMS,)),
            pltpu.SemaphoreType.REGULAR,
            pltpu.SemaphoreType.REGULAR,
        ],
        compiler_params=pltpu.CompilerParams(
            collective_id=0, has_side_effects=True, vmem_limit_bytes=(52 * 1024 + 384) * 1024
        ),
        cost_estimate=pl.CostEstimate(flops=2_000_000_000, bytes_accessed=8_000_000, transcendentals=200_000),
    )(gradients.reshape(GRAD, D), momentum.reshape(MINE, D), wide, back)
    new_momentum, update = pl.pallas_call(
        write_out,
        out_shape=[jax.ShapeDtypeStruct((MINE, D), F32)] * 2,
        in_specs=[anywhere] * 2,
        out_specs=[anywhere] * 2,
        scratch_shapes=[pltpu.SemaphoreType.DMA((2, 4))],
        compiler_params=pltpu.CompilerParams(vmem_limit_bytes=4 * 1024 * 1024),
        cost_estimate=pl.CostEstimate(flops=0, bytes_accessed=2_600_000, transcendentals=0),
    )(new_momentum, update)
    return new_momentum.reshape(1, MATS, OWN, D), update.reshape(MATS, OWN, D)


def solution(mesh):
    return jax.shard_map(
        per_device,
        mesh=mesh,
        in_specs=(P("rep", "fsdp", None, None, None), P("rep", None, "fsdp", None)),
        out_specs=(P("rep", None, "fsdp", None), P(None, "fsdp", None)),
        check_vma=False,
    )
```

```python
import jax
import jax.numpy as jnp
import ml_dtypes
import numpy as np
from jax import lax
from jax.experimental import pallas as pl
from jax.experimental.pallas import tpu as pltpu
from jax.sharding import PartitionSpec as P

D, MATS, GROUP, KEEP, ROWS = 5120, 4, 64, 8, 64
BETA, EPS = 0.999, 1e-06
NX, NY, NZL, NZH, NC, N_REP = 4, 4, 2, 4, 2, 32
OWN = 8
LANES = 128
TILES = 8
SPAN = LANES * TILES
GROUPS = D // SPAN
HIGH = 7 * LANES
LOW = GROUPS * LANES
GRAD = MATS * ROWS
MINE = MATS * OWN
WIDE = 4 * LANES

F32, BF16 = jnp.float32, jnp.bfloat16
MESH = pl.DeviceIdType.MESH


def split(table):
    high = table.astype(ml_dtypes.bfloat16)
    low = (table - high.astype(np.float64)).astype(ml_dtypes.bfloat16)
    return high, low


def tables():
    n, k = np.arange(GROUP), np.arange(GROUP)[:, None]
    basis = np.sqrt(2.0 / GROUP) * np.cos(np.pi * (n + 0.5) * k / GROUP)
    basis[0] *= np.sqrt(0.5)
    rest = GROUP - KEEP
    high = np.zeros((LANES, 2 * rest))
    for b in range(2):
        high[b * GROUP : (b + 1) * GROUP, b * rest : (b + 1) * rest] = basis[KEEP:].T
    forward = np.zeros((7, 2 * LANES, LANES))
    for t in range(7):
        forward[t, :LANES, : 2 * rest] = high
        forward[t, LANES:, 2 * rest :] = high[:, 16 * t : 16 * t + 16]
    inverse = np.zeros((7, LANES, 2 * LANES))
    for t in range(7):
        inverse[t] = forward[t].T
    blocks = SPAN // GROUP
    keep = np.zeros((SPAN, LANES))
    mean = np.zeros((LANES, SPAN))
    for c in range(blocks):
        keep[c * GROUP : (c + 1) * GROUP, c * KEEP : (c + 1) * KEEP] = basis[:KEEP].T
        mean[c * KEEP : (c + 1) * KEEP, c * GROUP : (c + 1) * GROUP] = 1.0 / GROUP
    both = lambda table: np.concatenate(split(table), axis=-1)
    wide = np.concatenate([both(forward).reshape(-1, 2 * LANES), both(keep)], axis=0)
    back = np.concatenate([both(keep.T), mean.astype(ml_dtypes.bfloat16)], axis=-1)
    back = back.reshape(LANES, 6, WIDE).transpose(1, 0, 2).reshape(-1, WIDE)
    return wide, np.concatenate([both(inverse).reshape(-1, WIDE), back], axis=0)


def halves(value):
    top = value.astype(BF16)
    return top, (value - top.astype(F32)).astype(BF16)


def dot(a, b):
    return jnp.dot(a, b, preferred_element_type=F32)


X_UNITS = [(2, 0), (2, 2), (3, 0), (3, 2), (4, 0), (4, 2)]
Z_UNITS = [(0, 0), (0, 2), (1, 0), (1, 2)]
SENDS = ["x2", "xa", "xb", "xz", "z4", "z2", "za", "zb", "la", "lc", "ld", "lf"]
PLAN = [
    ("F", 4), ("XS", 4), ("F", 1), ("ZS", 3), ("FL", 4), ("FL", 3),
    ("XS", 5), ("FL", 2), ("FL", 1), ("FL", 0), ("LA", 0), ("F", 3),
    ("XS", 2), ("ZS", 2), ("F", 2), ("XS", 0), ("F", 0), ("XS", 3),
    ("XP", 5), ("ZS", 1), ("ZS", 0), ("XP", 2), ("LC", 0), ("XS", 1),
    ("XP", 3), ("XP", 4), ("ZC", 3), ("XP", 0), ("ZC", 1), ("LD", 0),
    ("ZC", 2), ("XP", 1), ("XC", 2), ("XC", 3), ("XC", 5), ("XC", 4),
    ("ZP", 3), ("ZC", 0), ("XE", 2), ("ZP", 2), ("XE", 3), ("BK", 3),
    ("XC", 0), ("XE", 5), ("LF", 0), ("ZP", 1), ("XC", 1), ("XE", 4),
    ("BK", 4), ("ZP", 0), ("ZE", 3), ("ZE", 2), ("BK", 1), ("XE", 1),
    ("XE", 0), ("BK", 2), ("ZE", 1), ("ZE", 0), ("BK", 0), ("N", 3),
    ("N", 1), ("N", 2), ("N", 0), ("N", 4),
]


def kernel(
    grads, momentum, wide_hbm, back_hbm, new_out, upd_out,
    xin, mom, wide, back, sx, sz, lw,
    xr2, xab, xrz, zr4, zr2, zab,
    la, lc, le, es, total, nm, up,
    load_sem, store_sem, send_sem, recv_sem, column_sem, stack_sem,
):
    rep, fsdp = lax.axis_index("rep"), lax.axis_index("fsdp")
    core, y, zh = lax.rem(rep, 2), lax.rem(lax.div(rep, 2), 4), lax.div(rep, 8)
    x, z = lax.rem(fsdp, 4), lax.div(fsdp, 4)

    def ring(v, d):
        return lax.rem(v + (d + 4), 4)

    xs, ys, zs = ([v] + [ring(v, d) for d in (1, 2, 3)] for v in (x, y, zh))
    other_core, other_z = 1 - core, 1 - z
    own_rep, own_fsdp = rep, fsdp
    places = {}

    def device(dzh=0, dy=0, dcore=0, dz=0, dx=0):
        key = (dzh, dy % 4, dcore, dz, dx % 4)
        if key not in places:
            c2, z2 = other_core if dcore else core, other_z if dz else z
            moved = dzh or dy or dcore
            r2 = (zs[dzh] * 4 + ys[dy % 4]) * 2 + c2 if moved else own_rep
            places[key] = (r2, z2 * 4 + xs[dx % 4] if dz or dx else own_fsdp)
        return places[key]

    for dy in range(4):
        for dc in range(2):
            device(dy=dy, dcore=dc)
    for d in range(4):
        for dz in range(2):
            device(dzh=d, dz=dz)
        device(dx=d)

    column = [(dy, dc) for dy in range(4) for dc in range(2) if dy or dc]
    barrier = pltpu.get_barrier_semaphore()

    def greet(sem, p):
        pl.semaphore_signal(sem, inc=1, device_id=p, device_id_type=MESH)

    def later_in_column(dy, dc):
        if dy:
            return ring(y, dy) > y
        return core == 1

    def later_in_stack(d):
        return ring(zh, d) > zh

    def greet_others(sem_of, later):
        def where(test, sem, places):
            @pl.when(test if later else jnp.logical_not(test))
            def _():
                for place in places:
                    greet(sem, place)

        for d in range(4):
            cores = range(2) if d else (1,)
            where(later_in_column(d, 1), sem_of[0], [device(dy=d, dcore=dc) for dc in cores])
        for d in (1, 2, 3):
            where(later_in_stack(d), sem_of[1], [device(dzh=d, dz=dz) for dz in range(2)])

    for d in (1, 2, 3):
        greet(barrier, device(dx=d))
    greet(barrier, device(dz=1))
    column_later = 2 * (3 - y) + core
    stack_later = 2 * (3 - zh)

    def enter():
        pl.semaphore_wait(barrier, 4 + (7 - column_later) + (6 - stack_later))
    def remote(kind, src, dst, to, recv):
        return pltpu.make_async_remote_copy(
            src_ref=src, dst_ref=dst, send_sem=send_sem.at[SENDS.index(kind)],
            recv_sem=recv_sem.at[recv], device_id=to, device_id_type=MESH,
        )

    def send(kind, src, dst, to, recv):
        remote(kind, src, dst, to, recv).start()

    def await_bytes(ref, sem):
        pltpu.make_async_copy(ref, ref, sem).wait()

    def received(ref, recv):
        await_bytes(ref, recv_sem.at[recv])

    def all_sent(kind, ref):
        await_bytes(ref, send_sem.at[SENDS.index(kind)])

    loads = []

    def load(src, dst):
        copy = pltpu.make_async_copy(src, dst, load_sem.at[len(loads)])
        copy.start()
        loads.append(copy)
        return copy

    waited = set()

    def arrived(copy):
        if id(copy) not in waited:
            waited.add(id(copy))
            copy.wait()

    def load_group(g):
        cols = pl.ds(g * SPAN, SPAN)
        return load(momentum.at[:, cols], mom.at[:, cols]), load(grads.at[:, cols], xin.at[pl.ds(0, GRAD), cols])

    order = [g for name, g in PLAN if name == "F"]
    front = pl.ds(0, 7 * 2 * LANES)
    rest = pl.ds(7 * 2 * LANES, SPAN)
    group_loads = {order[0]: load_group(order[0])}
    load_wide = load(wide_hbm.at[front], wide.at[front])
    load_rest = []
    greet_others((barrier, barrier), True)

    def load_others():
        for g in order[1:]:
            group_loads[g] = load_group(g)
        load_rest.append(load(wide_hbm.at[rest], wide.at[rest]))
        load_rest.append(load(back_hbm, back))

    ready = set()

    def prepare(g):
        if g not in ready:
            ready.add(g)
            for copy in group_loads[g]:
                copy.wait()
            cols = slice(g * SPAN, (g + 1) * SPAN)
            top, low_part = halves(BETA * mom[:, cols])
            xin[GRAD : GRAD + MINE, cols] = top
            xin[GRAD + MINE :, cols] = low_part

    def fold(v):
        v = v[:, :LANES] + v[:, LANES:]
        own = v[GRAD : GRAD + MINE] + v[GRAD + MINE :]
        return v[:GRAD].reshape(MATS, NZL, NX, OWN, LANES), own.reshape(MATS, OWN, LANES)

    def forward(g):
        prepare(g)
        arrived(load_wide)
        if not load_rest:
            load_others()
        base = g * SPAN
        last = xin[:, base + HIGH : base + SPAN]
        for t in range(7):
            both = jnp.concatenate([xin[:, base + t * LANES : base + (t + 1) * LANES], last], axis=1)
            value, own = fold(dot(both, wide[t * 2 * LANES : (t + 1) * 2 * LANES]))
            lanes = slice(t * LANES, (t + 1) * LANES)
            for h in range(2):
                mats = slice(2 * h, 2 * h + 2)
                if (g, 2 * h) in X_UNITS:
                    u = X_UNITS.index((g, 2 * h))
                    for m in range(2):
                        for k in range(NZL):
                            sx[u, :, k, m, :, lanes] = value[2 * h + m, k]
                    sx[u, x, z, :, :, lanes] += own[mats]
                else:
                    u = Z_UNITS.index((g, 2 * h))
                    for m in range(2):
                        for k in range(NZL):
                            sz[u, k, :, m, :, lanes] = value[2 * h + m, k]
                    sz[u, z, x, :, :, lanes] += own[mats]

    def forward_low(g):
        prepare(g)
        arrived(load_rest[0])
        value, own = fold(dot(xin[:, g * SPAN : (g + 1) * SPAN], wide[7 * 2 * LANES :]))
        lanes = slice(g * LANES, (g + 1) * LANES)
        lw[:, :, :, :, lanes] = value
        lw[:, z, x, :, lanes] += own

    way = lambda u: 1 if u % 2 == 0 else -1
    z_way = lambda u: -way(u)
    nx, nz = len(X_UNITS), len(Z_UNITS)
    X2, XAB, XZ = 0, nx, 2 * nx
    Z4, Z2, ZAB = 3 * nx, 3 * nx + nz, 3 * nx + 2 * nz
    LOW_A = 3 * nx + 3 * nz
    LOW_C, LOW_D, LOW_F = LOW_A + 1, LOW_A + 2, LOW_A + 3

    def x_start(u):
        d = way(u)
        send("x2", sx.at[u, xs[2]], xr2.at[u], device(dx=d), X2 + u)
        send("xa", sx.at[u, xs[-d]], xab.at[u, 0], device(dx=-d), XAB + u)

    def x_pass(u):
        d = way(u)
        received(xr2.at[u], X2 + u)
        sx[u, xs[d]] += xr2[u]
        send("xb", sx.at[u, xs[d]], xab.at[u, 1], device(dx=d), XAB + u)

    def x_cross(u):
        received(xab.at[u], XAB + u)
        sx[u, x] += xab[u, 0] + xab[u, 1]
        send("xz", sx.at[u, x, other_z], xrz.at[u], device(dz=1), XZ + u)

    def z_start(u):
        send("z4", sz.at[u, other_z], zr4.at[u], device(dz=1), Z4 + u)

    def z_cross(u):
        d = z_way(u)
        received(zr4.at[u], Z4 + u)
        sz[u, z] += zr4[u]
        send("z2", sz.at[u, z, xs[2]], zr2.at[u], device(dx=d), Z2 + u)
        send("za", sz.at[u, z, xs[-d]], zab.at[u, 0], device(dx=-d), ZAB + u)

    def z_pass(u):
        d = z_way(u)
        received(zr2.at[u], Z2 + u)
        sz[u, z, xs[d]] += zr2[u]
        send("zb", sz.at[u, z, xs[d]], zab.at[u, 1], device(dx=d), ZAB + u)

    parts = {}

    def x_end(u):
        received(xrz.at[u], XZ + u)
        parts[X_UNITS[u]] = sx[u, x, z] + xrz[u]

    def z_end(u):
        received(zab.at[u], ZAB + u)
        parts[Z_UNITS[u]] = sz[u, z, x] + (zab[u, 0] + zab[u, 1])

    stores = []

    def store(src, dst):
        copy = pltpu.make_async_copy(src, dst, store_sem.at[len(stores)])
        copy.start()
        stores.append(copy)

    def backward(g):
        arrived(load_rest[1])
        field = jnp.concatenate([parts[k] for k in sorted(parts) if k[0] == g], axis=0).reshape(MINE, HIGH)
        last = jnp.zeros((MINE, LANES), F32)
        for t in range(7):
            top, rest = halves(field[:, t * LANES : (t + 1) * LANES])
            v = dot(jnp.concatenate([top, rest], axis=0), back[t * LANES : (t + 1) * LANES])
            v = v[:MINE, : 2 * LANES] + (v[MINE:, : 2 * LANES] + v[:MINE, 2 * LANES :])
            base = g * SPAN + t * LANES
            nm[:, base : base + LANES] = v[:, :LANES]
            last += v[:, LANES:]
        nm[:, g * SPAN + HIGH : (g + 1) * SPAN] = last
        cols = pl.ds(g * SPAN, SPAN)
        store(nm.at[:, cols], new_out.at[:, cols])

    def low_a(_):
        @pl.when(column_later > 0)
        def _():
            pl.semaphore_wait(column_sem, column_later)

        for k, (dy, dc) in enumerate(column):
            send("la", lw.at[ys[dy], other_core if dc else core], la.at[k], device(dy=dy, dcore=dc), LOW_A)

    def low_d(_):
        received(la, LOW_A)
        lw[y, core] += ((la[0] + la[1]) + (la[2] + la[3])) + ((la[4] + la[5]) + la[6])
        for d in (1, 2, 3):
            send("lc", lw.at[y, core, xs[d]], lc.at[d - 1], device(dx=d), LOW_C)

    def low_e(_):
        received(lc, LOW_C)
        es[...] = lw[y, core, x] + (lc[0] + lc[1] + lc[2])

        @pl.when(stack_later > 0)
        def _():
            pl.semaphore_wait(stack_sem, stack_later)

        @pl.when(core == z)
        def _():
            for d in (1, 2, 3):
                send("ld", es, le.at[d - 1], device(dzh=d), LOW_D)

        @pl.when(core != z)
        def _():
            for d in range(4):
                send("ld", es, le.at[3 + d], device(dzh=d, dz=1), LOW_D)

    def low_i(_):
        @pl.when(core == z)
        def _():
            received(le, LOW_D)
            total[y] = es[...] + ((le[0] + le[1] + le[2]) + (le[3] + le[4] + le[5] + le[6]))
            for dy, dc in column:
                send("lf", total.at[y], total.at[y], device(dy=dy, dcore=dc), LOW_F)

    def low_end():
        arrived(load_rest[1])

        @pl.when(core == z)
        def _():
            received(total.at[pl.ds(0, 3)], LOW_F)

        @pl.when(core != z)
        def _():
            received(total, LOW_F)

    normalised = set()

    def normalise(g):
        if not normalised:
            low_end()
        normalised.add(g)
        table = lambda i: back[(7 + i) * LANES : (8 + i) * LANES]
        lanes = slice(g * LANES, (g + 1) * LANES)
        mean = total[:, :, lanes].reshape(MINE, LANES) * (1.0 / N_REP)
        top, rest = halves(mean)
        pair = jnp.concatenate([top, rest], axis=0)
        squares = jnp.concatenate(halves(mean * mean), axis=0)
        for h in range(2):
            v, w = dot(pair, table(h)), dot(squares, table(4 + h))
            field = v[:MINE] + (v[MINE:] + dot(top, table(2 + h)))
            square = w[:MINE] + w[MINE:]
            base = g * SPAN + h * WIDE
            up[:, base : base + WIDE] = field * lax.rsqrt(field * field + square + EPS)
        cols = pl.ds(g * SPAN, SPAN)
        store(up.at[:, cols], upd_out.at[:, cols])

    steps = {
        "F": forward, "FL": forward_low,
        "XS": x_start, "XP": x_pass, "XC": x_cross, "XE": x_end,
        "ZS": z_start, "ZC": z_cross, "ZP": z_pass, "ZE": z_end,
        "LA": low_a, "LC": low_d, "LD": low_e, "LF": low_i,
        "N": normalise, "BK": backward,
    }
    entered = answered = False
    for name, u in PLAN:
        if not entered and name not in ("F", "FL"):
            enter()
            entered = True
        if entered and not answered and name not in ("XS", "ZS"):
            greet_others((column_sem, stack_sem), False)
            answered = True
        steps[name](u)

    all_sent("x2", xr2)
    all_sent("xa", xr2)
    all_sent("xb", xr2)
    all_sent("xz", xrz)
    all_sent("z4", zr4)
    all_sent("z2", zr2)
    all_sent("za", zr2)
    all_sent("zb", zr2)
    all_sent("la", la)
    all_sent("lc", lc)

    @pl.when(core != z)
    def _():
        all_sent("ld", le.at[pl.ds(0, 4)])

    @pl.when(core == z)
    def _():
        all_sent("ld", le.at[pl.ds(0, 3)])
        all_sent("lf", le)

    for copy in stores:
        copy.wait()


def write_out(new_in, upd_in, new_out, upd_out, sems):
    copies = []
    for k, (src, dst) in enumerate([(new_in, new_out), (upd_in, upd_out)]):
        for m in range(MATS):
            rows = pl.ds(m * OWN, OWN)
            copies.append(pltpu.make_async_copy(src.at[rows], dst.at[rows], sems.at[k, m]))
    for copy in copies:
        copy.start()
    for copy in copies:
        copy.wait()


def per_device(gradients, momentum):
    wide, back = tables()
    anywhere = pl.BlockSpec(memory_space=pl.ANY)
    new_momentum, update = pl.pallas_call(
        kernel,
        out_shape=[jax.ShapeDtypeStruct((MINE, D), F32)] * 2,
        in_specs=[anywhere] * 4,
        out_specs=[anywhere] * 2,
        scratch_shapes=[
            pltpu.VMEM((GRAD + 2 * MINE, D), BF16),
            pltpu.VMEM((MINE, D), F32),
            pltpu.VMEM(wide.shape, BF16),
            pltpu.VMEM(back.shape, BF16),
            pltpu.VMEM((len(X_UNITS), NX, NZL, 2, OWN, HIGH), F32),
            pltpu.VMEM((len(Z_UNITS), NZL, NX, 2, OWN, HIGH), F32),
            pltpu.VMEM((MATS, NZL, NX, OWN, LOW), F32),
            pltpu.VMEM((len(X_UNITS), NZL, 2, OWN, HIGH), F32),
            pltpu.VMEM((len(X_UNITS), 2, NZL, 2, OWN, HIGH), F32),
            pltpu.VMEM((len(X_UNITS), 2, OWN, HIGH), F32),
            pltpu.VMEM((len(Z_UNITS), NX, 2, OWN, HIGH), F32),
            pltpu.VMEM((len(Z_UNITS), 2, OWN, HIGH), F32),
            pltpu.VMEM((len(Z_UNITS), 2, 2, OWN, HIGH), F32),
            pltpu.VMEM((7, NX, OWN, LOW), F32),
            pltpu.VMEM((3, OWN, LOW), F32),
            pltpu.VMEM((7, OWN, LOW), F32),
            pltpu.VMEM((OWN, LOW), F32),
            pltpu.VMEM((MATS, OWN, LOW), F32),
            pltpu.VMEM((MINE, D), F32),
            pltpu.VMEM((MINE, D), F32),
            pltpu.SemaphoreType.DMA((2 * GROUPS + 3,)),
            pltpu.SemaphoreType.DMA((2 * GROUPS,)),
            pltpu.SemaphoreType.DMA((len(SENDS),)),
            pltpu.SemaphoreType.DMA((3 * len(X_UNITS) + 3 * len(Z_UNITS) + 4,)),
            pltpu.SemaphoreType.REGULAR,
            pltpu.SemaphoreType.REGULAR,
        ],
        compiler_params=pltpu.CompilerParams(
            collective_id=0, has_side_effects=True, vmem_limit_bytes=(52 * 1024 + 384) * 1024
        ),
        cost_estimate=pl.CostEstimate(flops=2_000_000_000, bytes_accessed=8_000_000, transcendentals=200_000),
    )(gradients.reshape(GRAD, D), momentum.reshape(MINE, D), wide, back)
    new_momentum, update = pl.pallas_call(
        write_out,
        out_shape=[jax.ShapeDtypeStruct((MINE, D), F32)] * 2,
        in_specs=[anywhere] * 2,
        out_specs=[anywhere] * 2,
        scratch_shapes=[pltpu.SemaphoreType.DMA((2, 4))],
        compiler_params=pltpu.CompilerParams(vmem_limit_bytes=4 * 1024 * 1024),
        cost_estimate=pl.CostEstimate(flops=0, bytes_accessed=2_600_000, transcendentals=0),
    )(new_momentum, update)
    return new_momentum.reshape(1, MATS, OWN, D), update.reshape(MATS, OWN, D)


def solution(mesh):
    return jax.shard_map(
        per_device,
        mesh=mesh,
        in_specs=(P("rep", "fsdp", None, None, None), P("rep", None, "fsdp", None)),
        out_specs=(P("rep", None, "fsdp", None), P(None, "fsdp", None)),
        check_vma=False,
    )
```

```python
import jax
import jax.numpy as jnp
import ml_dtypes
import numpy as np
from jax import lax
from jax.experimental import pallas as pl
from jax.experimental.pallas import tpu as pltpu
from jax.sharding import PartitionSpec as P

D, MATS, GROUP, KEEP, ROWS = 5120, 4, 64, 8, 64
BETA, EPS = 0.999, 1e-06
NX, NY, NZL, NZH, NC, N_REP = 4, 4, 2, 4, 2, 32
OWN = 8
LANES = 128
TILES = 8
SPAN = LANES * TILES
GROUPS = D // SPAN
HIGH = 7 * LANES
LOW = GROUPS * LANES
GRAD = MATS * ROWS
MINE = MATS * OWN
WIDE = 4 * LANES

F32, BF16 = jnp.float32, jnp.bfloat16
MESH = pl.DeviceIdType.MESH


def split(table):
    high = table.astype(ml_dtypes.bfloat16)
    low = (table - high.astype(np.float64)).astype(ml_dtypes.bfloat16)
    return high, low


def tables():
    n, k = np.arange(GROUP), np.arange(GROUP)[:, None]
    basis = np.sqrt(2.0 / GROUP) * np.cos(np.pi * (n + 0.5) * k / GROUP)
    basis[0] *= np.sqrt(0.5)
    rest = GROUP - KEEP
    high = np.zeros((LANES, 2 * rest))
    for b in range(2):
        high[b * GROUP : (b + 1) * GROUP, b * rest : (b + 1) * rest] = basis[KEEP:].T
    forward = np.zeros((7, 2 * LANES, LANES))
    for t in range(7):
        forward[t, :LANES, : 2 * rest] = high
        forward[t, LANES:, 2 * rest :] = high[:, 16 * t : 16 * t + 16]
    inverse = np.zeros((7, LANES, 2 * LANES))
    for t in range(7):
        inverse[t] = forward[t].T
    blocks = SPAN // GROUP
    keep = np.zeros((SPAN, LANES))
    mean = np.zeros((LANES, SPAN))
    for c in range(blocks):
        keep[c * GROUP : (c + 1) * GROUP, c * KEEP : (c + 1) * KEEP] = basis[:KEEP].T
        mean[c * KEEP : (c + 1) * KEEP, c * GROUP : (c + 1) * GROUP] = 1.0 / GROUP
    both = lambda table: np.concatenate(split(table), axis=-1)
    wide = np.concatenate([both(forward).reshape(-1, 2 * LANES), both(keep)], axis=0)
    back = np.concatenate([both(keep.T), mean.astype(ml_dtypes.bfloat16)], axis=-1)
    back = back.reshape(LANES, 6, WIDE).transpose(1, 0, 2).reshape(-1, WIDE)
    return wide, np.concatenate([both(inverse).reshape(-1, WIDE), back], axis=0)


def halves(value):
    top = value.astype(BF16)
    return top, (value - top.astype(F32)).astype(BF16)


def dot(a, b):
    return jnp.dot(a, b, preferred_element_type=F32)


X_UNITS = [(2, 0), (2, 2), (3, 0), (3, 2), (4, 0), (4, 2)]
Z_UNITS = [(0, 0), (0, 2), (1, 0), (1, 2)]
SENDS = ["x2", "xa", "xb", "xz", "z4", "z2", "za", "zb", "la", "lc", "ld", "lf"]
EARLY = [
    ("F", 2), ("XS", 1), ("F", 1), ("ZS", 3), ("FL", 1), ("XS", 0),
    ("F", 4), ("FL", 2), ("ZS", 2), ("XS", 4), ("FL", 4), ("FL", 0),
    ("FL", 3), ("LA", 0), ("XS", 5), ("F", 0), ("XP", 1), ("XP", 0),
    ("ZS", 1), ("F", 3), ("ZC", 3), ("XS", 2), ("XC", 1), ("XP", 5),
    ("ZS", 0), ("ZP", 3), ("LC", 0), ("XP", 4), ("XP", 2), ("XS", 3),
    ("ZC", 1), ("ZC", 2), ("LD", 0), ("XC", 0), ("XC", 5), ("ZE", 3),
    ("XE", 1), ("XP", 3), ("XC", 4), ("ZC", 0), ("XC", 2), ("ZP", 2),
    ("LF", 0), ("XE", 0), ("BK", 2), ("XC", 3), ("ZP", 1), ("XE", 5),
    ("ZP", 0), ("XE", 4), ("BK", 4), ("ZE", 2), ("BK", 1), ("XE", 2),
    ("N", 0), ("N", 1), ("N", 2), ("N", 3), ("N", 4), ("XE", 3),
    ("BK", 3), ("ZE", 1), ("ZE", 0), ("BK", 0),
]
LATE = [
    ("F", 2), ("XS", 0), ("F", 1), ("ZS", 3), ("FL", 2), ("FL", 1),
    ("XS", 1), ("FL", 4), ("FL", 3), ("FL", 0), ("LA", 0), ("XP", 0),
    ("F", 3), ("XS", 3), ("ZS", 2), ("XP", 1), ("F", 0), ("XS", 2),
    ("ZS", 1), ("ZC", 3), ("F", 4), ("LC", 0), ("XS", 4), ("XP", 2),
    ("XC", 1), ("XS", 5), ("XP", 3), ("LD", 0), ("ZC", 1), ("ZS", 0),
    ("XC", 0), ("XE", 1), ("XP", 4), ("ZC", 2), ("XP", 5), ("ZP", 3),
    ("XC", 2), ("LF", 0), ("ZP", 1), ("XC", 3), ("ZC", 0), ("ZP", 2),
    ("XE", 0), ("BK", 2), ("XC", 4), ("XE", 2), ("N", 2), ("XC", 5),
    ("N", 4), ("N", 0), ("XE", 3), ("ZP", 0), ("BK", 3), ("N", 3),
    ("XE", 4), ("ZE", 3), ("N", 1), ("ZE", 2), ("BK", 1), ("ZE", 1),
    ("XE", 5), ("BK", 4), ("ZE", 0), ("BK", 0),
]


def kernel(
    grads, momentum, wide_hbm, back_hbm, new_out, upd_out,
    xin, mom, wide, back, sx, sz, lw,
    xr2, xab, xrz, zr4, zr2, zab,
    la, lc, le, es, total, nm, up,
    load_sem, store_sem, send_sem, recv_sem, column_sem, stack_sem,
):
    rep, fsdp = lax.axis_index("rep"), lax.axis_index("fsdp")
    core, y, zh = lax.rem(rep, 2), lax.rem(lax.div(rep, 2), 4), lax.div(rep, 8)
    x, z = lax.rem(fsdp, 4), lax.div(fsdp, 4)

    def ring(v, d):
        return lax.rem(v + (d + 4), 4)

    xs, ys, zs = ([v] + [ring(v, d) for d in (1, 2, 3)] for v in (x, y, zh))
    other_core, other_z = 1 - core, 1 - z
    own_rep, own_fsdp = rep, fsdp
    places = {}

    def device(dzh=0, dy=0, dcore=0, dz=0, dx=0):
        key = (dzh, dy % 4, dcore, dz, dx % 4)
        if key not in places:
            c2, z2 = other_core if dcore else core, other_z if dz else z
            moved = dzh or dy or dcore
            r2 = (zs[dzh] * 4 + ys[dy % 4]) * 2 + c2 if moved else own_rep
            places[key] = (r2, z2 * 4 + xs[dx % 4] if dz or dx else own_fsdp)
        return places[key]

    for dy in range(4):
        for dc in range(2):
            device(dy=dy, dcore=dc)
    for d in range(4):
        for dz in range(2):
            device(dzh=d, dz=dz)
        device(dx=d)

    column = [(dy, dc) for dy in range(4) for dc in range(2) if dy or dc]
    barrier = pltpu.get_barrier_semaphore()

    def greet(sem, p):
        pl.semaphore_signal(sem, inc=1, device_id=p, device_id_type=MESH)

    def later_in_column(dy, dc):
        if dy:
            return ring(y, dy) > y
        return core == 1

    def later_in_stack(d):
        return ring(zh, d) > zh

    def greet_others(sem_of, later):
        def where(test, sem, places):
            @pl.when(test if later else jnp.logical_not(test))
            def _():
                for place in places:
                    greet(sem, place)

        for d in range(4):
            cores = range(2) if d else (1,)
            where(later_in_column(d, 1), sem_of[0], [device(dy=d, dcore=dc) for dc in cores])
        for d in (1, 2, 3):
            where(later_in_stack(d), sem_of[1], [device(dzh=d, dz=dz) for dz in range(2)])

    for d in (1, 2, 3):
        greet(barrier, device(dx=d))
    greet(barrier, device(dz=1))
    column_later = 2 * (3 - y) + core
    stack_later = 2 * (3 - zh)

    def enter():
        pl.semaphore_wait(barrier, 4 + (7 - column_later) + (6 - stack_later))
    def remote(kind, src, dst, to, recv):
        return pltpu.make_async_remote_copy(
            src_ref=src, dst_ref=dst, send_sem=send_sem.at[SENDS.index(kind)],
            recv_sem=recv_sem.at[recv], device_id=to, device_id_type=MESH,
        )

    def send(kind, src, dst, to, recv):
        remote(kind, src, dst, to, recv).start()

    def await_bytes(ref, sem):
        pltpu.make_async_copy(ref, ref, sem).wait()

    def received(ref, recv):
        await_bytes(ref, recv_sem.at[recv])

    def all_sent(kind, ref):
        await_bytes(ref, send_sem.at[SENDS.index(kind)])

    loads = []

    def load(src, dst):
        copy = pltpu.make_async_copy(src, dst, load_sem.at[len(loads)])
        copy.start()
        loads.append(copy)
        return copy

    waited, ready, parts, normalised = set(), set(), {}, set()

    def arrived(copy):
        if id(copy) not in waited:
            waited.add(id(copy))
            copy.wait()

    def load_group(g):
        cols = pl.ds(g * SPAN, SPAN)
        return load(momentum.at[:, cols], mom.at[:, cols]), load(grads.at[:, cols], xin.at[pl.ds(0, GRAD), cols])

    order = [g for name, g in EARLY if name == "F"]
    front = pl.ds(0, 7 * 2 * LANES)
    rest = pl.ds(7 * 2 * LANES, SPAN)
    group_loads = {order[0]: load_group(order[0])}
    load_wide = load(wide_hbm.at[front], wide.at[front])
    load_rest = []
    greet_others((barrier, barrier), True)

    def load_others():
        for g in order[1:]:
            group_loads[g] = load_group(g)
        load_rest.append(load(wide_hbm.at[rest], wide.at[rest]))
        load_rest.append(load(back_hbm, back))

    def prepare(g):
        if g not in ready:
            ready.add(g)
            for copy in group_loads[g]:
                copy.wait()
            cols = slice(g * SPAN, (g + 1) * SPAN)
            top, low_part = halves(BETA * mom[:, cols])
            xin[GRAD : GRAD + MINE, cols] = top
            xin[GRAD + MINE :, cols] = low_part

    def fold(v):
        v = v[:, :LANES] + v[:, LANES:]
        own = v[GRAD : GRAD + MINE] + v[GRAD + MINE :]
        return v[:GRAD].reshape(MATS, NZL, NX, OWN, LANES), own.reshape(MATS, OWN, LANES)

    def forward(g):
        prepare(g)
        arrived(load_wide)
        if not load_rest:
            load_others()
        base = g * SPAN
        last = xin[:, base + HIGH : base + SPAN]
        for t in range(7):
            both = jnp.concatenate([xin[:, base + t * LANES : base + (t + 1) * LANES], last], axis=1)
            value, own = fold(dot(both, wide[t * 2 * LANES : (t + 1) * 2 * LANES]))
            lanes = slice(t * LANES, (t + 1) * LANES)
            for h in range(2):
                mats = slice(2 * h, 2 * h + 2)
                if (g, 2 * h) in X_UNITS:
                    u = X_UNITS.index((g, 2 * h))
                    for m in range(2):
                        for k in range(NZL):
                            sx[u, :, k, m, :, lanes] = value[2 * h + m, k]
                    sx[u, x, z, :, :, lanes] += own[mats]
                else:
                    u = Z_UNITS.index((g, 2 * h))
                    for m in range(2):
                        for k in range(NZL):
                            sz[u, k, :, m, :, lanes] = value[2 * h + m, k]
                    sz[u, z, x, :, :, lanes] += own[mats]

    def forward_low(g):
        prepare(g)
        arrived(load_rest[0])
        value, own = fold(dot(xin[:, g * SPAN : (g + 1) * SPAN], wide[7 * 2 * LANES :]))
        lanes = slice(g * LANES, (g + 1) * LANES)
        lw[:, :, :, :, lanes] = value
        lw[:, z, x, :, lanes] += own

    way = lambda u: 1 if u % 2 == 0 else -1
    z_way = lambda u: -way(u)
    nx, nz = len(X_UNITS), len(Z_UNITS)
    X2, XAB, XZ = 0, nx, 2 * nx
    Z4, Z2, ZAB = 3 * nx, 3 * nx + nz, 3 * nx + 2 * nz
    LOW_A = 3 * nx + 3 * nz
    LOW_C, LOW_D, LOW_F = LOW_A + 1, LOW_A + 2, LOW_A + 3

    def x_start(u):
        d = way(u)
        send("x2", sx.at[u, xs[2]], xr2.at[u], device(dx=d), X2 + u)
        send("xa", sx.at[u, xs[-d]], xab.at[u, 0], device(dx=-d), XAB + u)

    def x_pass(u):
        d = way(u)
        received(xr2.at[u], X2 + u)
        sx[u, xs[d]] += xr2[u]
        send("xb", sx.at[u, xs[d]], xab.at[u, 1], device(dx=d), XAB + u)

    def x_cross(u):
        received(xab.at[u], XAB + u)
        sx[u, x] += xab[u, 0] + xab[u, 1]
        send("xz", sx.at[u, x, other_z], xrz.at[u], device(dz=1), XZ + u)

    def z_start(u):
        send("z4", sz.at[u, other_z], zr4.at[u], device(dz=1), Z4 + u)

    def z_cross(u):
        d = z_way(u)
        received(zr4.at[u], Z4 + u)
        sz[u, z] += zr4[u]
        send("z2", sz.at[u, z, xs[2]], zr2.at[u], device(dx=d), Z2 + u)
        send("za", sz.at[u, z, xs[-d]], zab.at[u, 0], device(dx=-d), ZAB + u)

    def z_pass(u):
        d = z_way(u)
        received(zr2.at[u], Z2 + u)
        sz[u, z, xs[d]] += zr2[u]
        send("zb", sz.at[u, z, xs[d]], zab.at[u, 1], device(dx=d), ZAB + u)

    def x_end(u):
        received(xrz.at[u], XZ + u)
        parts[X_UNITS[u]] = sx[u, x, z] + xrz[u]

    def z_end(u):
        received(zab.at[u], ZAB + u)
        parts[Z_UNITS[u]] = sz[u, z, x] + (zab[u, 0] + zab[u, 1])

    stores = []

    def store(src, dst):
        copy = pltpu.make_async_copy(src, dst, store_sem.at[len(stores)])
        copy.start()
        stores.append(copy)

    def backward(g):
        arrived(load_rest[1])
        field = jnp.concatenate([parts[k] for k in sorted(parts) if k[0] == g], axis=0).reshape(MINE, HIGH)
        last = jnp.zeros((MINE, LANES), F32)
        for t in range(7):
            top, rest = halves(field[:, t * LANES : (t + 1) * LANES])
            v = dot(jnp.concatenate([top, rest], axis=0), back[t * LANES : (t + 1) * LANES])
            v = v[:MINE, : 2 * LANES] + (v[MINE:, : 2 * LANES] + v[:MINE, 2 * LANES :])
            base = g * SPAN + t * LANES
            nm[:, base : base + LANES] = v[:, :LANES]
            last += v[:, LANES:]
        nm[:, g * SPAN + HIGH : (g + 1) * SPAN] = last
        cols = pl.ds(g * SPAN, SPAN)
        store(nm.at[:, cols], new_out.at[:, cols])

    def low_a(_):
        @pl.when(column_later > 0)
        def _():
            pl.semaphore_wait(column_sem, column_later)

        for k, (dy, dc) in enumerate(column):
            send("la", lw.at[ys[dy], other_core if dc else core], la.at[k], device(dy=dy, dcore=dc), LOW_A)

    def low_d(_):
        received(la, LOW_A)
        lw[y, core] += ((la[0] + la[1]) + (la[2] + la[3])) + ((la[4] + la[5]) + la[6])
        for d in (1, 2, 3):
            send("lc", lw.at[y, core, xs[d]], lc.at[d - 1], device(dx=d), LOW_C)

    def low_e(_):
        received(lc, LOW_C)
        es[...] = lw[y, core, x] + (lc[0] + lc[1] + lc[2])

        @pl.when(stack_later > 0)
        def _():
            pl.semaphore_wait(stack_sem, stack_later)

        @pl.when(core == z)
        def _():
            for d in (1, 2, 3):
                send("ld", es, le.at[d - 1], device(dzh=d), LOW_D)

        @pl.when(core != z)
        def _():
            for d in range(4):
                send("ld", es, le.at[3 + d], device(dzh=d, dz=1), LOW_D)

    def low_i(_):
        @pl.when(core == z)
        def _():
            received(le, LOW_D)
            total[y] = es[...] + ((le[0] + le[1] + le[2]) + (le[3] + le[4] + le[5] + le[6]))
            for dy, dc in column:
                send("lf", total.at[y], total.at[y], device(dy=dy, dcore=dc), LOW_F)

    def low_end():
        arrived(load_rest[1])

        @pl.when(core == z)
        def _():
            received(total.at[pl.ds(0, 3)], LOW_F)

        @pl.when(core != z)
        def _():
            received(total, LOW_F)

    def normalise(g):
        if not normalised:
            low_end()
        normalised.add(g)
        table = lambda i: back[(7 + i) * LANES : (8 + i) * LANES]
        lanes = slice(g * LANES, (g + 1) * LANES)
        mean = total[:, :, lanes].reshape(MINE, LANES) * (1.0 / N_REP)
        top, rest = halves(mean)
        pair = jnp.concatenate([top, rest], axis=0)
        squares = jnp.concatenate(halves(mean * mean), axis=0)
        for h in range(2):
            v, w = dot(pair, table(h)), dot(squares, table(4 + h))
            field = v[:MINE] + (v[MINE:] + dot(top, table(2 + h)))
            square = w[:MINE] + w[MINE:]
            base = g * SPAN + h * WIDE
            up[:, base : base + WIDE] = field * lax.rsqrt(field * field + square + EPS)
        cols = pl.ds(g * SPAN, SPAN)
        store(up.at[:, cols], upd_out.at[:, cols])

    steps = {
        "F": forward, "FL": forward_low,
        "XS": x_start, "XP": x_pass, "XC": x_cross, "XE": x_end,
        "ZS": z_start, "ZC": z_cross, "ZP": z_pass, "ZE": z_end,
        "LA": low_a, "LC": low_d, "LD": low_e, "LF": low_i,
        "N": normalise, "BK": backward,
    }
    steps[EARLY[0][0]](EARLY[0][1])
    enter()
    before = set(ready), set(waited)

    def run(plan):
        ready.clear()
        ready.update(before[0])
        waited.clear()
        waited.update(before[1])
        for state in (parts, normalised):
            state.clear()
        stores.clear()
        answered = False
        for name, u in plan[1:]:
            if not answered and name not in ("XS", "ZS"):
                greet_others((column_sem, stack_sem), False)
                answered = True
            steps[name](u)
        all_sent("x2", xr2)
        all_sent("xa", xr2)
        all_sent("xb", xr2)
        all_sent("xz", xrz)
        all_sent("z4", zr4)
        all_sent("z2", zr2)
        all_sent("za", zr2)
        all_sent("zb", zr2)
        all_sent("la", la)
        all_sent("lc", lc)

        @pl.when(core != z)
        def _():
            all_sent("ld", le.at[pl.ds(0, 4)])

        @pl.when(core == z)
        def _():
            all_sent("ld", le.at[pl.ds(0, 3)])
            all_sent("lf", le)

        for copy in stores:
            copy.wait()

    @pl.when(zh < 2)
    def _():
        run(EARLY)

    @pl.when(zh >= 2)
    def _():
        run(LATE)


def write_out(new_in, upd_in, new_out, upd_out, sems):
    copies = []
    for k, (src, dst) in enumerate([(new_in, new_out), (upd_in, upd_out)]):
        for m in range(MATS):
            rows = pl.ds(m * OWN, OWN)
            copies.append(pltpu.make_async_copy(src.at[rows], dst.at[rows], sems.at[k, m]))
    for copy in copies:
        copy.start()
    for copy in copies:
        copy.wait()


def per_device(gradients, momentum):
    wide, back = tables()
    anywhere = pl.BlockSpec(memory_space=pl.ANY)
    new_momentum, update = pl.pallas_call(
        kernel,
        out_shape=[jax.ShapeDtypeStruct((MINE, D), F32)] * 2,
        in_specs=[anywhere] * 4,
        out_specs=[anywhere] * 2,
        scratch_shapes=[
            pltpu.VMEM((GRAD + 2 * MINE, D), BF16),
            pltpu.VMEM((MINE, D), F32),
            pltpu.VMEM(wide.shape, BF16),
            pltpu.VMEM(back.shape, BF16),
            pltpu.VMEM((len(X_UNITS), NX, NZL, 2, OWN, HIGH), F32),
            pltpu.VMEM((len(Z_UNITS), NZL, NX, 2, OWN, HIGH), F32),
            pltpu.VMEM((MATS, NZL, NX, OWN, LOW), F32),
            pltpu.VMEM((len(X_UNITS), NZL, 2, OWN, HIGH), F32),
            pltpu.VMEM((len(X_UNITS), 2, NZL, 2, OWN, HIGH), F32),
            pltpu.VMEM((len(X_UNITS), 2, OWN, HIGH), F32),
            pltpu.VMEM((len(Z_UNITS), NX, 2, OWN, HIGH), F32),
            pltpu.VMEM((len(Z_UNITS), 2, OWN, HIGH), F32),
            pltpu.VMEM((len(Z_UNITS), 2, 2, OWN, HIGH), F32),
            pltpu.VMEM((7, NX, OWN, LOW), F32),
            pltpu.VMEM((3, OWN, LOW), F32),
            pltpu.VMEM((7, OWN, LOW), F32),
            pltpu.VMEM((OWN, LOW), F32),
            pltpu.VMEM((MATS, OWN, LOW), F32),
            pltpu.VMEM((MINE, D), F32),
            pltpu.VMEM((MINE, D), F32),
            pltpu.SemaphoreType.DMA((2 * GROUPS + 3,)),
            pltpu.SemaphoreType.DMA((2 * GROUPS,)),
            pltpu.SemaphoreType.DMA((len(SENDS),)),
            pltpu.SemaphoreType.DMA((3 * len(X_UNITS) + 3 * len(Z_UNITS) + 4,)),
            pltpu.SemaphoreType.REGULAR,
            pltpu.SemaphoreType.REGULAR,
        ],
        compiler_params=pltpu.CompilerParams(
            collective_id=0, has_side_effects=True, vmem_limit_bytes=(52 * 1024 + 384) * 1024
        ),
        cost_estimate=pl.CostEstimate(flops=2_000_000_000, bytes_accessed=8_000_000, transcendentals=200_000),
    )(gradients.reshape(GRAD, D), momentum.reshape(MINE, D), wide, back)
    new_momentum, update = pl.pallas_call(
        write_out,
        out_shape=[jax.ShapeDtypeStruct((MINE, D), F32)] * 2,
        in_specs=[anywhere] * 2,
        out_specs=[anywhere] * 2,
        scratch_shapes=[pltpu.SemaphoreType.DMA((2, 4))],
        compiler_params=pltpu.CompilerParams(vmem_limit_bytes=4 * 1024 * 1024),
        cost_estimate=pl.CostEstimate(flops=0, bytes_accessed=2_600_000, transcendentals=0),
    )(new_momentum, update)
    return new_momentum.reshape(1, MATS, OWN, D), update.reshape(MATS, OWN, D)


def solution(mesh):
    return jax.shard_map(
        per_device,
        mesh=mesh,
        in_specs=(P("rep", "fsdp", None, None, None), P("rep", None, "fsdp", None)),
        out_specs=(P("rep", None, "fsdp", None), P(None, "fsdp", None)),
        check_vma=False,
    )
```

```python
import jax
import jax.numpy as jnp
import ml_dtypes
import numpy as np
from jax import lax
from jax.experimental import pallas as pl
from jax.experimental.pallas import tpu as pltpu
from jax.sharding import PartitionSpec as P

D, MATS, GROUP, KEEP, ROWS = 5120, 4, 64, 8, 64
BETA, EPS = 0.999, 1e-06
NX, NY, NZL, NZH, NC, N_REP = 4, 4, 2, 4, 2, 32
OWN = 8
LANES = 128
TILES = 8
SPAN = LANES * TILES
GROUPS = D // SPAN
HIGH = 7 * LANES
LOW = GROUPS * LANES
GRAD = MATS * ROWS
MINE = MATS * OWN
WIDE = 4 * LANES

F32, BF16 = jnp.float32, jnp.bfloat16
MESH = pl.DeviceIdType.MESH


def split(table):
    high = table.astype(ml_dtypes.bfloat16)
    low = (table - high.astype(np.float64)).astype(ml_dtypes.bfloat16)
    return high, low


def tables():
    n, k = np.arange(GROUP), np.arange(GROUP)[:, None]
    basis = np.sqrt(2.0 / GROUP) * np.cos(np.pi * (n + 0.5) * k / GROUP)
    basis[0] *= np.sqrt(0.5)
    rest = GROUP - KEEP
    high = np.zeros((LANES, 2 * rest))
    for b in range(2):
        high[b * GROUP : (b + 1) * GROUP, b * rest : (b + 1) * rest] = basis[KEEP:].T
    forward = np.zeros((7, 2 * LANES, LANES))
    for t in range(7):
        forward[t, :LANES, : 2 * rest] = high
        forward[t, LANES:, 2 * rest :] = high[:, 16 * t : 16 * t + 16]
    inverse = np.zeros((7, LANES, 2 * LANES))
    for t in range(7):
        inverse[t] = forward[t].T
    blocks = SPAN // GROUP
    keep = np.zeros((SPAN, LANES))
    mean = np.zeros((LANES, SPAN))
    for c in range(blocks):
        keep[c * GROUP : (c + 1) * GROUP, c * KEEP : (c + 1) * KEEP] = basis[:KEEP].T
        mean[c * KEEP : (c + 1) * KEEP, c * GROUP : (c + 1) * GROUP] = 1.0 / GROUP
    both = lambda table: np.concatenate(split(table), axis=-1)
    wide = np.concatenate([both(forward).reshape(-1, 2 * LANES), both(keep)], axis=0)
    back = np.concatenate([both(keep.T), mean.astype(ml_dtypes.bfloat16)], axis=-1)
    back = back.reshape(LANES, 6, WIDE).transpose(1, 0, 2).reshape(-1, WIDE)
    return wide, np.concatenate([both(inverse).reshape(-1, WIDE), back], axis=0)


def halves(value):
    top = value.astype(BF16)
    return top, (value - top.astype(F32)).astype(BF16)


def dot(a, b):
    return jnp.dot(a, b, preferred_element_type=F32)


X_UNITS = [(2, 0), (2, 2), (3, 0), (3, 2), (4, 0), (4, 2)]
Z_UNITS = [(0, 0), (0, 2), (1, 0), (1, 2)]
SENDS = ["x2", "xa", "xb", "xz", "z4", "z2", "za", "zb", "la", "lc", "ld", "lf"]
EARLY = [
    ("F", 2), ("XS", 0), ("F", 0), ("ZS", 1), ("XS", 1), ("FL", 3),
    ("ZS", 0), ("FL", 2), ("F", 4), ("FL", 1), ("FL", 0), ("XS", 4),
    ("FL", 4), ("LA", 0), ("XS", 5), ("F", 3), ("XS", 2), ("F", 1),
    ("ZS", 3), ("ZC", 1), ("ZS", 2), ("XP", 4), ("XP", 5), ("LC", 0),
    ("XS", 3), ("XP", 0), ("XC", 4), ("XP", 2), ("XP", 1), ("LD", 0),
    ("ZC", 3), ("ZP", 1), ("ZC", 0), ("XC", 5), ("XP", 3), ("XC", 1),
    ("ZC", 2), ("XC", 0), ("XE", 5), ("XE", 4), ("BK", 4), ("XC", 2),
    ("ZP", 0), ("XE", 1), ("ZP", 3), ("XC", 3), ("XE", 0), ("BK", 2),
    ("ZE", 1), ("ZP", 2), ("LF", 0), ("ZE", 0), ("BK", 0), ("XE", 2),
    ("XE", 3), ("BK", 3), ("ZE", 3), ("ZE", 2), ("BK", 1), ("N", 2),
    ("N", 4), ("N", 3), ("N", 0), ("N", 1),
]
LATE = [
    ("FL", 1), ("FL", 4), ("FL", 0), ("FL", 2), ("FL", 3), ("LA", 0),
    ("F", 3), ("XS", 2), ("F", 0), ("ZS", 1), ("XS", 3), ("F", 2),
    ("XS", 0), ("F", 1), ("ZS", 3), ("F", 4), ("XS", 1), ("LC", 0),
    ("XP", 3), ("ZS", 0), ("ZC", 1), ("XS", 4), ("XP", 2), ("LD", 0),
    ("XP", 0), ("ZC", 3), ("ZS", 2), ("XP", 4), ("XS", 5), ("XC", 3),
    ("XP", 1), ("ZP", 1), ("ZC", 0), ("XC", 2), ("XC", 0), ("LF", 0),
    ("XP", 5), ("ZP", 3), ("XC", 1), ("ZC", 2), ("XC", 4), ("ZP", 0),
    ("XE", 3), ("N", 0), ("N", 4), ("N", 3), ("XE", 2), ("BK", 3),
    ("XC", 5), ("N", 1), ("N", 2), ("ZP", 2), ("ZE", 1), ("XE", 1),
    ("XE", 0), ("BK", 2), ("ZE", 0), ("BK", 0), ("XE", 4), ("ZE", 3),
    ("XE", 5), ("BK", 4), ("ZE", 2), ("BK", 1),
]


def kernel(
    grads, momentum, wide_hbm, back_hbm, new_out, upd_out,
    xin, mom, wide, back, sx, sz, lw,
    xr2, xab, xrz, zr4, zr2, zab,
    la, lc, le, es, total, nm, up,
    load_sem, store_sem, send_sem, recv_sem, column_sem, stack_sem,
):
    rep, fsdp = lax.axis_index("rep"), lax.axis_index("fsdp")
    core, y, zh = lax.rem(rep, 2), lax.rem(lax.div(rep, 2), 4), lax.div(rep, 8)
    x, z = lax.rem(fsdp, 4), lax.div(fsdp, 4)

    def ring(v, d):
        return lax.rem(v + (d + 4), 4)

    xs, ys, zs = ([v] + [ring(v, d) for d in (1, 2, 3)] for v in (x, y, zh))
    other_core, other_z = 1 - core, 1 - z
    own_rep, own_fsdp = rep, fsdp
    places = {}

    def device(dzh=0, dy=0, dcore=0, dz=0, dx=0):
        key = (dzh, dy % 4, dcore, dz, dx % 4)
        if key not in places:
            c2, z2 = other_core if dcore else core, other_z if dz else z
            moved = dzh or dy or dcore
            r2 = (zs[dzh] * 4 + ys[dy % 4]) * 2 + c2 if moved else own_rep
            places[key] = (r2, z2 * 4 + xs[dx % 4] if dz or dx else own_fsdp)
        return places[key]

    for dy in range(4):
        for dc in range(2):
            device(dy=dy, dcore=dc)
    for d in range(4):
        for dz in range(2):
            device(dzh=d, dz=dz)
        device(dx=d)

    column = [(dy, dc) for dy in range(4) for dc in range(2) if dy or dc]
    barrier = pltpu.get_barrier_semaphore()

    def greet(sem, p):
        pl.semaphore_signal(sem, inc=1, device_id=p, device_id_type=MESH)

    def later_in_column(dy, dc):
        if dy:
            return ring(y, dy) > y
        return core == 1

    def later_in_stack(d):
        return ring(zh, d) > zh

    def greet_others(sem_of, later):
        def where(test, sem, places):
            @pl.when(test if later else jnp.logical_not(test))
            def _():
                for place in places:
                    greet(sem, place)

        for d in range(4):
            cores = range(2) if d else (1,)
            where(later_in_column(d, 1), sem_of[0], [device(dy=d, dcore=dc) for dc in cores])
        for d in (1, 2, 3):
            where(later_in_stack(d), sem_of[1], [device(dzh=d, dz=dz) for dz in range(2)])

    for d in (1, 2, 3):
        greet(barrier, device(dx=d))
    greet(barrier, device(dz=1))
    column_later = 2 * (3 - y) + core
    stack_later = 2 * (3 - zh)

    def enter():
        pl.semaphore_wait(barrier, 4 + (7 - column_later) + (6 - stack_later))
    def remote(kind, src, dst, to, recv):
        return pltpu.make_async_remote_copy(
            src_ref=src, dst_ref=dst, send_sem=send_sem.at[SENDS.index(kind)],
            recv_sem=recv_sem.at[recv], device_id=to, device_id_type=MESH,
        )

    def send(kind, src, dst, to, recv):
        remote(kind, src, dst, to, recv).start()

    def await_bytes(ref, sem):
        pltpu.make_async_copy(ref, ref, sem).wait()

    def received(ref, recv):
        await_bytes(ref, recv_sem.at[recv])

    def all_sent(kind, ref):
        await_bytes(ref, send_sem.at[SENDS.index(kind)])

    loads = []

    def load(src, dst):
        copy = pltpu.make_async_copy(src, dst, load_sem.at[len(loads)])
        copy.start()
        loads.append(copy)
        return copy

    waited, ready, parts, normalised = set(), set(), {}, set()

    def arrived(copy):
        if id(copy) not in waited:
            waited.add(id(copy))
            copy.wait()

    def load_group(g):
        cols = pl.ds(g * SPAN, SPAN)
        return load(momentum.at[:, cols], mom.at[:, cols]), load(grads.at[:, cols], xin.at[pl.ds(0, GRAD), cols])

    order = [g for name, g in EARLY if name == "F"]
    front = pl.ds(0, 7 * 2 * LANES)
    rest = pl.ds(7 * 2 * LANES, SPAN)
    group_loads = {order[0]: load_group(order[0])}
    load_wide = load(wide_hbm.at[front], wide.at[front])
    load_rest = []
    greet_others((barrier, barrier), True)

    def load_others():
        for g in order[1:]:
            group_loads[g] = load_group(g)
        load_rest.append(load(wide_hbm.at[rest], wide.at[rest]))
        load_rest.append(load(back_hbm, back))

    def prepare(g):
        if g not in ready:
            ready.add(g)
            for copy in group_loads[g]:
                copy.wait()
            cols = slice(g * SPAN, (g + 1) * SPAN)
            top, low_part = halves(BETA * mom[:, cols])
            xin[GRAD : GRAD + MINE, cols] = top
            xin[GRAD + MINE :, cols] = low_part

    def fold(v):
        v = v[:, :LANES] + v[:, LANES:]
        own = v[GRAD : GRAD + MINE] + v[GRAD + MINE :]
        return v[:GRAD].reshape(MATS, NZL, NX, OWN, LANES), own.reshape(MATS, OWN, LANES)

    def forward(g):
        prepare(g)
        arrived(load_wide)
        base = g * SPAN
        last = xin[:, base + HIGH : base + SPAN]
        for t in range(7):
            both = jnp.concatenate([xin[:, base + t * LANES : base + (t + 1) * LANES], last], axis=1)
            value, own = fold(dot(both, wide[t * 2 * LANES : (t + 1) * 2 * LANES]))
            lanes = slice(t * LANES, (t + 1) * LANES)
            for h in range(2):
                mats = slice(2 * h, 2 * h + 2)
                if (g, 2 * h) in X_UNITS:
                    u = X_UNITS.index((g, 2 * h))
                    for m in range(2):
                        for k in range(NZL):
                            sx[u, :, k, m, :, lanes] = value[2 * h + m, k]
                    sx[u, x, z, :, :, lanes] += own[mats]
                else:
                    u = Z_UNITS.index((g, 2 * h))
                    for m in range(2):
                        for k in range(NZL):
                            sz[u, k, :, m, :, lanes] = value[2 * h + m, k]
                    sz[u, z, x, :, :, lanes] += own[mats]

    def forward_low(g):
        prepare(g)
        arrived(load_rest[0])
        value, own = fold(dot(xin[:, g * SPAN : (g + 1) * SPAN], wide[7 * 2 * LANES :]))
        lanes = slice(g * LANES, (g + 1) * LANES)
        lw[:, :, :, :, lanes] = value
        lw[:, z, x, :, lanes] += own

    way = lambda u: 1 if u % 2 == 0 else -1
    z_way = lambda u: -way(u)
    nx, nz = len(X_UNITS), len(Z_UNITS)
    X2, XAB, XZ = 0, nx, 2 * nx
    Z4, Z2, ZAB = 3 * nx, 3 * nx + nz, 3 * nx + 2 * nz
    LOW_A = 3 * nx + 3 * nz
    LOW_C, LOW_D, LOW_F = LOW_A + 1, LOW_A + 2, LOW_A + 3

    def x_start(u):
        d = way(u)
        send("x2", sx.at[u, xs[2]], xr2.at[u], device(dx=d), X2 + u)
        send("xa", sx.at[u, xs[-d]], xab.at[u, 0], device(dx=-d), XAB + u)

    def x_pass(u):
        d = way(u)
        received(xr2.at[u], X2 + u)
        sx[u, xs[d]] += xr2[u]
        send("xb", sx.at[u, xs[d]], xab.at[u, 1], device(dx=d), XAB + u)

    def x_cross(u):
        received(xab.at[u], XAB + u)
        sx[u, x] += xab[u, 0] + xab[u, 1]
        send("xz", sx.at[u, x, other_z], xrz.at[u], device(dz=1), XZ + u)

    def z_start(u):
        send("z4", sz.at[u, other_z], zr4.at[u], device(dz=1), Z4 + u)

    def z_cross(u):
        d = z_way(u)
        received(zr4.at[u], Z4 + u)
        sz[u, z] += zr4[u]
        send("z2", sz.at[u, z, xs[2]], zr2.at[u], device(dx=d), Z2 + u)
        send("za", sz.at[u, z, xs[-d]], zab.at[u, 0], device(dx=-d), ZAB + u)

    def z_pass(u):
        d = z_way(u)
        received(zr2.at[u], Z2 + u)
        sz[u, z, xs[d]] += zr2[u]
        send("zb", sz.at[u, z, xs[d]], zab.at[u, 1], device(dx=d), ZAB + u)

    def x_end(u):
        received(xrz.at[u], XZ + u)
        parts[X_UNITS[u]] = sx[u, x, z] + xrz[u]

    def z_end(u):
        received(zab.at[u], ZAB + u)
        parts[Z_UNITS[u]] = sz[u, z, x] + (zab[u, 0] + zab[u, 1])

    stores = []

    def store(src, dst):
        copy = pltpu.make_async_copy(src, dst, store_sem.at[len(stores)])
        copy.start()
        stores.append(copy)

    def backward(g):
        arrived(load_rest[1])
        field = jnp.concatenate([parts[k] for k in sorted(parts) if k[0] == g], axis=0).reshape(MINE, HIGH)
        last = jnp.zeros((MINE, LANES), F32)
        for t in range(7):
            top, rest = halves(field[:, t * LANES : (t + 1) * LANES])
            v = dot(jnp.concatenate([top, rest], axis=0), back[t * LANES : (t + 1) * LANES])
            v = v[:MINE, : 2 * LANES] + (v[MINE:, : 2 * LANES] + v[:MINE, 2 * LANES :])
            base = g * SPAN + t * LANES
            nm[:, base : base + LANES] = v[:, :LANES]
            last += v[:, LANES:]
        nm[:, g * SPAN + HIGH : (g + 1) * SPAN] = last
        cols = pl.ds(g * SPAN, SPAN)
        store(nm.at[:, cols], new_out.at[:, cols])

    def low_a(_):
        @pl.when(column_later > 0)
        def _():
            pl.semaphore_wait(column_sem, column_later)

        for k, (dy, dc) in enumerate(column):
            send("la", lw.at[ys[dy], other_core if dc else core], la.at[k], device(dy=dy, dcore=dc), LOW_A)

    def low_d(_):
        received(la, LOW_A)
        lw[y, core] += ((la[0] + la[1]) + (la[2] + la[3])) + ((la[4] + la[5]) + la[6])
        for d in (1, 2, 3):
            send("lc", lw.at[y, core, xs[d]], lc.at[d - 1], device(dx=d), LOW_C)

    def low_e(_):
        received(lc, LOW_C)
        es[...] = lw[y, core, x] + (lc[0] + lc[1] + lc[2])

        @pl.when(stack_later > 0)
        def _():
            pl.semaphore_wait(stack_sem, stack_later)

        @pl.when(core == z)
        def _():
            for d in (1, 2, 3):
                send("ld", es, le.at[d - 1], device(dzh=d), LOW_D)

        @pl.when(core != z)
        def _():
            for d in range(4):
                send("ld", es, le.at[3 + d], device(dzh=d, dz=1), LOW_D)

    def low_i(_):
        @pl.when(core == z)
        def _():
            received(le, LOW_D)
            total[y] = es[...] + ((le[0] + le[1] + le[2]) + (le[3] + le[4] + le[5] + le[6]))
            for dy, dc in column:
                send("lf", total.at[y], total.at[y], device(dy=dy, dcore=dc), LOW_F)

    def low_end():
        arrived(load_rest[1])

        @pl.when(core == z)
        def _():
            received(total.at[pl.ds(0, 3)], LOW_F)

        @pl.when(core != z)
        def _():
            received(total, LOW_F)

    def normalise(g):
        if not normalised:
            low_end()
        normalised.add(g)
        table = lambda i: back[(7 + i) * LANES : (8 + i) * LANES]
        lanes = slice(g * LANES, (g + 1) * LANES)
        mean = total[:, :, lanes].reshape(MINE, LANES) * (1.0 / N_REP)
        top, rest = halves(mean)
        pair = jnp.concatenate([top, rest], axis=0)
        squares = jnp.concatenate(halves(mean * mean), axis=0)
        for h in range(2):
            v, w = dot(pair, table(h)), dot(squares, table(4 + h))
            field = v[:MINE] + (v[MINE:] + dot(top, table(2 + h)))
            square = w[:MINE] + w[MINE:]
            base = g * SPAN + h * WIDE
            up[:, base : base + WIDE] = field * lax.rsqrt(field * field + square + EPS)
        cols = pl.ds(g * SPAN, SPAN)
        store(up.at[:, cols], upd_out.at[:, cols])

    steps = {
        "F": forward, "FL": forward_low,
        "XS": x_start, "XP": x_pass, "XC": x_cross, "XE": x_end,
        "ZS": z_start, "ZC": z_cross, "ZP": z_pass, "ZE": z_end,
        "LA": low_a, "LC": low_d, "LD": low_e, "LF": low_i,
        "N": normalise, "BK": backward,
    }
    load_others()

    def run(plan):
        for state in (ready, waited, parts, normalised, stores):
            state.clear()
        entered = answered = False
        for name, u in plan:
            if not entered and name not in ("F", "FL"):
                enter()
                entered = True
            if entered and not answered and name not in ("XS", "ZS"):
                greet_others((column_sem, stack_sem), False)
                answered = True
            steps[name](u)
        all_sent("x2", xr2)
        all_sent("xa", xr2)
        all_sent("xb", xr2)
        all_sent("xz", xrz)
        all_sent("z4", zr4)
        all_sent("z2", zr2)
        all_sent("za", zr2)
        all_sent("zb", zr2)
        all_sent("la", la)
        all_sent("lc", lc)

        @pl.when(core != z)
        def _():
            all_sent("ld", le.at[pl.ds(0, 4)])

        @pl.when(core == z)
        def _():
            all_sent("ld", le.at[pl.ds(0, 3)])
            all_sent("lf", le)

        for copy in stores:
            copy.wait()

    @pl.when(zh == 0)
    def _():
        run(EARLY)

    @pl.when(zh > 0)
    def _():
        run(LATE)


def write_out(new_in, upd_in, new_out, upd_out, sems):
    copies = []
    for k, (src, dst) in enumerate([(new_in, new_out), (upd_in, upd_out)]):
        for m in range(MATS):
            rows = pl.ds(m * OWN, OWN)
            copies.append(pltpu.make_async_copy(src.at[rows], dst.at[rows], sems.at[k, m]))
    for copy in copies:
        copy.start()
    for copy in copies:
        copy.wait()


def per_device(gradients, momentum):
    wide, back = tables()
    anywhere = pl.BlockSpec(memory_space=pl.ANY)
    new_momentum, update = pl.pallas_call(
        kernel,
        out_shape=[jax.ShapeDtypeStruct((MINE, D), F32)] * 2,
        in_specs=[anywhere] * 4,
        out_specs=[anywhere] * 2,
        scratch_shapes=[
            pltpu.VMEM((GRAD + 2 * MINE, D), BF16),
            pltpu.VMEM((MINE, D), F32),
            pltpu.VMEM(wide.shape, BF16),
            pltpu.VMEM(back.shape, BF16),
            pltpu.VMEM((len(X_UNITS), NX, NZL, 2, OWN, HIGH), F32),
            pltpu.VMEM((len(Z_UNITS), NZL, NX, 2, OWN, HIGH), F32),
            pltpu.VMEM((MATS, NZL, NX, OWN, LOW), F32),
            pltpu.VMEM((len(X_UNITS), NZL, 2, OWN, HIGH), F32),
            pltpu.VMEM((len(X_UNITS), 2, NZL, 2, OWN, HIGH), F32),
            pltpu.VMEM((len(X_UNITS), 2, OWN, HIGH), F32),
            pltpu.VMEM((len(Z_UNITS), NX, 2, OWN, HIGH), F32),
            pltpu.VMEM((len(Z_UNITS), 2, OWN, HIGH), F32),
            pltpu.VMEM((len(Z_UNITS), 2, 2, OWN, HIGH), F32),
            pltpu.VMEM((7, NX, OWN, LOW), F32),
            pltpu.VMEM((3, OWN, LOW), F32),
            pltpu.VMEM((7, OWN, LOW), F32),
            pltpu.VMEM((OWN, LOW), F32),
            pltpu.VMEM((MATS, OWN, LOW), F32),
            pltpu.VMEM((MINE, D), F32),
            pltpu.VMEM((MINE, D), F32),
            pltpu.SemaphoreType.DMA((2 * GROUPS + 3,)),
            pltpu.SemaphoreType.DMA((2 * GROUPS,)),
            pltpu.SemaphoreType.DMA((len(SENDS),)),
            pltpu.SemaphoreType.DMA((3 * len(X_UNITS) + 3 * len(Z_UNITS) + 4,)),
            pltpu.SemaphoreType.REGULAR,
            pltpu.SemaphoreType.REGULAR,
        ],
        compiler_params=pltpu.CompilerParams(
            collective_id=0, has_side_effects=True, vmem_limit_bytes=(52 * 1024 + 384) * 1024
        ),
        cost_estimate=pl.CostEstimate(flops=2_000_000_000, bytes_accessed=8_000_000, transcendentals=200_000),
    )(gradients.reshape(GRAD, D), momentum.reshape(MINE, D), wide, back)
    new_momentum, update = pl.pallas_call(
        write_out,
        out_shape=[jax.ShapeDtypeStruct((MINE, D), F32)] * 2,
        in_specs=[anywhere] * 2,
        out_specs=[anywhere] * 2,
        scratch_shapes=[pltpu.SemaphoreType.DMA((2, 4))],
        compiler_params=pltpu.CompilerParams(vmem_limit_bytes=4 * 1024 * 1024),
        cost_estimate=pl.CostEstimate(flops=0, bytes_accessed=2_600_000, transcendentals=0),
    )(new_momentum, update)
    return new_momentum.reshape(1, MATS, OWN, D), update.reshape(MATS, OWN, D)


def solution(mesh):
    return jax.shard_map(
        per_device,
        mesh=mesh,
        in_specs=(P("rep", "fsdp", None, None, None), P("rep", None, "fsdp", None)),
        out_specs=(P("rep", None, "fsdp", None), P(None, "fsdp", None)),
        check_vma=False,
    )
```

```python
import jax
import jax.numpy as jnp
import ml_dtypes
import numpy as np
from jax import lax
from jax.experimental import pallas as pl
from jax.experimental.pallas import tpu as pltpu
from jax.sharding import PartitionSpec as P

D, MATS, GROUP, KEEP, ROWS = 5120, 4, 64, 8, 64
BETA, EPS = 0.999, 1e-06
NX, NY, NZL, NZH, NC, N_REP = 4, 4, 2, 4, 2, 32
OWN = 8
LANES = 128
TILES = 8
SPAN = LANES * TILES
GROUPS = D // SPAN
HIGH = 7 * LANES
LOW = GROUPS * LANES
GRAD = MATS * ROWS
MINE = MATS * OWN
WIDE = 4 * LANES

F32, BF16 = jnp.float32, jnp.bfloat16
MESH = pl.DeviceIdType.MESH


def split(table):
    high = table.astype(ml_dtypes.bfloat16)
    low = (table - high.astype(np.float64)).astype(ml_dtypes.bfloat16)
    return high, low


def tables():
    n, k = np.arange(GROUP), np.arange(GROUP)[:, None]
    basis = np.sqrt(2.0 / GROUP) * np.cos(np.pi * (n + 0.5) * k / GROUP)
    basis[0] *= np.sqrt(0.5)
    rest = GROUP - KEEP
    high = np.zeros((LANES, 2 * rest))
    for b in range(2):
        high[b * GROUP : (b + 1) * GROUP, b * rest : (b + 1) * rest] = basis[KEEP:].T
    forward = np.zeros((7, 2 * LANES, LANES))
    for t in range(7):
        forward[t, :LANES, : 2 * rest] = high
        forward[t, LANES:, 2 * rest :] = high[:, 16 * t : 16 * t + 16]
    inverse = np.zeros((7, LANES, 2 * LANES))
    for t in range(7):
        inverse[t] = forward[t].T
    blocks = SPAN // GROUP
    keep = np.zeros((SPAN, LANES))
    mean = np.zeros((LANES, SPAN))
    for c in range(blocks):
        keep[c * GROUP : (c + 1) * GROUP, c * KEEP : (c + 1) * KEEP] = basis[:KEEP].T
        mean[c * KEEP : (c + 1) * KEEP, c * GROUP : (c + 1) * GROUP] = 1.0 / GROUP
    both = lambda table: np.concatenate(split(table), axis=-1)
    wide = np.concatenate([both(forward).reshape(-1, 2 * LANES), both(keep)], axis=0)
    back = np.concatenate([both(keep.T), mean.astype(ml_dtypes.bfloat16)], axis=-1)
    back = back.reshape(LANES, 6, WIDE).transpose(1, 0, 2).reshape(-1, WIDE)
    return wide, np.concatenate([both(inverse).reshape(-1, WIDE), back], axis=0)


def halves(value):
    top = value.astype(BF16)
    return top, (value - top.astype(F32)).astype(BF16)


def dot(a, b):
    return jnp.dot(a, b, preferred_element_type=F32)


X_UNITS = [(2, 0), (2, 2), (3, 0), (3, 2), (4, 0), (4, 2)]
Z_UNITS = [(0, 0), (0, 2), (1, 0), (1, 2)]
SENDS = ["x2", "xa", "xb", "xz", "z4", "z2", "za", "zb", "la", "lc", "ld", "lf"]
EARLY = [
    ("F", 2), ("XS", 0), ("F", 1), ("ZS", 3), ("F", 3), ("XS", 1),
    ("XS", 2), ("ZS", 2), ("FL", 4), ("FL", 0), ("FL", 3), ("FL", 2),
    ("FL", 1), ("LA", 0), ("XS", 3), ("F", 0), ("F", 4), ("XP", 1),
    ("XP", 0), ("ZS", 0), ("ZC", 3), ("XS", 4), ("ZS", 1), ("LC", 0),
    ("XS", 5), ("XP", 2), ("XP", 4), ("XP", 3), ("LD", 0), ("ZC", 2),
    ("XP", 5), ("XC", 0), ("ZP", 3), ("XC", 1), ("ZC", 1), ("XC", 2),
    ("XC", 3), ("ZC", 0), ("ZP", 2), ("XC", 5), ("XE", 0), ("XE", 1),
    ("XE", 2), ("XC", 4), ("LF", 0), ("ZP", 0), ("ZE", 3), ("XE", 3),
    ("BK", 2), ("ZP", 1), ("BK", 3), ("XE", 5), ("ZE", 2), ("BK", 1),
    ("XE", 4), ("BK", 4), ("ZE", 0), ("N", 2), ("N", 4), ("N", 3),
    ("N", 0), ("ZE", 1), ("BK", 0), ("N", 1),
]
LATE = [
    ("F", 2), ("XS", 0), ("F", 1), ("ZS", 2), ("XS", 1), ("FL", 4),
    ("FL", 1), ("FL", 2), ("FL", 3), ("FL", 0), ("LA", 0), ("XP", 0),
    ("F", 4), ("XS", 5), ("ZS", 3), ("F", 0), ("F", 3), ("XP", 1),
    ("XC", 0), ("XS", 4), ("XS", 2), ("ZS", 0), ("LC", 0), ("XS", 3),
    ("XP", 2), ("XC", 1), ("ZC", 3), ("LD", 0), ("ZC", 0), ("ZS", 1),
    ("XP", 4), ("ZC", 2), ("XP", 3), ("XP", 5), ("XE", 1), ("XE", 0),
    ("XC", 2), ("ZP", 2), ("BK", 2), ("LF", 0), ("ZP", 0), ("XC", 3),
    ("ZC", 1), ("ZP", 3), ("XC", 4), ("XC", 5), ("N", 1), ("N", 4),
    ("N", 0), ("XE", 3), ("XE", 2), ("ZP", 1), ("ZE", 2), ("N", 2),
    ("N", 3), ("XE", 4), ("BK", 3), ("ZE", 3), ("BK", 1), ("XE", 5),
    ("ZE", 0), ("BK", 4), ("ZE", 1), ("BK", 0),
]


def kernel(
    grads, momentum, wide_hbm, back_hbm, new_out, upd_out,
    xin, mom, wide, back, sx, sz, lw,
    xr2, xab, xrz, zr4, zr2, zab,
    la, lc, le, es, total, nm, up,
    load_sem, store_sem, send_sem, recv_sem, column_sem, stack_sem,
):
    rep, fsdp = lax.axis_index("rep"), lax.axis_index("fsdp")
    core, y, zh = lax.rem(rep, 2), lax.rem(lax.div(rep, 2), 4), lax.div(rep, 8)
    x, z = lax.rem(fsdp, 4), lax.div(fsdp, 4)

    def ring(v, d):
        return lax.rem(v + (d + 4), 4)

    xs, ys, zs = ([v] + [ring(v, d) for d in (1, 2, 3)] for v in (x, y, zh))
    other_core, other_z = 1 - core, 1 - z
    own_rep, own_fsdp = rep, fsdp
    places = {}

    def device(dzh=0, dy=0, dcore=0, dz=0, dx=0):
        key = (dzh, dy % 4, dcore, dz, dx % 4)
        if key not in places:
            c2, z2 = other_core if dcore else core, other_z if dz else z
            moved = dzh or dy or dcore
            r2 = (zs[dzh] * 4 + ys[dy % 4]) * 2 + c2 if moved else own_rep
            places[key] = (r2, z2 * 4 + xs[dx % 4] if dz or dx else own_fsdp)
        return places[key]

    for dy in range(4):
        for dc in range(2):
            device(dy=dy, dcore=dc)
    for d in range(4):
        for dz in range(2):
            device(dzh=d, dz=dz)
        device(dx=d)

    column = [(dy, dc) for dy in range(4) for dc in range(2) if dy or dc]
    barrier = pltpu.get_barrier_semaphore()

    def greet(sem, p):
        pl.semaphore_signal(sem, inc=1, device_id=p, device_id_type=MESH)

    def later_in_column(dy, dc):
        if dy:
            return ring(y, dy) > y
        return core == 1

    def later_in_stack(d):
        return ring(zh, d) > zh

    def greet_others(sem_of, later):
        def where(test, sem, places):
            @pl.when(test if later else jnp.logical_not(test))
            def _():
                for place in places:
                    greet(sem, place)

        for d in range(4):
            cores = range(2) if d else (1,)
            where(later_in_column(d, 1), sem_of[0], [device(dy=d, dcore=dc) for dc in cores])
        for d in (1, 2, 3):
            where(later_in_stack(d), sem_of[1], [device(dzh=d, dz=dz) for dz in range(2)])

    for d in (1, 2, 3):
        greet(barrier, device(dx=d))
    greet(barrier, device(dz=1))
    column_later = 2 * (3 - y) + core
    stack_later = 2 * (3 - zh)

    def enter():
        pl.semaphore_wait(barrier, 4 + (7 - column_later) + (6 - stack_later))
    def remote(kind, src, dst, to, recv):
        return pltpu.make_async_remote_copy(
            src_ref=src, dst_ref=dst, send_sem=send_sem.at[SENDS.index(kind)],
            recv_sem=recv_sem.at[recv], device_id=to, device_id_type=MESH,
        )

    def send(kind, src, dst, to, recv):
        remote(kind, src, dst, to, recv).start()

    def await_bytes(ref, sem):
        pltpu.make_async_copy(ref, ref, sem).wait()

    def received(ref, recv):
        await_bytes(ref, recv_sem.at[recv])

    def all_sent(kind, ref):
        await_bytes(ref, send_sem.at[SENDS.index(kind)])

    loads = []

    def load(src, dst):
        copy = pltpu.make_async_copy(src, dst, load_sem.at[len(loads)])
        copy.start()
        loads.append(copy)
        return copy

    waited, ready, parts, normalised = set(), set(), {}, set()

    def arrived(copy):
        if id(copy) not in waited:
            waited.add(id(copy))
            copy.wait()

    def load_group(g):
        cols = pl.ds(g * SPAN, SPAN)
        return load(momentum.at[:, cols], mom.at[:, cols]), load(grads.at[:, cols], xin.at[pl.ds(0, GRAD), cols])

    order = [g for name, g in EARLY if name == "F"]
    front = pl.ds(0, 7 * 2 * LANES)
    rest = pl.ds(7 * 2 * LANES, SPAN)
    group_loads = {order[0]: load_group(order[0])}
    load_wide = load(wide_hbm.at[front], wide.at[front])
    load_rest = []
    greet_others((barrier, barrier), True)

    def load_others():
        for g in order[1:]:
            group_loads[g] = load_group(g)
        load_rest.append(load(wide_hbm.at[rest], wide.at[rest]))
        load_rest.append(load(back_hbm, back))

    def prepare(g):
        if g not in ready:
            ready.add(g)
            for copy in group_loads[g]:
                copy.wait()
            cols = slice(g * SPAN, (g + 1) * SPAN)
            top, low_part = halves(BETA * mom[:, cols])
            xin[GRAD : GRAD + MINE, cols] = top
            xin[GRAD + MINE :, cols] = low_part

    def fold(v, count=2):
        v = v[:, :LANES] + v[:, LANES:]
        rows, mine = count * GRAD // 2, count * MINE // 2
        own = v[rows : rows + mine] + v[rows + mine :]
        return v[:rows].reshape(2 * count, NZL, NX, OWN, LANES), own.reshape(2 * count, OWN, LANES)

    def forward_rows(g, parts_of):
        base = g * SPAN

        def rows(start):
            cols = slice(base + start, base + start + LANES)
            if len(parts_of) == 2:
                return xin[:, cols]
            h, n, k = parts_of[0], GRAD // 2, MINE // 2
            spans = [(h * n, n), (GRAD + h * k, k), (GRAD + MINE + h * k, k)]
            return jnp.concatenate([xin[at : at + size, cols] for at, size in spans], axis=0)

        last = rows(HIGH)
        for t in range(7):
            both = jnp.concatenate([rows(t * LANES), last], axis=1)
            value, own = fold(dot(both, wide[t * 2 * LANES : (t + 1) * 2 * LANES]), len(parts_of))
            lanes = slice(t * LANES, (t + 1) * LANES)
            for i, h in enumerate(parts_of):
                mats = slice(2 * i, 2 * i + 2)
                if (g, 2 * h) in X_UNITS:
                    u = X_UNITS.index((g, 2 * h))
                    for m in range(2):
                        for k in range(NZL):
                            sx[u, :, k, m, :, lanes] = value[2 * i + m, k]
                    sx[u, x, z, :, :, lanes] += own[mats]
                else:
                    u = Z_UNITS.index((g, 2 * h))
                    for m in range(2):
                        for k in range(NZL):
                            sz[u, k, :, m, :, lanes] = value[2 * i + m, k]
                    sz[u, z, x, :, :, lanes] += own[mats]

    def forward(g):
        prepare(g)
        forward_rows(g, (0, 1))

    def forward_low(g):
        prepare(g)
        arrived(load_rest[0])
        value, own = fold(dot(xin[:, g * SPAN : (g + 1) * SPAN], wide[7 * 2 * LANES :]))
        lanes = slice(g * LANES, (g + 1) * LANES)
        lw[:, :, :, :, lanes] = value
        lw[:, z, x, :, lanes] += own

    way = lambda u: 1 if u % 2 == 0 else -1
    z_way = lambda u: -way(u)
    nx, nz = len(X_UNITS), len(Z_UNITS)
    X2, XAB, XZ = 0, nx, 2 * nx
    Z4, Z2, ZAB = 3 * nx, 3 * nx + nz, 3 * nx + 2 * nz
    LOW_A = 3 * nx + 3 * nz
    LOW_C, LOW_D, LOW_F = LOW_A + 1, LOW_A + 2, LOW_A + 3

    def x_start(u):
        d = way(u)
        send("x2", sx.at[u, xs[2]], xr2.at[u], device(dx=d), X2 + u)
        send("xa", sx.at[u, xs[-d]], xab.at[u, 0], device(dx=-d), XAB + u)

    def x_pass(u):
        d = way(u)
        received(xr2.at[u], X2 + u)
        sx[u, xs[d]] += xr2[u]
        send("xb", sx.at[u, xs[d]], xab.at[u, 1], device(dx=d), XAB + u)

    def x_cross(u):
        received(xab.at[u], XAB + u)
        sx[u, x] += xab[u, 0] + xab[u, 1]
        send("xz", sx.at[u, x, other_z], xrz.at[u], device(dz=1), XZ + u)

    def z_start(u):
        send("z4", sz.at[u, other_z], zr4.at[u], device(dz=1), Z4 + u)

    def z_cross(u):
        d = z_way(u)
        received(zr4.at[u], Z4 + u)
        sz[u, z] += zr4[u]
        send("z2", sz.at[u, z, xs[2]], zr2.at[u], device(dx=d), Z2 + u)
        send("za", sz.at[u, z, xs[-d]], zab.at[u, 0], device(dx=-d), ZAB + u)

    def z_pass(u):
        d = z_way(u)
        received(zr2.at[u], Z2 + u)
        sz[u, z, xs[d]] += zr2[u]
        send("zb", sz.at[u, z, xs[d]], zab.at[u, 1], device(dx=d), ZAB + u)

    def x_end(u):
        received(xrz.at[u], XZ + u)
        parts[X_UNITS[u]] = sx[u, x, z] + xrz[u]

    def z_end(u):
        received(zab.at[u], ZAB + u)
        parts[Z_UNITS[u]] = sz[u, z, x] + (zab[u, 0] + zab[u, 1])

    stores = []

    def store(src, dst):
        copy = pltpu.make_async_copy(src, dst, store_sem.at[len(stores)])
        copy.start()
        stores.append(copy)

    def backward(g):
        arrived(load_rest[1])
        field = jnp.concatenate([parts[k] for k in sorted(parts) if k[0] == g], axis=0).reshape(MINE, HIGH)
        last = jnp.zeros((MINE, LANES), F32)
        for t in range(7):
            top, rest = halves(field[:, t * LANES : (t + 1) * LANES])
            v = dot(jnp.concatenate([top, rest], axis=0), back[t * LANES : (t + 1) * LANES])
            v = v[:MINE, : 2 * LANES] + (v[MINE:, : 2 * LANES] + v[:MINE, 2 * LANES :])
            base = g * SPAN + t * LANES
            nm[:, base : base + LANES] = v[:, :LANES]
            last += v[:, LANES:]
        nm[:, g * SPAN + HIGH : (g + 1) * SPAN] = last
        cols = pl.ds(g * SPAN, SPAN)
        store(nm.at[:, cols], new_out.at[:, cols])

    def low_a(_):
        @pl.when(column_later > 0)
        def _():
            pl.semaphore_wait(column_sem, column_later)

        for k, (dy, dc) in enumerate(column):
            send("la", lw.at[ys[dy], other_core if dc else core], la.at[k], device(dy=dy, dcore=dc), LOW_A)

    def low_d(_):
        received(la, LOW_A)
        lw[y, core] += ((la[0] + la[1]) + (la[2] + la[3])) + ((la[4] + la[5]) + la[6])
        for d in (1, 2, 3):
            send("lc", lw.at[y, core, xs[d]], lc.at[d - 1], device(dx=d), LOW_C)

    def low_e(_):
        received(lc, LOW_C)
        es[...] = lw[y, core, x] + (lc[0] + lc[1] + lc[2])

        @pl.when(stack_later > 0)
        def _():
            pl.semaphore_wait(stack_sem, stack_later)

        @pl.when(core == z)
        def _():
            for d in (1, 2, 3):
                send("ld", es, le.at[d - 1], device(dzh=d), LOW_D)

        @pl.when(core != z)
        def _():
            for d in range(4):
                send("ld", es, le.at[3 + d], device(dzh=d, dz=1), LOW_D)

    def low_i(_):
        @pl.when(core == z)
        def _():
            received(le, LOW_D)
            total[y] = es[...] + ((le[0] + le[1] + le[2]) + (le[3] + le[4] + le[5] + le[6]))
            for dy, dc in column:
                send("lf", total.at[y], total.at[y], device(dy=dy, dcore=dc), LOW_F)

    def low_end():
        arrived(load_rest[1])

        @pl.when(core == z)
        def _():
            received(total.at[pl.ds(0, 3)], LOW_F)

        @pl.when(core != z)
        def _():
            received(total, LOW_F)

    def normalise(g):
        if not normalised:
            low_end()
        normalised.add(g)
        table = lambda i: back[(7 + i) * LANES : (8 + i) * LANES]
        lanes = slice(g * LANES, (g + 1) * LANES)
        mean = total[:, :, lanes].reshape(MINE, LANES) * (1.0 / N_REP)
        top, rest = halves(mean)
        pair = jnp.concatenate([top, rest], axis=0)
        squares = jnp.concatenate(halves(mean * mean), axis=0)
        for h in range(2):
            v, w = dot(pair, table(h)), dot(squares, table(4 + h))
            field = v[:MINE] + (v[MINE:] + dot(top, table(2 + h)))
            square = w[:MINE] + w[MINE:]
            base = g * SPAN + h * WIDE
            up[:, base : base + WIDE] = field * lax.rsqrt(field * field + square + EPS)
        cols = pl.ds(g * SPAN, SPAN)
        store(up.at[:, cols], upd_out.at[:, cols])

    steps = {
        "F": forward, "FL": forward_low,
        "XS": x_start, "XP": x_pass, "XC": x_cross, "XE": x_end,
        "ZS": z_start, "ZC": z_cross, "ZP": z_pass, "ZE": z_end,
        "LA": low_a, "LC": low_d, "LD": low_e, "LF": low_i,
        "N": normalise, "BK": backward,
    }
    first = EARLY[0][1]
    prepare(first)
    arrived(load_wide)
    load_others()
    forward_rows(first, (0,))
    enter()
    before = set(ready), set(waited)

    def run(plan):
        ready.clear()
        ready.update(before[0])
        waited.clear()
        waited.update(before[1])
        for state in (parts, normalised):
            state.clear()
        stores.clear()
        answered = False
        for name, u in plan[1:]:
            if not answered and name not in ("XS", "ZS"):
                greet_others((column_sem, stack_sem), False)
                answered = True
            steps[name](u)
            if (name, u) == plan[1]:
                forward_rows(first, (1,))
        all_sent("x2", xr2)
        all_sent("xa", xr2)
        all_sent("xb", xr2)
        all_sent("xz", xrz)
        all_sent("z4", zr4)
        all_sent("z2", zr2)
        all_sent("za", zr2)
        all_sent("zb", zr2)
        all_sent("la", la)
        all_sent("lc", lc)

        @pl.when(core != z)
        def _():
            all_sent("ld", le.at[pl.ds(0, 4)])

        @pl.when(core == z)
        def _():
            all_sent("ld", le.at[pl.ds(0, 3)])
            all_sent("lf", le)

        for copy in stores:
            copy.wait()

    @pl.when(zh < 2)
    def _():
        run(EARLY)

    @pl.when(zh >= 2)
    def _():
        run(LATE)


def write_out(new_in, upd_in, new_out, upd_out, sems):
    copies = []
    for k, (src, dst) in enumerate([(new_in, new_out), (upd_in, upd_out)]):
        for m in range(MATS):
            rows = pl.ds(m * OWN, OWN)
            copies.append(pltpu.make_async_copy(src.at[rows], dst.at[rows], sems.at[k, m]))
    for copy in copies:
        copy.start()
    for copy in copies:
        copy.wait()


def per_device(gradients, momentum):
    wide, back = tables()
    anywhere = pl.BlockSpec(memory_space=pl.ANY)
    new_momentum, update = pl.pallas_call(
        kernel,
        out_shape=[jax.ShapeDtypeStruct((MINE, D), F32)] * 2,
        in_specs=[anywhere] * 4,
        out_specs=[anywhere] * 2,
        scratch_shapes=[
            pltpu.VMEM((GRAD + 2 * MINE, D), BF16),
            pltpu.VMEM((MINE, D), F32),
            pltpu.VMEM(wide.shape, BF16),
            pltpu.VMEM(back.shape, BF16),
            pltpu.VMEM((len(X_UNITS), NX, NZL, 2, OWN, HIGH), F32),
            pltpu.VMEM((len(Z_UNITS), NZL, NX, 2, OWN, HIGH), F32),
            pltpu.VMEM((MATS, NZL, NX, OWN, LOW), F32),
            pltpu.VMEM((len(X_UNITS), NZL, 2, OWN, HIGH), F32),
            pltpu.VMEM((len(X_UNITS), 2, NZL, 2, OWN, HIGH), F32),
            pltpu.VMEM((len(X_UNITS), 2, OWN, HIGH), F32),
            pltpu.VMEM((len(Z_UNITS), NX, 2, OWN, HIGH), F32),
            pltpu.VMEM((len(Z_UNITS), 2, OWN, HIGH), F32),
            pltpu.VMEM((len(Z_UNITS), 2, 2, OWN, HIGH), F32),
            pltpu.VMEM((7, NX, OWN, LOW), F32),
            pltpu.VMEM((3, OWN, LOW), F32),
            pltpu.VMEM((7, OWN, LOW), F32),
            pltpu.VMEM((OWN, LOW), F32),
            pltpu.VMEM((MATS, OWN, LOW), F32),
            pltpu.VMEM((MINE, D), F32),
            pltpu.VMEM((MINE, D), F32),
            pltpu.SemaphoreType.DMA((2 * GROUPS + 3,)),
            pltpu.SemaphoreType.DMA((2 * GROUPS,)),
            pltpu.SemaphoreType.DMA((len(SENDS),)),
            pltpu.SemaphoreType.DMA((3 * len(X_UNITS) + 3 * len(Z_UNITS) + 4,)),
            pltpu.SemaphoreType.REGULAR,
            pltpu.SemaphoreType.REGULAR,
        ],
        compiler_params=pltpu.CompilerParams(
            collective_id=0, has_side_effects=True, vmem_limit_bytes=(52 * 1024 + 384) * 1024
        ),
        cost_estimate=pl.CostEstimate(flops=2_000_000_000, bytes_accessed=8_000_000, transcendentals=200_000),
    )(gradients.reshape(GRAD, D), momentum.reshape(MINE, D), wide, back)
    new_momentum, update = pl.pallas_call(
        write_out,
        out_shape=[jax.ShapeDtypeStruct((MINE, D), F32)] * 2,
        in_specs=[anywhere] * 2,
        out_specs=[anywhere] * 2,
        scratch_shapes=[pltpu.SemaphoreType.DMA((2, 4))],
        compiler_params=pltpu.CompilerParams(vmem_limit_bytes=4 * 1024 * 1024),
        cost_estimate=pl.CostEstimate(flops=0, bytes_accessed=2_600_000, transcendentals=0),
    )(new_momentum, update)
    return new_momentum.reshape(1, MATS, OWN, D), update.reshape(MATS, OWN, D)


def solution(mesh):
    return jax.shard_map(
        per_device,
        mesh=mesh,
        in_specs=(P("rep", "fsdp", None, None, None), P("rep", None, "fsdp", None)),
        out_specs=(P("rep", None, "fsdp", None), P(None, "fsdp", None)),
        check_vma=False,
    )
```

```python
import jax
import jax.numpy as jnp
import ml_dtypes
import numpy as np
from jax import lax
from jax.experimental import pallas as pl
from jax.experimental.pallas import tpu as pltpu
from jax.sharding import PartitionSpec as P

D, MATS, GROUP, KEEP, ROWS = 5120, 4, 64, 8, 64
BETA, EPS = 0.999, 1e-06
NX, NY, NZL, NZH, NC, N_REP = 4, 4, 2, 4, 2, 32
OWN = 8
LANES = 128
TILES = 8
SPAN = LANES * TILES
GROUPS = D // SPAN
HIGH = 7 * LANES
LOW = GROUPS * LANES
GRAD = MATS * ROWS
MINE = MATS * OWN
WIDE = 4 * LANES

F32, BF16 = jnp.float32, jnp.bfloat16
MESH = pl.DeviceIdType.MESH


def split(table):
    high = table.astype(ml_dtypes.bfloat16)
    low = (table - high.astype(np.float64)).astype(ml_dtypes.bfloat16)
    return high, low


def tables():
    n, k = np.arange(GROUP), np.arange(GROUP)[:, None]
    basis = np.sqrt(2.0 / GROUP) * np.cos(np.pi * (n + 0.5) * k / GROUP)
    basis[0] *= np.sqrt(0.5)
    rest = GROUP - KEEP
    high = np.zeros((LANES, 2 * rest))
    for b in range(2):
        high[b * GROUP : (b + 1) * GROUP, b * rest : (b + 1) * rest] = basis[KEEP:].T
    forward = np.zeros((7, 2 * LANES, LANES))
    for t in range(7):
        forward[t, :LANES, : 2 * rest] = high
        forward[t, LANES:, 2 * rest :] = high[:, 16 * t : 16 * t + 16]
    inverse = np.zeros((7, LANES, 2 * LANES))
    for t in range(7):
        inverse[t] = forward[t].T
    blocks = SPAN // GROUP
    keep = np.zeros((SPAN, LANES))
    mean = np.zeros((LANES, SPAN))
    for c in range(blocks):
        keep[c * GROUP : (c + 1) * GROUP, c * KEEP : (c + 1) * KEEP] = basis[:KEEP].T
        mean[c * KEEP : (c + 1) * KEEP, c * GROUP : (c + 1) * GROUP] = 1.0 / GROUP
    both = lambda table: np.concatenate(split(table), axis=-1)
    wide = np.concatenate([both(forward).reshape(-1, 2 * LANES), both(keep)], axis=0)
    back = np.concatenate([both(keep.T), mean.astype(ml_dtypes.bfloat16)], axis=-1)
    back = back.reshape(LANES, 6, WIDE).transpose(1, 0, 2).reshape(-1, WIDE)
    return wide, np.concatenate([both(inverse).reshape(-1, WIDE), back], axis=0)


def halves(value):
    top = value.astype(BF16)
    return top, (value - top.astype(F32)).astype(BF16)


def dot(a, b):
    return jnp.dot(a, b, preferred_element_type=F32)


X_UNITS = [(2, 0), (2, 2), (3, 0), (3, 2), (4, 0), (4, 2)]
Z_UNITS = [(0, 0), (0, 2), (1, 0), (1, 2)]
SENDS = ["x2", "xa", "xb", "xz", "z4", "z2", "za", "zb", "la", "lc", "ld", "lf"]
EARLY = [
    ("F", 2), ("XS", 1), ("F", 1), ("ZS", 3), ("FL", 1), ("XS", 0),
    ("F", 4), ("FL", 2), ("ZS", 2), ("XS", 4), ("FL", 4), ("FL", 0),
    ("FL", 3), ("LA", 0), ("XS", 5), ("F", 0), ("XP", 1), ("XP", 0),
    ("ZS", 1), ("F", 3), ("ZC", 3), ("XS", 2), ("XC", 1), ("XP", 5),
    ("ZS", 0), ("ZP", 3), ("LC", 0), ("XP", 4), ("XP", 2), ("XS", 3),
    ("ZC", 1), ("ZC", 2), ("LD", 0), ("XC", 0), ("XC", 5), ("ZE", 3),
    ("XE", 1), ("XP", 3), ("XC", 4), ("ZC", 0), ("XC", 2), ("ZP", 2),
    ("XE", 0), ("BK", 2), ("XC", 3), ("ZP", 1), ("XE", 5), ("ZP", 0),
    ("LF", 0), ("XE", 4), ("BK", 4), ("ZE", 2), ("BK", 1), ("XE", 2),
    ("XE", 3), ("BK", 3), ("ZE", 1), ("ZE", 0), ("BK", 0), ("N", 0),
    ("N", 1), ("N", 2), ("N", 3), ("N", 4),
]
LATE = [
    ("F", 2), ("XS", 0), ("F", 1), ("ZS", 3), ("FL", 2), ("FL", 1),
    ("XS", 1), ("FL", 4), ("FL", 3), ("FL", 0), ("LA", 0), ("XP", 0),
    ("F", 3), ("XS", 3), ("ZS", 2), ("XP", 1), ("F", 0), ("XS", 2),
    ("ZS", 1), ("ZC", 3), ("F", 4), ("LC", 0), ("XS", 4), ("XP", 2),
    ("XC", 1), ("XS", 5), ("XP", 3), ("LD", 0), ("ZC", 1), ("ZS", 0),
    ("XC", 0), ("XE", 1), ("XP", 4), ("ZC", 2), ("XP", 5), ("ZP", 3),
    ("XC", 2), ("LF", 0), ("ZP", 1), ("XC", 3), ("ZC", 0), ("ZP", 2),
    ("XE", 0), ("BK", 2), ("XC", 4), ("XE", 2), ("N", 2), ("XC", 5),
    ("N", 4), ("N", 0), ("XE", 3), ("ZP", 0), ("BK", 3), ("N", 3),
    ("XE", 4), ("ZE", 3), ("N", 1), ("ZE", 2), ("BK", 1), ("ZE", 1),
    ("XE", 5), ("BK", 4), ("ZE", 0), ("BK", 0),
]


def kernel(
    grads, momentum, wide_hbm, back_hbm, new_out, upd_out,
    xin, mom, wide, back, sx, sz, lw,
    xr2, xab, xrz, zr4, zr2, zab,
    la, lc, le, es, total, nm, up,
    load_sem, store_sem, send_sem, recv_sem, column_sem, stack_sem,
):
    rep, fsdp = lax.axis_index("rep"), lax.axis_index("fsdp")
    core, y, zh = lax.rem(rep, 2), lax.rem(lax.div(rep, 2), 4), lax.div(rep, 8)
    x, z = lax.rem(fsdp, 4), lax.div(fsdp, 4)

    def ring(v, d):
        return lax.rem(v + (d + 4), 4)

    xs, ys, zs = ([v] + [ring(v, d) for d in (1, 2, 3)] for v in (x, y, zh))
    other_core, other_z = 1 - core, 1 - z
    own_rep, own_fsdp = rep, fsdp
    places = {}

    def device(dzh=0, dy=0, dcore=0, dz=0, dx=0):
        key = (dzh, dy % 4, dcore, dz, dx % 4)
        if key not in places:
            c2, z2 = other_core if dcore else core, other_z if dz else z
            moved = dzh or dy or dcore
            r2 = (zs[dzh] * 4 + ys[dy % 4]) * 2 + c2 if moved else own_rep
            places[key] = (r2, z2 * 4 + xs[dx % 4] if dz or dx else own_fsdp)
        return places[key]

    for dy in range(4):
        for dc in range(2):
            device(dy=dy, dcore=dc)
    for d in range(4):
        for dz in range(2):
            device(dzh=d, dz=dz)
        device(dx=d)

    column = [(dy, dc) for dy in range(4) for dc in range(2) if dy or dc]
    barrier = pltpu.get_barrier_semaphore()

    def greet(sem, p):
        pl.semaphore_signal(sem, inc=1, device_id=p, device_id_type=MESH)

    def later_in_column(dy, dc):
        if dy:
            return ring(y, dy) > y
        return core == 1

    def later_in_stack(d):
        return ring(zh, d) > zh

    def greet_others(sem_of, later):
        def where(test, sem, places):
            @pl.when(test if later else jnp.logical_not(test))
            def _():
                for place in places:
                    greet(sem, place)

        for d in range(4):
            cores = range(2) if d else (1,)
            where(later_in_column(d, 1), sem_of[0], [device(dy=d, dcore=dc) for dc in cores])
        for d in (1, 2, 3):
            where(later_in_stack(d), sem_of[1], [device(dzh=d, dz=dz) for dz in range(2)])

    for d in (1, 2, 3):
        greet(barrier, device(dx=d))
    greet(barrier, device(dz=1))
    column_later = 2 * (3 - y) + core
    stack_later = 2 * (3 - zh)

    def enter():
        pl.semaphore_wait(barrier, 4 + (7 - column_later) + (6 - stack_later))
    def remote(kind, src, dst, to, recv):
        return pltpu.make_async_remote_copy(
            src_ref=src, dst_ref=dst, send_sem=send_sem.at[SENDS.index(kind)],
            recv_sem=recv_sem.at[recv], device_id=to, device_id_type=MESH,
        )

    def send(kind, src, dst, to, recv):
        remote(kind, src, dst, to, recv).start()

    def await_bytes(ref, sem):
        pltpu.make_async_copy(ref, ref, sem).wait()

    def received(ref, recv):
        await_bytes(ref, recv_sem.at[recv])

    def all_sent(kind, ref):
        await_bytes(ref, send_sem.at[SENDS.index(kind)])

    loads = []

    def load(src, dst):
        copy = pltpu.make_async_copy(src, dst, load_sem.at[len(loads)])
        copy.start()
        loads.append(copy)
        return copy

    waited, ready, parts, normalised = set(), set(), {}, set()

    def arrived(copy):
        if id(copy) not in waited:
            waited.add(id(copy))
            copy.wait()

    def load_group(g):
        cols = pl.ds(g * SPAN, SPAN)
        return load(momentum.at[:, cols], mom.at[:, cols]), load(grads.at[:, cols], xin.at[pl.ds(0, GRAD), cols])

    order = [g for name, g in EARLY if name == "F"]
    front = pl.ds(0, 7 * 2 * LANES)
    rest = pl.ds(7 * 2 * LANES, SPAN)
    group_loads = {order[0]: load_group(order[0])}
    load_wide = load(wide_hbm.at[front], wide.at[front])
    load_rest = []
    greet_others((barrier, barrier), True)

    def load_others():
        for g in order[1:]:
            group_loads[g] = load_group(g)
        load_rest.append(load(wide_hbm.at[rest], wide.at[rest]))
        load_rest.append(load(back_hbm, back))

    def prepare(g):
        if g not in ready:
            ready.add(g)
            for copy in group_loads[g]:
                copy.wait()
            cols = slice(g * SPAN, (g + 1) * SPAN)
            top, low_part = halves(BETA * mom[:, cols])
            xin[GRAD : GRAD + MINE, cols] = top
            xin[GRAD + MINE :, cols] = low_part

    def fold(v, count=2):
        v = v[:, :LANES] + v[:, LANES:]
        rows, mine = count * GRAD // 2, count * MINE // 2
        own = v[rows : rows + mine] + v[rows + mine :]
        return v[:rows].reshape(2 * count, NZL, NX, OWN, LANES), own.reshape(2 * count, OWN, LANES)

    def forward_rows(g, parts_of):
        base = g * SPAN

        def rows(start):
            cols = slice(base + start, base + start + LANES)
            if len(parts_of) == 2:
                return xin[:, cols]
            h, n, k = parts_of[0], GRAD // 2, MINE // 2
            spans = [(h * n, n), (GRAD + h * k, k), (GRAD + MINE + h * k, k)]
            return jnp.concatenate([xin[at : at + size, cols] for at, size in spans], axis=0)

        last = rows(HIGH)
        for t in range(7):
            both = jnp.concatenate([rows(t * LANES), last], axis=1)
            value, own = fold(dot(both, wide[t * 2 * LANES : (t + 1) * 2 * LANES]), len(parts_of))
            lanes = slice(t * LANES, (t + 1) * LANES)
            for i, h in enumerate(parts_of):
                mats = slice(2 * i, 2 * i + 2)
                if (g, 2 * h) in X_UNITS:
                    u = X_UNITS.index((g, 2 * h))
                    for m in range(2):
                        for k in range(NZL):
                            sx[u, :, k, m, :, lanes] = value[2 * i + m, k]
                    sx[u, x, z, :, :, lanes] += own[mats]
                else:
                    u = Z_UNITS.index((g, 2 * h))
                    for m in range(2):
                        for k in range(NZL):
                            sz[u, k, :, m, :, lanes] = value[2 * i + m, k]
                    sz[u, z, x, :, :, lanes] += own[mats]

    def forward(g):
        prepare(g)
        forward_rows(g, (0, 1))

    def forward_low(g):
        prepare(g)
        arrived(load_rest[0])
        value, own = fold(dot(xin[:, g * SPAN : (g + 1) * SPAN], wide[7 * 2 * LANES :]))
        lanes = slice(g * LANES, (g + 1) * LANES)
        lw[:, :, :, :, lanes] = value
        lw[:, z, x, :, lanes] += own

    way = lambda u: 1 if u % 2 == 0 else -1
    z_way = lambda u: -way(u)
    nx, nz = len(X_UNITS), len(Z_UNITS)
    X2, XAB, XZ = 0, nx, 2 * nx
    Z4, Z2, ZAB = 3 * nx, 3 * nx + nz, 3 * nx + 2 * nz
    LOW_A = 3 * nx + 3 * nz
    LOW_C, LOW_D, LOW_F = LOW_A + 1, LOW_A + 2, LOW_A + 3

    def x_start(u):
        d = way(u)
        send("x2", sx.at[u, xs[2]], xr2.at[u], device(dx=d), X2 + u)
        send("xa", sx.at[u, xs[-d]], xab.at[u, 0], device(dx=-d), XAB + u)

    def x_pass(u):
        d = way(u)
        received(xr2.at[u], X2 + u)
        sx[u, xs[d]] += xr2[u]
        send("xb", sx.at[u, xs[d]], xab.at[u, 1], device(dx=d), XAB + u)

    def x_cross(u):
        received(xab.at[u], XAB + u)
        sx[u, x] += xab[u, 0] + xab[u, 1]
        send("xz", sx.at[u, x, other_z], xrz.at[u], device(dz=1), XZ + u)

    def z_start(u):
        send("z4", sz.at[u, other_z], zr4.at[u], device(dz=1), Z4 + u)

    def z_cross(u):
        d = z_way(u)
        received(zr4.at[u], Z4 + u)
        sz[u, z] += zr4[u]
        send("z2", sz.at[u, z, xs[2]], zr2.at[u], device(dx=d), Z2 + u)
        send("za", sz.at[u, z, xs[-d]], zab.at[u, 0], device(dx=-d), ZAB + u)

    def z_pass(u):
        d = z_way(u)
        received(zr2.at[u], Z2 + u)
        sz[u, z, xs[d]] += zr2[u]
        send("zb", sz.at[u, z, xs[d]], zab.at[u, 1], device(dx=d), ZAB + u)

    def x_end(u):
        received(xrz.at[u], XZ + u)
        parts[X_UNITS[u]] = sx[u, x, z] + xrz[u]

    def z_end(u):
        received(zab.at[u], ZAB + u)
        parts[Z_UNITS[u]] = sz[u, z, x] + (zab[u, 0] + zab[u, 1])

    stores = []

    def store(src, dst):
        copy = pltpu.make_async_copy(src, dst, store_sem.at[len(stores)])
        copy.start()
        stores.append(copy)

    def backward(g):
        arrived(load_rest[1])
        field = jnp.concatenate([parts[k] for k in sorted(parts) if k[0] == g], axis=0).reshape(MINE, HIGH)
        last = jnp.zeros((MINE, LANES), F32)
        for t in range(7):
            top, rest = halves(field[:, t * LANES : (t + 1) * LANES])
            v = dot(jnp.concatenate([top, rest], axis=0), back[t * LANES : (t + 1) * LANES])
            v = v[:MINE, : 2 * LANES] + (v[MINE:, : 2 * LANES] + v[:MINE, 2 * LANES :])
            base = g * SPAN + t * LANES
            nm[:, base : base + LANES] = v[:, :LANES]
            last += v[:, LANES:]
        nm[:, g * SPAN + HIGH : (g + 1) * SPAN] = last
        cols = pl.ds(g * SPAN, SPAN)
        store(nm.at[:, cols], new_out.at[:, cols])

    def low_a(_):
        @pl.when(column_later > 0)
        def _():
            pl.semaphore_wait(column_sem, column_later)

        for k, (dy, dc) in enumerate(column):
            send("la", lw.at[ys[dy], other_core if dc else core], la.at[k], device(dy=dy, dcore=dc), LOW_A)

    def low_d(_):
        received(la, LOW_A)
        lw[y, core] += ((la[0] + la[1]) + (la[2] + la[3])) + ((la[4] + la[5]) + la[6])
        for d in (1, 2, 3):
            send("lc", lw.at[y, core, xs[d]], lc.at[d - 1], device(dx=d), LOW_C)

    def low_e(_):
        received(lc, LOW_C)
        es[...] = lw[y, core, x] + (lc[0] + lc[1] + lc[2])

        @pl.when(stack_later > 0)
        def _():
            pl.semaphore_wait(stack_sem, stack_later)

        @pl.when(core == z)
        def _():
            for d in (1, 2, 3):
                send("ld", es, le.at[d - 1], device(dzh=d), LOW_D)

        @pl.when(core != z)
        def _():
            for d in range(4):
                send("ld", es, le.at[3 + d], device(dzh=d, dz=1), LOW_D)

    def low_i(_):
        @pl.when(core == z)
        def _():
            received(le, LOW_D)
            total[y] = es[...] + ((le[0] + le[1] + le[2]) + (le[3] + le[4] + le[5] + le[6]))
            for dy, dc in column:
                send("lf", total.at[y], total.at[y], device(dy=dy, dcore=dc), LOW_F)

    def low_end():
        arrived(load_rest[1])

        @pl.when(core == z)
        def _():
            received(total.at[pl.ds(0, 3)], LOW_F)

        @pl.when(core != z)
        def _():
            received(total, LOW_F)

    def normalise(g):
        if not normalised:
            low_end()
        normalised.add(g)
        table = lambda i: back[(7 + i) * LANES : (8 + i) * LANES]
        lanes = slice(g * LANES, (g + 1) * LANES)
        mean = total[:, :, lanes].reshape(MINE, LANES) * (1.0 / N_REP)
        top, rest = halves(mean)
        pair = jnp.concatenate([top, rest], axis=0)
        squares = jnp.concatenate(halves(mean * mean), axis=0)
        for h in range(2):
            v, w = dot(pair, table(h)), dot(squares, table(4 + h))
            field = v[:MINE] + (v[MINE:] + dot(top, table(2 + h)))
            square = w[:MINE] + w[MINE:]
            base = g * SPAN + h * WIDE
            up[:, base : base + WIDE] = field * lax.rsqrt(field * field + square + EPS)
        cols = pl.ds(g * SPAN, SPAN)
        store(up.at[:, cols], upd_out.at[:, cols])

    steps = {
        "F": forward, "FL": forward_low,
        "XS": x_start, "XP": x_pass, "XC": x_cross, "XE": x_end,
        "ZS": z_start, "ZC": z_cross, "ZP": z_pass, "ZE": z_end,
        "LA": low_a, "LC": low_d, "LD": low_e, "LF": low_i,
        "N": normalise, "BK": backward,
    }
    first = EARLY[0][1]
    prepare(first)
    arrived(load_wide)
    load_others()
    before = set(ready), set(waited)

    def run(plan):
        ready.clear()
        ready.update(before[0])
        waited.clear()
        waited.update(before[1])
        for state in (parts, normalised):
            state.clear()
        stores.clear()
        answered = False
        half = X_UNITS[plan[1][1]][1] // 2
        forward_rows(first, (half,))
        enter()
        for name, u in plan[1:]:
            if not answered and name not in ("XS", "ZS"):
                greet_others((column_sem, stack_sem), False)
                answered = True
            steps[name](u)
            if (name, u) == plan[1]:
                forward_rows(first, (1 - half,))
        all_sent("x2", xr2)
        all_sent("xa", xr2)
        all_sent("xb", xr2)
        all_sent("xz", xrz)
        all_sent("z4", zr4)
        all_sent("z2", zr2)
        all_sent("za", zr2)
        all_sent("zb", zr2)
        all_sent("la", la)
        all_sent("lc", lc)

        @pl.when(core != z)
        def _():
            all_sent("ld", le.at[pl.ds(0, 4)])

        @pl.when(core == z)
        def _():
            all_sent("ld", le.at[pl.ds(0, 3)])
            all_sent("lf", le)

        for copy in stores:
            copy.wait()

    @pl.when(zh < 2)
    def _():
        run(EARLY)

    @pl.when(zh >= 2)
    def _():
        run(LATE)


def write_out(new_in, upd_in, new_out, upd_out, sems):
    copies = []
    for k, (src, dst) in enumerate([(new_in, new_out), (upd_in, upd_out)]):
        for m in range(MATS):
            rows = pl.ds(m * OWN, OWN)
            copies.append(pltpu.make_async_copy(src.at[rows], dst.at[rows], sems.at[k, m]))
    for copy in copies:
        copy.start()
    for copy in copies:
        copy.wait()


def per_device(gradients, momentum):
    wide, back = tables()
    anywhere = pl.BlockSpec(memory_space=pl.ANY)
    new_momentum, update = pl.pallas_call(
        kernel,
        out_shape=[jax.ShapeDtypeStruct((MINE, D), F32)] * 2,
        in_specs=[anywhere] * 4,
        out_specs=[anywhere] * 2,
        scratch_shapes=[
            pltpu.VMEM((GRAD + 2 * MINE, D), BF16),
            pltpu.VMEM((MINE, D), F32),
            pltpu.VMEM(wide.shape, BF16),
            pltpu.VMEM(back.shape, BF16),
            pltpu.VMEM((len(X_UNITS), NX, NZL, 2, OWN, HIGH), F32),
            pltpu.VMEM((len(Z_UNITS), NZL, NX, 2, OWN, HIGH), F32),
            pltpu.VMEM((MATS, NZL, NX, OWN, LOW), F32),
            pltpu.VMEM((len(X_UNITS), NZL, 2, OWN, HIGH), F32),
            pltpu.VMEM((len(X_UNITS), 2, NZL, 2, OWN, HIGH), F32),
            pltpu.VMEM((len(X_UNITS), 2, OWN, HIGH), F32),
            pltpu.VMEM((len(Z_UNITS), NX, 2, OWN, HIGH), F32),
            pltpu.VMEM((len(Z_UNITS), 2, OWN, HIGH), F32),
            pltpu.VMEM((len(Z_UNITS), 2, 2, OWN, HIGH), F32),
            pltpu.VMEM((7, NX, OWN, LOW), F32),
            pltpu.VMEM((3, OWN, LOW), F32),
            pltpu.VMEM((7, OWN, LOW), F32),
            pltpu.VMEM((OWN, LOW), F32),
            pltpu.VMEM((MATS, OWN, LOW), F32),
            pltpu.VMEM((MINE, D), F32),
            pltpu.VMEM((MINE, D), F32),
            pltpu.SemaphoreType.DMA((2 * GROUPS + 3,)),
            pltpu.SemaphoreType.DMA((2 * GROUPS,)),
            pltpu.SemaphoreType.DMA((len(SENDS),)),
            pltpu.SemaphoreType.DMA((3 * len(X_UNITS) + 3 * len(Z_UNITS) + 4,)),
            pltpu.SemaphoreType.REGULAR,
            pltpu.SemaphoreType.REGULAR,
        ],
        compiler_params=pltpu.CompilerParams(
            collective_id=0, has_side_effects=True, vmem_limit_bytes=(52 * 1024 + 384) * 1024
        ),
        cost_estimate=pl.CostEstimate(flops=2_000_000_000, bytes_accessed=8_000_000, transcendentals=200_000),
    )(gradients.reshape(GRAD, D), momentum.reshape(MINE, D), wide, back)
    new_momentum, update = pl.pallas_call(
        write_out,
        out_shape=[jax.ShapeDtypeStruct((MINE, D), F32)] * 2,
        in_specs=[anywhere] * 2,
        out_specs=[anywhere] * 2,
        scratch_shapes=[pltpu.SemaphoreType.DMA((2, 4))],
        compiler_params=pltpu.CompilerParams(vmem_limit_bytes=4 * 1024 * 1024),
        cost_estimate=pl.CostEstimate(flops=0, bytes_accessed=2_600_000, transcendentals=0),
    )(new_momentum, update)
    return new_momentum.reshape(1, MATS, OWN, D), update.reshape(MATS, OWN, D)


def solution(mesh):
    return jax.shard_map(
        per_device,
        mesh=mesh,
        in_specs=(P("rep", "fsdp", None, None, None), P("rep", None, "fsdp", None)),
        out_specs=(P("rep", None, "fsdp", None), P(None, "fsdp", None)),
        check_vma=False,
    )
```

```python
import jax
import jax.numpy as jnp
import ml_dtypes
import numpy as np
from jax import lax
from jax.experimental import pallas as pl
from jax.experimental.pallas import tpu as pltpu
from jax.sharding import PartitionSpec as P

D, MATS, GROUP, KEEP, ROWS = 5120, 4, 64, 8, 64
BETA, EPS = 0.999, 1e-06
NX, NY, NZL, NZH, NC, N_REP = 4, 4, 2, 4, 2, 32
OWN = 8
LANES = 128
TILES = 8
SPAN = LANES * TILES
GROUPS = D // SPAN
HIGH = 7 * LANES
LOW = GROUPS * LANES
GRAD = MATS * ROWS
MINE = MATS * OWN
WIDE = 4 * LANES

F32, BF16 = jnp.float32, jnp.bfloat16
MESH = pl.DeviceIdType.MESH


def split(table):
    high = table.astype(ml_dtypes.bfloat16)
    low = (table - high.astype(np.float64)).astype(ml_dtypes.bfloat16)
    return high, low


def tables():
    n, k = np.arange(GROUP), np.arange(GROUP)[:, None]
    basis = np.sqrt(2.0 / GROUP) * np.cos(np.pi * (n + 0.5) * k / GROUP)
    basis[0] *= np.sqrt(0.5)
    rest = GROUP - KEEP
    high = np.zeros((LANES, 2 * rest))
    for b in range(2):
        high[b * GROUP : (b + 1) * GROUP, b * rest : (b + 1) * rest] = basis[KEEP:].T
    forward = np.zeros((7, 2 * LANES, LANES))
    for t in range(7):
        forward[t, :LANES, : 2 * rest] = high
        forward[t, LANES:, 2 * rest :] = high[:, 16 * t : 16 * t + 16]
    inverse = np.zeros((7, LANES, 2 * LANES))
    for t in range(7):
        inverse[t] = forward[t].T
    blocks = SPAN // GROUP
    keep = np.zeros((SPAN, LANES))
    mean = np.zeros((LANES, SPAN))
    for c in range(blocks):
        keep[c * GROUP : (c + 1) * GROUP, c * KEEP : (c + 1) * KEEP] = basis[:KEEP].T
        mean[c * KEEP : (c + 1) * KEEP, c * GROUP : (c + 1) * GROUP] = 1.0 / GROUP
    both = lambda table: np.concatenate(split(table), axis=-1)
    wide = np.concatenate([both(forward).reshape(-1, 2 * LANES), both(keep)], axis=0)
    back = np.concatenate([both(keep.T), mean.astype(ml_dtypes.bfloat16)], axis=-1)
    back = back.reshape(LANES, 6, WIDE).transpose(1, 0, 2).reshape(-1, WIDE)
    return wide, np.concatenate([both(inverse).reshape(-1, WIDE), back], axis=0)


def halves(value):
    top = value.astype(BF16)
    return top, (value - top.astype(F32)).astype(BF16)


def dot(a, b):
    return jnp.dot(a, b, preferred_element_type=F32)


X_UNITS = [(2, 0), (2, 2), (3, 0), (3, 2), (4, 0), (4, 2)]
Z_UNITS = [(0, 0), (0, 2), (1, 0), (1, 2)]
SENDS = ["x2", "xa", "xb", "xz", "z4", "z2", "za", "zb", "la", "lc", "ld", "lf"]
EARLY = [
    ("F", 2), ("XS", 1), ("F", 1), ("ZS", 3), ("FL", 1), ("XS", 0),
    ("F", 4), ("FL", 2), ("ZS", 2), ("XS", 4), ("FL", 4), ("FL", 0),
    ("FL", 3), ("LA", 0), ("XS", 5), ("F", 0), ("XP", 1), ("XP", 0),
    ("ZS", 1), ("F", 3), ("ZC", 3), ("XS", 2), ("XC", 1), ("XP", 5),
    ("ZS", 0), ("ZP", 3), ("LC", 0), ("XP", 4), ("XP", 2), ("XS", 3),
    ("ZC", 1), ("ZC", 2), ("LD", 0), ("XC", 0), ("XC", 5), ("ZE", 3),
    ("XE", 1), ("XP", 3), ("XC", 4), ("ZC", 0), ("XC", 2), ("ZP", 2),
    ("XE", 0), ("BK", 2), ("XC", 3), ("ZP", 1), ("LF", 0), ("XE", 5),
    ("ZP", 0), ("XE", 4), ("BK", 4), ("ZE", 2), ("BK", 1), ("XE", 2),
    ("N", 0), ("XE", 3), ("BK", 3), ("ZE", 1), ("ZE", 0), ("BK", 0),
]
LATE = [
    ("F", 2), ("XS", 0), ("F", 1), ("ZS", 3), ("FL", 2), ("FL", 1),
    ("XS", 1), ("FL", 4), ("FL", 3), ("FL", 0), ("LA", 0), ("XP", 0),
    ("F", 3), ("XS", 3), ("ZS", 2), ("XP", 1), ("F", 0), ("XS", 2),
    ("ZS", 1), ("ZC", 3), ("F", 4), ("LC", 0), ("XS", 4), ("XP", 2),
    ("XC", 1), ("XS", 5), ("XP", 3), ("LD", 0), ("ZC", 1), ("ZS", 0),
    ("XC", 0), ("XE", 1), ("XP", 4), ("ZC", 2), ("XP", 5), ("ZP", 3),
    ("XC", 2), ("LF", 0), ("ZP", 1), ("XC", 3), ("ZC", 0), ("ZP", 2),
    ("XE", 0), ("BK", 2), ("XC", 4), ("XE", 2), ("XC", 5), ("XE", 3),
    ("ZP", 0), ("N", 0), ("BK", 3), ("XE", 4), ("ZE", 3), ("ZE", 2),
    ("BK", 1), ("ZE", 1), ("XE", 5), ("BK", 4), ("ZE", 0), ("BK", 0),
]


def kernel(
    grads, momentum, wide_hbm, back_hbm, new_out, upd_out,
    xin, mom, wide, back, sx, sz, lw,
    xr2, xab, xrz, zr4, zr2, zab,
    la, lc, le, es, total, nm, up,
    load_sem, store_sem, send_sem, recv_sem, column_sem, stack_sem,
):
    rep, fsdp = lax.axis_index("rep"), lax.axis_index("fsdp")
    core, y, zh = lax.rem(rep, 2), lax.rem(lax.div(rep, 2), 4), lax.div(rep, 8)
    x, z = lax.rem(fsdp, 4), lax.div(fsdp, 4)

    def ring(v, d):
        return lax.rem(v + (d + 4), 4)

    xs, ys, zs = ([v] + [ring(v, d) for d in (1, 2, 3)] for v in (x, y, zh))
    other_core, other_z = 1 - core, 1 - z
    own_rep, own_fsdp = rep, fsdp
    places = {}

    def device(dzh=0, dy=0, dcore=0, dz=0, dx=0):
        key = (dzh, dy % 4, dcore, dz, dx % 4)
        if key not in places:
            c2, z2 = other_core if dcore else core, other_z if dz else z
            moved = dzh or dy or dcore
            r2 = (zs[dzh] * 4 + ys[dy % 4]) * 2 + c2 if moved else own_rep
            places[key] = (r2, z2 * 4 + xs[dx % 4] if dz or dx else own_fsdp)
        return places[key]

    for dy in range(4):
        for dc in range(2):
            device(dy=dy, dcore=dc)
    for d in range(4):
        for dz in range(2):
            device(dzh=d, dz=dz)
        device(dx=d)

    column = [(dy, dc) for dy in range(4) for dc in range(2) if dy or dc]
    barrier = pltpu.get_barrier_semaphore()

    def greet(sem, p):
        pl.semaphore_signal(sem, inc=1, device_id=p, device_id_type=MESH)

    def later_in_column(dy, dc):
        if dy:
            return ring(y, dy) > y
        return core == 1

    def later_in_stack(d):
        return ring(zh, d) > zh

    def greet_others(sem_of, later):
        def where(test, sem, places):
            @pl.when(test if later else jnp.logical_not(test))
            def _():
                for place in places:
                    greet(sem, place)

        for d in range(4):
            cores = range(2) if d else (1,)
            where(later_in_column(d, 1), sem_of[0], [device(dy=d, dcore=dc) for dc in cores])
        for d in (1, 2, 3):
            where(later_in_stack(d), sem_of[1], [device(dzh=d, dz=dz) for dz in range(2)])

    for d in (1, 2, 3):
        greet(barrier, device(dx=d))
    greet(barrier, device(dz=1))
    column_later = 2 * (3 - y) + core
    stack_later = 2 * (3 - zh)

    def enter():
        pl.semaphore_wait(barrier, 4 + (7 - column_later) + (6 - stack_later))
    def remote(kind, src, dst, to, recv):
        return pltpu.make_async_remote_copy(
            src_ref=src, dst_ref=dst, send_sem=send_sem.at[SENDS.index(kind)],
            recv_sem=recv_sem.at[recv], device_id=to, device_id_type=MESH,
        )

    def send(kind, src, dst, to, recv):
        remote(kind, src, dst, to, recv).start()

    def await_bytes(ref, sem):
        pltpu.make_async_copy(ref, ref, sem).wait()

    def received(ref, recv):
        await_bytes(ref, recv_sem.at[recv])

    def all_sent(kind, ref):
        await_bytes(ref, send_sem.at[SENDS.index(kind)])

    loads = []

    def load(src, dst):
        copy = pltpu.make_async_copy(src, dst, load_sem.at[len(loads)])
        copy.start()
        loads.append(copy)
        return copy

    waited, ready, parts = set(), set(), {}

    def arrived(copy):
        if id(copy) not in waited:
            waited.add(id(copy))
            copy.wait()

    def load_group(g):
        cols = pl.ds(g * SPAN, SPAN)
        return load(momentum.at[:, cols], mom.at[:, cols]), load(grads.at[:, cols], xin.at[pl.ds(0, GRAD), cols])

    order = [g for name, g in EARLY if name == "F"]
    front = pl.ds(0, 7 * 2 * LANES)
    rest = pl.ds(7 * 2 * LANES, SPAN)
    group_loads = {order[0]: load_group(order[0])}
    load_wide = load(wide_hbm.at[front], wide.at[front])
    load_rest = []
    greet_others((barrier, barrier), True)

    def load_others():
        for g in order[1:]:
            group_loads[g] = load_group(g)
        load_rest.append(load(wide_hbm.at[rest], wide.at[rest]))
        load_rest.append(load(back_hbm, back))

    def prepare(g):
        if g not in ready:
            ready.add(g)
            for copy in group_loads[g]:
                copy.wait()
            cols = slice(g * SPAN, (g + 1) * SPAN)
            top, low_part = halves(BETA * mom[:, cols])
            xin[GRAD : GRAD + MINE, cols] = top
            xin[GRAD + MINE :, cols] = low_part

    def fold(v, count=2):
        v = v[:, :LANES] + v[:, LANES:]
        rows, mine = count * GRAD // 2, count * MINE // 2
        own = v[rows : rows + mine] + v[rows + mine :]
        return v[:rows].reshape(2 * count, NZL, NX, OWN, LANES), own.reshape(2 * count, OWN, LANES)

    def forward_rows(g, parts_of):
        base = g * SPAN

        def rows(start):
            cols = slice(base + start, base + start + LANES)
            if len(parts_of) == 2:
                return xin[:, cols]
            h, n, k = parts_of[0], GRAD // 2, MINE // 2
            spans = [(h * n, n), (GRAD + h * k, k), (GRAD + MINE + h * k, k)]
            return jnp.concatenate([xin[at : at + size, cols] for at, size in spans], axis=0)

        last = rows(HIGH)
        for t in range(7):
            both = jnp.concatenate([rows(t * LANES), last], axis=1)
            value, own = fold(dot(both, wide[t * 2 * LANES : (t + 1) * 2 * LANES]), len(parts_of))
            lanes = slice(t * LANES, (t + 1) * LANES)
            for i, h in enumerate(parts_of):
                mats = slice(2 * i, 2 * i + 2)
                if (g, 2 * h) in X_UNITS:
                    u = X_UNITS.index((g, 2 * h))
                    for m in range(2):
                        for k in range(NZL):
                            sx[u, :, k, m, :, lanes] = value[2 * i + m, k]
                    sx[u, x, z, :, :, lanes] += own[mats]
                else:
                    u = Z_UNITS.index((g, 2 * h))
                    for m in range(2):
                        for k in range(NZL):
                            sz[u, k, :, m, :, lanes] = value[2 * i + m, k]
                    sz[u, z, x, :, :, lanes] += own[mats]

    def forward(g):
        prepare(g)
        forward_rows(g, (0, 1))

    def forward_low(g):
        prepare(g)
        arrived(load_rest[0])
        value, own = fold(dot(xin[:, g * SPAN : (g + 1) * SPAN], wide[7 * 2 * LANES :]))
        lanes = slice(g * LANES, (g + 1) * LANES)
        lw[:, :, :, :, lanes] = value
        lw[:, z, x, :, lanes] += own

    way = lambda u: 1 if u % 2 == 0 else -1
    z_way = lambda u: -way(u)
    nx, nz = len(X_UNITS), len(Z_UNITS)
    X2, XAB, XZ = 0, nx, 2 * nx
    Z4, Z2, ZAB = 3 * nx, 3 * nx + nz, 3 * nx + 2 * nz
    LOW_A = 3 * nx + 3 * nz
    LOW_C, LOW_D, LOW_F = LOW_A + 1, LOW_A + 2, LOW_A + 3

    def x_start(u):
        d = way(u)
        send("x2", sx.at[u, xs[2]], xr2.at[u], device(dx=d), X2 + u)
        send("xa", sx.at[u, xs[-d]], xab.at[u, 0], device(dx=-d), XAB + u)

    def x_pass(u):
        d = way(u)
        received(xr2.at[u], X2 + u)
        sx[u, xs[d]] += xr2[u]
        send("xb", sx.at[u, xs[d]], xab.at[u, 1], device(dx=d), XAB + u)

    def x_cross(u):
        received(xab.at[u], XAB + u)
        sx[u, x] += xab[u, 0] + xab[u, 1]
        send("xz", sx.at[u, x, other_z], xrz.at[u], device(dz=1), XZ + u)

    def z_start(u):
        send("z4", sz.at[u, other_z], zr4.at[u], device(dz=1), Z4 + u)

    def z_cross(u):
        d = z_way(u)
        received(zr4.at[u], Z4 + u)
        sz[u, z] += zr4[u]
        send("z2", sz.at[u, z, xs[2]], zr2.at[u], device(dx=d), Z2 + u)
        send("za", sz.at[u, z, xs[-d]], zab.at[u, 0], device(dx=-d), ZAB + u)

    def z_pass(u):
        d = z_way(u)
        received(zr2.at[u], Z2 + u)
        sz[u, z, xs[d]] += zr2[u]
        send("zb", sz.at[u, z, xs[d]], zab.at[u, 1], device(dx=d), ZAB + u)

    def x_end(u):
        received(xrz.at[u], XZ + u)
        parts[X_UNITS[u]] = sx[u, x, z] + xrz[u]

    def z_end(u):
        received(zab.at[u], ZAB + u)
        parts[Z_UNITS[u]] = sz[u, z, x] + (zab[u, 0] + zab[u, 1])

    stores = []

    def store(src, dst):
        copy = pltpu.make_async_copy(src, dst, store_sem.at[len(stores)])
        copy.start()
        stores.append(copy)

    def backward(g):
        arrived(load_rest[1])
        field = jnp.concatenate([parts[k] for k in sorted(parts) if k[0] == g], axis=0).reshape(MINE, HIGH)
        last = jnp.zeros((MINE, LANES), F32)
        for t in range(7):
            top, rest = halves(field[:, t * LANES : (t + 1) * LANES])
            v = dot(jnp.concatenate([top, rest], axis=0), back[t * LANES : (t + 1) * LANES])
            v = v[:MINE, : 2 * LANES] + (v[MINE:, : 2 * LANES] + v[:MINE, 2 * LANES :])
            base = g * SPAN + t * LANES
            nm[:, base : base + LANES] = v[:, :LANES]
            last += v[:, LANES:]
        nm[:, g * SPAN + HIGH : (g + 1) * SPAN] = last
        cols = pl.ds(g * SPAN, SPAN)
        store(nm.at[:, cols], new_out.at[:, cols])

    def low_a(_):
        @pl.when(column_later > 0)
        def _():
            pl.semaphore_wait(column_sem, column_later)

        for k, (dy, dc) in enumerate(column):
            send("la", lw.at[ys[dy], other_core if dc else core], la.at[k], device(dy=dy, dcore=dc), LOW_A)

    def low_d(_):
        received(la, LOW_A)
        lw[y, core] += ((la[0] + la[1]) + (la[2] + la[3])) + ((la[4] + la[5]) + la[6])
        for d in (1, 2, 3):
            send("lc", lw.at[y, core, xs[d]], lc.at[d - 1], device(dx=d), LOW_C)

    def low_e(_):
        received(lc, LOW_C)
        es[...] = lw[y, core, x] + (lc[0] + lc[1] + lc[2])

        @pl.when(stack_later > 0)
        def _():
            pl.semaphore_wait(stack_sem, stack_later)

        @pl.when(core == z)
        def _():
            for d in (1, 2, 3):
                send("ld", es, le.at[d - 1], device(dzh=d), LOW_D)

        @pl.when(core != z)
        def _():
            for d in range(4):
                send("ld", es, le.at[3 + d], device(dzh=d, dz=1), LOW_D)

    def low_i(_):
        @pl.when(core == z)
        def _():
            received(le, LOW_D)
            total[y] = es[...] + ((le[0] + le[1] + le[2]) + (le[3] + le[4] + le[5] + le[6]))
            for dy, dc in column:
                send("lf", total.at[y], total.at[y], device(dy=dy, dcore=dc), LOW_F)

    def low_end():
        arrived(load_rest[1])

        @pl.when(core == z)
        def _():
            received(total.at[pl.ds(0, 3)], LOW_F)

        @pl.when(core != z)
        def _():
            received(total, LOW_F)

    def normalise(_):
        low_end()
        table = lambda i: back[(7 + i) * LANES : (8 + i) * LANES]
        count = GROUPS * MINE
        mean = jnp.concatenate(
            [total[:, :, g * LANES : (g + 1) * LANES].reshape(MINE, LANES) for g in range(GROUPS)], axis=0
        ) * (1.0 / N_REP)
        top, rest = halves(mean)
        pair = jnp.concatenate([top, rest], axis=0)
        squares = jnp.concatenate(halves(mean * mean), axis=0)
        for h in range(2):
            v, w = dot(pair, table(h)), dot(squares, table(4 + h))
            field = v[:count] + (v[count:] + dot(top, table(2 + h)))
            square = w[:count] + w[count:]
            value = field * lax.rsqrt(field * field + square + EPS)
            for g in range(GROUPS):
                base = g * SPAN + h * WIDE
                up[:, base : base + WIDE] = value[g * MINE : (g + 1) * MINE]
        store(up, upd_out)

    steps = {
        "F": forward, "FL": forward_low,
        "XS": x_start, "XP": x_pass, "XC": x_cross, "XE": x_end,
        "ZS": z_start, "ZC": z_cross, "ZP": z_pass, "ZE": z_end,
        "LA": low_a, "LC": low_d, "LD": low_e, "LF": low_i,
        "N": normalise, "BK": backward,
    }
    first = EARLY[0][1]
    prepare(first)
    arrived(load_wide)
    load_others()
    before = set(ready), set(waited)

    def run(plan):
        ready.clear()
        ready.update(before[0])
        waited.clear()
        waited.update(before[1])
        parts.clear()
        stores.clear()
        answered = False
        half = X_UNITS[plan[1][1]][1] // 2
        forward_rows(first, (half,))
        enter()
        for name, u in plan[1:]:
            if not answered and name not in ("XS", "ZS"):
                greet_others((column_sem, stack_sem), False)
                answered = True
            steps[name](u)
            if (name, u) == plan[1]:
                forward_rows(first, (1 - half,))
        all_sent("x2", xr2)
        all_sent("xa", xr2)
        all_sent("xb", xr2)
        all_sent("xz", xrz)
        all_sent("z4", zr4)
        all_sent("z2", zr2)
        all_sent("za", zr2)
        all_sent("zb", zr2)
        all_sent("la", la)
        all_sent("lc", lc)

        @pl.when(core != z)
        def _():
            all_sent("ld", le.at[pl.ds(0, 4)])

        @pl.when(core == z)
        def _():
            all_sent("ld", le.at[pl.ds(0, 3)])
            all_sent("lf", le)

        for copy in stores:
            copy.wait()

    @pl.when(zh == 0)
    def _():
        run(EARLY)

    @pl.when(zh > 0)
    def _():
        run(LATE)


def write_out(new_in, upd_in, new_out, upd_out, sems):
    copies = []
    for k, (src, dst) in enumerate([(new_in, new_out), (upd_in, upd_out)]):
        for m in range(MATS):
            rows = pl.ds(m * OWN, OWN)
            copies.append(pltpu.make_async_copy(src.at[rows], dst.at[rows], sems.at[k, m]))
    for copy in copies:
        copy.start()
    for copy in copies:
        copy.wait()


def per_device(gradients, momentum):
    wide, back = tables()
    anywhere = pl.BlockSpec(memory_space=pl.ANY)
    new_momentum, update = pl.pallas_call(
        kernel,
        out_shape=[jax.ShapeDtypeStruct((MINE, D), F32)] * 2,
        in_specs=[anywhere] * 4,
        out_specs=[anywhere] * 2,
        scratch_shapes=[
            pltpu.VMEM((GRAD + 2 * MINE, D), BF16),
            pltpu.VMEM((MINE, D), F32),
            pltpu.VMEM(wide.shape, BF16),
            pltpu.VMEM(back.shape, BF16),
            pltpu.VMEM((len(X_UNITS), NX, NZL, 2, OWN, HIGH), F32),
            pltpu.VMEM((len(Z_UNITS), NZL, NX, 2, OWN, HIGH), F32),
            pltpu.VMEM((MATS, NZL, NX, OWN, LOW), F32),
            pltpu.VMEM((len(X_UNITS), NZL, 2, OWN, HIGH), F32),
            pltpu.VMEM((len(X_UNITS), 2, NZL, 2, OWN, HIGH), F32),
            pltpu.VMEM((len(X_UNITS), 2, OWN, HIGH), F32),
            pltpu.VMEM((len(Z_UNITS), NX, 2, OWN, HIGH), F32),
            pltpu.VMEM((len(Z_UNITS), 2, OWN, HIGH), F32),
            pltpu.VMEM((len(Z_UNITS), 2, 2, OWN, HIGH), F32),
            pltpu.VMEM((7, NX, OWN, LOW), F32),
            pltpu.VMEM((3, OWN, LOW), F32),
            pltpu.VMEM((7, OWN, LOW), F32),
            pltpu.VMEM((OWN, LOW), F32),
            pltpu.VMEM((MATS, OWN, LOW), F32),
            pltpu.VMEM((MINE, D), F32),
            pltpu.VMEM((MINE, D), F32),
            pltpu.SemaphoreType.DMA((2 * GROUPS + 3,)),
            pltpu.SemaphoreType.DMA((GROUPS + 1,)),
            pltpu.SemaphoreType.DMA((len(SENDS),)),
            pltpu.SemaphoreType.DMA((3 * len(X_UNITS) + 3 * len(Z_UNITS) + 4,)),
            pltpu.SemaphoreType.REGULAR,
            pltpu.SemaphoreType.REGULAR,
        ],
        compiler_params=pltpu.CompilerParams(
            collective_id=0, has_side_effects=True, vmem_limit_bytes=(52 * 1024 + 384) * 1024
        ),
        cost_estimate=pl.CostEstimate(flops=2_000_000_000, bytes_accessed=8_000_000, transcendentals=200_000),
    )(gradients.reshape(GRAD, D), momentum.reshape(MINE, D), wide, back)
    new_momentum, update = pl.pallas_call(
        write_out,
        out_shape=[jax.ShapeDtypeStruct((MINE, D), F32)] * 2,
        in_specs=[anywhere] * 2,
        out_specs=[anywhere] * 2,
        scratch_shapes=[pltpu.SemaphoreType.DMA((2, 4))],
        compiler_params=pltpu.CompilerParams(vmem_limit_bytes=4 * 1024 * 1024),
        cost_estimate=pl.CostEstimate(flops=0, bytes_accessed=2_600_000, transcendentals=0),
    )(new_momentum, update)
    return new_momentum.reshape(1, MATS, OWN, D), update.reshape(MATS, OWN, D)


def solution(mesh):
    return jax.shard_map(
        per_device,
        mesh=mesh,
        in_specs=(P("rep", "fsdp", None, None, None), P("rep", None, "fsdp", None)),
        out_specs=(P("rep", None, "fsdp", None), P(None, "fsdp", None)),
        check_vma=False,
    )
```

```python
import jax
import jax.numpy as jnp
import ml_dtypes
import numpy as np
from jax import lax
from jax.experimental import pallas as pl
from jax.experimental.pallas import tpu as pltpu
from jax.sharding import PartitionSpec as P

D, MATS, GROUP, KEEP, ROWS = 5120, 4, 64, 8, 64
BETA, EPS = 0.999, 1e-06
NX, NY, NZL, NZH, NC, N_REP = 4, 4, 2, 4, 2, 32
OWN = 8
LANES = 128
TILES = 8
SPAN = LANES * TILES
GROUPS = D // SPAN
HIGH = 7 * LANES
LOW = GROUPS * LANES
GRAD = MATS * ROWS
MINE = MATS * OWN
WIDE = 4 * LANES

F32, BF16 = jnp.float32, jnp.bfloat16
MESH = pl.DeviceIdType.MESH


def split(table):
    high = table.astype(ml_dtypes.bfloat16)
    low = (table - high.astype(np.float64)).astype(ml_dtypes.bfloat16)
    return high, low


def tables():
    n, k = np.arange(GROUP), np.arange(GROUP)[:, None]
    basis = np.sqrt(2.0 / GROUP) * np.cos(np.pi * (n + 0.5) * k / GROUP)
    basis[0] *= np.sqrt(0.5)
    rest = GROUP - KEEP
    high = np.zeros((LANES, 2 * rest))
    for b in range(2):
        high[b * GROUP : (b + 1) * GROUP, b * rest : (b + 1) * rest] = basis[KEEP:].T
    forward = np.zeros((7, 2 * LANES, LANES))
    for t in range(7):
        forward[t, :LANES, : 2 * rest] = high
        forward[t, LANES:, 2 * rest :] = high[:, 16 * t : 16 * t + 16]
    inverse = np.zeros((7, LANES, 2 * LANES))
    for t in range(7):
        inverse[t] = forward[t].T
    blocks = SPAN // GROUP
    keep = np.zeros((SPAN, LANES))
    mean = np.zeros((LANES, SPAN))
    for c in range(blocks):
        keep[c * GROUP : (c + 1) * GROUP, c * KEEP : (c + 1) * KEEP] = basis[:KEEP].T
        mean[c * KEEP : (c + 1) * KEEP, c * GROUP : (c + 1) * GROUP] = 1.0 / GROUP
    both = lambda table: np.concatenate(split(table), axis=-1)
    wide = np.concatenate([both(forward).reshape(-1, 2 * LANES), both(keep)], axis=0)
    back = np.concatenate([both(keep.T), mean.astype(ml_dtypes.bfloat16)], axis=-1)
    back = back.reshape(LANES, 6, WIDE).transpose(1, 0, 2).reshape(-1, WIDE)
    return wide, np.concatenate([both(inverse).reshape(-1, WIDE), back], axis=0)


def halves(value):
    top = value.astype(BF16)
    return top, (value - top.astype(F32)).astype(BF16)


def dot(a, b):
    return jnp.dot(a, b, preferred_element_type=F32)


X_UNITS = [(2, 0), (2, 2), (3, 0), (3, 2), (4, 0), (4, 2)]
Z_UNITS = [(0, 0), (0, 2), (1, 0), (1, 2)]
SENDS = ["x2", "xa", "xb", "xz", "z4", "z2", "za", "zb", "la", "lc", "ld", "lf"]
EARLY = [
    ("F", 2), ("XS", 1), ("F", 1), ("ZS", 3), ("FL", 1), ("XS", 0),
    ("F", 4), ("FL", 2), ("ZS", 2), ("XS", 4), ("FL", 4), ("FL", 0),
    ("FL", 3), ("LA", 0), ("XS", 5), ("F", 0), ("XP", 1), ("XP", 0),
    ("ZS", 1), ("F", 3), ("ZC", 3), ("XS", 2), ("XC", 1), ("XP", 5),
    ("ZS", 0), ("ZP", 3), ("LC", 0), ("XP", 4), ("XP", 2), ("XS", 3),
    ("ZC", 1), ("ZC", 2), ("LD", 0), ("XC", 0), ("XC", 5), ("ZE", 3),
    ("XE", 1), ("XP", 3), ("XC", 4), ("ZC", 0), ("XC", 2), ("ZP", 2),
    ("XE", 0), ("BK", 2), ("XC", 3), ("ZP", 1), ("LF", 0), ("XE", 5),
    ("ZP", 0), ("XE", 4), ("BK", 4), ("ZE", 2), ("BK", 1), ("XE", 2),
    ("XE", 3), ("BK", 3), ("ZE", 1), ("ZE", 0), ("BK", 0), ("N", 0),
]
LATE = [
    ("F", 2), ("XS", 0), ("F", 1), ("ZS", 3), ("FL", 2), ("FL", 1),
    ("XS", 1), ("FL", 4), ("FL", 3), ("FL", 0), ("LA", 0), ("XP", 0),
    ("F", 3), ("XS", 3), ("ZS", 2), ("XP", 1), ("F", 0), ("XS", 2),
    ("ZS", 1), ("ZC", 3), ("LC", 0), ("F", 4), ("XS", 4), ("XP", 2),
    ("XC", 1), ("LD", 0), ("XS", 5), ("XP", 3), ("ZC", 1), ("ZS", 0),
    ("XC", 0), ("XE", 1), ("XP", 4), ("ZC", 2), ("XP", 5), ("ZP", 3),
    ("XC", 2), ("LF", 0), ("ZP", 1), ("XC", 3), ("ZC", 0), ("ZP", 2),
    ("XE", 0), ("BK", 2), ("XC", 4), ("XE", 2), ("XC", 5), ("XE", 3),
    ("ZP", 0), ("N", 0), ("BK", 3), ("XE", 4), ("ZE", 3), ("ZE", 2),
    ("BK", 1), ("ZE", 1), ("XE", 5), ("BK", 4), ("ZE", 0), ("BK", 0),
]


def kernel(
    grads, momentum, wide_hbm, back_hbm, new_out, upd_out,
    xin, mom, wide, back, sx, sz, lw,
    xr2, xab, xrz, zr4, zr2, zab,
    la, lc, le, es, total, nm, up,
    load_sem, store_sem, send_sem, recv_sem, column_sem, stack_sem,
):
    rep, fsdp = lax.axis_index("rep"), lax.axis_index("fsdp")
    core, y, zh = lax.rem(rep, 2), lax.rem(lax.div(rep, 2), 4), lax.div(rep, 8)
    x, z = lax.rem(fsdp, 4), lax.div(fsdp, 4)

    def ring(v, d):
        return lax.rem(v + (d + 4), 4)

    xs, ys, zs = ([v] + [ring(v, d) for d in (1, 2, 3)] for v in (x, y, zh))
    other_core, other_z = 1 - core, 1 - z
    own_rep, own_fsdp = rep, fsdp
    places = {}

    def device(dzh=0, dy=0, dcore=0, dz=0, dx=0):
        key = (dzh, dy % 4, dcore, dz, dx % 4)
        if key not in places:
            c2, z2 = other_core if dcore else core, other_z if dz else z
            moved = dzh or dy or dcore
            r2 = (zs[dzh] * 4 + ys[dy % 4]) * 2 + c2 if moved else own_rep
            places[key] = (r2, z2 * 4 + xs[dx % 4] if dz or dx else own_fsdp)
        return places[key]

    for dy in range(4):
        for dc in range(2):
            device(dy=dy, dcore=dc)
    for d in range(4):
        for dz in range(2):
            device(dzh=d, dz=dz)
        device(dx=d)

    column = [(dy, dc) for dy in range(4) for dc in range(2) if dy or dc]
    barrier = pltpu.get_barrier_semaphore()

    def greet(sem, p):
        pl.semaphore_signal(sem, inc=1, device_id=p, device_id_type=MESH)

    def later_in_column(dy, dc):
        if dy:
            return ring(y, dy) > y
        return core == 1

    def later_in_stack(d):
        return ring(zh, d) > zh

    def greet_others(sem_of, later):
        def where(test, sem, places):
            @pl.when(test if later else jnp.logical_not(test))
            def _():
                for place in places:
                    greet(sem, place)

        for d in range(4):
            cores = range(2) if d else (1,)
            where(later_in_column(d, 1), sem_of[0], [device(dy=d, dcore=dc) for dc in cores])
        for d in (1, 2, 3):
            where(later_in_stack(d), sem_of[1], [device(dzh=d, dz=dz) for dz in range(2)])

    for d in (1, 2, 3):
        greet(barrier, device(dx=d))
    greet(barrier, device(dz=1))
    column_later = 2 * (3 - y) + core
    stack_later = 2 * (3 - zh)

    def enter():
        pl.semaphore_wait(barrier, 4 + (7 - column_later) + (6 - stack_later))
    def remote(kind, src, dst, to, recv):
        return pltpu.make_async_remote_copy(
            src_ref=src, dst_ref=dst, send_sem=send_sem.at[SENDS.index(kind)],
            recv_sem=recv_sem.at[recv], device_id=to, device_id_type=MESH,
        )

    def send(kind, src, dst, to, recv):
        remote(kind, src, dst, to, recv).start()

    def await_bytes(ref, sem):
        pltpu.make_async_copy(ref, ref, sem).wait()

    def received(ref, recv):
        await_bytes(ref, recv_sem.at[recv])

    def all_sent(kind, ref):
        await_bytes(ref, send_sem.at[SENDS.index(kind)])

    loads = []

    def load(src, dst):
        copy = pltpu.make_async_copy(src, dst, load_sem.at[len(loads)])
        copy.start()
        loads.append(copy)
        return copy

    waited, ready, parts = set(), set(), {}

    def arrived(copy):
        if id(copy) not in waited:
            waited.add(id(copy))
            copy.wait()

    def load_group(g):
        cols = pl.ds(g * SPAN, SPAN)
        return load(momentum.at[:, cols], mom.at[:, cols]), load(grads.at[:, cols], xin.at[pl.ds(0, GRAD), cols])

    order = [g for name, g in EARLY if name == "F"]
    front = pl.ds(0, 7 * 2 * LANES)
    rest = pl.ds(7 * 2 * LANES, SPAN)
    group_loads = {order[0]: load_group(order[0])}
    load_wide = load(wide_hbm.at[front], wide.at[front])
    load_rest = []
    greet_others((barrier, barrier), True)

    def load_others():
        for g in order[1:]:
            group_loads[g] = load_group(g)
        load_rest.append(load(wide_hbm.at[rest], wide.at[rest]))
        load_rest.append(load(back_hbm, back))

    def prepare(g):
        if g not in ready:
            ready.add(g)
            for copy in group_loads[g]:
                copy.wait()
            cols = slice(g * SPAN, (g + 1) * SPAN)
            top, low_part = halves(BETA * mom[:, cols])
            xin[GRAD : GRAD + MINE, cols] = top
            xin[GRAD + MINE :, cols] = low_part

    def fold(v, count=2):
        v = v[:, :LANES] + v[:, LANES:]
        rows, mine = count * GRAD // 2, count * MINE // 2
        own = v[rows : rows + mine] + v[rows + mine :]
        return v[:rows].reshape(2 * count, NZL, NX, OWN, LANES), own.reshape(2 * count, OWN, LANES)

    def forward_rows(g, parts_of):
        base = g * SPAN

        def rows(start):
            cols = slice(base + start, base + start + LANES)
            if len(parts_of) == 2:
                return xin[:, cols]
            h, n, k = parts_of[0], GRAD // 2, MINE // 2
            spans = [(h * n, n), (GRAD + h * k, k), (GRAD + MINE + h * k, k)]
            return jnp.concatenate([xin[at : at + size, cols] for at, size in spans], axis=0)

        last = rows(HIGH)
        for t in range(7):
            both = jnp.concatenate([rows(t * LANES), last], axis=1)
            value, own = fold(dot(both, wide[t * 2 * LANES : (t + 1) * 2 * LANES]), len(parts_of))
            lanes = slice(t * LANES, (t + 1) * LANES)
            for i, h in enumerate(parts_of):
                mats = slice(2 * i, 2 * i + 2)
                if (g, 2 * h) in X_UNITS:
                    u = X_UNITS.index((g, 2 * h))
                    for m in range(2):
                        for k in range(NZL):
                            sx[u, :, k, m, :, lanes] = value[2 * i + m, k]
                    sx[u, x, z, :, :, lanes] += own[mats]
                else:
                    u = Z_UNITS.index((g, 2 * h))
                    for m in range(2):
                        for k in range(NZL):
                            sz[u, k, :, m, :, lanes] = value[2 * i + m, k]
                    sz[u, z, x, :, :, lanes] += own[mats]

    def forward(g):
        prepare(g)
        forward_rows(g, (0, 1))

    def forward_low(g):
        prepare(g)
        arrived(load_rest[0])
        value, own = fold(dot(xin[:, g * SPAN : (g + 1) * SPAN], wide[7 * 2 * LANES :]))
        lanes = slice(g * LANES, (g + 1) * LANES)
        lw[:, :, :, :, lanes] = value
        lw[:, z, x, :, lanes] += own

    way = lambda u: 1 if u % 2 == 0 else -1
    z_way = lambda u: -way(u)
    nx, nz = len(X_UNITS), len(Z_UNITS)
    X2, XAB, XZ = 0, nx, 2 * nx
    Z4, Z2, ZAB = 3 * nx, 3 * nx + nz, 3 * nx + 2 * nz
    LOW_A = 3 * nx + 3 * nz
    LOW_C, LOW_D, LOW_F = LOW_A + 1, LOW_A + 2, LOW_A + 3

    def x_start(u):
        d = way(u)
        send("x2", sx.at[u, xs[2]], xr2.at[u], device(dx=d), X2 + u)
        send("xa", sx.at[u, xs[-d]], xab.at[u, 0], device(dx=-d), XAB + u)

    def x_pass(u):
        d = way(u)
        received(xr2.at[u], X2 + u)
        sx[u, xs[d]] += xr2[u]
        send("xb", sx.at[u, xs[d]], xab.at[u, 1], device(dx=d), XAB + u)

    def x_cross(u):
        received(xab.at[u], XAB + u)
        sx[u, x] += xab[u, 0] + xab[u, 1]
        send("xz", sx.at[u, x, other_z], xrz.at[u], device(dz=1), XZ + u)

    def z_start(u):
        send("z4", sz.at[u, other_z], zr4.at[u], device(dz=1), Z4 + u)

    def z_cross(u):
        d = z_way(u)
        received(zr4.at[u], Z4 + u)
        sz[u, z] += zr4[u]
        send("z2", sz.at[u, z, xs[2]], zr2.at[u], device(dx=d), Z2 + u)
        send("za", sz.at[u, z, xs[-d]], zab.at[u, 0], device(dx=-d), ZAB + u)

    def z_pass(u):
        d = z_way(u)
        received(zr2.at[u], Z2 + u)
        sz[u, z, xs[d]] += zr2[u]
        send("zb", sz.at[u, z, xs[d]], zab.at[u, 1], device(dx=d), ZAB + u)

    def x_end(u):
        received(xrz.at[u], XZ + u)
        parts[X_UNITS[u]] = sx[u, x, z] + xrz[u]

    def z_end(u):
        received(zab.at[u], ZAB + u)
        parts[Z_UNITS[u]] = sz[u, z, x] + (zab[u, 0] + zab[u, 1])

    stores = []

    def store(src, dst):
        copy = pltpu.make_async_copy(src, dst, store_sem.at[len(stores)])
        copy.start()
        stores.append(copy)

    def backward(g):
        arrived(load_rest[1])
        field = jnp.concatenate([parts[k] for k in sorted(parts) if k[0] == g], axis=0).reshape(MINE, HIGH)
        last = jnp.zeros((MINE, LANES), F32)
        for t in range(7):
            top, rest = halves(field[:, t * LANES : (t + 1) * LANES])
            v = dot(jnp.concatenate([top, rest], axis=0), back[t * LANES : (t + 1) * LANES])
            v = v[:MINE, : 2 * LANES] + (v[MINE:, : 2 * LANES] + v[:MINE, 2 * LANES :])
            base = g * SPAN + t * LANES
            nm[:, base : base + LANES] = v[:, :LANES]
            last += v[:, LANES:]
        nm[:, g * SPAN + HIGH : (g + 1) * SPAN] = last
        cols = pl.ds(g * SPAN, SPAN)
        store(nm.at[:, cols], new_out.at[:, cols])

    def low_a(_):
        @pl.when(column_later > 0)
        def _():
            pl.semaphore_wait(column_sem, column_later)

        for k, (dy, dc) in enumerate(column):
            send("la", lw.at[ys[dy], other_core if dc else core], la.at[k], device(dy=dy, dcore=dc), LOW_A)

    def low_d(_):
        received(la, LOW_A)
        lw[y, core] += ((la[0] + la[1]) + (la[2] + la[3])) + ((la[4] + la[5]) + la[6])
        for d in (1, 2, 3):
            send("lc", lw.at[y, core, xs[d]], lc.at[d - 1], device(dx=d), LOW_C)

    def low_e(_):
        received(lc, LOW_C)
        es[...] = lw[y, core, x] + (lc[0] + lc[1] + lc[2])

        @pl.when(stack_later > 0)
        def _():
            pl.semaphore_wait(stack_sem, stack_later)

        @pl.when(core == z)
        def _():
            for d in (1, 2, 3):
                send("ld", es, le.at[d - 1], device(dzh=d), LOW_D)

        @pl.when(core != z)
        def _():
            for d in range(4):
                send("ld", es, le.at[3 + d], device(dzh=d, dz=1), LOW_D)

    def low_i(_):
        @pl.when(core == z)
        def _():
            received(le, LOW_D)
            total[y] = es[...] + ((le[0] + le[1] + le[2]) + (le[3] + le[4] + le[5] + le[6]))
            for dy, dc in column:
                send("lf", total.at[y], total.at[y], device(dy=dy, dcore=dc), LOW_F)

    def low_end():
        arrived(load_rest[1])

        @pl.when(core == z)
        def _():
            received(total.at[pl.ds(0, 3)], LOW_F)

        @pl.when(core != z)
        def _():
            received(total, LOW_F)

    def normalise(_):
        low_end()
        table = lambda i: back[(7 + i) * LANES : (8 + i) * LANES]
        count = GROUPS * MINE
        mean = jnp.concatenate(
            [total[:, :, g * LANES : (g + 1) * LANES].reshape(MINE, LANES) for g in range(GROUPS)], axis=0
        ) * (1.0 / N_REP)
        top, rest = halves(mean)
        pair = jnp.concatenate([top, rest], axis=0)
        squares = jnp.concatenate(halves(mean * mean), axis=0)
        for h in range(2):
            v, w = dot(pair, table(h)), dot(squares, table(4 + h))
            field = v[:count] + (v[count:] + dot(top, table(2 + h)))
            square = w[:count] + w[count:]
            value = field * lax.rsqrt(field * field + square + EPS)
            for g in range(GROUPS):
                base = g * SPAN + h * WIDE
                up[:, base : base + WIDE] = value[g * MINE : (g + 1) * MINE]
        store(up, upd_out)

    steps = {
        "F": forward, "FL": forward_low,
        "XS": x_start, "XP": x_pass, "XC": x_cross, "XE": x_end,
        "ZS": z_start, "ZC": z_cross, "ZP": z_pass, "ZE": z_end,
        "LA": low_a, "LC": low_d, "LD": low_e, "LF": low_i,
        "N": normalise, "BK": backward,
    }
    first = EARLY[0][1]
    prepare(first)
    arrived(load_wide)
    load_others()
    before = set(ready), set(waited)

    def run(plan):
        ready.clear()
        ready.update(before[0])
        waited.clear()
        waited.update(before[1])
        parts.clear()
        stores.clear()
        answered = False
        half = X_UNITS[plan[1][1]][1] // 2
        forward_rows(first, (half,))
        enter()
        for name, u in plan[1:]:
            if not answered and name not in ("XS", "ZS"):
                greet_others((column_sem, stack_sem), False)
                answered = True
            steps[name](u)
            if (name, u) == plan[1]:
                forward_rows(first, (1 - half,))
        all_sent("x2", xr2)
        all_sent("xa", xr2)
        all_sent("xb", xr2)
        all_sent("xz", xrz)
        all_sent("z4", zr4)
        all_sent("z2", zr2)
        all_sent("za", zr2)
        all_sent("zb", zr2)
        all_sent("la", la)
        all_sent("lc", lc)

        @pl.when(core != z)
        def _():
            all_sent("ld", le.at[pl.ds(0, 4)])

        @pl.when(core == z)
        def _():
            all_sent("ld", le.at[pl.ds(0, 3)])
            all_sent("lf", le)

        for copy in stores:
            copy.wait()

    @pl.when(zh == 0)
    def _():
        run(EARLY)

    @pl.when(zh > 0)
    def _():
        run(LATE)


def write_out(new_in, upd_in, new_out, upd_out, sems):
    copies = []
    for k, (src, dst) in enumerate([(new_in, new_out), (upd_in, upd_out)]):
        for m in range(MATS):
            rows = pl.ds(m * OWN, OWN)
            copies.append(pltpu.make_async_copy(src.at[rows], dst.at[rows], sems.at[k, m]))
    for copy in copies:
        copy.start()
    for copy in copies:
        copy.wait()


def per_device(gradients, momentum):
    wide, back = tables()
    anywhere = pl.BlockSpec(memory_space=pl.ANY)
    new_momentum, update = pl.pallas_call(
        kernel,
        out_shape=[jax.ShapeDtypeStruct((MINE, D), F32)] * 2,
        in_specs=[anywhere] * 4,
        out_specs=[anywhere] * 2,
        scratch_shapes=[
            pltpu.VMEM((GRAD + 2 * MINE, D), BF16),
            pltpu.VMEM((MINE, D), F32),
            pltpu.VMEM(wide.shape, BF16),
            pltpu.VMEM(back.shape, BF16),
            pltpu.VMEM((len(X_UNITS), NX, NZL, 2, OWN, HIGH), F32),
            pltpu.VMEM((len(Z_UNITS), NZL, NX, 2, OWN, HIGH), F32),
            pltpu.VMEM((MATS, NZL, NX, OWN, LOW), F32),
            pltpu.VMEM((len(X_UNITS), NZL, 2, OWN, HIGH), F32),
            pltpu.VMEM((len(X_UNITS), 2, NZL, 2, OWN, HIGH), F32),
            pltpu.VMEM((len(X_UNITS), 2, OWN, HIGH), F32),
            pltpu.VMEM((len(Z_UNITS), NX, 2, OWN, HIGH), F32),
            pltpu.VMEM((len(Z_UNITS), 2, OWN, HIGH), F32),
            pltpu.VMEM((len(Z_UNITS), 2, 2, OWN, HIGH), F32),
            pltpu.VMEM((7, NX, OWN, LOW), F32),
            pltpu.VMEM((3, OWN, LOW), F32),
            pltpu.VMEM((7, OWN, LOW), F32),
            pltpu.VMEM((OWN, LOW), F32),
            pltpu.VMEM((MATS, OWN, LOW), F32),
            pltpu.VMEM((MINE, D), F32),
            pltpu.VMEM((MINE, D), F32),
            pltpu.SemaphoreType.DMA((2 * GROUPS + 3,)),
            pltpu.SemaphoreType.DMA((GROUPS + 1,)),
            pltpu.SemaphoreType.DMA((len(SENDS),)),
            pltpu.SemaphoreType.DMA((3 * len(X_UNITS) + 3 * len(Z_UNITS) + 4,)),
            pltpu.SemaphoreType.REGULAR,
            pltpu.SemaphoreType.REGULAR,
        ],
        compiler_params=pltpu.CompilerParams(
            collective_id=0, has_side_effects=True, vmem_limit_bytes=(52 * 1024 + 384) * 1024
        ),
        cost_estimate=pl.CostEstimate(flops=2_000_000_000, bytes_accessed=8_000_000, transcendentals=200_000),
    )(gradients.reshape(GRAD, D), momentum.reshape(MINE, D), wide, back)
    new_momentum, update = pl.pallas_call(
        write_out,
        out_shape=[jax.ShapeDtypeStruct((MINE, D), F32)] * 2,
        in_specs=[anywhere] * 2,
        out_specs=[anywhere] * 2,
        scratch_shapes=[pltpu.SemaphoreType.DMA((2, 4))],
        compiler_params=pltpu.CompilerParams(vmem_limit_bytes=4 * 1024 * 1024),
        cost_estimate=pl.CostEstimate(flops=0, bytes_accessed=2_600_000, transcendentals=0),
    )(new_momentum, update)
    return new_momentum.reshape(1, MATS, OWN, D), update.reshape(MATS, OWN, D)


def solution(mesh):
    return jax.shard_map(
        per_device,
        mesh=mesh,
        in_specs=(P("rep", "fsdp", None, None, None), P("rep", None, "fsdp", None)),
        out_specs=(P("rep", None, "fsdp", None), P(None, "fsdp", None)),
        check_vma=False,
    )
```

```python
import jax
import jax.numpy as jnp
import ml_dtypes
import numpy as np
from jax import lax
from jax.experimental import pallas as pl
from jax.experimental.pallas import tpu as pltpu
from jax.sharding import PartitionSpec as P

D, MATS, GROUP, KEEP, ROWS = 5120, 4, 64, 8, 64
BETA, EPS = 0.999, 1e-06
NX, NY, NZL, NZH, NC, N_REP = 4, 4, 2, 4, 2, 32
OWN = 8
LANES = 128
TILES = 8
SPAN = LANES * TILES
GROUPS = D // SPAN
HIGH = 7 * LANES
LOW = GROUPS * LANES
GRAD = MATS * ROWS
MINE = MATS * OWN
WIDE = 4 * LANES

F32, BF16 = jnp.float32, jnp.bfloat16
MESH = pl.DeviceIdType.MESH


def split(table):
    high = table.astype(ml_dtypes.bfloat16)
    low = (table - high.astype(np.float64)).astype(ml_dtypes.bfloat16)
    return high, low


def tables():
    n, k = np.arange(GROUP), np.arange(GROUP)[:, None]
    basis = np.sqrt(2.0 / GROUP) * np.cos(np.pi * (n + 0.5) * k / GROUP)
    basis[0] *= np.sqrt(0.5)
    rest = GROUP - KEEP
    high = np.zeros((LANES, 2 * rest))
    for b in range(2):
        high[b * GROUP : (b + 1) * GROUP, b * rest : (b + 1) * rest] = basis[KEEP:].T
    forward = np.zeros((7, 2 * LANES, LANES))
    for t in range(7):
        forward[t, :LANES, : 2 * rest] = high
        forward[t, LANES:, 2 * rest :] = high[:, 16 * t : 16 * t + 16]
    inverse = np.zeros((7, LANES, 2 * LANES))
    for t in range(7):
        inverse[t] = forward[t].T
    blocks = SPAN // GROUP
    keep = np.zeros((SPAN, LANES))
    mean = np.zeros((LANES, SPAN))
    for c in range(blocks):
        keep[c * GROUP : (c + 1) * GROUP, c * KEEP : (c + 1) * KEEP] = basis[:KEEP].T
        mean[c * KEEP : (c + 1) * KEEP, c * GROUP : (c + 1) * GROUP] = 1.0 / GROUP
    both = lambda table: np.concatenate(split(table), axis=-1)
    wide = np.concatenate([both(forward).reshape(-1, 2 * LANES), both(keep)], axis=0)
    back = np.concatenate([both(keep.T), mean.astype(ml_dtypes.bfloat16)], axis=-1)
    back = back.reshape(LANES, 6, WIDE).transpose(1, 0, 2).reshape(-1, WIDE)
    return wide, np.concatenate([both(inverse).reshape(-1, WIDE), back], axis=0)


def halves(value):
    top = value.astype(BF16)
    return top, (value - top.astype(F32)).astype(BF16)


def dot(a, b):
    return jnp.dot(a, b, preferred_element_type=F32)


X_UNITS = [(2, 0), (2, 2), (3, 0), (3, 2), (4, 0), (4, 2)]
Z_UNITS = [(0, 0), (0, 2), (1, 0), (1, 2)]
SENDS = ["x2", "xa", "xb", "xz", "z4", "z2", "za", "zb", "la", "lc", "ld", "lf"]
EARLY = [
    ("F", 2), ("XS", 1), ("F", 1), ("ZS", 3), ("FL", 1), ("XS", 0),
    ("F", 4), ("FL", 2), ("ZS", 2), ("XS", 4), ("FL", 4), ("FL", 0),
    ("FL", 3), ("LA", 0), ("XS", 5), ("F", 0), ("XP", 1), ("XP", 0),
    ("ZS", 1), ("F", 3), ("ZC", 3), ("XS", 2), ("XC", 1), ("XP", 5),
    ("ZS", 0), ("ZP", 3), ("LC", 0), ("XP", 4), ("XP", 2), ("XS", 3),
    ("ZC", 1), ("ZC", 2), ("LD", 0), ("XC", 0), ("XC", 5), ("ZE", 3),
    ("XE", 1), ("XP", 3), ("XC", 4), ("ZC", 0), ("XC", 2), ("ZP", 2),
    ("XE", 0), ("BK", 2), ("LF", 0), ("XC", 3), ("ZP", 1), ("XE", 5),
    ("ZP", 0), ("XE", 4), ("BK", 4), ("ZE", 2), ("BK", 1), ("XE", 2),
    ("XE", 3), ("BK", 3), ("ZE", 1), ("ZE", 0), ("BK", 0), ("N", 0),
]
LATE = [
    ("F", 2), ("XS", 0), ("F", 1), ("ZS", 3), ("FL", 2), ("FL", 1),
    ("XS", 1), ("FL", 4), ("FL", 3), ("FL", 0), ("LA", 0), ("XP", 0),
    ("F", 3), ("XS", 3), ("ZS", 2), ("XP", 1), ("F", 0), ("LC", 0),
    ("XS", 2), ("ZS", 1), ("ZC", 3), ("F", 4), ("XS", 4), ("XP", 2),
    ("XC", 1), ("LD", 0), ("XS", 5), ("XP", 3), ("ZC", 1), ("ZS", 0),
    ("XC", 0), ("XE", 1), ("XP", 4), ("ZC", 2), ("XP", 5), ("ZP", 3),
    ("XC", 2), ("LF", 0), ("ZP", 1), ("XC", 3), ("ZC", 0), ("ZP", 2),
    ("XE", 0), ("BK", 2), ("XC", 4), ("XE", 2), ("XC", 5), ("XE", 3),
    ("ZP", 0), ("N", 0), ("BK", 3), ("XE", 4), ("ZE", 3), ("ZE", 2),
    ("BK", 1), ("ZE", 1), ("XE", 5), ("BK", 4), ("ZE", 0), ("BK", 0),
]


def kernel(
    grads, momentum, wide_hbm, back_hbm, new_out, upd_out,
    xin, mom, wide, back, sx, sz, lw,
    xr2, xab, xrz, zr4, zr2, zab,
    la, lc, le, es, total, nm, up,
    load_sem, store_sem, send_sem, recv_sem, column_sem, stack_sem,
):
    rep, fsdp = lax.axis_index("rep"), lax.axis_index("fsdp")
    core, y, zh = lax.rem(rep, 2), lax.rem(lax.div(rep, 2), 4), lax.div(rep, 8)
    x, z = lax.rem(fsdp, 4), lax.div(fsdp, 4)

    def ring(v, d):
        return lax.rem(v + (d + 4), 4)

    xs, ys, zs = ([v] + [ring(v, d) for d in (1, 2, 3)] for v in (x, y, zh))
    other_core, other_z = 1 - core, 1 - z
    own_rep, own_fsdp = rep, fsdp
    places = {}

    def device(dzh=0, dy=0, dcore=0, dz=0, dx=0):
        key = (dzh, dy % 4, dcore, dz, dx % 4)
        if key not in places:
            c2, z2 = other_core if dcore else core, other_z if dz else z
            moved = dzh or dy or dcore
            r2 = (zs[dzh] * 4 + ys[dy % 4]) * 2 + c2 if moved else own_rep
            places[key] = (r2, z2 * 4 + xs[dx % 4] if dz or dx else own_fsdp)
        return places[key]

    for dy in range(4):
        for dc in range(2):
            device(dy=dy, dcore=dc)
    for d in range(4):
        for dz in range(2):
            device(dzh=d, dz=dz)
        device(dx=d)

    column = [(dy, dc) for dy in range(4) for dc in range(2) if dy or dc]
    barrier = pltpu.get_barrier_semaphore()

    def greet(sem, p):
        pl.semaphore_signal(sem, inc=1, device_id=p, device_id_type=MESH)

    def later_in_column(dy, dc):
        if dy:
            return ring(y, dy) > y
        return core == 1

    def later_in_stack(d):
        return ring(zh, d) > zh

    def greet_others(sem_of, later):
        def where(test, sem, places):
            @pl.when(test if later else jnp.logical_not(test))
            def _():
                for place in places:
                    greet(sem, place)

        for d in range(4):
            cores = range(2) if d else (1,)
            where(later_in_column(d, 1), sem_of[0], [device(dy=d, dcore=dc) for dc in cores])
        for d in (1, 2, 3):
            where(later_in_stack(d), sem_of[1], [device(dzh=d, dz=dz) for dz in range(2)])

    for d in (1, 2, 3):
        greet(barrier, device(dx=d))
    greet(barrier, device(dz=1))
    column_later = 2 * (3 - y) + core
    stack_later = 2 * (3 - zh)

    def enter():
        pl.semaphore_wait(barrier, 4 + (7 - column_later) + (6 - stack_later))
    def remote(kind, src, dst, to, recv):
        return pltpu.make_async_remote_copy(
            src_ref=src, dst_ref=dst, send_sem=send_sem.at[SENDS.index(kind)],
            recv_sem=recv_sem.at[recv], device_id=to, device_id_type=MESH,
        )

    def send(kind, src, dst, to, recv):
        remote(kind, src, dst, to, recv).start()

    def await_bytes(ref, sem):
        pltpu.make_async_copy(ref, ref, sem).wait()

    def received(ref, recv):
        await_bytes(ref, recv_sem.at[recv])

    def all_sent(kind, ref):
        await_bytes(ref, send_sem.at[SENDS.index(kind)])

    loads = []

    def load(src, dst):
        copy = pltpu.make_async_copy(src, dst, load_sem.at[len(loads)])
        copy.start()
        loads.append(copy)
        return copy

    waited, ready, parts = set(), set(), {}

    def arrived(copy):
        if id(copy) not in waited:
            waited.add(id(copy))
            copy.wait()

    def load_group(g):
        cols = pl.ds(g * SPAN, SPAN)
        return load(momentum.at[:, cols], mom.at[:, cols]), load(grads.at[:, cols], xin.at[pl.ds(0, GRAD), cols])

    order = [g for name, g in EARLY if name == "F"]
    front = pl.ds(0, 7 * 2 * LANES)
    rest = pl.ds(7 * 2 * LANES, SPAN)
    group_loads = {order[0]: load_group(order[0])}
    load_wide = load(wide_hbm.at[front], wide.at[front])
    load_rest = []
    greet_others((barrier, barrier), True)

    def load_others():
        for g in order[1:]:
            group_loads[g] = load_group(g)
        load_rest.append(load(wide_hbm.at[rest], wide.at[rest]))
        load_rest.append(load(back_hbm, back))

    def prepare(g):
        if g not in ready:
            ready.add(g)
            for copy in group_loads[g]:
                copy.wait()
            cols = slice(g * SPAN, (g + 1) * SPAN)
            top, low_part = halves(BETA * mom[:, cols])
            xin[GRAD : GRAD + MINE, cols] = top
            xin[GRAD + MINE :, cols] = low_part

    def fold(v, count=2):
        v = v[:, :LANES] + v[:, LANES:]
        rows, mine = count * GRAD // 2, count * MINE // 2
        own = v[rows : rows + mine] + v[rows + mine :]
        return v[:rows].reshape(2 * count, NZL, NX, OWN, LANES), own.reshape(2 * count, OWN, LANES)

    def forward_rows(g, parts_of):
        base = g * SPAN

        def rows(start):
            cols = slice(base + start, base + start + LANES)
            if len(parts_of) == 2:
                return xin[:, cols]
            h, n, k = parts_of[0], GRAD // 2, MINE // 2
            spans = [(h * n, n), (GRAD + h * k, k), (GRAD + MINE + h * k, k)]
            return jnp.concatenate([xin[at : at + size, cols] for at, size in spans], axis=0)

        last = rows(HIGH)
        for t in range(7):
            both = jnp.concatenate([rows(t * LANES), last], axis=1)
            value, own = fold(dot(both, wide[t * 2 * LANES : (t + 1) * 2 * LANES]), len(parts_of))
            lanes = slice(t * LANES, (t + 1) * LANES)
            for i, h in enumerate(parts_of):
                mats = slice(2 * i, 2 * i + 2)
                if (g, 2 * h) in X_UNITS:
                    u = X_UNITS.index((g, 2 * h))
                    for m in range(2):
                        for k in range(NZL):
                            sx[u, :, k, m, :, lanes] = value[2 * i + m, k]
                    sx[u, x, z, :, :, lanes] += own[mats]
                else:
                    u = Z_UNITS.index((g, 2 * h))
                    for m in range(2):
                        for k in range(NZL):
                            sz[u, k, :, m, :, lanes] = value[2 * i + m, k]
                    sz[u, z, x, :, :, lanes] += own[mats]

    def forward(g):
        prepare(g)
        forward_rows(g, (0, 1))

    def forward_low(g):
        prepare(g)
        arrived(load_rest[0])
        value, own = fold(dot(xin[:, g * SPAN : (g + 1) * SPAN], wide[7 * 2 * LANES :]))
        lanes = slice(g * LANES, (g + 1) * LANES)
        lw[:, :, :, :, lanes] = value
        lw[:, z, x, :, lanes] += own

    way = lambda u: 1 if u % 2 == 0 else -1
    z_way = lambda u: -way(u)
    nx, nz = len(X_UNITS), len(Z_UNITS)
    X2, XAB, XZ = 0, nx, 2 * nx
    Z4, Z2, ZAB = 3 * nx, 3 * nx + nz, 3 * nx + 2 * nz
    LOW_A = 3 * nx + 3 * nz
    LOW_C, LOW_D, LOW_F = LOW_A + 1, LOW_A + 2, LOW_A + 3

    def x_start(u):
        d = way(u)
        send("x2", sx.at[u, xs[2]], xr2.at[u], device(dx=d), X2 + u)
        send("xa", sx.at[u, xs[-d]], xab.at[u, 0], device(dx=-d), XAB + u)

    def x_pass(u):
        d = way(u)
        received(xr2.at[u], X2 + u)
        sx[u, xs[d]] += xr2[u]
        send("xb", sx.at[u, xs[d]], xab.at[u, 1], device(dx=d), XAB + u)

    def x_cross(u):
        received(xab.at[u], XAB + u)
        sx[u, x] += xab[u, 0] + xab[u, 1]
        send("xz", sx.at[u, x, other_z], xrz.at[u], device(dz=1), XZ + u)

    def z_start(u):
        send("z4", sz.at[u, other_z], zr4.at[u], device(dz=1), Z4 + u)

    def z_cross(u):
        d = z_way(u)
        received(zr4.at[u], Z4 + u)
        sz[u, z] += zr4[u]
        send("z2", sz.at[u, z, xs[2]], zr2.at[u], device(dx=d), Z2 + u)
        send("za", sz.at[u, z, xs[-d]], zab.at[u, 0], device(dx=-d), ZAB + u)

    def z_pass(u):
        d = z_way(u)
        received(zr2.at[u], Z2 + u)
        sz[u, z, xs[d]] += zr2[u]
        send("zb", sz.at[u, z, xs[d]], zab.at[u, 1], device(dx=d), ZAB + u)

    def x_end(u):
        received(xrz.at[u], XZ + u)
        parts[X_UNITS[u]] = sx[u, x, z] + xrz[u]

    def z_end(u):
        received(zab.at[u], ZAB + u)
        parts[Z_UNITS[u]] = sz[u, z, x] + (zab[u, 0] + zab[u, 1])

    stores = []

    def store(src, dst):
        copy = pltpu.make_async_copy(src, dst, store_sem.at[len(stores)])
        copy.start()
        stores.append(copy)

    def backward(g):
        arrived(load_rest[1])
        field = jnp.concatenate([parts[k] for k in sorted(parts) if k[0] == g], axis=0).reshape(MINE, HIGH)
        last = jnp.zeros((MINE, LANES), F32)
        for t in range(7):
            top, rest = halves(field[:, t * LANES : (t + 1) * LANES])
            v = dot(jnp.concatenate([top, rest], axis=0), back[t * LANES : (t + 1) * LANES])
            v = v[:MINE, : 2 * LANES] + (v[MINE:, : 2 * LANES] + v[:MINE, 2 * LANES :])
            base = g * SPAN + t * LANES
            nm[:, base : base + LANES] = v[:, :LANES]
            last += v[:, LANES:]
        nm[:, g * SPAN + HIGH : (g + 1) * SPAN] = last
        cols = pl.ds(g * SPAN, SPAN)
        store(nm.at[:, cols], new_out.at[:, cols])

    def low_a(_):
        @pl.when(column_later > 0)
        def _():
            pl.semaphore_wait(column_sem, column_later)

        for k, (dy, dc) in enumerate(column):
            send("la", lw.at[ys[dy], other_core if dc else core], la.at[k], device(dy=dy, dcore=dc), LOW_A)

    def low_d(_):
        received(la, LOW_A)
        lw[y, core] += ((la[0] + la[1]) + (la[2] + la[3])) + ((la[4] + la[5]) + la[6])
        for d in (1, 2, 3):
            send("lc", lw.at[y, core, xs[d]], lc.at[d - 1], device(dx=d), LOW_C)

    def low_e(_):
        received(lc, LOW_C)
        es[...] = lw[y, core, x] + (lc[0] + lc[1] + lc[2])

        @pl.when(stack_later > 0)
        def _():
            pl.semaphore_wait(stack_sem, stack_later)

        @pl.when(core == z)
        def _():
            for d in (1, 2, 3):
                send("ld", es, le.at[d - 1], device(dzh=d), LOW_D)

        @pl.when(core != z)
        def _():
            for d in range(4):
                send("ld", es, le.at[3 + d], device(dzh=d, dz=1), LOW_D)

    def low_i(_):
        @pl.when(core == z)
        def _():
            received(le, LOW_D)
            total[y] = es[...] + ((le[0] + le[1] + le[2]) + (le[3] + le[4] + le[5] + le[6]))
            for dy, dc in column:
                send("lf", total.at[y], total.at[y], device(dy=dy, dcore=dc), LOW_F)

    def low_end():
        arrived(load_rest[1])

        @pl.when(core == z)
        def _():
            received(total.at[pl.ds(0, 3)], LOW_F)

        @pl.when(core != z)
        def _():
            received(total, LOW_F)

    def normalise(_):
        low_end()
        table = lambda i: back[(7 + i) * LANES : (8 + i) * LANES]
        count = GROUPS * MINE
        mean = jnp.concatenate(
            [total[:, :, g * LANES : (g + 1) * LANES].reshape(MINE, LANES) for g in range(GROUPS)], axis=0
        ) * (1.0 / N_REP)
        top, rest = halves(mean)
        pair = jnp.concatenate([top, rest], axis=0)
        squares = jnp.concatenate(halves(mean * mean), axis=0)
        for h in range(2):
            v, w = dot(pair, table(h)), dot(squares, table(4 + h))
            field = v[:count] + (v[count:] + dot(top, table(2 + h)))
            square = w[:count] + w[count:]
            value = field * lax.rsqrt(field * field + square + EPS)
            for g in range(GROUPS):
                base = g * SPAN + h * WIDE
                up[:, base : base + WIDE] = value[g * MINE : (g + 1) * MINE]
        store(up, upd_out)

    steps = {
        "F": forward, "FL": forward_low,
        "XS": x_start, "XP": x_pass, "XC": x_cross, "XE": x_end,
        "ZS": z_start, "ZC": z_cross, "ZP": z_pass, "ZE": z_end,
        "LA": low_a, "LC": low_d, "LD": low_e, "LF": low_i,
        "N": normalise, "BK": backward,
    }
    first = EARLY[0][1]
    prepare(first)
    arrived(load_wide)
    load_others()
    before = set(ready), set(waited)

    def run(plan):
        ready.clear()
        ready.update(before[0])
        waited.clear()
        waited.update(before[1])
        parts.clear()
        stores.clear()
        answered = False
        half = X_UNITS[plan[1][1]][1] // 2
        forward_rows(first, (half,))
        enter()
        for name, u in plan[1:]:
            if not answered and name not in ("XS", "ZS"):
                greet_others((column_sem, stack_sem), False)
                answered = True
            steps[name](u)
            if (name, u) == plan[1]:
                forward_rows(first, (1 - half,))
        all_sent("x2", xr2)
        all_sent("xa", xr2)
        all_sent("xb", xr2)
        all_sent("xz", xrz)
        all_sent("z4", zr4)
        all_sent("z2", zr2)
        all_sent("za", zr2)
        all_sent("zb", zr2)
        all_sent("la", la)
        all_sent("lc", lc)

        @pl.when(core != z)
        def _():
            all_sent("ld", le.at[pl.ds(0, 4)])

        @pl.when(core == z)
        def _():
            all_sent("ld", le.at[pl.ds(0, 3)])
            all_sent("lf", le)

        for copy in stores:
            copy.wait()

    @pl.when(zh == 0)
    def _():
        run(EARLY)

    @pl.when(zh > 0)
    def _():
        run(LATE)


def write_out(new_in, upd_in, new_out, upd_out, sems):
    copies = []
    for k, (src, dst) in enumerate([(new_in, new_out), (upd_in, upd_out)]):
        for m in range(MATS):
            rows = pl.ds(m * OWN, OWN)
            copies.append(pltpu.make_async_copy(src.at[rows], dst.at[rows], sems.at[k, m]))
    for copy in copies:
        copy.start()
    for copy in copies:
        copy.wait()


def per_device(gradients, momentum):
    wide, back = tables()
    anywhere = pl.BlockSpec(memory_space=pl.ANY)
    new_momentum, update = pl.pallas_call(
        kernel,
        out_shape=[jax.ShapeDtypeStruct((MINE, D), F32)] * 2,
        in_specs=[anywhere] * 4,
        out_specs=[anywhere] * 2,
        scratch_shapes=[
            pltpu.VMEM((GRAD + 2 * MINE, D), BF16),
            pltpu.VMEM((MINE, D), F32),
            pltpu.VMEM(wide.shape, BF16),
            pltpu.VMEM(back.shape, BF16),
            pltpu.VMEM((len(X_UNITS), NX, NZL, 2, OWN, HIGH), F32),
            pltpu.VMEM((len(Z_UNITS), NZL, NX, 2, OWN, HIGH), F32),
            pltpu.VMEM((MATS, NZL, NX, OWN, LOW), F32),
            pltpu.VMEM((len(X_UNITS), NZL, 2, OWN, HIGH), F32),
            pltpu.VMEM((len(X_UNITS), 2, NZL, 2, OWN, HIGH), F32),
            pltpu.VMEM((len(X_UNITS), 2, OWN, HIGH), F32),
            pltpu.VMEM((len(Z_UNITS), NX, 2, OWN, HIGH), F32),
            pltpu.VMEM((len(Z_UNITS), 2, OWN, HIGH), F32),
            pltpu.VMEM((len(Z_UNITS), 2, 2, OWN, HIGH), F32),
            pltpu.VMEM((7, NX, OWN, LOW), F32),
            pltpu.VMEM((3, OWN, LOW), F32),
            pltpu.VMEM((7, OWN, LOW), F32),
            pltpu.VMEM((OWN, LOW), F32),
            pltpu.VMEM((MATS, OWN, LOW), F32),
            pltpu.VMEM((MINE, D), F32),
            pltpu.VMEM((MINE, D), F32),
            pltpu.SemaphoreType.DMA((2 * GROUPS + 3,)),
            pltpu.SemaphoreType.DMA((GROUPS + 1,)),
            pltpu.SemaphoreType.DMA((len(SENDS),)),
            pltpu.SemaphoreType.DMA((3 * len(X_UNITS) + 3 * len(Z_UNITS) + 4,)),
            pltpu.SemaphoreType.REGULAR,
            pltpu.SemaphoreType.REGULAR,
        ],
        compiler_params=pltpu.CompilerParams(
            collective_id=0, has_side_effects=True, vmem_limit_bytes=(52 * 1024 + 384) * 1024
        ),
        cost_estimate=pl.CostEstimate(flops=2_000_000_000, bytes_accessed=8_000_000, transcendentals=200_000),
    )(gradients.reshape(GRAD, D), momentum.reshape(MINE, D), wide, back)
    new_momentum, update = pl.pallas_call(
        write_out,
        out_shape=[jax.ShapeDtypeStruct((MINE, D), F32)] * 2,
        in_specs=[anywhere] * 2,
        out_specs=[anywhere] * 2,
        scratch_shapes=[pltpu.SemaphoreType.DMA((2, 4))],
        compiler_params=pltpu.CompilerParams(vmem_limit_bytes=4 * 1024 * 1024),
        cost_estimate=pl.CostEstimate(flops=0, bytes_accessed=2_600_000, transcendentals=0),
    )(new_momentum, update)
    return new_momentum.reshape(1, MATS, OWN, D), update.reshape(MATS, OWN, D)


def solution(mesh):
    return jax.shard_map(
        per_device,
        mesh=mesh,
        in_specs=(P("rep", "fsdp", None, None, None), P("rep", None, "fsdp", None)),
        out_specs=(P("rep", None, "fsdp", None), P(None, "fsdp", None)),
        check_vma=False,
    )
```

```python
import jax
import jax.numpy as jnp
import ml_dtypes
import numpy as np
from jax import lax
from jax.experimental import pallas as pl
from jax.experimental.pallas import tpu as pltpu
from jax.sharding import PartitionSpec as P

D, MATS, GROUP, KEEP, ROWS = 5120, 4, 64, 8, 64
BETA, EPS = 0.999, 1e-06
NX, NY, NZL, NZH, NC, N_REP = 4, 4, 2, 4, 2, 32
OWN = 8
LANES = 128
TILES = 8
SPAN = LANES * TILES
GROUPS = D // SPAN
HIGH = 7 * LANES
LOW = GROUPS * LANES
GRAD = MATS * ROWS
MINE = MATS * OWN
WIDE = 4 * LANES

F32, BF16 = jnp.float32, jnp.bfloat16
MESH = pl.DeviceIdType.MESH


def split(table):
    high = table.astype(ml_dtypes.bfloat16)
    low = (table - high.astype(np.float64)).astype(ml_dtypes.bfloat16)
    return high, low


def tables():
    n, k = np.arange(GROUP), np.arange(GROUP)[:, None]
    basis = np.sqrt(2.0 / GROUP) * np.cos(np.pi * (n + 0.5) * k / GROUP)
    basis[0] *= np.sqrt(0.5)
    rest = GROUP - KEEP
    high = np.zeros((LANES, 2 * rest))
    for b in range(2):
        high[b * GROUP : (b + 1) * GROUP, b * rest : (b + 1) * rest] = basis[KEEP:].T
    forward = np.zeros((7, 2 * LANES, LANES))
    for t in range(7):
        forward[t, :LANES, : 2 * rest] = high
        forward[t, LANES:, 2 * rest :] = high[:, 16 * t : 16 * t + 16]
    inverse = np.zeros((7, LANES, 2 * LANES))
    for t in range(7):
        inverse[t] = forward[t].T
    blocks = SPAN // GROUP
    keep = np.zeros((SPAN, LANES))
    mean = np.zeros((LANES, SPAN))
    for c in range(blocks):
        keep[c * GROUP : (c + 1) * GROUP, c * KEEP : (c + 1) * KEEP] = basis[:KEEP].T
        mean[c * KEEP : (c + 1) * KEEP, c * GROUP : (c + 1) * GROUP] = 1.0 / GROUP
    both = lambda table: np.concatenate(split(table), axis=-1)
    wide = np.concatenate([both(forward).reshape(-1, 2 * LANES), both(keep)], axis=0)
    back = np.concatenate([both(keep.T), mean.astype(ml_dtypes.bfloat16)], axis=-1)
    back = back.reshape(LANES, 6, WIDE).transpose(1, 0, 2).reshape(-1, WIDE)
    return wide, np.concatenate([both(inverse).reshape(-1, WIDE), back], axis=0)


def halves(value):
    top = value.astype(BF16)
    return top, (value - top.astype(F32)).astype(BF16)


def dot(a, b):
    return jnp.dot(a, b, preferred_element_type=F32)


X_UNITS = [(2, 0), (2, 2), (3, 0), (3, 2), (4, 0), (4, 2)]
Z_UNITS = [(0, 0), (0, 2), (1, 0), (1, 2)]
SENDS = ["x2", "xa", "xb", "xz", "z4", "z2", "za", "zb", "la", "lc", "ld", "lf"]
EARLY = [
    ("F", 2), ("XS", 1), ("F", 1), ("ZS", 3), ("FL", 1), ("XS", 0),
    ("F", 4), ("FL", 2), ("ZS", 2), ("XS", 4), ("FL", 4), ("FL", 0),
    ("FL", 3), ("LA", 0), ("XS", 5), ("F", 0), ("XP", 1), ("XP", 0),
    ("ZS", 1), ("F", 3), ("ZC", 3), ("XS", 2), ("XC", 1), ("XP", 5),
    ("ZS", 0), ("ZP", 3), ("LC", 0), ("XP", 4), ("XP", 2), ("XS", 3),
    ("ZC", 1), ("ZC", 2), ("LD", 0), ("XC", 0), ("XC", 5), ("ZE", 3),
    ("XE", 1), ("XP", 3), ("XC", 4), ("ZC", 0), ("XC", 2), ("ZP", 2),
    ("LF", 0), ("XE", 0), ("BK", 2), ("XC", 3), ("ZP", 1), ("XE", 5),
    ("ZP", 0), ("XE", 4), ("BK", 4), ("ZE", 2), ("BK", 1), ("XE", 2),
    ("XE", 3), ("BK", 3), ("ZE", 1), ("ZE", 0), ("BK", 0), ("N", 0),
]
LATE = [
    ("F", 2), ("XS", 0), ("F", 1), ("ZS", 3), ("FL", 2), ("FL", 1),
    ("XS", 1), ("FL", 4), ("FL", 3), ("FL", 0), ("LA", 0), ("XP", 0),
    ("F", 3), ("XS", 3), ("ZS", 2), ("XP", 1), ("F", 0), ("XS", 2),
    ("ZS", 1), ("ZC", 3), ("LC", 0), ("F", 4), ("XS", 4), ("XP", 2),
    ("XC", 1), ("LD", 0), ("XS", 5), ("XP", 3), ("ZC", 1), ("ZS", 0),
    ("XC", 0), ("XE", 1), ("XP", 4), ("ZC", 2), ("XP", 5), ("ZP", 3),
    ("XC", 2), ("LF", 0), ("ZP", 1), ("XC", 3), ("ZC", 0), ("ZP", 2),
    ("XE", 0), ("BK", 2), ("XC", 4), ("XE", 2), ("XC", 5), ("XE", 3),
    ("ZP", 0), ("N", 0), ("BK", 3), ("XE", 4), ("ZE", 3), ("ZE", 2),
    ("BK", 1), ("ZE", 1), ("XE", 5), ("BK", 4), ("ZE", 0), ("BK", 0),
]


def kernel(
    grads, momentum, wide_hbm, back_hbm, new_out, upd_out,
    xin, mom, wide, back, sx, sz, lw,
    xr2, xab, xrz, zr4, zr2, zab,
    la, lc, le, es, total, nm, up,
    load_sem, store_sem, send_sem, recv_sem, column_sem, stack_sem,
):
    rep, fsdp = lax.axis_index("rep"), lax.axis_index("fsdp")
    core, y, zh = lax.rem(rep, 2), lax.rem(lax.div(rep, 2), 4), lax.div(rep, 8)
    x, z = lax.rem(fsdp, 4), lax.div(fsdp, 4)

    def ring(v, d):
        return lax.rem(v + (d + 4), 4)

    xs, ys, zs = ([v] + [ring(v, d) for d in (1, 2, 3)] for v in (x, y, zh))
    other_core, other_z = 1 - core, 1 - z
    own_rep, own_fsdp = rep, fsdp
    places = {}

    def device(dzh=0, dy=0, dcore=0, dz=0, dx=0):
        key = (dzh, dy % 4, dcore, dz, dx % 4)
        if key not in places:
            c2, z2 = other_core if dcore else core, other_z if dz else z
            moved = dzh or dy or dcore
            r2 = (zs[dzh] * 4 + ys[dy % 4]) * 2 + c2 if moved else own_rep
            places[key] = (r2, z2 * 4 + xs[dx % 4] if dz or dx else own_fsdp)
        return places[key]

    for dy in range(4):
        for dc in range(2):
            device(dy=dy, dcore=dc)
    for d in range(4):
        for dz in range(2):
            device(dzh=d, dz=dz)
        device(dx=d)

    column = [(dy, dc) for dy in range(4) for dc in range(2) if dy or dc]
    barrier = pltpu.get_barrier_semaphore()

    def greet(sem, p):
        pl.semaphore_signal(sem, inc=1, device_id=p, device_id_type=MESH)

    def later_in_column(dy, dc):
        if dy:
            return ring(y, dy) > y
        return core == 1

    def later_in_stack(d):
        return ring(zh, d) > zh

    def greet_others(sem_of, later):
        def where(test, sem, places):
            @pl.when(test if later else jnp.logical_not(test))
            def _():
                for place in places:
                    greet(sem, place)

        for d in range(4):
            cores = range(2) if d else (1,)
            where(later_in_column(d, 1), sem_of[0], [device(dy=d, dcore=dc) for dc in cores])
        for d in (1, 2, 3):
            where(later_in_stack(d), sem_of[1], [device(dzh=d, dz=dz) for dz in range(2)])

    for d in (1, 2, 3):
        greet(barrier, device(dx=d))
    greet(barrier, device(dz=1))
    column_later = 2 * (3 - y) + core
    stack_later = 2 * (3 - zh)

    def enter():
        pl.semaphore_wait(barrier, 4 + (7 - column_later) + (6 - stack_later))
    def remote(kind, src, dst, to, recv):
        return pltpu.make_async_remote_copy(
            src_ref=src, dst_ref=dst, send_sem=send_sem.at[SENDS.index(kind)],
            recv_sem=recv_sem.at[recv], device_id=to, device_id_type=MESH,
        )

    def send(kind, src, dst, to, recv):
        remote(kind, src, dst, to, recv).start()

    def await_bytes(ref, sem):
        pltpu.make_async_copy(ref, ref, sem).wait()

    def received(ref, recv):
        await_bytes(ref, recv_sem.at[recv])

    def all_sent(kind, ref):
        await_bytes(ref, send_sem.at[SENDS.index(kind)])

    loads = []

    def load(src, dst):
        copy = pltpu.make_async_copy(src, dst, load_sem.at[len(loads)])
        copy.start()
        loads.append(copy)
        return copy

    waited, ready, parts = set(), set(), {}

    def arrived(copy):
        if id(copy) not in waited:
            waited.add(id(copy))
            copy.wait()

    def load_group(g):
        cols = pl.ds(g * SPAN, SPAN)
        return load(momentum.at[:, cols], mom.at[:, cols]), load(grads.at[:, cols], xin.at[pl.ds(0, GRAD), cols])

    order = [g for name, g in EARLY if name == "F"]
    front = pl.ds(0, 7 * 2 * LANES)
    rest = pl.ds(7 * 2 * LANES, SPAN)
    group_loads = {order[0]: load_group(order[0])}
    load_wide = load(wide_hbm.at[front], wide.at[front])
    load_rest = []
    greet_others((barrier, barrier), True)

    def load_others():
        for g in order[1:]:
            group_loads[g] = load_group(g)
        load_rest.append(load(wide_hbm.at[rest], wide.at[rest]))
        load_rest.append(load(back_hbm, back))

    def prepare(g):
        if g not in ready:
            ready.add(g)
            for copy in group_loads[g]:
                copy.wait()
            cols = slice(g * SPAN, (g + 1) * SPAN)
            top, low_part = halves(BETA * mom[:, cols])
            xin[GRAD : GRAD + MINE, cols] = top
            xin[GRAD + MINE :, cols] = low_part

    def fold(v, count=2):
        v = v[:, :LANES] + v[:, LANES:]
        rows, mine = count * GRAD // 2, count * MINE // 2
        own = v[rows : rows + mine] + v[rows + mine :]
        return v[:rows].reshape(2 * count, NZL, NX, OWN, LANES), own.reshape(2 * count, OWN, LANES)

    def forward_rows(g, parts_of):
        base = g * SPAN

        def rows(start):
            cols = slice(base + start, base + start + LANES)
            if len(parts_of) == 2:
                return xin[:, cols]
            h, n, k = parts_of[0], GRAD // 2, MINE // 2
            spans = [(h * n, n), (GRAD + h * k, k), (GRAD + MINE + h * k, k)]
            return jnp.concatenate([xin[at : at + size, cols] for at, size in spans], axis=0)

        last = rows(HIGH)
        for t in range(7):
            both = jnp.concatenate([rows(t * LANES), last], axis=1)
            value, own = fold(dot(both, wide[t * 2 * LANES : (t + 1) * 2 * LANES]), len(parts_of))
            lanes = slice(t * LANES, (t + 1) * LANES)
            for i, h in enumerate(parts_of):
                mats = slice(2 * i, 2 * i + 2)
                if (g, 2 * h) in X_UNITS:
                    u = X_UNITS.index((g, 2 * h))
                    for m in range(2):
                        for k in range(NZL):
                            sx[u, :, k, m, :, lanes] = value[2 * i + m, k]
                    sx[u, x, z, :, :, lanes] += own[mats]
                else:
                    u = Z_UNITS.index((g, 2 * h))
                    for m in range(2):
                        for k in range(NZL):
                            sz[u, k, :, m, :, lanes] = value[2 * i + m, k]
                    sz[u, z, x, :, :, lanes] += own[mats]

    def forward(g):
        prepare(g)
        forward_rows(g, (0, 1))

    def forward_low(g):
        prepare(g)
        arrived(load_rest[0])
        value, own = fold(dot(xin[:, g * SPAN : (g + 1) * SPAN], wide[7 * 2 * LANES :]))
        lanes = slice(g * LANES, (g + 1) * LANES)
        lw[:, :, :, :, lanes] = value
        lw[:, z, x, :, lanes] += own

    way = lambda u: 1 if u % 2 == 0 else -1
    z_way = lambda u: -way(u)
    nx, nz = len(X_UNITS), len(Z_UNITS)
    X2, XAB, XZ = 0, nx, 2 * nx
    Z4, Z2, ZAB = 3 * nx, 3 * nx + nz, 3 * nx + 2 * nz
    LOW_A = 3 * nx + 3 * nz
    LOW_C, LOW_D, LOW_F = LOW_A + 1, LOW_A + 2, LOW_A + 3

    def x_start(u):
        d = way(u)
        send("x2", sx.at[u, xs[2]], xr2.at[u], device(dx=d), X2 + u)
        send("xa", sx.at[u, xs[-d]], xab.at[u, 0], device(dx=-d), XAB + u)

    def x_pass(u):
        d = way(u)
        received(xr2.at[u], X2 + u)
        sx[u, xs[d]] += xr2[u]
        send("xb", sx.at[u, xs[d]], xab.at[u, 1], device(dx=d), XAB + u)

    def x_cross(u):
        received(xab.at[u], XAB + u)
        sx[u, x] += xab[u, 0] + xab[u, 1]
        send("xz", sx.at[u, x, other_z], xrz.at[u], device(dz=1), XZ + u)

    def z_start(u):
        send("z4", sz.at[u, other_z], zr4.at[u], device(dz=1), Z4 + u)

    def z_cross(u):
        d = z_way(u)
        received(zr4.at[u], Z4 + u)
        sz[u, z] += zr4[u]
        send("z2", sz.at[u, z, xs[2]], zr2.at[u], device(dx=d), Z2 + u)
        send("za", sz.at[u, z, xs[-d]], zab.at[u, 0], device(dx=-d), ZAB + u)

    def z_pass(u):
        d = z_way(u)
        received(zr2.at[u], Z2 + u)
        sz[u, z, xs[d]] += zr2[u]
        send("zb", sz.at[u, z, xs[d]], zab.at[u, 1], device(dx=d), ZAB + u)

    def x_end(u):
        received(xrz.at[u], XZ + u)
        parts[X_UNITS[u]] = sx[u, x, z] + xrz[u]

    def z_end(u):
        received(zab.at[u], ZAB + u)
        parts[Z_UNITS[u]] = sz[u, z, x] + (zab[u, 0] + zab[u, 1])

    stores = []

    def store(src, dst):
        copy = pltpu.make_async_copy(src, dst, store_sem.at[len(stores)])
        copy.start()
        stores.append(copy)

    def backward(g):
        arrived(load_rest[1])
        field = jnp.concatenate([parts[k] for k in sorted(parts) if k[0] == g], axis=0).reshape(MINE, HIGH)
        last = jnp.zeros((MINE, LANES), F32)
        for t in range(7):
            top, rest = halves(field[:, t * LANES : (t + 1) * LANES])
            v = dot(jnp.concatenate([top, rest], axis=0), back[t * LANES : (t + 1) * LANES])
            v = v[:MINE, : 2 * LANES] + (v[MINE:, : 2 * LANES] + v[:MINE, 2 * LANES :])
            base = g * SPAN + t * LANES
            nm[:, base : base + LANES] = v[:, :LANES]
            last += v[:, LANES:]
        nm[:, g * SPAN + HIGH : (g + 1) * SPAN] = last
        cols = pl.ds(g * SPAN, SPAN)
        store(nm.at[:, cols], new_out.at[:, cols])

    def low_a(_):
        @pl.when(column_later > 0)
        def _():
            pl.semaphore_wait(column_sem, column_later)

        for k, (dy, dc) in enumerate(column):
            send("la", lw.at[ys[dy], other_core if dc else core], la.at[k], device(dy=dy, dcore=dc), LOW_A)

    def low_d(_):
        received(la, LOW_A)
        lw[y, core] += ((la[0] + la[1]) + (la[2] + la[3])) + ((la[4] + la[5]) + la[6])
        for d in (1, 2, 3):
            send("lc", lw.at[y, core, xs[d]], lc.at[d - 1], device(dx=d), LOW_C)

    def low_e(_):
        received(lc, LOW_C)
        es[...] = lw[y, core, x] + (lc[0] + lc[1] + lc[2])

        @pl.when(stack_later > 0)
        def _():
            pl.semaphore_wait(stack_sem, stack_later)

        @pl.when(core == z)
        def _():
            for d in (1, 2, 3):
                send("ld", es, le.at[d - 1], device(dzh=d), LOW_D)

        @pl.when(core != z)
        def _():
            for d in range(4):
                send("ld", es, le.at[3 + d], device(dzh=d, dz=1), LOW_D)

    def low_i(_):
        @pl.when(core == z)
        def _():
            received(le, LOW_D)
            total[y] = es[...] + ((le[0] + le[1] + le[2]) + (le[3] + le[4] + le[5] + le[6]))
            for dy, dc in column:
                send("lf", total.at[y], total.at[y], device(dy=dy, dcore=dc), LOW_F)

    def low_end():
        arrived(load_rest[1])

        @pl.when(core == z)
        def _():
            received(total.at[pl.ds(0, 3)], LOW_F)

        @pl.when(core != z)
        def _():
            received(total, LOW_F)

    def normalise(_):
        low_end()
        table = lambda i: back[(7 + i) * LANES : (8 + i) * LANES]
        count = GROUPS * MINE
        mean = jnp.concatenate(
            [total[:, :, g * LANES : (g + 1) * LANES].reshape(MINE, LANES) for g in range(GROUPS)], axis=0
        ) * (1.0 / N_REP)
        top, rest = halves(mean)
        pair = jnp.concatenate([top, rest], axis=0)
        squares = jnp.concatenate(halves(mean * mean), axis=0)
        for h in range(2):
            v, w = dot(pair, table(h)), dot(squares, table(4 + h))
            field = v[:count] + (v[count:] + dot(top, table(2 + h)))
            square = w[:count] + w[count:]
            value = field * lax.rsqrt(field * field + square + EPS)
            for g in range(GROUPS):
                base = g * SPAN + h * WIDE
                up[:, base : base + WIDE] = value[g * MINE : (g + 1) * MINE]
        store(up, upd_out)

    steps = {
        "F": forward, "FL": forward_low,
        "XS": x_start, "XP": x_pass, "XC": x_cross, "XE": x_end,
        "ZS": z_start, "ZC": z_cross, "ZP": z_pass, "ZE": z_end,
        "LA": low_a, "LC": low_d, "LD": low_e, "LF": low_i,
        "N": normalise, "BK": backward,
    }
    first = EARLY[0][1]
    prepare(first)
    arrived(load_wide)
    load_others()
    before = set(ready), set(waited)

    def run(plan):
        ready.clear()
        ready.update(before[0])
        waited.clear()
        waited.update(before[1])
        parts.clear()
        stores.clear()
        answered = False
        half = X_UNITS[plan[1][1]][1] // 2
        forward_rows(first, (half,))
        enter()
        for name, u in plan[1:]:
            if not answered and name not in ("XS", "ZS"):
                greet_others((column_sem, stack_sem), False)
                answered = True
            steps[name](u)
            if (name, u) == plan[1]:
                forward_rows(first, (1 - half,))
        all_sent("x2", xr2)
        all_sent("xa", xr2)
        all_sent("xb", xr2)
        all_sent("xz", xrz)
        all_sent("z4", zr4)
        all_sent("z2", zr2)
        all_sent("za", zr2)
        all_sent("zb", zr2)
        all_sent("la", la)
        all_sent("lc", lc)

        @pl.when(core != z)
        def _():
            all_sent("ld", le.at[pl.ds(0, 4)])

        @pl.when(core == z)
        def _():
            all_sent("ld", le.at[pl.ds(0, 3)])
            all_sent("lf", le)

        for copy in stores:
            copy.wait()

    @pl.when(zh == 0)
    def _():
        run(EARLY)

    @pl.when(zh > 0)
    def _():
        run(LATE)


def write_out(new_in, upd_in, new_out, upd_out, sems):
    copies = []
    for k, (src, dst) in enumerate([(new_in, new_out), (upd_in, upd_out)]):
        for m in range(MATS):
            rows = pl.ds(m * OWN, OWN)
            copies.append(pltpu.make_async_copy(src.at[rows], dst.at[rows], sems.at[k, m]))
    for copy in copies:
        copy.start()
    for copy in copies:
        copy.wait()


def per_device(gradients, momentum):
    wide, back = tables()
    anywhere = pl.BlockSpec(memory_space=pl.ANY)
    new_momentum, update = pl.pallas_call(
        kernel,
        out_shape=[jax.ShapeDtypeStruct((MINE, D), F32)] * 2,
        in_specs=[anywhere] * 4,
        out_specs=[anywhere] * 2,
        scratch_shapes=[
            pltpu.VMEM((GRAD + 2 * MINE, D), BF16),
            pltpu.VMEM((MINE, D), F32),
            pltpu.VMEM(wide.shape, BF16),
            pltpu.VMEM(back.shape, BF16),
            pltpu.VMEM((len(X_UNITS), NX, NZL, 2, OWN, HIGH), F32),
            pltpu.VMEM((len(Z_UNITS), NZL, NX, 2, OWN, HIGH), F32),
            pltpu.VMEM((MATS, NZL, NX, OWN, LOW), F32),
            pltpu.VMEM((len(X_UNITS), NZL, 2, OWN, HIGH), F32),
            pltpu.VMEM((len(X_UNITS), 2, NZL, 2, OWN, HIGH), F32),
            pltpu.VMEM((len(X_UNITS), 2, OWN, HIGH), F32),
            pltpu.VMEM((len(Z_UNITS), NX, 2, OWN, HIGH), F32),
            pltpu.VMEM((len(Z_UNITS), 2, OWN, HIGH), F32),
            pltpu.VMEM((len(Z_UNITS), 2, 2, OWN, HIGH), F32),
            pltpu.VMEM((7, NX, OWN, LOW), F32),
            pltpu.VMEM((3, OWN, LOW), F32),
            pltpu.VMEM((7, OWN, LOW), F32),
            pltpu.VMEM((OWN, LOW), F32),
            pltpu.VMEM((MATS, OWN, LOW), F32),
            pltpu.VMEM((MINE, D), F32),
            pltpu.VMEM((MINE, D), F32),
            pltpu.SemaphoreType.DMA((2 * GROUPS + 3,)),
            pltpu.SemaphoreType.DMA((GROUPS + 1,)),
            pltpu.SemaphoreType.DMA((len(SENDS),)),
            pltpu.SemaphoreType.DMA((3 * len(X_UNITS) + 3 * len(Z_UNITS) + 4,)),
            pltpu.SemaphoreType.REGULAR,
            pltpu.SemaphoreType.REGULAR,
        ],
        compiler_params=pltpu.CompilerParams(
            collective_id=0, has_side_effects=True, vmem_limit_bytes=(52 * 1024 + 384) * 1024
        ),
        cost_estimate=pl.CostEstimate(flops=2_000_000_000, bytes_accessed=8_000_000, transcendentals=200_000),
    )(gradients.reshape(GRAD, D), momentum.reshape(MINE, D), wide, back)
    new_momentum, update = pl.pallas_call(
        write_out,
        out_shape=[jax.ShapeDtypeStruct((MINE, D), F32)] * 2,
        in_specs=[anywhere] * 2,
        out_specs=[anywhere] * 2,
        scratch_shapes=[pltpu.SemaphoreType.DMA((2, 4))],
        compiler_params=pltpu.CompilerParams(vmem_limit_bytes=4 * 1024 * 1024),
        cost_estimate=pl.CostEstimate(flops=0, bytes_accessed=2_600_000, transcendentals=0),
    )(new_momentum, update)
    return new_momentum.reshape(1, MATS, OWN, D), update.reshape(MATS, OWN, D)


def solution(mesh):
    return jax.shard_map(
        per_device,
        mesh=mesh,
        in_specs=(P("rep", "fsdp", None, None, None), P("rep", None, "fsdp", None)),
        out_specs=(P("rep", None, "fsdp", None), P(None, "fsdp", None)),
        check_vma=False,
    )
```

```python
import jax
import jax.numpy as jnp
import ml_dtypes
import numpy as np
from jax import lax
from jax.experimental import pallas as pl
from jax.experimental.pallas import tpu as pltpu
from jax.sharding import PartitionSpec as P

D, MATS, GROUP, KEEP, ROWS = 5120, 4, 64, 8, 64
BETA, EPS = 0.999, 1e-06
NX, NY, NZL, NZH, NC, N_REP = 4, 4, 2, 4, 2, 32
OWN = 8
LANES = 128
TILES = 8
SPAN = LANES * TILES
GROUPS = D // SPAN
HIGH = 7 * LANES
LOW = GROUPS * LANES
GRAD = MATS * ROWS
MINE = MATS * OWN
WIDE = 4 * LANES

F32, BF16 = jnp.float32, jnp.bfloat16
MESH = pl.DeviceIdType.MESH


def split(table):
    high = table.astype(ml_dtypes.bfloat16)
    low = (table - high.astype(np.float64)).astype(ml_dtypes.bfloat16)
    return high, low


def tables():
    n, k = np.arange(GROUP), np.arange(GROUP)[:, None]
    basis = np.sqrt(2.0 / GROUP) * np.cos(np.pi * (n + 0.5) * k / GROUP)
    basis[0] *= np.sqrt(0.5)
    rest = GROUP - KEEP
    high = np.zeros((LANES, 2 * rest))
    for b in range(2):
        high[b * GROUP : (b + 1) * GROUP, b * rest : (b + 1) * rest] = basis[KEEP:].T
    forward = np.zeros((7, 2 * LANES, LANES))
    for t in range(7):
        forward[t, :LANES, : 2 * rest] = high
        forward[t, LANES:, 2 * rest :] = high[:, 16 * t : 16 * t + 16]
    inverse = np.zeros((7, LANES, 2 * LANES))
    for t in range(7):
        inverse[t] = forward[t].T
    blocks = SPAN // GROUP
    keep = np.zeros((SPAN, LANES))
    mean = np.zeros((LANES, SPAN))
    for c in range(blocks):
        keep[c * GROUP : (c + 1) * GROUP, c * KEEP : (c + 1) * KEEP] = basis[:KEEP].T
        mean[c * KEEP : (c + 1) * KEEP, c * GROUP : (c + 1) * GROUP] = 1.0 / GROUP
    both = lambda table: np.concatenate(split(table), axis=-1)
    wide = np.concatenate([both(forward).reshape(-1, 2 * LANES), both(keep)], axis=0)
    back = np.concatenate([both(keep.T), mean.astype(ml_dtypes.bfloat16)], axis=-1)
    back = back.reshape(LANES, 6, WIDE).transpose(1, 0, 2).reshape(-1, WIDE)
    return wide, np.concatenate([both(inverse).reshape(-1, WIDE), back], axis=0)


def halves(value):
    top = value.astype(BF16)
    return top, (value - top.astype(F32)).astype(BF16)


def dot(a, b):
    return jnp.dot(a, b, preferred_element_type=F32)


X_UNITS = [(2, 0), (2, 2), (3, 0), (3, 2), (4, 0), (4, 2)]
Z_UNITS = [(0, 0), (0, 2), (1, 0), (1, 2)]
SENDS = ["x2", "xa", "xb", "xz", "z4", "z2", "za", "zb", "la", "lc", "ld", "lf"]
EARLY = [
    ("F", 2), ("XS", 1), ("F", 1), ("ZS", 3), ("FL", 1), ("XS", 0),
    ("F", 4), ("FL", 2), ("ZS", 2), ("XS", 4), ("FL", 4), ("FL", 0),
    ("FL", 3), ("LA", 0), ("XS", 5), ("F", 0), ("XP", 1), ("XP", 0),
    ("ZS", 1), ("F", 3), ("ZC", 3), ("XS", 2), ("XC", 1), ("XP", 5),
    ("ZS", 0), ("ZP", 3), ("LC", 0), ("XP", 4), ("XP", 2), ("XS", 3),
    ("ZC", 1), ("ZC", 2), ("LD", 0), ("XC", 0), ("XC", 5), ("ZE", 3),
    ("XE", 1), ("XP", 3), ("XC", 4), ("ZC", 0), ("XC", 2), ("ZP", 2),
    ("LF", 0), ("XE", 0), ("BK", 2), ("XC", 3), ("ZP", 1), ("XE", 5),
    ("ZP", 0), ("XE", 4), ("BK", 4), ("ZE", 2), ("BK", 1), ("XE", 2),
    ("XE", 3), ("BK", 3), ("N", 0), ("ZE", 1), ("ZE", 0), ("BK", 0),
]
LATE = [
    ("F", 2), ("XS", 0), ("F", 1), ("ZS", 3), ("FL", 2), ("FL", 1),
    ("XS", 1), ("FL", 4), ("FL", 3), ("FL", 0), ("LA", 0), ("XP", 0),
    ("F", 3), ("XS", 3), ("ZS", 2), ("XP", 1), ("F", 0), ("XS", 2),
    ("ZS", 1), ("ZC", 3), ("LC", 0), ("F", 4), ("XS", 4), ("XP", 2),
    ("XC", 1), ("LD", 0), ("XS", 5), ("XP", 3), ("ZC", 1), ("ZS", 0),
    ("XC", 0), ("XE", 1), ("XP", 4), ("ZC", 2), ("XP", 5), ("ZP", 3),
    ("XC", 2), ("LF", 0), ("ZP", 1), ("XC", 3), ("ZC", 0), ("ZP", 2),
    ("XE", 0), ("BK", 2), ("XC", 4), ("XE", 2), ("XC", 5), ("XE", 3),
    ("ZP", 0), ("N", 0), ("BK", 3), ("XE", 4), ("ZE", 3), ("ZE", 2),
    ("BK", 1), ("ZE", 1), ("XE", 5), ("BK", 4), ("ZE", 0), ("BK", 0),
]


def kernel(
    grads, momentum, wide_hbm, back_hbm, new_out, upd_out,
    xin, mom, wide, back, sx, sz, lw,
    xr2, xab, xrz, zr4, zr2, zab,
    la, lc, le, es, total, nm, up,
    load_sem, store_sem, send_sem, recv_sem, column_sem, stack_sem,
):
    rep, fsdp = lax.axis_index("rep"), lax.axis_index("fsdp")
    core, y, zh = lax.rem(rep, 2), lax.rem(lax.div(rep, 2), 4), lax.div(rep, 8)
    x, z = lax.rem(fsdp, 4), lax.div(fsdp, 4)

    def ring(v, d):
        return lax.rem(v + (d + 4), 4)

    xs, ys, zs = ([v] + [ring(v, d) for d in (1, 2, 3)] for v in (x, y, zh))
    other_core, other_z = 1 - core, 1 - z
    own_rep, own_fsdp = rep, fsdp
    places = {}

    def device(dzh=0, dy=0, dcore=0, dz=0, dx=0):
        key = (dzh, dy % 4, dcore, dz, dx % 4)
        if key not in places:
            c2, z2 = other_core if dcore else core, other_z if dz else z
            moved = dzh or dy or dcore
            r2 = (zs[dzh] * 4 + ys[dy % 4]) * 2 + c2 if moved else own_rep
            places[key] = (r2, z2 * 4 + xs[dx % 4] if dz or dx else own_fsdp)
        return places[key]

    for dy in range(4):
        for dc in range(2):
            device(dy=dy, dcore=dc)
    for d in range(4):
        for dz in range(2):
            device(dzh=d, dz=dz)
        device(dx=d)

    column = [(dy, dc) for dy in range(4) for dc in range(2) if dy or dc]
    barrier = pltpu.get_barrier_semaphore()

    def greet(sem, p):
        pl.semaphore_signal(sem, inc=1, device_id=p, device_id_type=MESH)

    def later_in_column(dy, dc):
        if dy:
            return ring(y, dy) > y
        return core == 1

    def later_in_stack(d):
        return ring(zh, d) > zh

    def greet_others(sem_of, later):
        def where(test, sem, places):
            @pl.when(test if later else jnp.logical_not(test))
            def _():
                for place in places:
                    greet(sem, place)

        for d in range(4):
            cores = range(2) if d else (1,)
            where(later_in_column(d, 1), sem_of[0], [device(dy=d, dcore=dc) for dc in cores])
        for d in (1, 2, 3):
            where(later_in_stack(d), sem_of[1], [device(dzh=d, dz=dz) for dz in range(2)])

    for d in (1, 2, 3):
        greet(barrier, device(dx=d))
    greet(barrier, device(dz=1))
    column_later = 2 * (3 - y) + core
    stack_later = 2 * (3 - zh)

    def enter():
        pl.semaphore_wait(barrier, 4 + (7 - column_later) + (6 - stack_later))
    def remote(kind, src, dst, to, recv):
        return pltpu.make_async_remote_copy(
            src_ref=src, dst_ref=dst, send_sem=send_sem.at[SENDS.index(kind)],
            recv_sem=recv_sem.at[recv], device_id=to, device_id_type=MESH,
        )

    def send(kind, src, dst, to, recv):
        remote(kind, src, dst, to, recv).start()

    def await_bytes(ref, sem):
        pltpu.make_async_copy(ref, ref, sem).wait()

    def received(ref, recv):
        await_bytes(ref, recv_sem.at[recv])

    def all_sent(kind, ref):
        await_bytes(ref, send_sem.at[SENDS.index(kind)])

    loads = []

    def load(src, dst):
        copy = pltpu.make_async_copy(src, dst, load_sem.at[len(loads)])
        copy.start()
        loads.append(copy)
        return copy

    waited, ready, parts = set(), set(), {}

    def arrived(copy):
        if id(copy) not in waited:
            waited.add(id(copy))
            copy.wait()

    def load_group(g):
        cols = pl.ds(g * SPAN, SPAN)
        return load(momentum.at[:, cols], mom.at[:, cols]), load(grads.at[:, cols], xin.at[pl.ds(0, GRAD), cols])

    order = [g for name, g in EARLY if name == "F"]
    front = pl.ds(0, 7 * 2 * LANES)
    rest = pl.ds(7 * 2 * LANES, SPAN)
    group_loads = {order[0]: load_group(order[0])}
    load_wide = load(wide_hbm.at[front], wide.at[front])
    load_rest = []
    greet_others((barrier, barrier), True)

    def load_others():
        for g in order[1:]:
            group_loads[g] = load_group(g)
        load_rest.append(load(wide_hbm.at[rest], wide.at[rest]))
        load_rest.append(load(back_hbm, back))

    def prepare(g):
        if g not in ready:
            ready.add(g)
            for copy in group_loads[g]:
                copy.wait()
            cols = slice(g * SPAN, (g + 1) * SPAN)
            top, low_part = halves(BETA * mom[:, cols])
            xin[GRAD : GRAD + MINE, cols] = top
            xin[GRAD + MINE :, cols] = low_part

    def fold(v, count=2):
        v = v[:, :LANES] + v[:, LANES:]
        rows, mine = count * GRAD // 2, count * MINE // 2
        own = v[rows : rows + mine] + v[rows + mine :]
        return v[:rows].reshape(2 * count, NZL, NX, OWN, LANES), own.reshape(2 * count, OWN, LANES)

    def forward_rows(g, parts_of):
        base = g * SPAN

        def rows(start):
            cols = slice(base + start, base + start + LANES)
            if len(parts_of) == 2:
                return xin[:, cols]
            h, n, k = parts_of[0], GRAD // 2, MINE // 2
            spans = [(h * n, n), (GRAD + h * k, k), (GRAD + MINE + h * k, k)]
            return jnp.concatenate([xin[at : at + size, cols] for at, size in spans], axis=0)

        last = rows(HIGH)
        for t in range(7):
            both = jnp.concatenate([rows(t * LANES), last], axis=1)
            value, own = fold(dot(both, wide[t * 2 * LANES : (t + 1) * 2 * LANES]), len(parts_of))
            lanes = slice(t * LANES, (t + 1) * LANES)
            for i, h in enumerate(parts_of):
                mats = slice(2 * i, 2 * i + 2)
                if (g, 2 * h) in X_UNITS:
                    u = X_UNITS.index((g, 2 * h))
                    for m in range(2):
                        for k in range(NZL):
                            sx[u, :, k, m, :, lanes] = value[2 * i + m, k]
                    sx[u, x, z, :, :, lanes] += own[mats]
                else:
                    u = Z_UNITS.index((g, 2 * h))
                    for m in range(2):
                        for k in range(NZL):
                            sz[u, k, :, m, :, lanes] = value[2 * i + m, k]
                    sz[u, z, x, :, :, lanes] += own[mats]

    def forward(g):
        prepare(g)
        forward_rows(g, (0, 1))

    def forward_low(g):
        prepare(g)
        arrived(load_rest[0])
        value, own = fold(dot(xin[:, g * SPAN : (g + 1) * SPAN], wide[7 * 2 * LANES :]))
        lanes = slice(g * LANES, (g + 1) * LANES)
        lw[:, :, :, :, lanes] = value
        lw[:, z, x, :, lanes] += own

    way = lambda u: 1 if u % 2 == 0 else -1
    z_way = lambda u: -way(u)
    nx, nz = len(X_UNITS), len(Z_UNITS)
    X2, XAB, XZ = 0, nx, 2 * nx
    Z4, Z2, ZAB = 3 * nx, 3 * nx + nz, 3 * nx + 2 * nz
    LOW_A = 3 * nx + 3 * nz
    LOW_C, LOW_D, LOW_F = LOW_A + 1, LOW_A + 2, LOW_A + 3

    def x_start(u):
        d = way(u)
        send("x2", sx.at[u, xs[2]], xr2.at[u], device(dx=d), X2 + u)
        send("xa", sx.at[u, xs[-d]], xab.at[u, 0], device(dx=-d), XAB + u)

    def x_pass(u):
        d = way(u)
        received(xr2.at[u], X2 + u)
        sx[u, xs[d]] += xr2[u]
        send("xb", sx.at[u, xs[d]], xab.at[u, 1], device(dx=d), XAB + u)

    def x_cross(u):
        received(xab.at[u], XAB + u)
        sx[u, x] += xab[u, 0] + xab[u, 1]
        send("xz", sx.at[u, x, other_z], xrz.at[u], device(dz=1), XZ + u)

    def z_start(u):
        send("z4", sz.at[u, other_z], zr4.at[u], device(dz=1), Z4 + u)

    def z_cross(u):
        d = z_way(u)
        received(zr4.at[u], Z4 + u)
        sz[u, z] += zr4[u]
        send("z2", sz.at[u, z, xs[2]], zr2.at[u], device(dx=d), Z2 + u)
        send("za", sz.at[u, z, xs[-d]], zab.at[u, 0], device(dx=-d), ZAB + u)

    def z_pass(u):
        d = z_way(u)
        received(zr2.at[u], Z2 + u)
        sz[u, z, xs[d]] += zr2[u]
        send("zb", sz.at[u, z, xs[d]], zab.at[u, 1], device(dx=d), ZAB + u)

    def x_end(u):
        received(xrz.at[u], XZ + u)
        parts[X_UNITS[u]] = sx[u, x, z] + xrz[u]

    def z_end(u):
        received(zab.at[u], ZAB + u)
        parts[Z_UNITS[u]] = sz[u, z, x] + (zab[u, 0] + zab[u, 1])

    stores = []

    def store(src, dst):
        copy = pltpu.make_async_copy(src, dst, store_sem.at[len(stores)])
        copy.start()
        stores.append(copy)

    def backward(g):
        arrived(load_rest[1])
        field = jnp.concatenate([parts[k] for k in sorted(parts) if k[0] == g], axis=0).reshape(MINE, HIGH)
        last = jnp.zeros((MINE, LANES), F32)
        for t in range(7):
            top, rest = halves(field[:, t * LANES : (t + 1) * LANES])
            v = dot(jnp.concatenate([top, rest], axis=0), back[t * LANES : (t + 1) * LANES])
            v = v[:MINE, : 2 * LANES] + (v[MINE:, : 2 * LANES] + v[:MINE, 2 * LANES :])
            base = g * SPAN + t * LANES
            nm[:, base : base + LANES] = v[:, :LANES]
            last += v[:, LANES:]
        nm[:, g * SPAN + HIGH : (g + 1) * SPAN] = last
        cols = pl.ds(g * SPAN, SPAN)
        store(nm.at[:, cols], new_out.at[:, cols])

    def low_a(_):
        @pl.when(column_later > 0)
        def _():
            pl.semaphore_wait(column_sem, column_later)

        for k, (dy, dc) in enumerate(column):
            send("la", lw.at[ys[dy], other_core if dc else core], la.at[k], device(dy=dy, dcore=dc), LOW_A)

    def low_d(_):
        received(la, LOW_A)
        lw[y, core] += ((la[0] + la[1]) + (la[2] + la[3])) + ((la[4] + la[5]) + la[6])
        for d in (1, 2, 3):
            send("lc", lw.at[y, core, xs[d]], lc.at[d - 1], device(dx=d), LOW_C)

    def low_e(_):
        received(lc, LOW_C)
        es[...] = lw[y, core, x] + (lc[0] + lc[1] + lc[2])

        @pl.when(stack_later > 0)
        def _():
            pl.semaphore_wait(stack_sem, stack_later)

        @pl.when(core == z)
        def _():
            for d in (1, 2, 3):
                send("ld", es, le.at[d - 1], device(dzh=d), LOW_D)

        @pl.when(core != z)
        def _():
            for d in range(4):
                send("ld", es, le.at[3 + d], device(dzh=d, dz=1), LOW_D)

    def low_i(_):
        @pl.when(core == z)
        def _():
            received(le, LOW_D)
            total[y] = es[...] + ((le[0] + le[1] + le[2]) + (le[3] + le[4] + le[5] + le[6]))
            for dy, dc in column:
                send("lf", total.at[y], total.at[y], device(dy=dy, dcore=dc), LOW_F)

    def low_end():
        arrived(load_rest[1])

        @pl.when(core == z)
        def _():
            received(total.at[pl.ds(0, 3)], LOW_F)

        @pl.when(core != z)
        def _():
            received(total, LOW_F)

    def normalise(_):
        low_end()
        table = lambda i: back[(7 + i) * LANES : (8 + i) * LANES]
        count = GROUPS * MINE
        mean = jnp.concatenate(
            [total[:, :, g * LANES : (g + 1) * LANES].reshape(MINE, LANES) for g in range(GROUPS)], axis=0
        ) * (1.0 / N_REP)
        top, rest = halves(mean)
        pair = jnp.concatenate([top, rest], axis=0)
        squares = jnp.concatenate(halves(mean * mean), axis=0)
        for h in range(2):
            v, w = dot(pair, table(h)), dot(squares, table(4 + h))
            field = v[:count] + (v[count:] + dot(top, table(2 + h)))
            square = w[:count] + w[count:]
            value = field * lax.rsqrt(field * field + square + EPS)
            for g in range(GROUPS):
                base = g * SPAN + h * WIDE
                up[:, base : base + WIDE] = value[g * MINE : (g + 1) * MINE]
        store(up, upd_out)

    steps = {
        "F": forward, "FL": forward_low,
        "XS": x_start, "XP": x_pass, "XC": x_cross, "XE": x_end,
        "ZS": z_start, "ZC": z_cross, "ZP": z_pass, "ZE": z_end,
        "LA": low_a, "LC": low_d, "LD": low_e, "LF": low_i,
        "N": normalise, "BK": backward,
    }
    first = EARLY[0][1]
    prepare(first)
    arrived(load_wide)
    load_others()
    before = set(ready), set(waited)

    def run(plan):
        ready.clear()
        ready.update(before[0])
        waited.clear()
        waited.update(before[1])
        parts.clear()
        stores.clear()
        answered = False
        half = X_UNITS[plan[1][1]][1] // 2
        forward_rows(first, (half,))
        enter()
        for name, u in plan[1:]:
            if not answered and name not in ("XS", "ZS"):
                greet_others((column_sem, stack_sem), False)
                answered = True
            steps[name](u)
            if (name, u) == plan[1]:
                forward_rows(first, (1 - half,))
        all_sent("x2", xr2)
        all_sent("xa", xr2)
        all_sent("xb", xr2)
        all_sent("xz", xrz)
        all_sent("z4", zr4)
        all_sent("z2", zr2)
        all_sent("za", zr2)
        all_sent("zb", zr2)
        all_sent("la", la)
        all_sent("lc", lc)

        @pl.when(core != z)
        def _():
            all_sent("ld", le.at[pl.ds(0, 4)])

        @pl.when(core == z)
        def _():
            all_sent("ld", le.at[pl.ds(0, 3)])
            all_sent("lf", le)

        for copy in stores:
            copy.wait()

    @pl.when(zh == 0)
    def _():
        run(EARLY)

    @pl.when(zh > 0)
    def _():
        run(LATE)


def write_out(new_in, upd_in, new_out, upd_out, sems):
    copies = []
    for k, (src, dst) in enumerate([(new_in, new_out), (upd_in, upd_out)]):
        for m in range(MATS):
            rows = pl.ds(m * OWN, OWN)
            copies.append(pltpu.make_async_copy(src.at[rows], dst.at[rows], sems.at[k, m]))
    for copy in copies:
        copy.start()
    for copy in copies:
        copy.wait()


def per_device(gradients, momentum):
    wide, back = tables()
    anywhere = pl.BlockSpec(memory_space=pl.ANY)
    new_momentum, update = pl.pallas_call(
        kernel,
        out_shape=[jax.ShapeDtypeStruct((MINE, D), F32)] * 2,
        in_specs=[anywhere] * 4,
        out_specs=[anywhere] * 2,
        scratch_shapes=[
            pltpu.VMEM((GRAD + 2 * MINE, D), BF16),
            pltpu.VMEM((MINE, D), F32),
            pltpu.VMEM(wide.shape, BF16),
            pltpu.VMEM(back.shape, BF16),
            pltpu.VMEM((len(X_UNITS), NX, NZL, 2, OWN, HIGH), F32),
            pltpu.VMEM((len(Z_UNITS), NZL, NX, 2, OWN, HIGH), F32),
            pltpu.VMEM((MATS, NZL, NX, OWN, LOW), F32),
            pltpu.VMEM((len(X_UNITS), NZL, 2, OWN, HIGH), F32),
            pltpu.VMEM((len(X_UNITS), 2, NZL, 2, OWN, HIGH), F32),
            pltpu.VMEM((len(X_UNITS), 2, OWN, HIGH), F32),
            pltpu.VMEM((len(Z_UNITS), NX, 2, OWN, HIGH), F32),
            pltpu.VMEM((len(Z_UNITS), 2, OWN, HIGH), F32),
            pltpu.VMEM((len(Z_UNITS), 2, 2, OWN, HIGH), F32),
            pltpu.VMEM((7, NX, OWN, LOW), F32),
            pltpu.VMEM((3, OWN, LOW), F32),
            pltpu.VMEM((7, OWN, LOW), F32),
            pltpu.VMEM((OWN, LOW), F32),
            pltpu.VMEM((MATS, OWN, LOW), F32),
            pltpu.VMEM((MINE, D), F32),
            pltpu.VMEM((MINE, D), F32),
            pltpu.SemaphoreType.DMA((2 * GROUPS + 3,)),
            pltpu.SemaphoreType.DMA((GROUPS + 1,)),
            pltpu.SemaphoreType.DMA((len(SENDS),)),
            pltpu.SemaphoreType.DMA((3 * len(X_UNITS) + 3 * len(Z_UNITS) + 4,)),
            pltpu.SemaphoreType.REGULAR,
            pltpu.SemaphoreType.REGULAR,
        ],
        compiler_params=pltpu.CompilerParams(
            collective_id=0, has_side_effects=True, vmem_limit_bytes=(52 * 1024 + 384) * 1024
        ),
        cost_estimate=pl.CostEstimate(flops=2_000_000_000, bytes_accessed=8_000_000, transcendentals=200_000),
    )(gradients.reshape(GRAD, D), momentum.reshape(MINE, D), wide, back)
    new_momentum, update = pl.pallas_call(
        write_out,
        out_shape=[jax.ShapeDtypeStruct((MINE, D), F32)] * 2,
        in_specs=[anywhere] * 2,
        out_specs=[anywhere] * 2,
        scratch_shapes=[pltpu.SemaphoreType.DMA((2, 4))],
        compiler_params=pltpu.CompilerParams(vmem_limit_bytes=4 * 1024 * 1024),
        cost_estimate=pl.CostEstimate(flops=0, bytes_accessed=2_600_000, transcendentals=0),
    )(new_momentum, update)
    return new_momentum.reshape(1, MATS, OWN, D), update.reshape(MATS, OWN, D)


def solution(mesh):
    return jax.shard_map(
        per_device,
        mesh=mesh,
        in_specs=(P("rep", "fsdp", None, None, None), P("rep", None, "fsdp", None)),
        out_specs=(P("rep", None, "fsdp", None), P(None, "fsdp", None)),
        check_vma=False,
    )
```
